128 devices in a mesh: row: 32 (over y_hi, z, x), col: 4 (over y_lo, core).
Axes of the slice: x: 4, y: 4 (y_hi: 2, y_lo: 2; y = y_hi * 2 + y_lo), z: 4, core: 2. Of those that a mesh axis runs over, the one named last changes fastest.
Arguments:
- layer_input: bfloat16 [16384, 1088], P('row', 'col'), may hold values from -32 to 32
- first_norm_gain: float32 [1088], P('col'), may hold values from 0.5 to 1.5
- first_norm_bias: float32 [1088], P('col'), may hold values from -1.5 to 1.5
- w_qkv: bfloat16 [1088, 3264], P('row', 'col'), may hold values from -0.7276069 to 0.7276069
- w_out: bfloat16 [1088, 1088], P('col', 'row'), may hold values from -3 to 3
- second_norm_gain: float32 [1088], P('col'), may hold values from 0.5 to 1.5
- second_norm_bias: float32 [1088], P('col'), may hold values from -1.5 to 1.5
- w_up: bfloat16 [1088, 4352], P('row', 'col'), may hold values from -0.1875 to 0.1875
- w_down: bfloat16 [4352, 1088], P('col', 'row'), may hold values from -0.09375 to 0.09375
- gradient_of_output: bfloat16 [16384, 1088], P('row', 'col'), may hold values from -6 to 6
Outputs:
- layer_output: bfloat16 [16384, 1088], P('row', 'col')
- gradient_of_input: float32 [16384, 1088], P('row', 'col')
- first_gain_gradient: float32 [1088], P('col')
- grad_norm1_bias: float32 [1088], P('col')
- grad_w_qkv: float32 [1088, 3264], P('row', 'col')
- grad_w_out: float32 [1088, 1088], P('col', 'row')
- second_gain_gradient: float32 [1088], P('col')
- grad_norm2_bias: float32 [1088], P('col')
- grad_w_up: float32 [1088, 4352], P('row', 'col')
- grad_w_down: float32 [4352, 1088], P('col', 'row')
The draws below stay inside these ranges and needn't reach their ends.
All inputs are finite; a program needn't handle non-finite values.
Results may differ from the reference program's by a relative error of at most 0.025.
Values may be sent and summed in bfloat16 or wider, within the bound.
A program may use at most 128 MiB of HBM per device.

```python
import math
import jax
import jax.numpy as jnp
from jax import lax

HEADS = 17
HEAD_DIM = 64
D = 1088
FF = 4352
SEQ = 2048
TOKENS = 16384


def draw_layer_input(key, part):
    key_first = jax.random.fold_in(key, 11)
    key_second = jax.random.fold_in(key, 12)
    key_third = jax.random.fold_in(key, 13)
    feature = jnp.arange(D).astype(jnp.float32)
    rising = (1.0 + 2.0 * feature / (D - 1)) * jnp.exp(jax.random.uniform(key_second, (D,), jnp.float32, -0.5, 0.5))
    offset = jnp.clip(0.5 * jax.random.normal(key_third, (D,), jnp.float32), -1.5, 1.5)
    fresh_noise = jnp.clip(jax.random.normal(key_first, (TOKENS, D), jnp.float32), -6.0, 6.0)
    return (fresh_noise * rising + offset).astype(jnp.bfloat16)


def draw_w_qkv(key, part):
    base = jnp.clip(jax.random.normal(jax.random.fold_in(key, 21), (D, 3 * D), jnp.float32), -6.0, 6.0) * D ** (-0.5)
    return base.astype(jnp.bfloat16)


def spiked(values, stream_key, source, target, blocks, factor):
    def block_of(axis_at):
        return (jnp.arange(values.shape[axis_at]) // (values.shape[axis_at] // blocks)).reshape((-1,) + (1,) * (values.ndim - 1 - axis_at))

    one_side = jax.random.permutation(stream_key, blocks)[block_of(target)]
    other_side = (block_of(target) + blocks // 2) % blocks
    return jnp.where((block_of(source) == one_side) | (block_of(source) == other_side), factor * values, values)


def steps_of(own_key, extent, pieces, least, top_value):
    level = 1.0
    for axis_at, blocks in pieces:
        heights = jax.random.uniform(jax.random.fold_in(jax.random.fold_in(own_key, 6), axis_at), (blocks,), jnp.float32, least / len(pieces), top_value / len(pieces))
        level = level * jnp.repeat(jnp.exp(heights), extent[axis_at] // blocks).reshape((-1,) + (1,) * (len(extent) - 1 - axis_at))
    return level


def centred(stream_key, extent, deviation, limit, shards=(), held_as=jnp.bfloat16):
    values = deviation * jax.random.normal(stream_key, extent, jnp.float32)
    if shards:
        values = values * steps_of(stream_key, extent, shards, -0.22, 0.18)
    return jnp.clip(values, -limit, limit).astype(held_as)


def bell_draw_with(key, extent, spread, most, split, heavy, kind=jnp.bfloat16):
    drawn = spread * jax.random.normal(key, extent, jnp.float32)
    if split:
        drawn = drawn * steps_of(key, extent, split, -0.22, 0.18)
    return jnp.clip(spiked(drawn, jax.random.fold_in(key, 3), *heavy), -most, most).astype(kind)


def setup_inputs(seed: int = 0) -> dict:
    keys = jax.random.split(jax.random.key(seed), 11)
    layer_input = draw_layer_input(jax.random.fold_in(keys[10], 71), 0)
    first_norm_gain = jnp.clip(1.0 + 0.1 * jax.random.normal(keys[1], (D,), jnp.float32), 0.5, 1.5)
    first_norm_bias = centred(keys[2], (D,), 0.3, 1.5, ((0, 4),), jnp.float32)
    w_qkv = draw_w_qkv(jax.random.fold_in(keys[10], 71), 0)
    w_out = centred(keys[4], (D, D), (max(D // 256, 1)) ** -0.5, 3.0, ((0, 4), (1, 32)))
    second_norm_gain = jnp.clip(1.0 + 0.1 * jax.random.normal(keys[5], (D,), jnp.float32), 0.5, 1.5)
    second_norm_bias = centred(keys[6], (D,), 0.3, 1.5, ((0, 4),), jnp.float32)
    w_up = centred(keys[7], (D, FF), D ** -0.5, 0.1875, ((0, 32), (1, 4)))
    w_down = centred(keys[8], (FF, D), FF ** -0.5, 0.09375, ((0, 4), (1, 32)))
    gradient_of_output = bell_draw_with(keys[9], (TOKENS, D), 1.0, 6.0, ((0, 32), (1, 4)), (0, 1, 32, 2.75))
    return {"layer_input": layer_input, "first_norm_gain": first_norm_gain, "first_norm_bias": first_norm_bias, "w_qkv": w_qkv, "w_out": w_out, "second_norm_gain": second_norm_gain, "second_norm_bias": second_norm_bias, "w_up": w_up, "w_down": w_down, "gradient_of_output": gradient_of_output}


gelu_coef = math.sqrt(2.0 / math.pi)
norm_epsilon = 1e-05

def gelu_value(values):
    tanh_input = gelu_coef * (values + 0.044715 * values * values * values)
    return 0.5 * values * (1.0 + jnp.tanh(tanh_input))

def gelu_slope(values):
    tanh_input = gelu_coef * (values + 0.044715 * values * values * values)
    tanh_value = jnp.tanh(tanh_input)
    return 0.5 * (1.0 + tanh_value) + 0.5 * values * (1.0 - tanh_value * tanh_value) * gelu_coef * (1.0 + 0.134145 * values * values)

def layernorm_apply(value_rows):
    mean_value = lax.optimization_barrier(jnp.mean(value_rows, axis=1, keepdims=True))
    inverse_std = lax.rsqrt(lax.optimization_barrier(jnp.mean(value_rows * value_rows, axis=1, keepdims=True)) - mean_value * mean_value + norm_epsilon)
    return ((value_rows - mean_value) * inverse_std, inverse_std)

def layernorm_reverse(grad_rows, normed, inverse_std, gain_row):
    scaled = grad_rows * gain_row
    first_mean = lax.optimization_barrier(jnp.mean(scaled, axis=1, keepdims=True))
    second_mean = lax.optimization_barrier(jnp.mean(scaled * normed, axis=1, keepdims=True))
    return inverse_std * (scaled - first_mean - normed * second_mean)

def block_scores(query_heads, key_heads, block_start, seq_index):
    scores = jnp.einsum('qhe,khe->hqk', query_heads.astype(jnp.float32), key_heads.astype(jnp.float32)) * HEAD_DIM ** (-0.5)
    query_pos = block_start + jnp.arange(query_heads.shape[0], dtype=jnp.int32)
    key_pos = jnp.arange(key_heads.shape[0], dtype=jnp.int32)
    lowest = jnp.where((seq_index == 0) & (query_pos >= SEQ // 2), SEQ // 2, 0).astype(jnp.int32)
    allowed = ((key_pos[None, :] <= query_pos[:, None]) & (key_pos[None, :] >= lowest[:, None]))[None]
    return (scores, allowed)

def attend_forward(query_heads, key_heads, value_heads, block_start, seq_index):
    scores, allowed = block_scores(query_heads, key_heads, block_start, seq_index)
    masked = jnp.where(allowed, scores, -jnp.inf)
    peak = lax.optimization_barrier(jnp.max(masked, axis=2, keepdims=True))
    log_total = peak + jnp.log(lax.optimization_barrier(jnp.sum(jnp.where(allowed, jnp.exp(masked - peak), 0.0), axis=2, keepdims=True)))
    probs = jnp.where(allowed, jnp.exp(scores - log_total), 0.0).astype(jnp.bfloat16)
    mixed_heads = jnp.einsum('hqk,khe->qhe', probs.astype(jnp.float32), value_heads.astype(jnp.float32))
    return (mixed_heads.astype(jnp.bfloat16), log_total)

def attend_backward(query_heads, key_heads, value_heads, mixed_heads, log_total, grad_mix, block_start, seq_index):
    scores, allowed = block_scores(query_heads, key_heads, block_start, seq_index)
    probs = jnp.where(allowed, jnp.exp(scores - log_total), 0.0).astype(jnp.bfloat16)
    grad_wide = grad_mix.astype(jnp.float32)
    delta = jnp.einsum('qhe,qhe->hq', grad_wide, mixed_heads.astype(jnp.float32))[:, :, None]
    d_value = jnp.einsum('hqk,qhe->khe', probs.astype(jnp.float32), grad_wide)
    d_prob = jnp.einsum('qhe,khe->hqk', grad_wide, value_heads.astype(jnp.float32))
    d_scores = (probs.astype(jnp.float32) * (d_prob - delta)).astype(jnp.bfloat16).astype(jnp.float32)
    d_query = jnp.einsum('hqk,khe->qhe', d_scores, key_heads.astype(jnp.float32)) * HEAD_DIM ** (-0.5)
    d_key = jnp.einsum('hqk,qhe->khe', d_scores, query_heads.astype(jnp.float32)) * HEAD_DIM ** (-0.5)
    return (d_query, d_key, d_value)

def reference(layer_input, first_norm_gain, first_norm_bias, w_qkv, w_out, second_norm_gain, second_norm_bias, w_up, w_down, gradient_of_output):
    total_rows = layer_input.shape[0]
    block_rows = min(512, SEQ)
    block_count = SEQ // block_rows
    seq_count = total_rows // SEQ
    half_seq = SEQ // 2
    starts = jnp.arange(block_count, dtype=jnp.int32) * block_rows
    seq_indices = jnp.arange(seq_count, dtype=jnp.int32)
    sender_block = layer_input.astype(jnp.float32)
    first_centered_input, first_reciprocal_deviation = layernorm_apply(sender_block)
    first_normalized = (first_centered_input * first_norm_gain + first_norm_bias).astype(jnp.bfloat16)
    qkv = jnp.dot(first_normalized, w_qkv, preferred_element_type=jnp.float32).astype(jnp.bfloat16)
    seq_parts = jnp.roll(qkv, half_seq, axis=0).reshape(seq_count, SEQ, 3, HEADS, HEAD_DIM)

    def forward_seq(item):
        seq_part, seq_index = item
        queries = seq_part[:, 0].reshape(block_count, block_rows, HEADS, HEAD_DIM)
        key_heads = seq_part[:, 1]
        value_heads = seq_part[:, 2]

        def one_block(inner):
            return attend_forward(inner[0], key_heads, value_heads, inner[1], seq_index)
        return lax.map(one_block, (queries, starts))
    mixed_all, log_totals = lax.map(forward_seq, (seq_parts, seq_indices))
    attn_mix = jnp.roll(mixed_all.reshape(total_rows, D), -half_seq, axis=0)
    residual_stream = sender_block + jnp.dot(attn_mix, w_out, preferred_element_type=jnp.float32)
    second_centered_input, second_reciprocal_deviation = layernorm_apply(residual_stream)
    second_normalized = (second_centered_input * second_norm_gain + second_norm_bias).astype(jnp.bfloat16)
    pre = jnp.dot(second_normalized, w_up, preferred_element_type=jnp.float32)
    hidden = gelu_value(pre).astype(jnp.bfloat16)
    layer_output = (residual_stream + jnp.dot(hidden, w_down, preferred_element_type=jnp.float32)).astype(jnp.bfloat16)
    d_hidden = jnp.dot(gradient_of_output, w_down.T, preferred_element_type=jnp.float32)
    d_pre = (d_hidden * gelu_slope(pre)).astype(jnp.bfloat16)
    grad_w_down = jnp.dot(hidden.T, gradient_of_output, preferred_element_type=jnp.float32)
    grad_w_up = jnp.dot(second_normalized.T, d_pre, preferred_element_type=jnp.float32)
    second_norm_gradient = jnp.dot(d_pre, w_up.T, preferred_element_type=jnp.float32)
    second_gain_gradient = lax.optimization_barrier(jnp.sum(second_norm_gradient * second_centered_input, axis=0))
    grad_norm2_bias = lax.optimization_barrier(jnp.sum(second_norm_gradient, axis=0))
    residual_gradient = gradient_of_output.astype(jnp.float32) + layernorm_reverse(second_norm_gradient, second_centered_input, second_reciprocal_deviation, second_norm_gain)
    d_resid_b = residual_gradient.astype(jnp.bfloat16)
    grad_w_out = jnp.dot(attn_mix.T, d_resid_b, preferred_element_type=jnp.float32)
    d_mix = jnp.dot(d_resid_b, w_out.T, preferred_element_type=jnp.float32).astype(jnp.bfloat16)
    d_mix_parts = jnp.roll(d_mix, half_seq, axis=0).reshape(seq_count, block_count, block_rows, HEADS, HEAD_DIM)

    def backward_seq(item):
        seq_part, seq_mixed, seq_totals, seq_grad, seq_index = item
        queries = seq_part[:, 0].reshape(block_count, block_rows, HEADS, HEAD_DIM)
        key_heads = seq_part[:, 1]
        value_heads = seq_part[:, 2]

        def one_block(carry, inner_item):
            query_heads, mixed_heads, log_total, grad_mix, block_start = inner_item
            d_query, d_key, d_value = attend_backward(query_heads, key_heads, value_heads, mixed_heads, log_total, grad_mix, block_start, seq_index)
            return ((carry[0] + d_key, carry[1] + d_value), d_query)
        zeros = jnp.zeros((SEQ, HEADS, HEAD_DIM), jnp.float32)
        sums, d_queries = lax.scan(one_block, (zeros, zeros), (queries, seq_mixed, seq_totals, seq_grad, starts))
        return jnp.stack([d_queries.reshape(SEQ, HEADS, HEAD_DIM), sums[0], sums[1]], axis=1)
    d_parts = lax.map(backward_seq, (seq_parts, mixed_all, log_totals, d_mix_parts, seq_indices))
    d_qkv = jnp.roll(d_parts.reshape(total_rows, 3 * D), -half_seq, axis=0).astype(jnp.bfloat16)
    grad_w_qkv = jnp.dot(first_normalized.T, d_qkv, preferred_element_type=jnp.float32)
    first_norm_gradient = jnp.dot(d_qkv, w_qkv.T, preferred_element_type=jnp.float32)
    first_gain_gradient = lax.optimization_barrier(jnp.sum(first_norm_gradient * first_centered_input, axis=0))
    grad_norm1_bias = lax.optimization_barrier(jnp.sum(first_norm_gradient, axis=0))
    gradient_of_input = residual_gradient + layernorm_reverse(first_norm_gradient, first_centered_input, first_reciprocal_deviation, first_norm_gain)
    return (layer_output, gradient_of_input, first_gain_gradient, grad_norm1_bias, grad_w_qkv, grad_w_out, second_gain_gradient, grad_norm2_bias, grad_w_up, grad_w_down)
```

```python
import math

import jax
import jax.numpy as jnp
from jax import lax
from jax.experimental import pallas as pl
from jax.experimental.pallas import tpu as pltpu
from jax.sharding import PartitionSpec as P

HEADS = 17
HEAD_DIM = 64
D = 1088
SEQ = 2048
MAIN = 1024
WIDE = 1152
PACK = 1280
QKV_COLS = 816
QUARTER = 128
MSG = 384
KEYS = 512

gelu_coef = math.sqrt(2.0 / math.pi)
norm_epsilon = 1e-05
masked_score = -1e30
MESH = pl.DeviceIdType.MESH
F32 = jnp.float32
BF16 = jnp.bfloat16
VMEM_LIMIT = 60 * 1024 * 1024
ANY = pl.BlockSpec(memory_space=pl.ANY)

GATHER_ORDERS = (("x", "y", "z"), ("y", "z", "x"), ("z", "x", "y"))
SCATTER_ORDERS = (("z", "y", "x"), ("x", "z", "y"), ("y", "x", "z"))


def dot_nn(a, b):
    return lax.dot_general(a, b, (((1,), (0,)), ((), ())), preferred_element_type=F32)


def dot_nt(a, b):
    return lax.dot_general(a, b, (((1,), (1,)), ((), ())), preferred_element_type=F32)


class Place:
    def __init__(self):
        self.row = lax.axis_index("row")
        self.col = lax.axis_index("col")
        self.at = {
            "x": lax.rem(self.row, 4),
            "z": lax.rem(self.row // 4, 4),
            "y": (self.row // 16) * 2 + self.col // 2,
        }
        self.core = lax.rem(self.col, 2)

    def device(self, at, core):
        return ((at["y"] // 2) * 16 + at["z"] * 4 + at["x"], lax.rem(at["y"], 2) * 2 + core)

    def step(self, axis, distance):
        at = dict(self.at)
        at[axis] = lax.rem(at[axis] + distance + 4, 4)
        return self.device(at, self.core)

    def partner(self):
        return (self.row, self.col + 1 - 2 * self.core)

    def beside(self, distance):
        return (self.row, lax.rem(self.col + distance, 4))

    def neighbours(self):
        found = [self.step(axis, d) for axis in ("x", "y", "z") for d in (1, -1)]
        found.append(self.partner())
        other = lax.rem(self.col // 2 + 1, 2)
        found.append((self.row, other * 2 + 1 - self.core))
        return found


def greet(devices):
    barrier = pltpu.get_barrier_semaphore()
    for device in devices:
        pl.semaphore_signal(barrier, inc=1, device_id=device, device_id_type=MESH)
    pl.semaphore_wait(barrier, len(devices))


def everything():
    return slice(None)


def place_index(fixed):
    if "y" in fixed:
        y_lo, y_hi = lax.rem(fixed["y"], 2), fixed["y"] // 2
    else:
        y_lo, y_hi = everything(), everything()
    return (y_lo, y_hi, fixed.get("z", everything()), fixed.get("x", everything()))


def with_core(index, core):
    return (index[0], core) + tuple(index[1:])


def gather_kernel(
    block0, block1, block2, x_ref, g_ref, v_ref,
    all0, all1, all2, x_out, g_out, v_out,
    send, recv, local, core_send, core_recv, in_send, in_recv, in_local,
):
    me = Place()
    blocks = (block0, block1, block2)
    wholes = (all0, all1, all2)
    greet(me.neighbours())

    def region(piece, stage, value, rows=None):
        order = GATHER_ORDERS[piece]
        fixed = {order[stage]: value}
        for axis in order[stage + 1 :]:
            fixed[axis] = me.at[axis]
        index = with_core(place_index(fixed), me.core)
        if rows is not None:
            index = index + (pl.ds(rows, 16),)
        else:
            index = index + (everything(),)
        return wholes[piece].at[index]

    def remote(source, target, ssem, rsem, device):
        return pltpu.make_async_remote_copy(
            src_ref=source, dst_ref=target, send_sem=ssem, recv_sem=rsem,
            device_id=device, device_id_type=MESH,
        )

    sent = []

    pairs = ((x_ref, x_out), (g_ref, g_out))
    waits = []
    for n, (source, target) in enumerate(pairs):
        own = pltpu.make_async_copy(
            source.at[pl.ds(pl.multiple_of(me.col * QUARTER, QUARTER), QUARTER), :], target.at[me.col], in_local.at[n]
        )
        own.start()
        waits.append(own)
    own = pltpu.make_async_copy(v_ref, v_out.at[me.col], in_local.at[2])
    own.start()
    waits.append(own)
    arrivals = []

    own_copies = []
    for piece in range(3):
        copy = pltpu.make_async_copy(
            blocks[piece], region(piece, 0, me.at[GATHER_ORDERS[piece][0]]), local.at[piece]
        )
        copy.start()
        own_copies.append(copy)

    def begin(piece, stage):
        axis = GATHER_ORDERS[piece][stage]
        mine = region(piece, stage, me.at[axis])
        source = blocks[piece] if stage == 0 else mine
        for n, distance in enumerate((1, -1)):
            copy = remote(
                source, mine, send.at[piece, stage, n], recv.at[piece, stage, n], me.step(axis, distance)
            )
            copy.start()
            sent.append(copy)

    def arrived(piece, stage, n):
        axis = GATHER_ORDERS[piece][stage]
        value = lax.rem(me.at[axis] + (3, 1, 2, 2)[n], 4)
        rows = (None, None, 0, 16)[n]
        there = region(piece, stage, value, rows)
        remote(
            there, there, send.at[piece, stage, n], recv.at[piece, stage, n], me.step(axis, 1)
        ).wait_recv()
        return value

    def forward(piece, stage, n, value):
        axis = GATHER_ORDERS[piece][stage]
        part = region(piece, stage, value, (0, 16)[n])
        copy = remote(
            part, part, send.at[piece, stage, 2 + n], recv.at[piece, stage, 2 + n],
            me.step(axis, (1, -1)[n]),
        )
        copy.start()
        sent.append(copy)

    def share(piece, n, value, rows=None):
        part = region(piece, 2, value, rows)
        copy = remote(part, part, core_send.at[piece, n], core_recv.at[piece, n], me.partner())
        copy.start()
        sent.append(copy)

    for piece in range(3):
        begin(piece, 0)
    for distance in (1, 2, 3):
        peer = me.beside(distance)
        for n, (source, target) in enumerate(pairs):
            copy = remote(
                source.at[pl.ds(pl.multiple_of(peer[1] * QUARTER, QUARTER), QUARTER), :], target.at[me.col],
                in_send.at[n, distance - 1], in_recv.at[n, distance - 1], peer,
            )
            copy.start()
            sent.append(copy)
            arrivals.append(
                remote(
                    source.at[pl.ds(0, QUARTER), :], target.at[lax.rem(me.col + 4 - distance, 4)],
                    in_send.at[n, distance - 1], in_recv.at[n, distance - 1], peer,
                )
            )
        copy = remote(v_ref, v_out.at[me.col], in_send.at[2, distance - 1], in_recv.at[2, distance - 1], peer)
        copy.start()
        sent.append(copy)
        arrivals.append(
            remote(
                v_ref, v_out.at[lax.rem(me.col + 4 - distance, 4)],
                in_send.at[2, distance - 1], in_recv.at[2, distance - 1], peer,
            )
        )
    for copy in own_copies:
        copy.wait()
    for stage in range(3):
        if stage > 0:
            for piece in range(3):
                begin(piece, stage)
        if stage == 2:
            for piece in range(3):
                share(piece, 0, me.at[GATHER_ORDERS[piece][2]])
        for n in range(2):
            for piece in range(3):
                value = arrived(piece, stage, n)
                forward(piece, stage, n, value)
                if stage == 2:
                    share(piece, 1 + n, value)
        for n in (2, 3):
            for piece in range(3):
                value = arrived(piece, stage, n)
                if stage == 2:
                    share(piece, 1 + n, value, (0, 16)[n - 2])
    for piece in range(3):
        axis = GATHER_ORDERS[piece][2]
        fixed_rows = (None, None, None, 0, 16)
        for n, offset in enumerate((0, 3, 1, 2, 2)):
            value = lax.rem(me.at[axis] + offset, 4)
            index = with_core(place_index({axis: value}), 1 - me.core)
            rows = fixed_rows[n]
            index = index + ((everything(),) if rows is None else (pl.ds(rows, 16),))
            there = wholes[piece].at[index]
            remote(there, there, core_send.at[piece, n], core_recv.at[piece, n], me.partner()).wait_recv()
    for copy in arrivals:
        copy.wait_recv()
    for copy in waits:
        copy.wait()
    for copy in sent:
        copy.wait_send()


def gather_all(blocks, x, g, v):
    whole = jax.ShapeDtypeStruct((2, 2, 2, 4, 4, 32, PACK), BF16)
    quarter = jax.ShapeDtypeStruct((4, QUARTER, 272), BF16)
    return pl.pallas_call(
        gather_kernel,
        out_shape=(whole, whole, whole, quarter, quarter, jax.ShapeDtypeStruct((4, 8, 272), F32)),
        in_specs=[ANY] * 6,
        out_specs=(ANY,) * 6,
        scratch_shapes=[
            pltpu.SemaphoreType.DMA((3, 3, 4)),
            pltpu.SemaphoreType.DMA((3, 3, 4)),
            pltpu.SemaphoreType.DMA((3,)),
            pltpu.SemaphoreType.DMA((3, 5)),
            pltpu.SemaphoreType.DMA((3, 5)),
            pltpu.SemaphoreType.DMA((3, 3)),
            pltpu.SemaphoreType.DMA((3, 3)),
            pltpu.SemaphoreType.DMA((3,)),
        ],
        compiler_params=pltpu.CompilerParams(collective_id=0, has_side_effects=True),
        name="gather_weights",
    )(*blocks, x, g, v)


def exchange_kernel(source, target, send, recv, local):
    row, col = lax.axis_index("row"), lax.axis_index("col")
    in_group = lax.rem(row + 2, 4)
    rank = in_group * 4 + col

    def device(other):
        return (lax.rem(row - in_group + other // 4 + 32, 32), lax.rem(other, 4))

    greet([device(lax.rem(rank + d, 16)) for d in range(1, 16)])
    own = pltpu.make_async_copy(source.at[rank], target.at[rank], local)
    own.start()
    copies = []
    for d in range(1, 16):
        other = lax.rem(rank + d, 16)
        copy = pltpu.make_async_remote_copy(
            src_ref=source.at[other], dst_ref=target.at[rank], send_sem=send.at[d], recv_sem=recv.at[d],
            device_id=device(other), device_id_type=MESH,
        )
        copy.start()
        copies.append(copy)
    for d in range(1, 16):
        origin = lax.rem(rank + 16 - d, 16)
        pltpu.make_async_remote_copy(
            src_ref=source.at[origin], dst_ref=target.at[origin], send_sem=send.at[d], recv_sem=recv.at[d],
            device_id=device(origin), device_id_type=MESH,
        ).wait_recv()
    for copy in copies:
        copy.wait_send()
    own.wait()


def exchange(source, collective_id):
    return pl.pallas_call(
        exchange_kernel,
        out_shape=jax.ShapeDtypeStruct(source.shape, source.dtype),
        in_specs=[ANY],
        out_specs=ANY,
        scratch_shapes=[
            pltpu.SemaphoreType.DMA((16,)),
            pltpu.SemaphoreType.DMA((16,)),
            pltpu.SemaphoreType.DMA,
        ],
        compiler_params=pltpu.CompilerParams(collective_id=collective_id, has_side_effects=True),
        name="exchange_heads",
    )(source)


def free_axes(fixed):
    return [axis for axis in ("y", "z", "x") if axis not in fixed]


def buffer_shape(fixed, rows):
    shape = ()
    for axis in free_axes(fixed):
        shape = shape + ((2, 2) if axis == "y" else (4,))
    return shape + (rows, PACK)


def buffer_index(at):
    index = ()
    for axis in ("y", "z", "x"):
        if axis in at:
            index = index + ((lax.rem(at[axis], 2), at[axis] // 2) if axis == "y" else (at[axis],))
    return index


def scatter_kernel(part0, part1, part2, y_ref, gin_ref, out_ref, y_out, gin_out, *scratch):
    me = Place()
    parts = (part0, part1, part2)
    sums, others = scratch[0:3], scratch[3:6]
    halves = {}
    fulls = {}
    position = 6
    for piece in range(3):
        for stage in range(3):
            halves[piece, stage] = scratch[position : position + 2]
            fulls[piece, stage] = scratch[position + 2 : position + 4]
            position += 4
    local, core_send, core_recv, send, recv, out_send, out_recv, out_local = scratch[position:]
    greet(me.neighbours())

    def remote(source, target, ssem, rsem, device):
        return pltpu.make_async_remote_copy(
            src_ref=source, dst_ref=target, send_sem=ssem, recv_sem=rsem,
            device_id=device, device_id_type=MESH,
        )

    def chunk_value(piece, k):
        return lax.rem(me.at[SCATTER_ORDERS[piece][0]] + (2, 1, 3, 0)[k], 4)

    sent, loads, crossed = [], {}, {}
    for k in range(4):
        for piece in range(3):
            index = place_index({SCATTER_ORDERS[piece][0]: chunk_value(piece, k)})
            load = pltpu.make_async_copy(
                parts[piece].at[with_core(index, me.core)], sums[piece].at[index], local.at[piece, k]
            )
            load.start()
            loads[piece, k] = load
            copy = remote(
                parts[piece].at[with_core(index, 1 - me.core)], others[piece].at[index],
                core_send.at[piece, k], core_recv.at[piece, k], me.partner(),
            )
            copy.start()
            crossed[piece, k] = copy
            sent.append(copy)

    pairs = ((y_ref, y_out), (gin_ref, gin_out))
    arrivals, own_copies = [], []
    for n, (source, target) in enumerate(pairs):
        rows = pl.ds(pl.multiple_of(me.col * QUARTER, QUARTER), QUARTER)
        own = pltpu.make_async_copy(source.at[me.col], target.at[rows, :], out_local.at[n])
        own.start()
        own_copies.append(own)
        for distance in (1, 2, 3):
            peer = me.beside(distance)
            copy = remote(
                source.at[peer[1]], target.at[rows, :], out_send.at[n, distance - 1], out_recv.at[n, distance - 1], peer
            )
            copy.start()
            sent.append(copy)
            origin = pl.ds(pl.multiple_of(lax.rem(me.col + 4 - distance, 4) * QUARTER, QUARTER), QUARTER)
            arrivals.append(
                remote(
                    source.at[me.col], target.at[origin, :],
                    out_send.at[n, distance - 1], out_recv.at[n, distance - 1], peer,
                )
            )

    def stage_fixed(piece, stage):
        return {axis: me.at[axis] for axis in SCATTER_ORDERS[piece][:stage]}

    def each_tile(fixed, body):
        axes = free_axes(fixed)
        count = 4 ** len(axes)
        if count == 1:
            body({})
            return

        @pl.loop(0, count)
        def _(t):
            if len(axes) == 1:
                body({axes[0]: t})
            else:
                body({axes[0]: t // 4, axes[1]: lax.rem(t, 4)})

    def add_core(piece, k):
        axis = SCATTER_ORDERS[piece][0]
        fixed = {axis: chunk_value(piece, k)}

        def body(at):
            index = place_index({**fixed, **at})
            total = sums[piece][index].astype(F32) + others[piece][index].astype(F32)
            sums[piece][index] = total.astype(BF16)

        each_tile(fixed, body)

    def begin(piece, stage):
        axis = SCATTER_ORDERS[piece][stage]
        fixed = {**stage_fixed(piece, stage), axis: lax.rem(me.at[axis] + 2, 4)}
        for n in range(2):
            copy = remote(
                sums[piece].at[place_index(fixed) + (pl.ds(16 * n, 16),)], halves[piece, stage][n],
                send.at[piece, stage, n], recv.at[piece, stage, n], me.step(axis, (1, -1)[n]),
            )
            copy.start()
            sent.append(copy)

    def middle(piece, stage, n):
        axis = SCATTER_ORDERS[piece][stage]
        fixed = {**stage_fixed(piece, stage), axis: lax.rem(me.at[axis] + (1, 3)[n], 4)}
        part = halves[piece, stage][n]
        remote(part, part, send.at[piece, stage, n], recv.at[piece, stage, n], me.step(axis, 1)).wait_recv()

        def body(at):
            index = place_index({**fixed, **at}) + (pl.ds(16 * n, 16),)
            total = sums[piece][index].astype(F32) + part[buffer_index(at)].astype(F32)
            sums[piece][index] = total.astype(BF16)

        each_tile(fixed, body)
        copy = remote(
            sums[piece].at[place_index(fixed)], fulls[piece, stage][n],
            send.at[piece, stage, 2 + n], recv.at[piece, stage, 2 + n], me.step(axis, (1, -1)[n]),
        )
        copy.start()
        sent.append(copy)

    def finish(piece, stage):
        axis = SCATTER_ORDERS[piece][stage]
        fixed = {**stage_fixed(piece, stage), axis: me.at[axis]}
        first, second = fulls[piece, stage]
        for n, part in enumerate((first, second)):
            remote(
                part, part, send.at[piece, stage, 2 + n], recv.at[piece, stage, 2 + n], me.step(axis, 1)
            ).wait_recv()

        def body(at):
            index = place_index({**fixed, **at})
            place = buffer_index(at)
            if stage == 2:
                total = sums[piece][index].astype(F32) + (first[...].astype(F32) + second[...].astype(F32))
                out_ref[piece] = total
            else:
                total = sums[piece][index].astype(F32) + (first[place].astype(F32) + second[place].astype(F32))
                sums[piece][index] = total.astype(BF16)

        each_tile(fixed, body)

    for k in range(4):
        for piece in range(3):
            loads[piece, k].wait()
            crossed[piece, k].wait_recv()
            add_core(piece, k)
            if k == 0:
                begin(piece, 0)
            elif k < 3:
                middle(piece, 0, k - 1)
    for piece in range(3):
        finish(piece, 0)
        begin(piece, 1)
    for stage in (1, 2):
        for n in range(2):
            for piece in range(3):
                middle(piece, stage, n)
        for piece in range(3):
            finish(piece, stage)
            if stage == 1:
                begin(piece, 2)
    for copy in arrivals:
        copy.wait_recv()
    for copy in own_copies:
        copy.wait()
    for copy in sent:
        copy.wait_send()


def scatter_all(parts, y4, gin4):
    scratch = [pltpu.VMEM((2, 2, 4, 4, 32, PACK), BF16) for _ in range(6)]
    for piece in range(3):
        order = SCATTER_ORDERS[piece]
        for stage in range(3):
            fixed = order[: stage + 1]
            scratch += [pltpu.VMEM(buffer_shape(fixed, 16), BF16) for _ in range(2)]
            scratch += [pltpu.VMEM(buffer_shape(fixed, 32), BF16) for _ in range(2)]
    scratch += [
        pltpu.SemaphoreType.DMA((3, 4)),
        pltpu.SemaphoreType.DMA((3, 4)),
        pltpu.SemaphoreType.DMA((3, 4)),
        pltpu.SemaphoreType.DMA((3, 3, 4)),
        pltpu.SemaphoreType.DMA((3, 3, 4)),
        pltpu.SemaphoreType.DMA((2, 3)),
        pltpu.SemaphoreType.DMA((2, 3)),
        pltpu.SemaphoreType.DMA((2,)),
    ]
    back = jax.ShapeDtypeStruct((512, 272), BF16)
    return pl.pallas_call(
        scatter_kernel,
        out_shape=(jax.ShapeDtypeStruct((3, 32, PACK), F32), back, back),
        in_specs=[ANY] * 5,
        out_specs=(pl.BlockSpec(memory_space=pltpu.VMEM), ANY, ANY),
        scratch_shapes=scratch,
        compiler_params=pltpu.CompilerParams(
            collective_id=3, has_side_effects=True, vmem_limit_bytes=VMEM_LIMIT
        ),
        name="scatter_gradients",
    )(*parts, y4, gin4)


def unpack_tail(packed, tiles, wide, tail):
    tiles[...] = packed[0, :, WIDE:PACK].astype(F32)
    for j in range(2):
        for s in range(9):
            wide[pl.ds(32 * j, 32), pl.ds(128 * s, 128)] = tiles[pl.ds(9 * j + s, 32, stride=32), :]
    tail[0:64, :] = wide[0:64, :].astype(BF16)


def pack_tail(tail, tiles, packed):
    for j in range(2):
        for s in range(9):
            tiles[pl.ds(9 * j + s, 32, stride=32), :] = tail[32 * j : 32 * j + 32, 128 * s : 128 * s + 128]
    packed[0, :, WIDE:PACK] = tiles[...].astype(BF16)


def in_features(values, packed, tail, columns):
    return dot_nn(values[:, :MAIN], packed[0, :, columns]) + dot_nn(values[:, MAIN:], tail[:, columns])


def add_to_features(total, values, packed, tail):
    @pl.loop(0, 4)
    def _(b):
        rows = pl.ds(pl.multiple_of(b * 256, 256), 256)
        total[:, rows] += dot_nt(values, packed[0, rows, :WIDE])

    total[:, MAIN:] += dot_nt(values, tail[...])


def norm_forward(x, gain, bias):
    mean = jnp.sum(x, axis=1, keepdims=True) / D
    square = jnp.sum(x * x, axis=1, keepdims=True) / D
    inverse = lax.rsqrt(square - mean * mean + norm_epsilon)
    normed = (x - mean) * inverse
    return normed, inverse, (normed * gain + bias).astype(BF16)


def norm_reverse(grad, normed, inverse, gain):
    scaled = grad * gain
    first = jnp.sum(scaled, axis=1, keepdims=True) / D
    second = jnp.sum(scaled * normed, axis=1, keepdims=True) / D
    return inverse * (scaled - first - normed * second)


def permuted(pieces, perm):
    total = dot_nn(pieces[0], perm[0])
    for c in range(1, 4):
        total += dot_nn(pieces[c], perm[c])
    return total


def permuted_exact(pieces, perm):
    total = jnp.zeros((8, WIDE), F32)
    for c in range(4):
        total += lax.dot_general(
            pieces[c], perm[c].astype(F32), (((1,), (0,)), ((), ())),
            preferred_element_type=F32, precision=lax.Precision.HIGHEST,
        )
    return total


def real_features(values):
    lane = lax.broadcasted_iota(jnp.int32, values.shape, 1)
    return jnp.where(lane < D, values, 0.0)


def qkv_kernel(x4, v4, perm, packed, x_out, n1_out, v_out, qkv_out, tiles, wide, tail):
    @pl.when(pl.program_id(0) == 0)
    def _():
        x = permuted(x4, perm)
        vectors = permuted_exact(v4, perm)
        v_out[...] = vectors
        x_out[...] = x.astype(BF16)
        _, _, normed = norm_forward(x, vectors[0:1], vectors[1:2])
        n1_out[...] = normed
        tail[...] = jnp.zeros_like(tail)

    unpack_tail(packed, tiles, wide, tail)

    @pl.loop(0, 3)
    def _(b):
        columns = pl.ds(pl.multiple_of(b * 384, 128), 384)
        qkv_out[0, :, columns] = in_features(n1_out[...], packed, tail, columns).astype(BF16)


def whole_spec(shape):
    return pl.BlockSpec(shape, lambda s: (0,) * len(shape))


def qkv_call(x4, v4, perm, weights):
    row = jax.ShapeDtypeStruct((QUARTER, WIDE), BF16)
    return pl.pallas_call(
        qkv_kernel,
        grid=(4,),
        out_shape=(
            row, row, jax.ShapeDtypeStruct((8, WIDE), F32), jax.ShapeDtypeStruct((4, QUARTER, WIDE), BF16)
        ),
        in_specs=[
            whole_spec((4, QUARTER, 272)), whole_spec((4, 8, 272)), whole_spec((4, 272, WIDE)),
            pl.BlockSpec((1, MAIN, PACK), lambda s: (s, 0, 0)),
        ],
        out_specs=(
            whole_spec((QUARTER, WIDE)), whole_spec((QUARTER, WIDE)), whole_spec((8, WIDE)),
            pl.BlockSpec((1, QUARTER, WIDE), lambda s: (s, 0, 0)),
        ),
        scratch_shapes=[pltpu.VMEM((MAIN, 128), F32), pltpu.VMEM((128, WIDE), F32), pltpu.VMEM((128, WIDE), BF16)],
        compiler_params=pltpu.CompilerParams(vmem_limit_bytes=VMEM_LIMIT),
        name="norm_and_qkv",
    )(x4, v4, perm, weights)


def gelu_both(v):
    tanh_value = jnp.tanh(gelu_coef * (v + 0.044715 * v * v * v))
    value = 0.5 * v * (1.0 + tanh_value)
    slope = 0.5 * (1.0 + tanh_value) + 0.5 * v * (1.0 - tanh_value * tanh_value) * gelu_coef * (
        1.0 + 0.134145 * v * v
    )
    return value, slope


def weight_gradient(rows_t, values, tiles, tail_sum, packed):
    @pl.loop(0, 4)
    def _(b):
        rows = pl.ds(pl.multiple_of(b * 256, 256), 256)
        packed[0, rows, :WIDE] = dot_nn(rows_t[rows, :], values[...]).astype(BF16)

    tail_sum[...] = dot_nn(rows_t[MAIN:, :], values[...])
    pack_tail(tail_sum, tiles, packed)


def middle_kernel(
    x_ref, a0, w0, w1, w2, g4, perm, vec,
    y4, dres_out, dresb_out, gr1, gr2, dmix_out, vec_out,
    resid, normed2, n2, n2_t, cot, cot_t, total, dn2, inverse2, hidden, dpre, tiles, out_tiles, tail1, tail2, tail_sum,
):
    s = pl.program_id(0)

    @pl.when(s == 0)
    def _():
        total[...] = jnp.zeros_like(total)
        dn2[...] = jnp.zeros_like(dn2)
        tail1[...] = jnp.zeros_like(tail1)
        tail2[...] = jnp.zeros_like(tail2)
        out_tiles[...] = jnp.zeros_like(out_tiles)

    @pl.when((s < 4) | (s >= 8))
    def _():
        unpack_tail(w0, tiles, tail_sum, tail1)

    @pl.when(s < 4)
    def _():
        add_to_features(total, a0[0], w0, tail1)

    @pl.when(s == 3)
    def _():
        resid[...] = x_ref[...].astype(F32) + total[...]
        total[...] = jnp.zeros_like(total)
        normed, inverse, n2_value = norm_forward(resid[...], vec[2:3], vec[3:4])
        normed2[...] = normed
        inverse2[...] = jnp.broadcast_to(inverse, inverse2.shape)
        n2[...] = n2_value
        n2_t[...] = n2_value.astype(F32).T.astype(BF16)
        cot_value = permuted(g4, perm)
        cot[...] = cot_value.astype(BF16)
        cot_t[...] = cot_value.T.astype(BF16)

    @pl.when((s >= 4) & (s < 8))
    def _():
        unpack_tail(w1, tiles, tail_sum, tail1)
        unpack_tail(w2, tiles, tail_sum, tail2)

        @pl.loop(0, 3)
        def _(b):
            columns = pl.ds(pl.multiple_of(b * 384, 128), 384)
            pre = in_features(n2[...], w1, tail1, columns)
            d_hidden = in_features(cot[...], w2, tail2, columns)
            value, slope = gelu_both(pre)
            hidden[:, columns] = value.astype(BF16)
            dpre[:, columns] = (d_hidden * slope).astype(BF16)

        add_to_features(total, hidden[...], w2, tail2)
        add_to_features(dn2, dpre[...], w1, tail1)
        weight_gradient(n2_t, dpre, out_tiles, tail_sum, gr1)
        weight_gradient(cot_t, hidden, out_tiles, tail_sum, gr2)

    @pl.when(s == 7)
    def _():
        y = (resid[...] + total[...]).astype(BF16)
        for c in range(4):
            y4[c] = dot_nt(y, perm[c]).astype(BF16)
        grad = dn2[...]
        normed = normed2[...]
        vec_out[...] = jnp.zeros_like(vec_out)
        vec_out[0:1, :] = jnp.sum(grad * normed, axis=0, keepdims=True)
        vec_out[1:2, :] = jnp.sum(grad, axis=0, keepdims=True)
        back = cot[...].astype(F32) + norm_reverse(grad, normed, inverse2[:, 0:1], vec[2:3])
        back = real_features(back)
        dres_out[...] = back
        dresb_out[...] = back.astype(BF16)

    @pl.when(s >= 8)
    def _():
        @pl.loop(0, 3)
        def _(b):
            columns = pl.ds(pl.multiple_of(b * 384, 128), 384)
            dmix_out[0, :, columns] = in_features(dresb_out[...], w0, tail1, columns).astype(BF16)


def middle_call(x, a0, w0, w1, w2, g4, perm, vec):
    row_b = jax.ShapeDtypeStruct((QUARTER, WIDE), BF16)
    row_f = jax.ShapeDtypeStruct((QUARTER, WIDE), F32)
    packed = jax.ShapeDtypeStruct((4, MAIN, PACK), BF16)

    def early(s):
        return (jnp.minimum(s, 3), 0, 0)

    def outer(s):
        return (jnp.where(s < 8, jnp.minimum(s, 3), 11 - s), 0, 0)

    def inner(s):
        return (jnp.clip(s - 4, 0, 3), 0, 0)

    def late(s):
        return (jnp.where(s < 8, 3, 11 - s), 0, 0)

    block = (1, MAIN, PACK)
    rows = (1, QUARTER, WIDE)
    return pl.pallas_call(
        middle_kernel,
        grid=(12,),
        out_shape=(
            jax.ShapeDtypeStruct((4, QUARTER, 272), BF16), row_f, row_b, packed, packed,
            jax.ShapeDtypeStruct((4, QUARTER, WIDE), BF16), jax.ShapeDtypeStruct((8, WIDE), F32),
        ),
        in_specs=[
            whole_spec((QUARTER, WIDE)), pl.BlockSpec(rows, early), pl.BlockSpec(block, outer),
            pl.BlockSpec(block, inner), pl.BlockSpec(block, inner), whole_spec((4, QUARTER, 272)),
            whole_spec((4, 272, WIDE)), whole_spec((8, WIDE)),
        ],
        out_specs=(
            whole_spec((4, QUARTER, 272)), whole_spec((QUARTER, WIDE)), whole_spec((QUARTER, WIDE)),
            pl.BlockSpec(block, inner), pl.BlockSpec(block, inner), pl.BlockSpec(rows, late), whole_spec((8, WIDE)),
        ),
        scratch_shapes=[
            pltpu.VMEM((QUARTER, WIDE), F32), pltpu.VMEM((QUARTER, WIDE), F32), pltpu.VMEM((QUARTER, WIDE), BF16),
            pltpu.VMEM((WIDE, QUARTER), BF16), pltpu.VMEM((QUARTER, WIDE), BF16), pltpu.VMEM((WIDE, QUARTER), BF16),
            pltpu.VMEM((QUARTER, WIDE), F32), pltpu.VMEM((QUARTER, WIDE), F32), pltpu.VMEM((QUARTER, 128), F32),
            pltpu.VMEM((QUARTER, WIDE), BF16), pltpu.VMEM((QUARTER, WIDE), BF16),
            pltpu.VMEM((MAIN, 128), F32), pltpu.VMEM((MAIN, 128), F32),
            pltpu.VMEM((128, WIDE), BF16), pltpu.VMEM((128, WIDE), BF16), pltpu.VMEM((128, WIDE), F32),
        ],
        compiler_params=pltpu.CompilerParams(vmem_limit_bytes=VMEM_LIMIT),
        name="feed_forward",
    )(x, a0, w0, w1, w2, g4, perm, vec)


def first_kernel(
    x_ref, n1, dresb, dres, both, w0, perm, vec, vec2,
    gin4, gr0, sums,
    both_t, dn1, tiles, out_tiles, tail, tail_sum,
):
    s = pl.program_id(0)

    @pl.when(s == 0)
    def _():
        dn1[...] = jnp.zeros_like(dn1)
        tail[...] = jnp.zeros_like(tail)
        out_tiles[...] = jnp.zeros_like(out_tiles)
        both_t[:, 0:128] = n1[...].astype(F32).T.astype(BF16)
        both_t[:, 128:256] = dresb[...].astype(F32).T.astype(BF16)

    unpack_tail(w0, tiles, tail_sum, tail)
    add_to_features(dn1, both[0, 0:128, :], w0, tail)
    weight_gradient(both_t, both.at[0], out_tiles, tail_sum, gr0)

    @pl.when(s == 3)
    def _():
        normed, inverse, _ = norm_forward(x_ref[...].astype(F32), vec[0:1], vec[1:2])
        grad = dn1[...]
        back = dres[...] + norm_reverse(grad, normed, inverse, vec[0:1])
        back = real_features(back).astype(BF16)
        sums[...] = vec2[...]
        sums[4:5, :] = jnp.sum(grad * normed, axis=0, keepdims=True)
        sums[5:6, :] = jnp.sum(grad, axis=0, keepdims=True)
        for c in range(4):
            gin4[c] = dot_nt(back, perm[c]).astype(BF16)


def first_call(x, n1, dresb, dres, both, w0, perm, vec, vec2):
    block = (1, MAIN, PACK)

    def by_step(s):
        return (s, 0, 0)

    return pl.pallas_call(
        first_kernel,
        grid=(4,),
        out_shape=(
            jax.ShapeDtypeStruct((4, QUARTER, 272), BF16), jax.ShapeDtypeStruct((4, MAIN, PACK), BF16),
            jax.ShapeDtypeStruct((8, WIDE), F32),
        ),
        in_specs=[
            whole_spec((QUARTER, WIDE)), whole_spec((QUARTER, WIDE)), whole_spec((QUARTER, WIDE)),
            whole_spec((QUARTER, WIDE)), pl.BlockSpec((1, 256, WIDE), by_step),
            pl.BlockSpec(block, by_step), whole_spec((4, 272, WIDE)), whole_spec((8, WIDE)), whole_spec((8, WIDE)),
        ],
        out_specs=(whole_spec((4, QUARTER, 272)), pl.BlockSpec(block, by_step), whole_spec((8, WIDE))),
        scratch_shapes=[
            pltpu.VMEM((WIDE, 256), BF16), pltpu.VMEM((QUARTER, WIDE), F32),
            pltpu.VMEM((MAIN, 128), F32), pltpu.VMEM((MAIN, 128), F32), pltpu.VMEM((128, WIDE), BF16),
            pltpu.VMEM((128, WIDE), F32),
        ],
        compiler_params=pltpu.CompilerParams(vmem_limit_bytes=VMEM_LIMIT),
        name="first_norm_back",
    )(x, n1, dresb, dres, both, w0, perm, vec, vec2)


def allowed_pairs(shape, key_start, query_start):
    key = key_start + lax.broadcasted_iota(jnp.int32, shape, 0)
    query = query_start + lax.broadcasted_iota(jnp.int32, shape, 1)
    return key <= query


def transposed(values):
    return values.astype(F32).T


def attend_kernel(info, r_ref, q16, o_out, o16_out, l_out, l16_out, query, value_t, value16_t):
    rank, wraps = info[0], info[1]

    @pl.loop(0, 4)
    def _(b):
        rows = pl.ds(pl.multiple_of(b * KEYS, KEYS), KEYS)
        query[rows, :] = r_ref[rows, 0:64] * jnp.asarray(0.125, BF16)
        value_t[:, rows] = transposed(r_ref[rows, 128:256])[0:64].astype(BF16)
        value16_t[:, rows] = transposed(r_ref[rows, 256:384])[0:64].astype(BF16)

    def step(q, columns, v_t, j, carry, query_start=None):
        peak, running, mixed = carry
        rows = pl.ds(pl.multiple_of(j * KEYS, KEYS), KEYS)
        scores = dot_nt(r_ref[rows, columns], q)
        if query_start is not None:
            scores = jnp.where(allowed_pairs(scores.shape, j * KEYS, query_start), scores, masked_score)
        new_peak = jnp.maximum(peak, jnp.max(scores, axis=0, keepdims=True))
        shrink = jnp.exp(peak - new_peak)
        weights = jnp.exp(scores - new_peak)
        running = running * shrink + jnp.sum(weights, axis=0, keepdims=True)
        mixed = mixed * shrink + dot_nn(v_t[:, rows], weights.astype(BF16))
        return new_peak, running, mixed

    def empty(width):
        return (
            jnp.full((1, width), masked_score, F32), jnp.zeros((1, width), F32), jnp.zeros((64, width), F32)
        )

    @pl.loop(0, 4)
    def _(i):
        rows = pl.ds(pl.multiple_of(i * KEYS, KEYS), KEYS)
        q = query[rows, :]
        start = jnp.where((wraps == 1) & (i >= 2), 2, 0)
        carry = lax.fori_loop(
            start, i, lambda j, carry: step(q, slice(64, 128), value_t, j, carry), empty(KEYS)
        )
        peak, running, mixed = step(q, slice(64, 128), value_t, i, carry, i * KEYS)
        o_out[rows, :] = (mixed / running).T.astype(BF16)
        l_out[:, rows] = peak + jnp.log(running)

    q = q16[...] * jnp.asarray(0.125, BF16)
    start = jnp.where((wraps == 1) & (rank >= 8), 2, 0)
    peak, running, mixed = lax.fori_loop(
        start, rank // 4 + 1,
        lambda j, carry: step(q, slice(192, 256), value16_t, j, carry, rank * QUARTER), empty(QUARTER),
    )
    o16_out[...] = (mixed / running).T.astype(BF16)
    l16_out[...] = peak + jnp.log(running)


VMEM_SPEC = pl.BlockSpec(memory_space=pltpu.VMEM)
SMEM_SPEC = pl.BlockSpec(memory_space=pltpu.SMEM)


def attend_call(info, r, q16):
    return pl.pallas_call(
        attend_kernel,
        out_shape=(
            jax.ShapeDtypeStruct((SEQ, 64), BF16), jax.ShapeDtypeStruct((QUARTER, 64), BF16),
            jax.ShapeDtypeStruct((1, SEQ), F32), jax.ShapeDtypeStruct((1, QUARTER), F32),
        ),
        in_specs=[SMEM_SPEC, VMEM_SPEC, VMEM_SPEC],
        out_specs=(VMEM_SPEC,) * 4,
        scratch_shapes=[pltpu.VMEM((SEQ, 64), BF16), pltpu.VMEM((64, SEQ), BF16), pltpu.VMEM((64, SEQ), BF16)],
        compiler_params=pltpu.CompilerParams(vmem_limit_bytes=VMEM_LIMIT),
        name="attend_forward",
    )(info, r, q16)


def attend_back_kernel(
    info, r_ref, q16, o_ref, o16, do_ref, do16, l_ref, l16,
    msg, dq16_out, query, key_t, key16_t, delta, dq_t,
):
    rank, wraps = info[0], info[1]

    @pl.loop(0, 4)
    def _(b):
        rows = pl.ds(pl.multiple_of(b * KEYS, KEYS), KEYS)
        query[rows, :] = r_ref[rows, 0:64] * jnp.asarray(0.125, BF16)
        key_t[:, rows] = transposed(r_ref[rows, 0:128])[64:128].astype(BF16)
        key16_t[:, rows] = transposed(r_ref[rows, 128:256])[64:128].astype(BF16)
        product = do_ref[rows, :].astype(F32) * o_ref[rows, :].astype(F32)
        delta[:, rows] = jnp.sum(product.T, axis=0, keepdims=True)
        dq_t[:, rows] = jnp.zeros((64, KEYS), F32)

    def pair(keys, values, q, d_out, log_total, delta_row, mask):
        scores = dot_nt(keys, q)
        probs = jnp.exp(scores - log_total)
        if mask is not None:
            probs = jnp.where(mask(scores.shape), probs, 0.0)
        probs = probs.astype(BF16)
        d_prob = dot_nt(values, d_out)
        d_scores = (probs.astype(F32) * (d_prob - delta_row)).astype(BF16)
        return dot_nn(d_scores, q), dot_nn(probs, d_out), d_scores

    @pl.loop(0, 4)
    def _(j):
        rows = pl.ds(pl.multiple_of(j * KEYS, KEYS), KEYS)
        keys, values = r_ref[rows, 64:128], r_ref[rows, 128:192]

        def step(i, carry, mask=None):
            d_key, d_value = carry
            at = pl.ds(pl.multiple_of(i * KEYS, KEYS), KEYS)
            more_key, more_value, d_scores = pair(
                keys, values, query[at, :], do_ref[at, :], l_ref[:, at], delta[:, at], mask
            )
            dq_t[:, at] += dot_nn(key_t[:, rows], d_scores)
            return d_key + more_key, d_value + more_value

        zero = jnp.zeros((KEYS, 64), F32)
        carry = step(j, (zero, zero), lambda shape: allowed_pairs(shape, 0, 0))
        end = jnp.where((wraps == 1) & (j < 2), 2, 4)
        d_key, d_value = lax.fori_loop(j + 1, end, step, carry)
        msg[rows, 64:128] = d_key.astype(BF16)
        msg[rows, 128:192] = d_value.astype(BF16)

    q = q16[...] * jnp.asarray(0.125, BF16)
    d_out16 = do16[...]
    delta16 = jnp.sum((d_out16.astype(F32) * o16[...].astype(F32)).T, axis=0, keepdims=True)
    start = jnp.where((wraps == 1) & (rank >= 8), 2, 0)

    def last_step(j, dq):
        rows = pl.ds(pl.multiple_of(j * KEYS, KEYS), KEYS)
        d_key, d_value, d_scores = pair(
            r_ref[rows, 192:256], r_ref[rows, 256:320], q, d_out16, l16[...], delta16,
            lambda shape: allowed_pairs(shape, j * KEYS, rank * QUARTER),
        )
        msg[rows, 192:256] = d_key.astype(BF16)
        msg[rows, 256:320] = d_value.astype(BF16)
        return dq + dot_nn(key16_t[:, rows], d_scores)

    @pl.loop(0, 4)
    def _(j):
        rows = pl.ds(pl.multiple_of(j * KEYS, KEYS), KEYS)
        msg[rows, 192:256] = jnp.zeros((KEYS, 64), BF16)
        msg[rows, 256:384] = jnp.zeros((KEYS, 128), BF16)
        msg[rows, 0:64] = (dq_t[:, rows] * 0.125).T.astype(BF16)

    dq = lax.fori_loop(start, rank // 4 + 1, last_step, jnp.zeros((64, QUARTER), F32))
    dq16_out[...] = (dq * 0.125).T.astype(BF16)


def attend_back_call(info, r, q16, o, o16, do, do16, log_total, log16):
    return pl.pallas_call(
        attend_back_kernel,
        out_shape=(jax.ShapeDtypeStruct((SEQ, MSG), BF16), jax.ShapeDtypeStruct((QUARTER, 64), BF16)),
        in_specs=[SMEM_SPEC] + [VMEM_SPEC] * 8,
        out_specs=(VMEM_SPEC,) * 2,
        scratch_shapes=[
            pltpu.VMEM((SEQ, 64), BF16), pltpu.VMEM((64, SEQ), BF16), pltpu.VMEM((64, SEQ), BF16),
            pltpu.VMEM((1, SEQ), F32), pltpu.VMEM((64, SEQ), F32),
        ],
        compiler_params=pltpu.CompilerParams(vmem_limit_bytes=VMEM_LIMIT),
        name="attend_backward",
    )(info, r, q16, o, o16, do, do16, log_total, log16)


def packed_block(block):
    tail = jnp.pad(block[32:34], ((0, 0), (0, WIDE - D))).reshape(18, 128)
    return jnp.concatenate(
        [jnp.pad(block[:32], ((0, 0), (0, WIDE - D))), jnp.pad(tail, ((0, 14), (0, 0)))], axis=1
    )


def unpacked_block(packed):
    tail = packed[:18, WIDE:].reshape(2, WIDE)[:, :D]
    return jnp.concatenate([packed[:, :D], tail], axis=0)


def permutation():
    feature = jnp.arange(D, dtype=jnp.int32)
    block, inside = feature // 34, feature % 34
    place = jnp.where(inside < 32, 32 * block + inside, MAIN + 32 * (inside - 32) + block)
    chosen = place[:, None] == jnp.arange(WIDE, dtype=jnp.int32)[None, :]
    return chosen.astype(BF16).reshape(4, 272, WIDE)


def per_device(
    layer_input,
    first_norm_gain,
    first_norm_bias,
    w_qkv,
    w_out,
    second_norm_gain,
    second_norm_bias,
    w_up,
    w_down,
    gradient_of_output,
):
    row, col = lax.axis_index("row"), lax.axis_index("col")
    rank = (row + 2) % 4 * 4 + col
    wraps = ((row < 2) | (row >= 30)).astype(jnp.int32)
    info = jnp.stack([rank, wraps]).astype(jnp.int32)
    perm = permutation()
    vectors = jnp.concatenate(
        [
            jnp.stack([first_norm_gain, first_norm_bias, second_norm_gain, second_norm_bias]),
            jnp.zeros((4, 272), F32),
        ]
    )
    blocks = (
        packed_block(jnp.concatenate([w_qkv, w_out.T], axis=1)),
        packed_block(w_up),
        packed_block(w_down.T),
    )
    w0, w1, w2, x4, g4, v4 = gather_all(blocks, layer_input, gradient_of_output, vectors)
    w0, w1, w2 = (w.reshape(4, MAIN, PACK) for w in (w0, w1, w2))
    x, n1, vec, qkv4 = qkv_call(x4, v4, perm, w0)

    qkv = jnp.concatenate([qkv4[c, :, :QKV_COLS] for c in range(4)], axis=1).reshape(QUARTER, 3, HEADS, HEAD_DIM)
    last = [jnp.broadcast_to(qkv[:, n, 16:17], (QUARTER, 16, HEAD_DIM)) for n in (1, 2)]
    message = jnp.concatenate(
        [qkv[:, 0, :16], qkv[:, 1, :16], qkv[:, 2, :16], *last, jnp.zeros((QUARTER, 16, 64), BF16)], axis=2
    ).transpose(1, 0, 2)
    q16 = qkv[:, 0, 16]
    heads = exchange(message, 1).reshape(SEQ, MSG)
    o, o16, log_total, log16 = attend_call(info, heads, q16)
    mixed = exchange(o.reshape(16, QUARTER, 64), 2)
    attn = jnp.concatenate([mixed.transpose(1, 0, 2).reshape(QUARTER, 1024), o16], axis=1)
    a0 = jnp.pad(
        attn.reshape(QUARTER, 4, 272).transpose(1, 0, 2), ((0, 0), (0, 0), (QKV_COLS, WIDE - D))
    )
    y4, dres, dresb, gr1, gr2, dmix4, vec2 = middle_call(x, a0, w0, w1, w2, g4, perm, vec)
    dmix = jnp.concatenate([dmix4[c, :, QKV_COLS:D] for c in range(4)], axis=1).reshape(QUARTER, HEADS, HEAD_DIM)
    do = exchange(dmix[:, :16].transpose(1, 0, 2), 2).reshape(SEQ, 64)
    back, dq16 = attend_back_call(info, heads, q16, o, o16, do, dmix[:, 16], log_total, log16)
    back = exchange(back.reshape(16, QUARTER, MSG), 1)
    last_sums = jnp.sum(back[:, :, 192:320].astype(F32), axis=0).astype(BF16)

    def side_by_side(first, last_head):
        return jnp.concatenate(
            [back[:, :, first : first + 64].transpose(1, 0, 2).reshape(QUARTER, 1024), last_head], axis=1
        )

    d_qkv = jnp.concatenate(
        [side_by_side(0, dq16), side_by_side(64, last_sums[:, :64]), side_by_side(128, last_sums[:, 64:])], axis=1
    )
    dq0 = jnp.pad(
        d_qkv.reshape(QUARTER, 4, QKV_COLS).transpose(1, 0, 2), ((0, 0), (0, 0), (0, WIDE - QKV_COLS))
    )
    gin4, gr0, sums4 = first_call(
        x, n1, dresb, dres, jnp.concatenate([dq0, a0], axis=1), w0, perm, vec, vec2
    )
    grouped = tuple(g.reshape(2, 2, 2, 4, 4, 32, PACK) for g in (gr0, gr1, gr2))
    sums, layer_output, gin = scatter_all(grouped, y4, gin4)
    own_perm = lax.dynamic_index_in_dim(perm, col, 0, keepdims=False).astype(F32)
    vg = lax.dot_general(
        lax.psum(sums4, ("row", "col")), own_perm, (((1,), (1,)), ((), ())),
        preferred_element_type=F32, precision=lax.Precision.HIGHEST,
    )
    s0, s1, s2 = (unpacked_block(sums[n]) for n in range(3))
    return (
        layer_output,
        gin.astype(F32),
        vg[4],
        vg[5],
        s0[:, :QKV_COLS],
        s0[:, QKV_COLS:].T,
        vg[0],
        vg[1],
        s1,
        s2.T,
    )


def solution(mesh):
    placed = (
        P("row", "col"),
        P("col"),
        P("col"),
        P("row", "col"),
        P("col", "row"),
        P("col"),
        P("col"),
        P("row", "col"),
        P("col", "row"),
        P("row", "col"),
    )
    return jax.shard_map(
        per_device,
        mesh=mesh,
        in_specs=placed,
        out_specs=(
            P("row", "col"),
            P("row", "col"),
            P("col"),
            P("col"),
            P("row", "col"),
            P("col", "row"),
            P("col"),
            P("col"),
            P("row", "col"),
            P("col", "row"),
        ),
        check_vma=False,
    )
```

```python
import math

import jax
import jax.numpy as jnp
from jax import lax
from jax.experimental import pallas as pl
from jax.experimental.pallas import tpu as pltpu
from jax.sharding import PartitionSpec as P

HEADS = 17
HEAD_DIM = 64
D = 1088
SEQ = 2048
MAIN = 1024
WIDE = 1152
PACK = 1280
QKV_COLS = 816
QUARTER = 128
PAIR = 256
MSG = 384
KEYS = 512

gelu_coef = math.sqrt(2.0 / math.pi)
norm_epsilon = 1e-05
masked_score = -1e30
MESH = pl.DeviceIdType.MESH
F32 = jnp.float32
BF16 = jnp.bfloat16
VMEM_LIMIT = 60 * 1024 * 1024
ANY = pl.BlockSpec(memory_space=pl.ANY)
VMEM_SPEC = pl.BlockSpec(memory_space=pltpu.VMEM)
SMEM_SPEC = pl.BlockSpec(memory_space=pltpu.SMEM)

GATHER_ORDERS = (("x", "y", "z"), ("y", "z", "x"), ("z", "x", "y"))
SCATTER_ORDERS = (("z", "y", "x"), ("x", "z", "y"), ("y", "x", "z"))


def dot_nn(a, b):
    return lax.dot_general(a, b, (((1,), (0,)), ((), ())), preferred_element_type=F32)


def dot_nt(a, b):
    return lax.dot_general(a, b, (((1,), (1,)), ((), ())), preferred_element_type=F32)


class Place:
    def __init__(self):
        self.row = lax.axis_index("row")
        self.col = lax.axis_index("col")
        self.at = {
            "x": lax.rem(self.row, 4),
            "z": lax.rem(self.row // 4, 4),
            "y": (self.row // 16) * 2 + self.col // 2,
        }
        self.core = lax.rem(self.col, 2)

    def device(self, at, core):
        return ((at["y"] // 2) * 16 + at["z"] * 4 + at["x"], lax.rem(at["y"], 2) * 2 + core)

    def step(self, axis, distance):
        at = dict(self.at)
        at[axis] = lax.rem(at[axis] + distance + 4, 4)
        return self.device(at, self.core)

    def partner(self):
        return (self.row, self.col + 1 - 2 * self.core)

    def beside(self, distance):
        return (self.row, lax.rem(self.col + distance, 4))

    def neighbours(self):
        found = [self.step(axis, d) for axis in ("x", "y", "z") for d in (1, -1)]
        found.append(self.partner())
        other = lax.rem(self.col // 2 + 1, 2)
        found.append((self.row, other * 2 + 1 - self.core))
        return found


def greet(devices):
    barrier = pltpu.get_barrier_semaphore()
    for device in devices:
        pl.semaphore_signal(barrier, inc=1, device_id=device, device_id_type=MESH)
    pl.semaphore_wait(barrier, len(devices))


def everything():
    return slice(None)


def place_index(fixed):
    if "y" in fixed:
        y_lo, y_hi = lax.rem(fixed["y"], 2), fixed["y"] // 2
    else:
        y_lo, y_hi = everything(), everything()
    return (y_lo, y_hi, fixed.get("z", everything()), fixed.get("x", everything()))


def remote(source, target, ssem, rsem, device):
    return pltpu.make_async_remote_copy(
        src_ref=source, dst_ref=target, send_sem=ssem, recv_sem=rsem,
        device_id=device, device_id_type=MESH,
    )


def gather_kernel(
    block0, block1, block2, x_ref, g_ref, v_ref,
    all0, all1, all2, x_out, g_out, v_out,
    send, recv, last_send, last_recv, local, in_send, in_recv, in_local,
):
    me = Place()
    blocks = (block0, block1, block2)
    wholes = (all0, all1, all2)
    greet(me.neighbours())

    def region(piece, fixed, rows=None):
        index = place_index(fixed) + ((everything(),) if rows is None else (pl.ds(rows, 16),))
        return wholes[piece].at[index]

    def around(piece, stage, value):
        order = GATHER_ORDERS[piece]
        fixed = {order[stage]: value}
        for axis in order[stage + 1 :]:
            fixed[axis] = me.at[axis]
        return fixed

    sent = []
    pairs = ((x_ref, x_out), (g_ref, g_out))
    waits, arrivals, own_copies = [], [], []
    for piece in range(3):
        copy = pltpu.make_async_copy(
            blocks[piece], region(piece, around(piece, 0, me.at[GATHER_ORDERS[piece][0]])), local.at[piece]
        )
        copy.start()
        own_copies.append(copy)

    def semaphores(piece, stage, n, u):
        if stage == 2:
            return last_send.at[piece, u, n], last_recv.at[piece, u, n]
        return send.at[piece, stage, n], recv.at[piece, stage, n]

    def part(piece, stage, value, u, rows=None):
        fixed = around(piece, stage, value)
        if stage == 2:
            axis = GATHER_ORDERS[piece][1]
            fixed[axis] = lax.rem(me.at[axis] + (0, 3, 1, 2)[u], 4)
        return region(piece, fixed, rows)

    def begin(piece, stage, u=0):
        axis = GATHER_ORDERS[piece][stage]
        mine = part(piece, stage, me.at[axis], u)
        source = blocks[piece] if stage == 0 else mine
        for n, distance in enumerate((1, -1)):
            copy = remote(source, mine, *semaphores(piece, stage, n, u), me.step(axis, distance))
            copy.start()
            sent.append(copy)

    def arrived(piece, stage, n, u=0):
        axis = GATHER_ORDERS[piece][stage]
        value = lax.rem(me.at[axis] + (3, 1, 2, 2)[n], 4)
        there = part(piece, stage, value, u, (None, None, 0, 16)[n])
        remote(there, there, *semaphores(piece, stage, n, u), me.step(axis, 1)).wait_recv()
        if n < 2:
            half = part(piece, stage, value, u, (0, 16)[n])
            copy = remote(half, half, *semaphores(piece, stage, 2 + n, u), me.step(axis, (1, -1)[n]))
            copy.start()
            sent.append(copy)

    for piece in range(3):
        begin(piece, 0)
    for n, (source, target) in enumerate(pairs):
        own = pltpu.make_async_copy(
            source.at[pl.ds(pl.multiple_of(me.col // 2 * PAIR, PAIR), PAIR), :], target.at[me.col], in_local.at[n]
        )
        own.start()
        waits.append(own)
    own = pltpu.make_async_copy(v_ref, v_out.at[me.col], in_local.at[2])
    own.start()
    waits.append(own)
    for distance in (1, 2, 3):
        peer = me.beside(distance)
        origin = lax.rem(me.col + 4 - distance, 4)
        for n, (source, target) in enumerate(pairs):
            semaphore = (in_send.at[n, distance - 1], in_recv.at[n, distance - 1])
            copy = remote(
                source.at[pl.ds(pl.multiple_of(peer[1] // 2 * PAIR, PAIR), PAIR), :], target.at[me.col], *semaphore, peer
            )
            copy.start()
            sent.append(copy)
            arrivals.append(remote(source.at[pl.ds(0, PAIR), :], target.at[origin], *semaphore, peer))
        semaphore = (in_send.at[2, distance - 1], in_recv.at[2, distance - 1])
        copy = remote(v_ref, v_out.at[me.col], *semaphore, peer)
        copy.start()
        sent.append(copy)
        arrivals.append(remote(v_ref, v_out.at[origin], *semaphore, peer))
    for copy in own_copies:
        copy.wait()
    for n in range(4):
        for piece in range(3):
            arrived(piece, 0, n)
    for piece in range(3):
        begin(piece, 1)
    for piece in range(3):
        begin(piece, 2, 0)
    for n in range(4):
        for piece in range(3):
            arrived(piece, 1, n)
            if n < 2:
                begin(piece, 2, n + 1)
            elif n == 3:
                begin(piece, 2, 3)
    for n in (0, 1):
        for piece in range(3):
            arrived(piece, 2, n, 0)
    for u in range(1, 4):
        for n in (0, 1):
            for piece in range(3):
                arrived(piece, 2, n, u)
    for u in range(4):
        for n in (2, 3):
            for piece in range(3):
                arrived(piece, 2, n, u)
    for copy in arrivals:
        copy.wait_recv()
    for copy in waits:
        copy.wait()
    for copy in sent:
        copy.wait_send()


def gather_all(blocks, x, g, v):
    whole = jax.ShapeDtypeStruct((2, 2, 4, 4, 32, PACK), BF16)
    tokens = jax.ShapeDtypeStruct((4, PAIR, 272), BF16)
    return pl.pallas_call(
        gather_kernel,
        out_shape=(whole, whole, whole, tokens, tokens, jax.ShapeDtypeStruct((4, 8, 272), F32)),
        in_specs=[ANY] * 6,
        out_specs=(ANY,) * 6,
        scratch_shapes=[
            pltpu.SemaphoreType.DMA((3, 2, 4)),
            pltpu.SemaphoreType.DMA((3, 2, 4)),
            pltpu.SemaphoreType.DMA((3, 4, 4)),
            pltpu.SemaphoreType.DMA((3, 4, 4)),
            pltpu.SemaphoreType.DMA((3,)),
            pltpu.SemaphoreType.DMA((3, 3)),
            pltpu.SemaphoreType.DMA((3, 3)),
            pltpu.SemaphoreType.DMA((3,)),
        ],
        compiler_params=pltpu.CompilerParams(collective_id=0, has_side_effects=True),
        name="gather_weights",
    )(*blocks, x, g, v)


def exchange_kernel(source, target, send, recv, local):
    row, col = lax.axis_index("row"), lax.axis_index("col")
    in_group = lax.rem(row + 2, 4)
    rank = in_group * 4 + col

    def device(other):
        return (lax.rem(row - in_group + other // 4 + 32, 32), lax.rem(other, 4))

    greet([device(lax.rem(rank + d, 16)) for d in range(1, 16)])
    own = pltpu.make_async_copy(source.at[rank], target.at[rank], local)
    own.start()
    copies = []
    for d in range(1, 16):
        other = lax.rem(rank + d, 16)
        copy = pltpu.make_async_remote_copy(
            src_ref=source.at[other], dst_ref=target.at[rank], send_sem=send.at[d], recv_sem=recv.at[d],
            device_id=device(other), device_id_type=MESH,
        )
        copy.start()
        copies.append(copy)
    for d in range(1, 16):
        origin = lax.rem(rank + 16 - d, 16)
        pltpu.make_async_remote_copy(
            src_ref=source.at[origin], dst_ref=target.at[origin], send_sem=send.at[d], recv_sem=recv.at[d],
            device_id=device(origin), device_id_type=MESH,
        ).wait_recv()
    for copy in copies:
        copy.wait_send()
    own.wait()


def exchange(source, collective_id):
    return pl.pallas_call(
        exchange_kernel,
        out_shape=jax.ShapeDtypeStruct(source.shape, source.dtype),
        in_specs=[ANY],
        out_specs=ANY,
        scratch_shapes=[
            pltpu.SemaphoreType.DMA((16,)),
            pltpu.SemaphoreType.DMA((16,)),
            pltpu.SemaphoreType.DMA,
        ],
        compiler_params=pltpu.CompilerParams(collective_id=collective_id, has_side_effects=True),
        name="exchange_heads",
    )(source)


def exchange_pairs_kernel(source, last, target, last_out, send, recv, local, last_sem):
    row, col = lax.axis_index("row"), lax.axis_index("col")
    in_group = lax.rem(row + 2, 4)
    rank = in_group * 4 + col
    core = lax.rem(col, 2)

    def device(other):
        return (lax.rem(row - in_group + other // 4 + 32, 32), lax.rem(other, 4))

    greet([device(lax.rem(rank + d, 16)) for d in range(1, 16)])
    own = pltpu.make_async_copy(source.at[rank // 2], target.at[rank], local.at[0])
    own.start()
    own_last = pltpu.make_async_copy(last, last_out.at[core], local.at[1])
    own_last.start()
    copies = []
    for d in range(1, 16):
        other = lax.rem(rank + d, 16)
        copy = remote(source.at[other // 2], target.at[rank], send.at[d], recv.at[d], device(other))
        copy.start()
        copies.append(copy)
    partner = (row, col + 1 - 2 * core)
    copy = remote(last, last_out.at[core], last_sem.at[0], last_sem.at[1], partner)
    copy.start()
    copies.append(copy)
    for d in range(1, 16):
        origin = lax.rem(rank + 16 - d, 16)
        remote(source.at[rank // 2], target.at[origin], send.at[d], recv.at[d], device(origin)).wait_recv()
    remote(last, last_out.at[1 - core], last_sem.at[0], last_sem.at[1], partner).wait_recv()
    for copy in copies:
        copy.wait_send()
    own.wait()
    own_last.wait()


def exchange_pairs(source, last, collective_id):
    return pl.pallas_call(
        exchange_pairs_kernel,
        out_shape=(
            jax.ShapeDtypeStruct((16, 128, 128), source.dtype), jax.ShapeDtypeStruct((2, QUARTER, 64), last.dtype)
        ),
        in_specs=[ANY] * 2,
        out_specs=(ANY,) * 2,
        scratch_shapes=[
            pltpu.SemaphoreType.DMA((16,)),
            pltpu.SemaphoreType.DMA((16,)),
            pltpu.SemaphoreType.DMA((2,)),
            pltpu.SemaphoreType.DMA((2,)),
        ],
        compiler_params=pltpu.CompilerParams(collective_id=collective_id, has_side_effects=True),
        name="exchange_mixed",
    )(source, last)


def free_axes(fixed):
    return [axis for axis in ("y", "z", "x") if axis not in fixed]


def buffer_shape(fixed, rows):
    shape = ()
    for axis in free_axes(fixed):
        shape = shape + ((2, 2) if axis == "y" else (4,))
    return shape + (rows, PACK)


def buffer_index(at):
    index = ()
    for axis in ("y", "z", "x"):
        if axis in at:
            index = index + ((lax.rem(at[axis], 2), at[axis] // 2) if axis == "y" else (at[axis],))
    return index


VECTOR_AXES = ("z", "x", "y")


def scatter_kernel(part0, part1, part2, y_ref, gin_ref, v_ref, out_ref, y_out, gin_out, v_out, *scratch):
    me = Place()
    parts = (part0, part1, part2)
    sums = scratch[0:3]
    halves = {}
    fulls = {}
    position = 3
    for piece in range(3):
        for stage in range(3):
            halves[piece, stage] = scratch[position : position + 2]
            fulls[piece, stage] = scratch[position + 2 : position + 4]
            position += 4
    vectors = scratch[position : position + 3]
    position += 3
    local, big_send, big_recv, send, recv, out_send, out_recv, out_local, v_send, v_recv = scratch[position:]
    greet(me.neighbours() + [me.step(axis, 2) for axis in VECTOR_AXES])

    sent, loads = [], {}
    for k in range(3):
        for u in range(4):
            for piece in range(3):
                first, second = SCATTER_ORDERS[piece][:2]
                index = place_index(
                    {first: lax.rem(me.at[first] + (2, 1, 3)[k], 4), second: lax.rem(me.at[second] + (2, 1, 3, 0)[u], 4)}
                )
                load = pltpu.make_async_copy(parts[piece].at[index], sums[piece].at[index], local.at[piece, k, u])
                load.start()
                loads[piece, k, u] = load
    for u in range(4):
        for piece in range(3):
            first, second = SCATTER_ORDERS[piece][:2]
            index = place_index({first: me.at[first], second: lax.rem(me.at[second] + (2, 1, 3, 0)[u], 4)})
            load = pltpu.make_async_copy(parts[piece].at[index], sums[piece].at[index], local.at[piece, 3, u])
            load.start()
            loads[piece, 3, u] = load

    def vectors_begin(phase, value):
        axis = VECTOR_AXES[phase]
        mine = vectors[phase].at[me.at[axis]]
        mine[...] = value
        for distance in (1, 2, 3):
            copy = remote(
                mine, mine, v_send.at[phase, distance - 1], v_recv.at[phase, distance - 1], me.step(axis, distance)
            )
            copy.start()
            sent.append(copy)

    def vectors_end(phase):
        axis = VECTOR_AXES[phase]
        for distance in (1, 2, 3):
            there = vectors[phase].at[lax.rem(me.at[axis] + 4 - distance, 4)]
            remote(
                there, there, v_send.at[phase, distance - 1], v_recv.at[phase, distance - 1], me.step(axis, distance)
            ).wait_recv()
        buffer = vectors[phase]
        return (buffer[0] + buffer[1]) + (buffer[2] + buffer[3])

    def stage_fixed(piece, stage):
        return {axis: me.at[axis] for axis in SCATTER_ORDERS[piece][:stage]}

    def each_tile(fixed, body):
        axes = free_axes(fixed)
        count = 4 ** len(axes)
        if count == 1:
            body({})
            return

        @pl.loop(0, count)
        def _(t):
            if len(axes) == 1:
                body({axes[0]: t})
            else:
                body({axes[0]: t // 4, axes[1]: lax.rem(t, 4)})

    def chunk(piece, stage, u):
        if stage > 0:
            return {}
        axis = SCATTER_ORDERS[piece][1]
        return {axis: lax.rem(me.at[axis] + (2, 1, 3, 0)[u], 4)}

    def sems(piece, stage, n, u):
        if stage == 0:
            return big_send.at[piece, u, n], big_recv.at[piece, u, n]
        return send.at[piece, stage - 1, n], recv.at[piece, stage - 1, n]

    def part_of(buffer, piece, stage, u):
        if stage > 0:
            return buffer
        axis = SCATTER_ORDERS[piece][1]
        value = lax.rem(me.at[axis] + (2, 1, 3, 0)[u], 4)
        index = ()
        for name in free_axes({SCATTER_ORDERS[piece][0]: 0}):
            if name == "y":
                index += (lax.rem(value, 2), value // 2) if name == axis else (everything(), everything())
            else:
                index += (value,) if name == axis else (everything(),)
        return buffer.at[index]

    def begin(piece, stage, u=0):
        axis = SCATTER_ORDERS[piece][stage]
        fixed = {**stage_fixed(piece, stage), axis: lax.rem(me.at[axis] + 2, 4), **chunk(piece, stage, u)}
        for n in range(2):
            copy = remote(
                sums[piece].at[place_index(fixed) + (pl.ds(16 * n, 16),)],
                part_of(halves[piece, stage][n], piece, stage, u),
                *sems(piece, stage, n, u), me.step(axis, (1, -1)[n]),
            )
            copy.start()
            sent.append(copy)

    def middle(piece, stage, n, u=0):
        axis = SCATTER_ORDERS[piece][stage]
        more = chunk(piece, stage, u)
        fixed = {**stage_fixed(piece, stage), axis: lax.rem(me.at[axis] + (1, 3)[n], 4), **more}
        half = halves[piece, stage][n]
        there = part_of(half, piece, stage, u)
        remote(there, there, *sems(piece, stage, n, u), me.step(axis, 1)).wait_recv()

        def body(at):
            index = place_index({**fixed, **at}) + (pl.ds(16 * n, 16),)
            total = sums[piece][index].astype(F32) + half[buffer_index({**more, **at})].astype(F32)
            sums[piece][index] = total.astype(BF16)

        each_tile(fixed, body)
        copy = remote(
            sums[piece].at[place_index(fixed)], part_of(fulls[piece, stage][n], piece, stage, u),
            *sems(piece, stage, 2 + n, u), me.step(axis, (1, -1)[n]),
        )
        copy.start()
        sent.append(copy)

    def finish(piece, stage, u=0):
        axis = SCATTER_ORDERS[piece][stage]
        more = chunk(piece, stage, u)
        fixed = {**stage_fixed(piece, stage), axis: me.at[axis], **more}
        first, second = fulls[piece, stage]
        for n, buffer in enumerate((first, second)):
            there = part_of(buffer, piece, stage, u)
            remote(there, there, *sems(piece, stage, 2 + n, u), me.step(axis, 1)).wait_recv()

        def body(at):
            index = place_index({**fixed, **at})
            place = buffer_index({**more, **at})
            if stage == 2:
                total = sums[piece][index].astype(F32) + (first[...].astype(F32) + second[...].astype(F32))
                out_ref[piece] = total
            else:
                total = sums[piece][index].astype(F32) + (first[place].astype(F32) + second[place].astype(F32))
                sums[piece][index] = total.astype(BF16)

        each_tile(fixed, body)

    for u in range(4):
        for piece in range(3):
            loads[piece, 0, u].wait()
            begin(piece, 0, u)
    vectors_begin(0, v_ref[...])

    pairs = ((y_ref, y_out), (gin_ref, gin_out))
    arrivals, own_copies = [], []
    for n, (source, target) in enumerate(pairs):
        rows = pl.ds(pl.multiple_of(me.col * QUARTER, QUARTER), QUARTER)
        own = pltpu.make_async_copy(source.at[me.col], target.at[rows, :], out_local.at[n])
        own.start()
        own_copies.append(own)
        for distance in (1, 2, 3):
            peer = me.beside(distance)
            semaphore = (out_send.at[n, distance - 1], out_recv.at[n, distance - 1])
            copy = remote(source.at[peer[1]], target.at[rows, :], *semaphore, peer)
            copy.start()
            sent.append(copy)
            origin = pl.ds(pl.multiple_of(lax.rem(me.col + 4 - distance, 4) * QUARTER, QUARTER), QUARTER)
            arrivals.append(remote(source.at[me.col], target.at[origin, :], *semaphore, peer))

    def finish_chunk(u):
        for piece in range(3):
            loads[piece, 3, u].wait()
            finish(piece, 0, u)
            if u == 0:
                begin(piece, 1)
            elif u < 3:
                middle(piece, 1, u - 1)
            else:
                finish(piece, 1)
                begin(piece, 2)

    for u in range(4):
        for n in range(2):
            for piece in range(3):
                loads[piece, 1 + n, u].wait()
                middle(piece, 0, n, u)
        if u < 2:
            vectors_begin(u + 1, vectors_end(u))
        if u == 3:
            v_out[...] = vectors_end(2)
        if u > 0:
            finish_chunk(u - 1)
    finish_chunk(3)
    for n in range(2):
        for piece in range(3):
            middle(piece, 2, n)
    for piece in range(3):
        finish(piece, 2)
    for copy in arrivals:
        copy.wait_recv()
    for copy in own_copies:
        copy.wait()
    for copy in sent:
        copy.wait_send()


def scatter_all(parts, y4, gin4, vectors):
    scratch = [pltpu.VMEM((2, 2, 4, 4, 32, PACK), BF16) for _ in range(3)]
    for piece in range(3):
        order = SCATTER_ORDERS[piece]
        for stage in range(3):
            fixed = order[: stage + 1]
            scratch += [pltpu.VMEM(buffer_shape(fixed, 16), BF16) for _ in range(2)]
            scratch += [pltpu.VMEM(buffer_shape(fixed, 32), BF16) for _ in range(2)]
    scratch += [pltpu.VMEM((4, 8, WIDE), F32) for _ in range(3)]
    scratch += [
        pltpu.SemaphoreType.DMA((3, 4, 4)),
        pltpu.SemaphoreType.DMA((3, 4, 4)),
        pltpu.SemaphoreType.DMA((3, 4, 4)),
        pltpu.SemaphoreType.DMA((3, 2, 4)),
        pltpu.SemaphoreType.DMA((3, 2, 4)),
        pltpu.SemaphoreType.DMA((2, 3)),
        pltpu.SemaphoreType.DMA((2, 3)),
        pltpu.SemaphoreType.DMA((2,)),
        pltpu.SemaphoreType.DMA((3, 3)),
        pltpu.SemaphoreType.DMA((3, 3)),
    ]
    back = jax.ShapeDtypeStruct((512, 272), BF16)
    return pl.pallas_call(
        scatter_kernel,
        out_shape=(jax.ShapeDtypeStruct((3, 32, PACK), F32), back, back, jax.ShapeDtypeStruct((8, WIDE), F32)),
        in_specs=[ANY] * 5 + [VMEM_SPEC],
        out_specs=(VMEM_SPEC, ANY, ANY, VMEM_SPEC),
        scratch_shapes=scratch,
        compiler_params=pltpu.CompilerParams(
            collective_id=3, has_side_effects=True, vmem_limit_bytes=VMEM_LIMIT
        ),
        name="scatter_gradients",
    )(*parts, y4, gin4, vectors)


def unpack_tail(packed, tiles, wide, tail):
    tiles[...] = packed[:, WIDE:PACK].astype(F32)
    for j in range(2):
        for s in range(9):
            wide[pl.ds(32 * j, 32), pl.ds(128 * s, 128)] = tiles[pl.ds(9 * j + s, 32, stride=32), :]
    tail[0:64, :] = wide[0:64, :].astype(BF16)


def pack_tail(tail, tiles, packed):
    for j in range(2):
        for s in range(9):
            tiles[pl.ds(9 * j + s, 32, stride=32), :] = tail[32 * j : 32 * j + 32, 128 * s : 128 * s + 128]
    packed[:, WIDE:PACK] = tiles[...].astype(BF16)


def in_features(values, packed, tail, columns):
    return dot_nn(values[:, :MAIN], packed[:, columns]) + dot_nn(values[:, MAIN:], tail[:, columns])


def add_to_features(total_t, values_t, packed, tail):
    @pl.loop(0, 4)
    def _(b):
        rows = pl.ds(pl.multiple_of(b * 256, 256), 256)
        total_t[rows, :] += dot_nn(packed[rows, :WIDE], values_t[...])

    total_t[MAIN:, :] += dot_nn(tail[...], values_t[...])


def norm_forward(x, gain, bias):
    mean = jnp.sum(x, axis=1, keepdims=True) / D
    square = jnp.sum(x * x, axis=1, keepdims=True) / D
    inverse = lax.rsqrt(square - mean * mean + norm_epsilon)
    normed = (x - mean) * inverse
    return normed, inverse, (normed * gain + bias).astype(BF16)


def norm_reverse(grad, normed, inverse, gain):
    scaled = grad * gain
    first = jnp.sum(scaled, axis=1, keepdims=True) / D
    second = jnp.sum(scaled * normed, axis=1, keepdims=True) / D
    return inverse * (scaled - first - normed * second)


def permuted(pieces, perm):
    total = dot_nn(pieces[0], perm[0])
    for c in range(1, 4):
        total += dot_nn(pieces[c], perm[c])
    return total


def permuted_exact(pieces, perm):
    total = jnp.zeros((8, WIDE), F32)
    for c in range(4):
        left = pieces[c]
        for _ in range(3):
            part = left.astype(BF16)
            left = left - part.astype(F32)
            total += dot_nn(part, perm[c])
    return total


def real_features(values):
    lane = lax.broadcasted_iota(jnp.int32, values.shape, 1)
    return jnp.where(lane < D, values, 0.0)


def turned(values):
    return values.astype(F32).T.astype(BF16)


def own_half(core):
    return pl.ds(pl.multiple_of(core * QUARTER, QUARTER), QUARTER)


def load_weights(source, target, semaphores):
    copies = []
    for j in range(2):
        copy = pltpu.make_async_copy(source.at[j], target.at[j], semaphores.at[j])
        copy.start()
        copies.append(copy)
    return copies


def qkv_kernel(x4, v4, perm, w_ref, x_out, n1_out, v_out, qkv_out, w, qkv, tiles, wide, tail, load, send, recv, local):
    me = Place()
    partner = me.partner()
    copies = load_weights(w_ref, w, load)
    greet([partner])
    x = permuted(x4, perm)
    vectors = permuted_exact(v4, perm)
    v_out[...] = vectors
    x_out[...] = x.astype(BF16)
    _, _, normed = norm_forward(x, vectors[0:1], vectors[1:2])
    n1_out[...] = normed
    tail[...] = jnp.zeros_like(tail)
    mine, theirs = own_half(me.core), own_half(1 - me.core)
    sent, own_copies, arrivals = [], [], []
    for j in range(2):
        copies[j].wait()
        packed = w.at[j]
        unpack_tail(packed, tiles, wide, tail)

        @pl.loop(0, 3)
        def _(b):
            columns = pl.ds(pl.multiple_of(b * 384, 128), 384)
            qkv[j, :, columns] = in_features(n1_out[...], packed, tail, columns).astype(BF16)

        own = pltpu.make_async_copy(qkv.at[j, mine, :], qkv_out.at[j, me.core], local.at[j])
        own.start()
        own_copies.append(own)
        copy = remote(qkv.at[j, theirs, :], qkv_out.at[j, me.core], send.at[j], recv.at[j], partner)
        copy.start()
        sent.append(copy)
        arrivals.append(
            remote(qkv.at[j, theirs, :], qkv_out.at[j, 1 - me.core], send.at[j], recv.at[j], partner)
        )
    for copy in arrivals:
        copy.wait_recv()
    for copy in own_copies:
        copy.wait()
    for copy in sent:
        copy.wait_send()


def qkv_call(x4, v4, perm, weights):
    row = jax.ShapeDtypeStruct((PAIR, WIDE), BF16)
    return pl.pallas_call(
        qkv_kernel,
        out_shape=(
            row, row, jax.ShapeDtypeStruct((8, WIDE), F32), jax.ShapeDtypeStruct((2, 2, QUARTER, WIDE), BF16)
        ),
        in_specs=[VMEM_SPEC, VMEM_SPEC, VMEM_SPEC, ANY],
        out_specs=(VMEM_SPEC, VMEM_SPEC, VMEM_SPEC, ANY),
        scratch_shapes=[
            pltpu.VMEM((2, MAIN, PACK), BF16), pltpu.VMEM((2, PAIR, WIDE), BF16),
            pltpu.VMEM((MAIN, 128), F32), pltpu.VMEM((128, WIDE), F32), pltpu.VMEM((128, WIDE), BF16),
            pltpu.SemaphoreType.DMA((2,)), pltpu.SemaphoreType.DMA((2,)), pltpu.SemaphoreType.DMA((2,)),
            pltpu.SemaphoreType.DMA((2,)),
        ],
        compiler_params=pltpu.CompilerParams(
            collective_id=4, has_side_effects=True, vmem_limit_bytes=VMEM_LIMIT
        ),
        name="norm_and_qkv",
    )(x4, v4, perm, weights)


def gelu_both(v):
    square = v * v
    tanh_value = jnp.tanh(gelu_coef * (v + 0.044715 * v * square))
    half = 0.5 * (1.0 + tanh_value)
    value = v * half
    slope = half + 0.5 * v * (1.0 - tanh_value * tanh_value) * gelu_coef * (1.0 + 0.134145 * square)
    return value, slope


def weight_gradient(rows_t, values, tiles, tail_sum, packed):
    @pl.loop(0, 4)
    def _(b):
        rows = pl.ds(pl.multiple_of(b * 256, 256), 256)
        packed[rows, :WIDE] = dot_nn(rows_t[rows, :], values[...]).astype(BF16)

    tail_sum[...] = dot_nn(rows_t[MAIN:, :], values[...])
    pack_tail(tail_sum, tiles, packed)


def swap_start(total_t, mine, theirs, ssem, rsem, partner):
    mine[...] = total_t[...].astype(BF16)
    copy = remote(mine, theirs, ssem, rsem, partner)
    copy.start()
    return copy


def swap_end(copy, mine, theirs):
    copy.wait_recv()
    return mine[...].astype(F32) + theirs[...].astype(F32)


def middle_kernel(
    x_ref, a0, w0_ref, w1_ref, w2_ref, g4, perm, vec,
    y4, dres_out, dresb_out, gr1_out, gr2_out, dmix_out, vec_out,
    w0, w1, w2, gr1, gr2, resid, normed2, inverse2, n2, n2_t, cot, cot_t, total_t, dn2_t, hidden, dpre, turn1, turn2,
    dmix, tiles, out_tiles, tail1, tail2, tail_sum, mine1, theirs1, mine2, theirs2, mine_y, theirs_y,
    load, store, send, recv, local,
):
    me = Place()
    partner = me.partner()
    loads = [load_weights(source, target, load.at[n]) for n, (source, target) in enumerate(
        ((w0_ref, w0), (w1_ref, w1), (w2_ref, w2))
    )]
    greet([partner])
    for buffer in (tail1, tail2, out_tiles, total_t, dn2_t):
        buffer[...] = jnp.zeros_like(buffer)
    for j in range(2):
        turn1[...] = turned(a0[j])
        loads[0][j].wait()
        unpack_tail(w0.at[j], tiles, tail_sum, tail1)
        add_to_features(total_t, turn1, w0.at[j], tail1)
    first = swap_start(total_t, mine1, theirs1, send.at[0], recv.at[0], partner)
    cot_value = permuted(g4, perm)
    cot[...] = cot_value.astype(BF16)
    cot_t[...] = cot_value.T.astype(BF16)
    total_t[...] = jnp.zeros_like(total_t)
    attended = swap_end(first, mine1, theirs1)
    resid[...] = x_ref[...].astype(F32) + attended.T
    normed, inverse, n2_value = norm_forward(resid[...], vec[2:3], vec[3:4])
    normed2[...] = normed
    inverse2[...] = jnp.broadcast_to(inverse, inverse2.shape)
    n2[...] = n2_value
    n2_t[...] = turned(n2_value)
    stores = []
    for j in range(2):
        loads[1][j].wait()
        loads[2][j].wait()
        up, down = w1.at[j], w2.at[j]
        unpack_tail(up, tiles, tail_sum, tail1)
        unpack_tail(down, tiles, tail_sum, tail2)

        @pl.loop(0, 3)
        def _(b):
            columns = pl.ds(pl.multiple_of(b * 384, 128), 384)
            pre = in_features(n2[...], up, tail1, columns)
            d_hidden = in_features(cot[...], down, tail2, columns)
            value, slope = gelu_both(pre)
            hidden[:, columns] = value.astype(BF16)
            dpre[:, columns] = (d_hidden * slope).astype(BF16)

        turn1[...] = turned(hidden[...])
        turn2[...] = turned(dpre[...])
        add_to_features(total_t, turn1, down, tail2)
        add_to_features(dn2_t, turn2, up, tail1)
        if j == 1:
            second = swap_start(dn2_t, mine2, theirs2, send.at[1], recv.at[1], partner)
            half = own_half(1 - me.core)
            mine_y[...] = total_t[:, half].astype(BF16)
            third = remote(mine_y, theirs_y, send.at[2], recv.at[2], partner)
            third.start()
        weight_gradient(n2_t, dpre, out_tiles, tail_sum, gr1.at[j])
        weight_gradient(cot_t, hidden, out_tiles, tail_sum, gr2.at[j])
        for n, (source, target) in enumerate(((gr1, gr1_out), (gr2, gr2_out))):
            copy = pltpu.make_async_copy(source.at[j], target.at[j], store.at[n, j])
            copy.start()
            stores.append(copy)
    grad = swap_end(second, mine2, theirs2).T
    normed = normed2[...]
    vec_out[...] = jnp.zeros_like(vec_out)
    vec_out[0:1, :] = jnp.sum(grad * normed, axis=0, keepdims=True)
    vec_out[1:2, :] = jnp.sum(grad, axis=0, keepdims=True)
    back = cot[...].astype(F32) + norm_reverse(grad, normed, inverse2[:, 0:1], vec[2:3])
    back = real_features(back)
    dres_out[...] = back
    dresb_out[...] = back.astype(BF16)
    sent, own_copies, arrivals = [first, second, third], [], []
    columns = slice(768, WIDE)
    for j in range(2):
        unpack_tail(w0.at[j], tiles, tail_sum, tail1)
        dmix[j] = in_features(dresb_out[...], w0.at[j], tail1, columns).astype(BF16)
        own = pltpu.make_async_copy(dmix.at[j, own_half(me.core), :], dmix_out.at[j, me.core], local.at[j])
        own.start()
        own_copies.append(own)
        theirs = dmix.at[j, own_half(1 - me.core), :]
        copy = remote(theirs, dmix_out.at[j, me.core], send.at[3 + j], recv.at[3 + j], partner)
        copy.start()
        sent.append(copy)
        arrivals.append(remote(theirs, dmix_out.at[j, 1 - me.core], send.at[3 + j], recv.at[3 + j], partner))
    half = own_half(me.core)
    third.wait_recv()
    y = (resid[half, :] + (total_t[:, half] + theirs_y[...].astype(F32)).T).astype(BF16)
    for c in range(4):
        y4[c] = dot_nt(y, perm[c]).astype(BF16)
    for copy in arrivals:
        copy.wait_recv()
    for copy in own_copies + stores:
        copy.wait()
    for copy in sent:
        copy.wait_send()


def middle_call(x, a0, w0, w1, w2, g4, perm, vec):
    packed = jax.ShapeDtypeStruct((2, MAIN, PACK), BF16)
    weights = pltpu.VMEM((2, MAIN, PACK), BF16)
    row_f, row_b = pltpu.VMEM((PAIR, WIDE), F32), pltpu.VMEM((PAIR, WIDE), BF16)
    turn_f, turn_b = pltpu.VMEM((WIDE, PAIR), F32), pltpu.VMEM((WIDE, PAIR), BF16)
    tile, tail = pltpu.VMEM((MAIN, 128), F32), pltpu.VMEM((128, WIDE), BF16)
    half = pltpu.VMEM((WIDE, QUARTER), BF16)
    return pl.pallas_call(
        middle_kernel,
        out_shape=(
            jax.ShapeDtypeStruct((4, QUARTER, 272), BF16), jax.ShapeDtypeStruct((PAIR, WIDE), F32),
            jax.ShapeDtypeStruct((PAIR, WIDE), BF16), packed, packed,
            jax.ShapeDtypeStruct((2, 2, QUARTER, 384), BF16), jax.ShapeDtypeStruct((8, WIDE), F32),
        ),
        in_specs=[VMEM_SPEC, VMEM_SPEC, ANY, ANY, ANY, VMEM_SPEC, VMEM_SPEC, VMEM_SPEC],
        out_specs=(VMEM_SPEC, VMEM_SPEC, VMEM_SPEC, ANY, ANY, ANY, VMEM_SPEC),
        scratch_shapes=[
            weights, weights, weights, weights, weights, row_f, row_f, pltpu.VMEM((PAIR, 128), F32), row_b, turn_b,
            row_b, turn_b, turn_f, turn_f, row_b, row_b, turn_b, turn_b, pltpu.VMEM((2, PAIR, 384), BF16),
            tile, tile, tail, tail, pltpu.VMEM((128, WIDE), F32), turn_b, turn_b, turn_b, turn_b, half, half,
            pltpu.SemaphoreType.DMA((3, 2)), pltpu.SemaphoreType.DMA((2, 2)), pltpu.SemaphoreType.DMA((5,)),
            pltpu.SemaphoreType.DMA((5,)), pltpu.SemaphoreType.DMA((2,)),
        ],
        compiler_params=pltpu.CompilerParams(
            collective_id=5, has_side_effects=True, vmem_limit_bytes=VMEM_LIMIT
        ),
        name="feed_forward",
    )(x, a0, w0, w1, w2, g4, perm, vec)


def first_kernel(
    x_ref, n1, dresb, dres, dq_ref, a0, w0_ref, perm, vec, vec2,
    gin4, gr0_out, sums,
    w0, gr0, dq, n1_t, dres_t, turn, dn1_t, tiles, out_tiles, tail, tail_sum, mine, theirs,
    load, store, send, recv, local,
):
    me = Place()
    partner = me.partner()
    loads = load_weights(w0_ref, w0, load)
    greet([partner])
    mine_rows = own_half(me.core)
    copy = remote(dq_ref.at[1 - me.core], dq.at[:, mine_rows, :], send.at[0], recv.at[0], partner)
    copy.start()
    own = pltpu.make_async_copy(dq_ref.at[me.core], dq.at[:, mine_rows, :], local)
    own.start()
    for buffer in (tail, out_tiles, dn1_t):
        buffer[...] = jnp.zeros_like(buffer)
    n1_t[...] = turned(n1[...])
    dres_t[...] = turned(dresb[...])
    normed, inverse, _ = norm_forward(x_ref[...].astype(F32), vec[0:1], vec[1:2])
    own.wait()
    remote(
        dq_ref.at[me.core], dq.at[:, own_half(1 - me.core), :], send.at[0], recv.at[0], partner
    ).wait_recv()
    for j in range(2):
        loads[j].wait()
        unpack_tail(w0.at[j], tiles, tail_sum, tail)
        turn[...] = turned(dq[j])
        add_to_features(dn1_t, turn, w0.at[j], tail)
    swap = swap_start(dn1_t, mine, theirs, send.at[1], recv.at[1], partner)
    stores = []
    for j in range(2):
        packed = gr0.at[j]

        @pl.loop(0, 4)
        def _(b):
            rows = pl.ds(pl.multiple_of(b * 256, 256), 256)
            packed[rows, :768] = dot_nn(n1_t[rows, :], dq[j, :, :768]).astype(BF16)
            packed[rows, 768:WIDE] = (
                dot_nn(n1_t[rows, :], dq[j, :, 768:]) + dot_nn(dres_t[rows, :], a0[j, :, 768:])
            ).astype(BF16)

        tail_sum[:, :768] = dot_nn(n1_t[MAIN:, :], dq[j, :, :768])
        tail_sum[:, 768:] = dot_nn(n1_t[MAIN:, :], dq[j, :, 768:]) + dot_nn(dres_t[MAIN:, :], a0[j, :, 768:])
        pack_tail(tail_sum, out_tiles, packed)
        out = pltpu.make_async_copy(packed, gr0_out.at[j], store.at[j])
        out.start()
        stores.append(out)
    grad = swap_end(swap, mine, theirs).T
    sums[...] = vec2[...]
    sums[4:5, :] = jnp.sum(grad * normed, axis=0, keepdims=True)
    sums[5:6, :] = jnp.sum(grad, axis=0, keepdims=True)
    back = dres[...] + norm_reverse(grad, normed, inverse, vec[0:1])
    dn1_t[...] = real_features(back).T
    back = dn1_t[:, mine_rows].T.astype(BF16)
    for c in range(4):
        gin4[c] = dot_nt(back, perm[c]).astype(BF16)
    for out in stores:
        out.wait()
    copy.wait_send()
    swap.wait_send()


def first_call(x, n1, dresb, dres, dq, a0, w0, perm, vec, vec2):
    weights = pltpu.VMEM((2, MAIN, PACK), BF16)
    turn_b = pltpu.VMEM((WIDE, PAIR), BF16)
    tile = pltpu.VMEM((MAIN, 128), F32)
    return pl.pallas_call(
        first_kernel,
        out_shape=(
            jax.ShapeDtypeStruct((4, QUARTER, 272), BF16), jax.ShapeDtypeStruct((2, MAIN, PACK), BF16),
            jax.ShapeDtypeStruct((8, WIDE), F32),
        ),
        in_specs=[VMEM_SPEC] * 4 + [ANY, VMEM_SPEC, ANY] + [VMEM_SPEC] * 3,
        out_specs=(VMEM_SPEC, ANY, VMEM_SPEC),
        scratch_shapes=[
            weights, weights, pltpu.VMEM((2, PAIR, WIDE), BF16), turn_b, turn_b, turn_b,
            pltpu.VMEM((WIDE, PAIR), F32), tile, tile, pltpu.VMEM((128, WIDE), BF16), pltpu.VMEM((128, WIDE), F32),
            turn_b, turn_b,
            pltpu.SemaphoreType.DMA((2,)), pltpu.SemaphoreType.DMA((2,)), pltpu.SemaphoreType.DMA((2,)),
            pltpu.SemaphoreType.DMA((2,)), pltpu.SemaphoreType.DMA,
        ],
        compiler_params=pltpu.CompilerParams(
            collective_id=6, has_side_effects=True, vmem_limit_bytes=VMEM_LIMIT
        ),
        name="first_norm_back",
    )(x, n1, dresb, dres, dq, a0, w0, perm, vec, vec2)


def allowed_pairs(shape, key_start, query_start):
    key = key_start + lax.broadcasted_iota(jnp.int32, shape, 0)
    query = query_start + lax.broadcasted_iota(jnp.int32, shape, 1)
    return key <= query


def transposed(values):
    return values.astype(F32).T


def attend_kernel(info, r_ref, q16, o_out, dense_out, o16_out, l_out, l16_out, query, value_t, value16_t):
    rank, wraps = info[0], info[1]

    @pl.loop(0, 4)
    def _(b):
        rows = pl.ds(pl.multiple_of(b * KEYS, KEYS), KEYS)
        query[rows, :] = r_ref[rows, 0:64] * jnp.asarray(0.125, BF16)
        value_t[:, rows] = transposed(r_ref[rows, 128:256])[0:64].astype(BF16)
        value16_t[:, rows] = transposed(r_ref[rows, 256:384])[0:64].astype(BF16)

    def step(q, columns, v_t, j, carry, query_start=None):
        peak, running, mixed = carry
        rows = pl.ds(pl.multiple_of(j * KEYS, KEYS), KEYS)
        scores = dot_nt(r_ref[rows, columns], q)
        if query_start is not None:
            scores = jnp.where(allowed_pairs(scores.shape, j * KEYS, query_start), scores, masked_score)
        new_peak = jnp.maximum(peak, jnp.max(scores, axis=0, keepdims=True))
        shrink = jnp.exp(peak - new_peak)
        weights = jnp.exp(scores - new_peak)
        running = running * shrink + jnp.sum(weights, axis=0, keepdims=True)
        mixed = mixed * shrink + dot_nn(v_t[:, rows], weights.astype(BF16))
        return new_peak, running, mixed

    def empty(width):
        return (
            jnp.full((1, width), masked_score, F32), jnp.zeros((1, width), F32), jnp.zeros((64, width), F32)
        )

    @pl.loop(0, 4)
    def _(i):
        rows = pl.ds(pl.multiple_of(i * KEYS, KEYS), KEYS)
        q = query[rows, :]
        start = jnp.where((wraps == 1) & (i >= 2), 2, 0)
        carry = lax.fori_loop(
            start, i, lambda j, carry: step(q, slice(64, 128), value_t, j, carry), empty(KEYS)
        )
        peak, running, mixed = step(q, slice(64, 128), value_t, i, carry, i * KEYS)
        value = (mixed / running).T.astype(BF16)
        o_out[rows, :] = value
        for n in range(4):
            dense_out[2 * i + n // 2, :, 64 * (n % 2) : 64 * (n % 2) + 64] = value[128 * n : 128 * n + 128]
        l_out[:, rows] = peak + jnp.log(running)

    q = q16[...] * jnp.asarray(0.125, BF16)
    start = jnp.where((wraps == 1) & (rank >= 8), 2, 0)
    peak, running, mixed = lax.fori_loop(
        start, rank // 4 + 1,
        lambda j, carry: step(q, slice(192, 256), value16_t, j, carry, rank * QUARTER), empty(QUARTER),
    )
    o16_out[...] = (mixed / running).T.astype(BF16)
    l16_out[...] = peak + jnp.log(running)


def attend_call(info, r, q16):
    return pl.pallas_call(
        attend_kernel,
        out_shape=(
            jax.ShapeDtypeStruct((SEQ, 64), BF16), jax.ShapeDtypeStruct((8, 128, 128), BF16),
            jax.ShapeDtypeStruct((QUARTER, 64), BF16), jax.ShapeDtypeStruct((1, SEQ), F32), jax.ShapeDtypeStruct((1, QUARTER), F32),
        ),
        in_specs=[SMEM_SPEC, VMEM_SPEC, VMEM_SPEC],
        out_specs=(VMEM_SPEC,) * 5,
        scratch_shapes=[pltpu.VMEM((SEQ, 64), BF16), pltpu.VMEM((64, SEQ), BF16), pltpu.VMEM((64, SEQ), BF16)],
        compiler_params=pltpu.CompilerParams(vmem_limit_bytes=VMEM_LIMIT),
        name="attend_forward",
    )(info, r, q16)


def attend_back_kernel(
    info, r_ref, q16, o_ref, o16, do_ref, do16, l_ref, l16,
    msg, dq16_out, query, key_t, key16_t, delta, dq_t,
):
    rank, wraps = info[0], info[1]

    @pl.loop(0, 4)
    def _(b):
        rows = pl.ds(pl.multiple_of(b * KEYS, KEYS), KEYS)
        query[rows, :] = r_ref[rows, 0:64] * jnp.asarray(0.125, BF16)
        key_t[:, rows] = transposed(r_ref[rows, 0:128])[64:128].astype(BF16)
        key16_t[:, rows] = transposed(r_ref[rows, 128:256])[64:128].astype(BF16)
        product = do_ref[rows, :].astype(F32) * o_ref[rows, :].astype(F32)
        delta[:, rows] = jnp.sum(product.T, axis=0, keepdims=True)
        dq_t[:, rows] = jnp.zeros((64, KEYS), F32)

    def pair(keys, values, q, d_out, log_total, delta_row, mask):
        scores = dot_nt(keys, q)
        probs = jnp.exp(scores - log_total)
        if mask is not None:
            probs = jnp.where(mask(scores.shape), probs, 0.0)
        probs = probs.astype(BF16)
        d_prob = dot_nt(values, d_out)
        d_scores = (probs.astype(F32) * (d_prob - delta_row)).astype(BF16)
        return dot_nn(d_scores, q), dot_nn(probs, d_out), d_scores

    @pl.loop(0, 4)
    def _(j):
        rows = pl.ds(pl.multiple_of(j * KEYS, KEYS), KEYS)
        keys, values = r_ref[rows, 64:128], r_ref[rows, 128:192]

        def step(i, carry, mask=None):
            d_key, d_value = carry
            at = pl.ds(pl.multiple_of(i * KEYS, KEYS), KEYS)
            more_key, more_value, d_scores = pair(
                keys, values, query[at, :], do_ref[at, :], l_ref[:, at], delta[:, at], mask
            )
            dq_t[:, at] += dot_nn(key_t[:, rows], d_scores)
            return d_key + more_key, d_value + more_value

        zero = jnp.zeros((KEYS, 64), F32)
        carry = step(j, (zero, zero), lambda shape: allowed_pairs(shape, 0, 0))
        end = jnp.where((wraps == 1) & (j < 2), 2, 4)
        d_key, d_value = lax.fori_loop(j + 1, end, step, carry)
        msg[rows, 64:128] = d_key.astype(BF16)
        msg[rows, 128:192] = d_value.astype(BF16)

    q = q16[...] * jnp.asarray(0.125, BF16)
    d_out16 = do16[...]
    delta16 = jnp.sum((d_out16.astype(F32) * o16[...].astype(F32)).T, axis=0, keepdims=True)
    start = jnp.where((wraps == 1) & (rank >= 8), 2, 0)

    def last_step(j, dq):
        rows = pl.ds(pl.multiple_of(j * KEYS, KEYS), KEYS)
        d_key, d_value, d_scores = pair(
            r_ref[rows, 192:256], r_ref[rows, 256:320], q, d_out16, l16[...], delta16,
            lambda shape: allowed_pairs(shape, j * KEYS, rank * QUARTER),
        )
        msg[rows, 192:256] = d_key.astype(BF16)
        msg[rows, 256:320] = d_value.astype(BF16)
        return dq + dot_nn(key16_t[:, rows], d_scores)

    @pl.loop(0, 4)
    def _(j):
        rows = pl.ds(pl.multiple_of(j * KEYS, KEYS), KEYS)
        msg[rows, 192:256] = jnp.zeros((KEYS, 64), BF16)
        msg[rows, 256:384] = jnp.zeros((KEYS, 128), BF16)
        msg[rows, 0:64] = (dq_t[:, rows] * 0.125).T.astype(BF16)

    dq = lax.fori_loop(start, rank // 4 + 1, last_step, jnp.zeros((64, QUARTER), F32))
    dq16_out[...] = (dq * 0.125).T.astype(BF16)


def attend_back_call(info, r, q16, o, o16, do, do16, log_total, log16):
    return pl.pallas_call(
        attend_back_kernel,
        out_shape=(jax.ShapeDtypeStruct((SEQ, MSG), BF16), jax.ShapeDtypeStruct((QUARTER, 64), BF16)),
        in_specs=[SMEM_SPEC] + [VMEM_SPEC] * 8,
        out_specs=(VMEM_SPEC,) * 2,
        scratch_shapes=[
            pltpu.VMEM((SEQ, 64), BF16), pltpu.VMEM((64, SEQ), BF16), pltpu.VMEM((64, SEQ), BF16),
            pltpu.VMEM((1, SEQ), F32), pltpu.VMEM((64, SEQ), F32),
        ],
        compiler_params=pltpu.CompilerParams(vmem_limit_bytes=VMEM_LIMIT),
        name="attend_backward",
    )(info, r, q16, o, o16, do, do16, log_total, log16)


def packed_block(block):
    tail = jnp.pad(block[32:34], ((0, 0), (0, WIDE - D))).reshape(18, 128)
    return jnp.concatenate(
        [jnp.pad(block[:32], ((0, 0), (0, WIDE - D))), jnp.pad(tail, ((0, 14), (0, 0)))], axis=1
    )


def unpacked_block(packed):
    tail = packed[:18, WIDE:].reshape(2, WIDE)[:, :D]
    return jnp.concatenate([packed[:, :D], tail], axis=0)


def permutation():
    feature = jnp.arange(D, dtype=jnp.int32)
    block, inside = feature // 34, feature % 34
    place = jnp.where(inside < 32, 32 * block + inside, MAIN + 32 * (inside - 32) + block)
    chosen = place[:, None] == jnp.arange(WIDE, dtype=jnp.int32)[None, :]
    return chosen.astype(BF16).reshape(4, 272, WIDE)


def per_device(
    layer_input,
    first_norm_gain,
    first_norm_bias,
    w_qkv,
    w_out,
    second_norm_gain,
    second_norm_bias,
    w_up,
    w_down,
    gradient_of_output,
):
    row, col = lax.axis_index("row"), lax.axis_index("col")
    rank, core = (row + 2) % 4 * 4 + col, col % 2
    wraps = ((row < 2) | (row >= 30)).astype(jnp.int32)
    info = jnp.stack([rank, wraps]).astype(jnp.int32)
    perm = permutation()
    vectors = jnp.concatenate(
        [
            jnp.stack([first_norm_gain, first_norm_bias, second_norm_gain, second_norm_bias]),
            jnp.zeros((4, 272), F32),
        ]
    )
    blocks = (
        packed_block(jnp.concatenate([w_qkv, w_out.T], axis=1)),
        packed_block(w_up),
        packed_block(w_down.T),
    )
    w0, w1, w2, x4, g4, v4 = gather_all(blocks, layer_input, gradient_of_output, vectors)
    w0, w1, w2 = (w.reshape(2, MAIN, PACK) for w in (w0, w1, w2))
    x, n1, vec, qkv4 = qkv_call(x4, v4, perm, w0)
    qkv4 = qkv4.reshape(4, QUARTER, WIDE)

    qkv = jnp.concatenate([qkv4[c, :, :QKV_COLS] for c in range(4)], axis=1).reshape(QUARTER, 3, HEADS, HEAD_DIM)
    last = [jnp.broadcast_to(qkv[:, n, 16:17], (QUARTER, 16, HEAD_DIM)) for n in (1, 2)]
    message = jnp.concatenate(
        [qkv[:, 0, :16], qkv[:, 1, :16], qkv[:, 2, :16], *last, jnp.zeros((QUARTER, 16, 64), BF16)], axis=2
    ).transpose(1, 0, 2)
    q16 = qkv[:, 0, 16]
    heads = exchange(message, 1).reshape(SEQ, MSG)
    o, dense, o16, log_total, log16 = attend_call(info, heads, q16)
    mixed, both16 = exchange_pairs(dense, o16, 2)
    attn = jnp.concatenate(
        [
            mixed.reshape(16, QUARTER, 2, HEAD_DIM).transpose(2, 1, 0, 3).reshape(PAIR, 1024),
            both16.reshape(PAIR, HEAD_DIM),
        ],
        axis=1,
    ).reshape(PAIR, 2, 2, 272)
    attn = lax.dynamic_index_in_dim(attn, core, 2, keepdims=False)
    a0 = jnp.pad(attn.transpose(1, 0, 2), ((0, 0), (0, 0), (QKV_COLS, WIDE - D)))
    y4, dres, dresb, gr1, gr2, dmix4, vec2 = middle_call(x, a0, w0, w1, w2, g4, perm, vec)
    dmix4 = dmix4.reshape(4, QUARTER, 384)[:, :, 48:320]
    dmix = jnp.concatenate([dmix4[c] for c in range(4)], axis=1).reshape(QUARTER, HEADS, HEAD_DIM)
    do = exchange(dmix[:, :16].transpose(1, 0, 2), 7).reshape(SEQ, 64)
    back, dq16 = attend_back_call(info, heads, q16, o, o16, do, dmix[:, 16], log_total, log16)
    back = exchange(back.reshape(16, QUARTER, MSG), 1)
    last_sums = jnp.sum(back[:, :, 192:320].astype(F32), axis=0).astype(BF16)

    def side_by_side(first, last_head):
        return jnp.concatenate(
            [back[:, :, first : first + 64].transpose(1, 0, 2).reshape(QUARTER, 1024), last_head], axis=1
        )

    d_qkv = jnp.concatenate(
        [side_by_side(0, dq16), side_by_side(64, last_sums[:, :64]), side_by_side(128, last_sums[:, 64:])], axis=1
    )
    dq0 = jnp.pad(
        d_qkv.reshape(QUARTER, 2, 2, QKV_COLS).transpose(2, 1, 0, 3), ((0, 0), (0, 0), (0, 0), (0, WIDE - QKV_COLS))
    )
    gin4, gr0, sums4 = first_call(x, n1, dresb, dres, dq0, a0, w0, perm, vec, vec2)
    grouped = tuple(g.reshape(2, 2, 4, 4, 32, PACK) for g in (gr0, gr1, gr2))
    sums, layer_output, gin, sums4 = scatter_all(grouped, y4, gin4, sums4)
    own_perm = lax.dynamic_index_in_dim(perm, col, 0, keepdims=False).astype(F32)
    vg = lax.dot_general(
        sums4, own_perm, (((1,), (1,)), ((), ())),
        preferred_element_type=F32, precision=lax.Precision.HIGHEST,
    )
    s0, s1, s2 = (unpacked_block(sums[n]) for n in range(3))
    return (
        layer_output,
        gin.astype(F32),
        vg[4],
        vg[5],
        s0[:, :QKV_COLS],
        s0[:, QKV_COLS:].T,
        vg[0],
        vg[1],
        s1,
        s2.T,
    )


def solution(mesh):
    placed = (
        P("row", "col"),
        P("col"),
        P("col"),
        P("row", "col"),
        P("col", "row"),
        P("col"),
        P("col"),
        P("row", "col"),
        P("col", "row"),
        P("row", "col"),
    )
    return jax.shard_map(
        per_device,
        mesh=mesh,
        in_specs=placed,
        out_specs=(
            P("row", "col"),
            P("row", "col"),
            P("col"),
            P("col"),
            P("row", "col"),
            P("col", "row"),
            P("col"),
            P("col"),
            P("row", "col"),
            P("col", "row"),
        ),
        check_vma=False,
    )
```

```python
import math

import jax
import jax.numpy as jnp
from jax import lax
from jax.experimental import pallas as pl
from jax.experimental.pallas import tpu as pltpu
from jax.sharding import PartitionSpec as P

HEADS = 17
HEAD_DIM = 64
D = 1088
SEQ = 2048
MAIN = 1024
WIDE = 1152
PACK = 1280
QKV_COLS = 816
QUARTER = 128
PAIR = 256
KEYS = 512

gelu_coef = math.sqrt(2.0 / math.pi)
norm_epsilon = 1e-05
masked_score = -1e30
MESH = pl.DeviceIdType.MESH
F32 = jnp.float32
BF16 = jnp.bfloat16
VMEM_LIMIT = 60 * 1024 * 1024
ANY = pl.BlockSpec(memory_space=pl.ANY)
VMEM_SPEC = pl.BlockSpec(memory_space=pltpu.VMEM)
SMEM_SPEC = pl.BlockSpec(memory_space=pltpu.SMEM)

GATHER_ORDERS = (("x", "y", "z"), ("y", "z", "x"), ("z", "x", "y"))
SCATTER_ORDERS = (("z", "y", "x"), ("x", "z", "y"), ("y", "x", "z"))


def dot_nn(a, b):
    return lax.dot_general(a, b, (((1,), (0,)), ((), ())), preferred_element_type=F32)


def dot_nt(a, b):
    return lax.dot_general(a, b, (((1,), (1,)), ((), ())), preferred_element_type=F32)


class Place:
    def __init__(self):
        self.row = lax.axis_index("row")
        self.col = lax.axis_index("col")
        self.at = {
            "x": lax.rem(self.row, 4),
            "z": lax.rem(self.row // 4, 4),
            "y": (self.row // 16) * 2 + self.col // 2,
        }
        self.core = lax.rem(self.col, 2)

    def device(self, at, core):
        return ((at["y"] // 2) * 16 + at["z"] * 4 + at["x"], lax.rem(at["y"], 2) * 2 + core)

    def step(self, axis, distance):
        at = dict(self.at)
        at[axis] = lax.rem(at[axis] + distance + 4, 4)
        return self.device(at, self.core)

    def partner(self):
        return (self.row, self.col + 1 - 2 * self.core)

    def beside(self, distance):
        return (self.row, lax.rem(self.col + distance, 4))

    def neighbours(self):
        found = [self.step(axis, d) for axis in ("x", "y", "z") for d in (1, -1)]
        found.append(self.partner())
        other = lax.rem(self.col // 2 + 1, 2)
        found.append((self.row, other * 2 + 1 - self.core))
        return found


def greet(devices):
    barrier = pltpu.get_barrier_semaphore()
    for device in devices:
        pl.semaphore_signal(barrier, inc=1, device_id=device, device_id_type=MESH)
    pl.semaphore_wait(barrier, len(devices))


def everything():
    return slice(None)


def place_index(fixed):
    if "y" in fixed:
        y_lo, y_hi = lax.rem(fixed["y"], 2), fixed["y"] // 2
    else:
        y_lo, y_hi = everything(), everything()
    return (y_lo, y_hi, fixed.get("z", everything()), fixed.get("x", everything()))


def remote(source, target, ssem, rsem, device):
    return pltpu.make_async_remote_copy(
        src_ref=source, dst_ref=target, send_sem=ssem, recv_sem=rsem,
        device_id=device, device_id_type=MESH,
    )


def gather_kernel(
    block0, block1, block2, x_ref, g_ref, v_ref,
    all0, all1, all2, x_out, g_out, v_out,
    send, recv, last_send, last_recv, local, in_send, in_recv, in_local,
):
    me = Place()
    blocks = (block0, block1, block2)
    wholes = (all0, all1, all2)
    greet(me.neighbours())

    def region(piece, fixed, rows=None):
        index = place_index(fixed) + ((everything(),) if rows is None else (pl.ds(rows, 16),))
        return wholes[piece].at[index]

    def around(piece, stage, value):
        order = GATHER_ORDERS[piece]
        fixed = {order[stage]: value}
        for axis in order[stage + 1 :]:
            fixed[axis] = me.at[axis]
        return fixed

    sent = []
    pairs = ((x_ref, x_out), (g_ref, g_out))
    waits, arrivals, own_copies = [], [], []
    for piece in range(3):
        copy = pltpu.make_async_copy(
            blocks[piece], region(piece, around(piece, 0, me.at[GATHER_ORDERS[piece][0]])), local.at[piece]
        )
        copy.start()
        own_copies.append(copy)

    def semaphores(piece, stage, n, u):
        if stage == 2:
            return last_send.at[piece, u, n], last_recv.at[piece, u, n]
        return send.at[piece, stage, n], recv.at[piece, stage, n]

    def part(piece, stage, value, u, rows=None):
        fixed = around(piece, stage, value)
        if stage == 2:
            axis = GATHER_ORDERS[piece][1]
            fixed[axis] = lax.rem(me.at[axis] + (0, 3, 1, 2)[u], 4)
        return region(piece, fixed, rows)

    def begin(piece, stage, u=0):
        axis = GATHER_ORDERS[piece][stage]
        mine = part(piece, stage, me.at[axis], u)
        source = blocks[piece] if stage == 0 else mine
        for n, distance in enumerate((1, -1)):
            copy = remote(source, mine, *semaphores(piece, stage, n, u), me.step(axis, distance))
            copy.start()
            sent.append(copy)

    def arrived(piece, stage, n, u=0):
        axis = GATHER_ORDERS[piece][stage]
        value = lax.rem(me.at[axis] + (3, 1, 2, 2)[n], 4)
        there = part(piece, stage, value, u, (None, None, 0, 16)[n])
        remote(there, there, *semaphores(piece, stage, n, u), me.step(axis, 1)).wait_recv()
        if n < 2:
            half = part(piece, stage, value, u, (0, 16)[n])
            copy = remote(half, half, *semaphores(piece, stage, 2 + n, u), me.step(axis, (1, -1)[n]))
            copy.start()
            sent.append(copy)

    for piece in range(3):
        begin(piece, 0)
    partner, across = me.partner(), me.beside(2)

    def tokens_of(ref, col):
        return ref.at[:, pl.ds(pl.multiple_of(col // 2 * PAIR, PAIR), PAIR)]

    relays = []
    for n, (source, target) in enumerate(pairs + ((v_ref, v_out),)):
        here, there = (v_ref, v_ref) if n == 2 else (tokens_of(source, me.col), tokens_of(source, across[1]))
        own = pltpu.make_async_copy(here, target.at[me.col], in_local.at[n])
        own.start()
        waits.append(own)
        for k, (part_ref, device) in enumerate(((there, across), (here, partner))):
            copy = remote(part_ref, target.at[me.col], in_send.at[n, k], in_recv.at[n, k], device)
            copy.start()
            sent.append(copy)
        relays.append(remote(there, target.at[across[1]], in_send.at[n, 0], in_recv.at[n, 0], across))
        arrivals.append(remote(here, target.at[partner[1]], in_send.at[n, 1], in_recv.at[n, 1], partner))
    for copy in own_copies:
        copy.wait()
    for n in range(4):
        for piece in range(3):
            arrived(piece, 0, n)
    for piece in range(3):
        begin(piece, 1)
    for n, (_, target) in enumerate(pairs + ((v_ref, v_out),)):
        relays[n].wait_recv()
        block = target.at[across[1]]
        copy = remote(block, block, in_send.at[n, 2], in_recv.at[n, 2], partner)
        copy.start()
        sent.append(copy)
        far = target.at[lax.rem(partner[1] + 2, 4)]
        arrivals.append(remote(far, far, in_send.at[n, 2], in_recv.at[n, 2], partner))
    for piece in range(3):
        begin(piece, 2, 0)
    for n in range(4):
        for piece in range(3):
            arrived(piece, 1, n)
            if n < 2:
                begin(piece, 2, n + 1)
            elif n == 3:
                begin(piece, 2, 3)
    for n in (0, 1):
        for piece in range(3):
            arrived(piece, 2, n, 0)
    for u in range(1, 4):
        for n in (0, 1):
            for piece in range(3):
                arrived(piece, 2, n, u)
    for u in range(4):
        for n in (2, 3):
            for piece in range(3):
                arrived(piece, 2, n, u)
    for copy in arrivals:
        copy.wait_recv()
    for copy in waits:
        copy.wait()
    for copy in sent:
        copy.wait_send()


def gather_all(blocks, x, g, v):
    whole = jax.ShapeDtypeStruct((2, 2, 4, 4, 32, PACK), BF16)
    tokens = jax.ShapeDtypeStruct((4, 272, PAIR), BF16)
    return pl.pallas_call(
        gather_kernel,
        out_shape=(whole, whole, whole, tokens, tokens, jax.ShapeDtypeStruct((4, 8, 272), F32)),
        in_specs=[ANY] * 6,
        out_specs=(ANY,) * 6,
        scratch_shapes=[
            pltpu.SemaphoreType.DMA((3, 2, 4)),
            pltpu.SemaphoreType.DMA((3, 2, 4)),
            pltpu.SemaphoreType.DMA((3, 4, 4)),
            pltpu.SemaphoreType.DMA((3, 4, 4)),
            pltpu.SemaphoreType.DMA((3,)),
            pltpu.SemaphoreType.DMA((3, 3)),
            pltpu.SemaphoreType.DMA((3, 3)),
            pltpu.SemaphoreType.DMA((3,)),
        ],
        compiler_params=pltpu.CompilerParams(collective_id=0, has_side_effects=True),
        name="gather_weights",
    )(*blocks, x, g, v)


class Group:
    def __init__(self):
        self.row, self.col = lax.axis_index("row"), lax.axis_index("col")
        self.in_group = lax.rem(self.row + 2, 4)
        self.rank = self.in_group * 4 + self.col
        self.pair, self.core = self.rank // 2, lax.rem(self.col, 2)
        self.partner = (self.row, self.col + 1 - 2 * self.core)

    def device(self, other):
        return (lax.rem(self.row - self.in_group + other // 4 + 32, 32), lax.rem(other, 4))

    def greet(self):
        greet([self.device(lax.rem(self.rank + d, 16)) for d in range(1, 16)])

    def all_to_all(self, source, target, send, recv, local):
        own = pltpu.make_async_copy(source.at[self.rank], target.at[self.rank], local)
        own.start()
        sent, arrivals = [], []
        for d in range(1, 16):
            other = lax.rem(self.rank + d, 16)
            copy = remote(source.at[other], target.at[self.rank], send.at[d], recv.at[d], self.device(other))
            copy.start()
            sent.append(copy)
            origin = lax.rem(self.rank + 16 - d, 16)
            arrivals.append(remote(source.at[other], target.at[origin], send.at[d], recv.at[d], self.device(origin)))
        return own, sent, arrivals

    def finish(self, own, sent, arrivals):
        for copy in arrivals:
            copy.wait_recv()
        for copy in sent:
            copy.wait_send()
        own.wait()

    def relay(self, source_of, target, send, recv, local):
        own = pltpu.make_async_copy(source_of(self.pair), target.at[self.rank], local)
        own.start()
        beside = remote(source_of(self.pair), target.at[self.rank], send.at[0, 0], recv.at[0, 0], self.partner)
        beside.start()
        sent = [beside]
        for e in range(1, 8):
            other = lax.rem(self.pair + e, 8)
            copy = remote(
                source_of(other), target.at[self.rank], send.at[0, e], recv.at[0, e], self.device(other * 2 + self.core)
            )
            copy.start()
            sent.append(copy)
        return own, sent

    def pass_on(self, own, sent, target, send, recv):
        for e in range(1, 8):
            origin = lax.rem(self.pair + 8 - e, 8) * 2 + self.core
            block = target.at[origin]
            remote(block, block, send.at[0, e], recv.at[0, e], self.device(origin)).wait_recv()
            copy = remote(block, block, send.at[1, e], recv.at[1, e], self.partner)
            copy.start()
            sent.append(copy)
        for e in range(0, 8):
            block = target.at[lax.rem(self.pair + 8 - e, 8) * 2 + 1 - self.core]
            n = 0 if e == 0 else 1
            remote(block, block, send.at[n, e], recv.at[n, e], self.partner).wait_recv()
        for copy in sent:
            copy.wait_send()
        own.wait()


RELAY = [pltpu.SemaphoreType.DMA((2, 8)), pltpu.SemaphoreType.DMA((2, 8)), pltpu.SemaphoreType.DMA]
DIRECT = [pltpu.SemaphoreType.DMA((16,)), pltpu.SemaphoreType.DMA((16,)), pltpu.SemaphoreType.DMA]


def exchange_call(kernel, name, collective_id, outs, scratch, *args, in_specs=None):
    return pl.pallas_call(
        kernel,
        out_shape=outs,
        in_specs=in_specs or [ANY] * len(args),
        out_specs=(ANY,) * len(outs),
        scratch_shapes=scratch,
        compiler_params=pltpu.CompilerParams(collective_id=collective_id, has_side_effects=True),
        name=name,
    )(*args)


def qkv_exchange_kernel(source, last, target, last_out, send, recv, local, rsend, rrecv, rlocal):
    group = Group()
    group.greet()
    relayed = group.relay(lambda p: last, last_out, rsend, rrecv, rlocal)
    direct = group.all_to_all(source, target, send, recv, local)
    group.pass_on(*relayed, last_out, rsend, rrecv)
    group.finish(*direct)


def qkv_exchange(source, last):
    outs = (jax.ShapeDtypeStruct((16, 192, 128), BF16), jax.ShapeDtypeStruct((16, QUARTER, 128), BF16))
    return exchange_call(qkv_exchange_kernel, "exchange_qkv", 1, outs, DIRECT + RELAY, source, last)


def mixed_exchange_kernel(source, last, target, last_out, send, recv, local, last_send, last_recv, last_local):
    group = Group()
    group.greet()
    relayed = group.relay(lambda p: source.at[p], target, send, recv, local)
    own = pltpu.make_async_copy(last, last_out.at[group.core], last_local)
    own.start()
    copy = remote(last, last_out.at[group.core], last_send, last_recv, group.partner)
    copy.start()
    group.pass_on(*relayed, target, send, recv)
    remote(last, last_out.at[1 - group.core], last_send, last_recv, group.partner).wait_recv()
    copy.wait_send()
    own.wait()


def mixed_exchange(source, last):
    outs = (jax.ShapeDtypeStruct((16, 128, 128), BF16), jax.ShapeDtypeStruct((2, QUARTER, 64), BF16))
    return exchange_call(
        mixed_exchange_kernel, "exchange_mixed", 2, outs, RELAY + [pltpu.SemaphoreType.DMA] * 3, source, last
    )


def grad_exchange_kernel(source, target, send, recv, local):
    group = Group()
    group.greet()
    group.finish(*group.all_to_all(source, target, send, recv, local))


def grad_exchange(source):
    outs = (jax.ShapeDtypeStruct((16, 64, 128), BF16),)
    return exchange_call(grad_exchange_kernel, "exchange_d_mix", 7, outs, DIRECT, source)[0]


def back_exchange_kernel(
    source, parts, target, sums_out, send, recv, local, theirs, summed, swap_send, swap_recv, psend, precv, plocal
):
    group = Group()
    group.greet()
    swap = remote(parts.at[:, 1 - group.core], theirs, swap_send, swap_recv, group.partner)
    swap.start()
    direct = group.all_to_all(source, target, send, recv, local)
    swap.wait_recv()

    @pl.loop(0, 8)
    def _(p):
        summed[p] = (parts[p, group.core].astype(F32) + theirs[p].astype(F32)).astype(BF16)

    own = pltpu.make_async_copy(summed.at[group.pair], sums_out.at[group.pair], plocal)
    own.start()
    sent = [swap]
    for e in range(1, 8):
        other = lax.rem(group.pair + e, 8)
        copy = remote(
            summed.at[other], sums_out.at[group.pair], psend.at[e], precv.at[e], group.device(other * 2 + group.core)
        )
        copy.start()
        sent.append(copy)
    for e in range(1, 8):
        origin = lax.rem(group.pair + 8 - e, 8)
        block = sums_out.at[origin]
        remote(block, block, psend.at[e], precv.at[e], group.device(origin * 2 + group.core)).wait_recv()
    group.finish(*direct)
    for copy in sent:
        copy.wait_send()
    own.wait()


def back_exchange(source, parts):
    outs = (jax.ShapeDtypeStruct((16, 192, 128), BF16), jax.ShapeDtypeStruct((8, QUARTER, 128), BF16))
    block = pltpu.VMEM((8, QUARTER, 128), BF16)
    scratch = DIRECT + [block, block, pltpu.SemaphoreType.DMA, pltpu.SemaphoreType.DMA] + [
        pltpu.SemaphoreType.DMA((8,)), pltpu.SemaphoreType.DMA((8,)), pltpu.SemaphoreType.DMA
    ]
    return exchange_call(
        back_exchange_kernel, "exchange_d_qkv", 8, outs, scratch, source, parts, in_specs=[ANY, VMEM_SPEC]
    )


def free_axes(fixed):
    return [axis for axis in ("y", "z", "x") if axis not in fixed]


def buffer_shape(fixed, rows):
    shape = ()
    for axis in free_axes(fixed):
        shape = shape + ((2, 2) if axis == "y" else (4,))
    return shape + (rows, PACK)


def buffer_index(at):
    index = ()
    for axis in ("y", "z", "x"):
        if axis in at:
            index = index + ((lax.rem(at[axis], 2), at[axis] // 2) if axis == "y" else (at[axis],))
    return index


VECTOR_AXES = ("z", "x", "y")


def scatter_kernel(part0, part1, part2, y_ref, gin_ref, v_ref, out_ref, y_out, gin_out, v_out, *scratch):
    me = Place()
    parts = (part0, part1, part2)
    sums = scratch[0:3]
    halves = {}
    fulls = {}
    position = 3
    for piece in range(3):
        for stage in range(3):
            halves[piece, stage] = scratch[position : position + 2]
            fulls[piece, stage] = scratch[position + 2 : position + 4]
            position += 4
    vectors = scratch[position : position + 3]
    position += 3
    local, big_send, big_recv, send, recv, out_send, out_recv, out_local, v_send, v_recv = scratch[position:]
    greet(me.neighbours() + [me.step(axis, 2) for axis in VECTOR_AXES])

    sent, loads = [], {}
    for k in range(3):
        for u in range(4):
            for piece in range(3):
                first, second = SCATTER_ORDERS[piece][:2]
                index = place_index(
                    {first: lax.rem(me.at[first] + (2, 1, 3)[k], 4), second: lax.rem(me.at[second] + (2, 1, 3, 0)[u], 4)}
                )
                load = pltpu.make_async_copy(parts[piece].at[index], sums[piece].at[index], local.at[piece, k, u])
                load.start()
                loads[piece, k, u] = load
    for u in range(4):
        for piece in range(3):
            first, second = SCATTER_ORDERS[piece][:2]
            index = place_index({first: me.at[first], second: lax.rem(me.at[second] + (2, 1, 3, 0)[u], 4)})
            load = pltpu.make_async_copy(parts[piece].at[index], sums[piece].at[index], local.at[piece, 3, u])
            load.start()
            loads[piece, 3, u] = load

    def vectors_begin(phase, value):
        axis = VECTOR_AXES[phase]
        mine = vectors[phase].at[me.at[axis]]
        mine[...] = value
        for distance in (1, 2, 3):
            copy = remote(
                mine, mine, v_send.at[phase, distance - 1], v_recv.at[phase, distance - 1], me.step(axis, distance)
            )
            copy.start()
            sent.append(copy)

    def vectors_end(phase):
        axis = VECTOR_AXES[phase]
        for distance in (1, 2, 3):
            there = vectors[phase].at[lax.rem(me.at[axis] + 4 - distance, 4)]
            remote(
                there, there, v_send.at[phase, distance - 1], v_recv.at[phase, distance - 1], me.step(axis, distance)
            ).wait_recv()
        buffer = vectors[phase]
        return (buffer[0] + buffer[1]) + (buffer[2] + buffer[3])

    def stage_fixed(piece, stage):
        return {axis: me.at[axis] for axis in SCATTER_ORDERS[piece][:stage]}

    def each_tile(fixed, body):
        axes = free_axes(fixed)
        count = 4 ** len(axes)
        if count == 1:
            body({})
            return

        @pl.loop(0, count)
        def _(t):
            if len(axes) == 1:
                body({axes[0]: t})
            else:
                body({axes[0]: t // 4, axes[1]: lax.rem(t, 4)})

    def chunk(piece, stage, u):
        if stage > 0:
            return {}
        axis = SCATTER_ORDERS[piece][1]
        return {axis: lax.rem(me.at[axis] + (2, 1, 3, 0)[u], 4)}

    def sems(piece, stage, n, u):
        if stage == 0:
            return big_send.at[piece, u, n], big_recv.at[piece, u, n]
        return send.at[piece, stage - 1, n], recv.at[piece, stage - 1, n]

    def part_of(buffer, piece, stage, u):
        if stage > 0:
            return buffer
        axis = SCATTER_ORDERS[piece][1]
        value = lax.rem(me.at[axis] + (2, 1, 3, 0)[u], 4)
        index = ()
        for name in free_axes({SCATTER_ORDERS[piece][0]: 0}):
            if name == "y":
                index += (lax.rem(value, 2), value // 2) if name == axis else (everything(), everything())
            else:
                index += (value,) if name == axis else (everything(),)
        return buffer.at[index]

    def begin(piece, stage, u=0):
        axis = SCATTER_ORDERS[piece][stage]
        fixed = {**stage_fixed(piece, stage), axis: lax.rem(me.at[axis] + 2, 4), **chunk(piece, stage, u)}
        for n in range(2):
            copy = remote(
                sums[piece].at[place_index(fixed) + (pl.ds(16 * n, 16),)],
                part_of(halves[piece, stage][n], piece, stage, u),
                *sems(piece, stage, n, u), me.step(axis, (1, -1)[n]),
            )
            copy.start()
            sent.append(copy)

    def middle(piece, stage, n, u=0):
        axis = SCATTER_ORDERS[piece][stage]
        more = chunk(piece, stage, u)
        fixed = {**stage_fixed(piece, stage), axis: lax.rem(me.at[axis] + (1, 3)[n], 4), **more}
        half = halves[piece, stage][n]
        there = part_of(half, piece, stage, u)
        remote(there, there, *sems(piece, stage, n, u), me.step(axis, 1)).wait_recv()

        def body(at):
            index = place_index({**fixed, **at}) + (pl.ds(16 * n, 16),)
            total = sums[piece][index].astype(F32) + half[buffer_index({**more, **at})].astype(F32)
            sums[piece][index] = total.astype(BF16)

        each_tile(fixed, body)
        copy = remote(
            sums[piece].at[place_index(fixed)], part_of(fulls[piece, stage][n], piece, stage, u),
            *sems(piece, stage, 2 + n, u), me.step(axis, (1, -1)[n]),
        )
        copy.start()
        sent.append(copy)

    def finish(piece, stage, u=0):
        axis = SCATTER_ORDERS[piece][stage]
        more = chunk(piece, stage, u)
        fixed = {**stage_fixed(piece, stage), axis: me.at[axis], **more}
        first, second = fulls[piece, stage]
        for n, buffer in enumerate((first, second)):
            there = part_of(buffer, piece, stage, u)
            remote(there, there, *sems(piece, stage, 2 + n, u), me.step(axis, 1)).wait_recv()

        def body(at):
            index = place_index({**fixed, **at})
            place = buffer_index({**more, **at})
            if stage == 2:
                total = sums[piece][index].astype(F32) + (first[...].astype(F32) + second[...].astype(F32))
                out_ref[piece] = total
            else:
                total = sums[piece][index].astype(F32) + (first[place].astype(F32) + second[place].astype(F32))
                sums[piece][index] = total.astype(BF16)

        each_tile(fixed, body)

    for u in range(4):
        for piece in range(3):
            loads[piece, 0, u].wait()
            begin(piece, 0, u)
    vectors_begin(0, v_ref[...])

    pairs = ((y_ref, y_out), (gin_ref, gin_out))
    arrivals, own_copies = [], []
    for n, (source, target) in enumerate(pairs):
        rows = pl.ds(pl.multiple_of(me.col * QUARTER, QUARTER), QUARTER)
        own = pltpu.make_async_copy(source.at[me.col], target.at[:, rows], out_local.at[n])
        own.start()
        own_copies.append(own)
        for distance in (1, 2, 3):
            peer = me.beside(distance)
            semaphore = (out_send.at[n, distance - 1], out_recv.at[n, distance - 1])
            copy = remote(source.at[peer[1]], target.at[:, rows], *semaphore, peer)
            copy.start()
            sent.append(copy)
            origin = pl.ds(pl.multiple_of(lax.rem(me.col + 4 - distance, 4) * QUARTER, QUARTER), QUARTER)
            arrivals.append(remote(source.at[me.col], target.at[:, origin], *semaphore, peer))

    def finish_chunk(u):
        for piece in range(3):
            loads[piece, 3, u].wait()
            finish(piece, 0, u)
            if u == 0:
                begin(piece, 1)
            elif u < 3:
                middle(piece, 1, u - 1)
            else:
                finish(piece, 1)
                begin(piece, 2)

    for u in range(4):
        for n in range(2):
            for piece in range(3):
                loads[piece, 1 + n, u].wait()
                middle(piece, 0, n, u)
        if u < 2:
            vectors_begin(u + 1, vectors_end(u))
        if u == 3:
            v_out[...] = vectors_end(2)
        if u > 0:
            finish_chunk(u - 1)
    finish_chunk(3)
    for n in range(2):
        for piece in range(3):
            middle(piece, 2, n)
    for piece in range(3):
        finish(piece, 2)
    for copy in arrivals:
        copy.wait_recv()
    for copy in own_copies:
        copy.wait()
    for copy in sent:
        copy.wait_send()


def scatter_all(parts, y4, gin4, vectors):
    scratch = [pltpu.VMEM((2, 2, 4, 4, 32, PACK), BF16) for _ in range(3)]
    for piece in range(3):
        order = SCATTER_ORDERS[piece]
        for stage in range(3):
            fixed = order[: stage + 1]
            scratch += [pltpu.VMEM(buffer_shape(fixed, 16), BF16) for _ in range(2)]
            scratch += [pltpu.VMEM(buffer_shape(fixed, 32), BF16) for _ in range(2)]
    scratch += [pltpu.VMEM((4, 8, WIDE), F32) for _ in range(3)]
    scratch += [
        pltpu.SemaphoreType.DMA((3, 4, 4)),
        pltpu.SemaphoreType.DMA((3, 4, 4)),
        pltpu.SemaphoreType.DMA((3, 4, 4)),
        pltpu.SemaphoreType.DMA((3, 2, 4)),
        pltpu.SemaphoreType.DMA((3, 2, 4)),
        pltpu.SemaphoreType.DMA((2, 3)),
        pltpu.SemaphoreType.DMA((2, 3)),
        pltpu.SemaphoreType.DMA((2,)),
        pltpu.SemaphoreType.DMA((3, 3)),
        pltpu.SemaphoreType.DMA((3, 3)),
    ]
    back = jax.ShapeDtypeStruct((272, 512), BF16)
    return pl.pallas_call(
        scatter_kernel,
        out_shape=(jax.ShapeDtypeStruct((3, 32, PACK), F32), back, back, jax.ShapeDtypeStruct((8, WIDE), F32)),
        in_specs=[ANY] * 5 + [VMEM_SPEC],
        out_specs=(VMEM_SPEC, ANY, ANY, VMEM_SPEC),
        scratch_shapes=scratch,
        compiler_params=pltpu.CompilerParams(
            collective_id=3, has_side_effects=True, vmem_limit_bytes=VMEM_LIMIT
        ),
        name="scatter_gradients",
    )(*parts, y4, gin4, vectors)


def unpack_tail(packed, tiles, wide, tail):
    tiles[...] = packed[:, WIDE:PACK].astype(F32)
    for j in range(2):
        for s in range(9):
            wide[pl.ds(32 * j, 32), pl.ds(128 * s, 128)] = tiles[pl.ds(9 * j + s, 32, stride=32), :]
    tail[0:64, :] = wide[0:64, :].astype(BF16)


def pack_tail(tail, tiles, packed):
    for j in range(2):
        for s in range(9):
            tiles[pl.ds(9 * j + s, 32, stride=32), :] = tail[32 * j : 32 * j + 32, 128 * s : 128 * s + 128]
    packed[:, WIDE:PACK] = tiles[...].astype(BF16)


def in_features(values, packed, tail, columns):
    return dot_nn(values[:, :MAIN], packed[:, columns]) + dot_nn(values[:, MAIN:], tail[:, columns])


def add_to_features(total_t, values_t, packed, tail):
    @pl.loop(0, 4)
    def _(b):
        rows = pl.ds(pl.multiple_of(b * 256, 256), 256)
        total_t[rows, :] += dot_nn(packed[rows, :WIDE], values_t[...])

    total_t[MAIN:, :] += dot_nn(tail[...], values_t[...])


def norm_forward(x, gain, bias):
    mean = jnp.sum(x, axis=1, keepdims=True) / D
    square = jnp.sum(x * x, axis=1, keepdims=True) / D
    inverse = lax.rsqrt(square - mean * mean + norm_epsilon)
    normed = (x - mean) * inverse
    return normed, inverse, (normed * gain + bias).astype(BF16)


def norm_reverse(grad, normed, inverse, gain):
    scaled = grad * gain
    first = jnp.sum(scaled, axis=1, keepdims=True) / D
    second = jnp.sum(scaled * normed, axis=1, keepdims=True) / D
    return inverse * (scaled - first - normed * second)


def permuted(pieces, perm):
    total = dot_nn(pieces[0].astype(F32).T.astype(BF16), perm[0])
    for c in range(1, 4):
        total += dot_nn(pieces[c].astype(F32).T.astype(BF16), perm[c])
    return total


def permuted_exact(pieces, perm):
    total = jnp.zeros((8, WIDE), F32)
    for c in range(4):
        left = pieces[c]
        for _ in range(3):
            part = left.astype(BF16)
            left = left - part.astype(F32)
            total += dot_nn(part, perm[c])
    return total


def real_features(values):
    lane = lax.broadcasted_iota(jnp.int32, values.shape, 1)
    return jnp.where(lane < D, values, 0.0)


def turned(values):
    return values.astype(F32).T.astype(BF16)


def own_half(core):
    return pl.ds(pl.multiple_of(core * QUARTER, QUARTER), QUARTER)


def load_weights(source, target, semaphores):
    copies = []
    for j in range(2):
        copy = pltpu.make_async_copy(source.at[j], target.at[j], semaphores.at[j])
        copy.start()
        copies.append(copy)
    return copies


def qkv_kernel(
    x4, v4, perm, w_ref, x_out, n1_out, v_out, msg, last, q16, w, qkv, qkv_out, tiles, wide, tail, load, send, recv, local
):
    me = Place()
    partner = me.partner()
    copies = load_weights(w_ref, w, load)
    greet([partner])
    x = permuted(x4, perm)
    vectors = permuted_exact(v4, perm)
    v_out[...] = vectors
    x_out[...] = x.astype(BF16)
    _, _, normed = norm_forward(x, vectors[0:1], vectors[1:2])
    n1_out[...] = normed
    tail[...] = jnp.zeros_like(tail)
    mine, theirs = own_half(me.core), own_half(1 - me.core)
    sent, own_copies, arrivals = [], [], []
    for j in range(2):
        copies[j].wait()
        packed = w.at[j]
        unpack_tail(packed, tiles, wide, tail)

        @pl.loop(0, 3)
        def _(b):
            columns = pl.ds(pl.multiple_of(b * 384, 128), 384)
            qkv[j, :, columns] = in_features(n1_out[...], packed, tail, columns).astype(BF16)

        own = pltpu.make_async_copy(qkv.at[j, mine, :], qkv_out.at[j, me.core], local.at[j])
        own.start()
        own_copies.append(own)
        copy = remote(qkv.at[j, theirs, :], qkv_out.at[j, me.core], send.at[j], recv.at[j], partner)
        copy.start()
        sent.append(copy)
        arrivals.append(
            remote(qkv.at[j, theirs, :], qkv_out.at[j, 1 - me.core], send.at[j], recv.at[j], partner)
        )
    for copy in arrivals:
        copy.wait_recv()
    for copy in own_copies:
        copy.wait()
    for n in range(3):
        for head in range(HEADS):
            block = columns_of(qkv_out, n * D + head * HEAD_DIM, QKV_COLS, 0)
            if head == 16:
                if n == 0:
                    q16[...] = block
                else:
                    last[:, 64 * (n - 1) : 64 * n] = block
            else:
                msg[head, 64 * n : 64 * n + 64, 0:64] = block[0:64]
                msg[head, 64 * n : 64 * n + 64, 64:128] = block[64:128]
    for copy in sent:
        copy.wait_send()


def columns_of(blocks, start, width, offset):
    pieces = []
    position = start
    while position < start + HEAD_DIM:
        c = position // width
        end = min(start + HEAD_DIM, (c + 1) * width)
        first = position - c * width + offset
        pieces.append(blocks[c // 2, c % 2, :, first : first + end - position])
        position = end
    return pieces[0] if len(pieces) == 1 else jnp.concatenate(pieces, axis=1)


def qkv_call(x4, v4, perm, weights):
    row = jax.ShapeDtypeStruct((PAIR, WIDE), BF16)
    return pl.pallas_call(
        qkv_kernel,
        out_shape=(
            row, row, jax.ShapeDtypeStruct((8, WIDE), F32), jax.ShapeDtypeStruct((16, 192, 128), BF16),
            jax.ShapeDtypeStruct((QUARTER, 128), BF16), jax.ShapeDtypeStruct((QUARTER, 64), BF16),
        ),
        in_specs=[VMEM_SPEC, VMEM_SPEC, VMEM_SPEC, ANY],
        out_specs=(VMEM_SPEC,) * 6,
        scratch_shapes=[
            pltpu.VMEM((2, MAIN, PACK), BF16), pltpu.VMEM((2, PAIR, WIDE), BF16),
            pltpu.VMEM((2, 2, QUARTER, WIDE), BF16),
            pltpu.VMEM((MAIN, 128), F32), pltpu.VMEM((128, WIDE), F32), pltpu.VMEM((128, WIDE), BF16),
            pltpu.SemaphoreType.DMA((2,)), pltpu.SemaphoreType.DMA((2,)), pltpu.SemaphoreType.DMA((2,)),
            pltpu.SemaphoreType.DMA((2,)),
        ],
        compiler_params=pltpu.CompilerParams(
            collective_id=4, has_side_effects=True, vmem_limit_bytes=VMEM_LIMIT
        ),
        name="norm_and_qkv",
    )(x4, v4, perm, weights)


def gelu_both(v):
    square = v * v
    tanh_value = jnp.tanh(gelu_coef * (v + 0.044715 * v * square))
    half = 0.5 * (1.0 + tanh_value)
    value = v * half
    slope = half + 0.5 * v * (1.0 - tanh_value * tanh_value) * gelu_coef * (1.0 + 0.134145 * square)
    return value, slope


def weight_gradient(rows_t, values, tiles, tail_sum, packed):
    @pl.loop(0, 4)
    def _(b):
        rows = pl.ds(pl.multiple_of(b * 256, 256), 256)
        packed[rows, :WIDE] = dot_nn(rows_t[rows, :], values[...]).astype(BF16)

    tail_sum[...] = dot_nn(rows_t[MAIN:, :], values[...])
    pack_tail(tail_sum, tiles, packed)


def swap_start(total_t, mine, theirs, ssem, rsem, partner):
    mine[...] = total_t[...].astype(BF16)
    copy = remote(mine, theirs, ssem, rsem, partner)
    copy.start()
    return copy


def swap_end(copy, mine, theirs):
    copy.wait_recv()
    return mine[...].astype(F32) + theirs[...].astype(F32)


def middle_kernel(
    x_ref, a0, w0_ref, w1_ref, w2_ref, g4, perm, vec,
    y4, dres_out, dresb_out, gr1_out, gr2_out, dmsg, dlast, vec_out,
    w0, w1, w2, gr1, gr2, resid, normed2, inverse2, n2, n2_t, cot, cot_t, total_t, dn2_t, hidden, dpre, turn1, turn2,
    dmix, tiles, out_tiles, tail1, tail2, tail_sum, mine1, theirs1, mine2, theirs2, mine_y, theirs_y, dmix_out,
    load, store, send, recv, local,
):
    me = Place()
    partner = me.partner()
    loads = [load_weights(source, target, load.at[n]) for n, (source, target) in enumerate(
        ((w0_ref, w0), (w1_ref, w1), (w2_ref, w2))
    )]
    greet([partner])
    for buffer in (tail1, tail2, out_tiles, total_t, dn2_t):
        buffer[...] = jnp.zeros_like(buffer)
    for j in range(2):
        turn1[...] = turned(a0[j])
        loads[0][j].wait()
        unpack_tail(w0.at[j], tiles, tail_sum, tail1)
        add_to_features(total_t, turn1, w0.at[j], tail1)
    first = swap_start(total_t, mine1, theirs1, send.at[0], recv.at[0], partner)
    cot_value = permuted(g4, perm)
    cot[...] = cot_value.astype(BF16)
    cot_t[...] = cot_value.T.astype(BF16)
    total_t[...] = jnp.zeros_like(total_t)
    attended = swap_end(first, mine1, theirs1)
    resid[...] = x_ref[...].astype(F32) + attended.T
    normed, inverse, n2_value = norm_forward(resid[...], vec[2:3], vec[3:4])
    normed2[...] = normed
    inverse2[...] = jnp.broadcast_to(inverse, inverse2.shape)
    n2[...] = n2_value
    n2_t[...] = turned(n2_value)
    stores = []
    for j in range(2):
        loads[1][j].wait()
        loads[2][j].wait()
        up, down = w1.at[j], w2.at[j]
        unpack_tail(up, tiles, tail_sum, tail1)
        unpack_tail(down, tiles, tail_sum, tail2)

        @pl.loop(0, 3)
        def _(b):
            columns = pl.ds(pl.multiple_of(b * 384, 128), 384)
            pre = in_features(n2[...], up, tail1, columns)
            d_hidden = in_features(cot[...], down, tail2, columns)
            value, slope = gelu_both(pre)
            hidden[:, columns] = value.astype(BF16)
            dpre[:, columns] = (d_hidden * slope).astype(BF16)

        turn1[...] = turned(hidden[...])
        turn2[...] = turned(dpre[...])
        add_to_features(total_t, turn1, down, tail2)
        add_to_features(dn2_t, turn2, up, tail1)
        if j == 1:
            second = swap_start(dn2_t, mine2, theirs2, send.at[1], recv.at[1], partner)
            half = own_half(1 - me.core)
            mine_y[...] = total_t[:, half].astype(BF16)
            third = remote(mine_y, theirs_y, send.at[2], recv.at[2], partner)
            third.start()
        weight_gradient(n2_t, dpre, out_tiles, tail_sum, gr1.at[j])
        weight_gradient(cot_t, hidden, out_tiles, tail_sum, gr2.at[j])
        for n, (source, target) in enumerate(((gr1, gr1_out), (gr2, gr2_out))):
            copy = pltpu.make_async_copy(source.at[j], target.at[j], store.at[n, j])
            copy.start()
            stores.append(copy)
    grad = swap_end(second, mine2, theirs2).T
    normed = normed2[...]
    vec_out[...] = jnp.zeros_like(vec_out)
    vec_out[0:1, :] = jnp.sum(grad * normed, axis=0, keepdims=True)
    vec_out[1:2, :] = jnp.sum(grad, axis=0, keepdims=True)
    back = cot[...].astype(F32) + norm_reverse(grad, normed, inverse2[:, 0:1], vec[2:3])
    back = real_features(back)
    dres_out[...] = back
    dresb_out[...] = back.astype(BF16)
    sent, own_copies, arrivals = [first, second, third], [], []
    columns = slice(768, WIDE)
    for j in range(2):
        unpack_tail(w0.at[j], tiles, tail_sum, tail1)
        dmix[j] = in_features(dresb_out[...], w0.at[j], tail1, columns).astype(BF16)
        own = pltpu.make_async_copy(dmix.at[j, own_half(me.core), :], dmix_out.at[j, me.core], local.at[j])
        own.start()
        own_copies.append(own)
        theirs = dmix.at[j, own_half(1 - me.core), :]
        copy = remote(theirs, dmix_out.at[j, me.core], send.at[3 + j], recv.at[3 + j], partner)
        copy.start()
        sent.append(copy)
        arrivals.append(remote(theirs, dmix_out.at[j, 1 - me.core], send.at[3 + j], recv.at[3 + j], partner))
    half = own_half(me.core)
    third.wait_recv()
    y = (resid[half, :].T + (total_t[:, half] + theirs_y[...].astype(F32))).astype(BF16)
    for c in range(4):
        y4[c] = dot_nn(perm[c], y).astype(BF16)
    for copy in arrivals:
        copy.wait_recv()
    for copy in own_copies:
        copy.wait()
    for head in range(HEADS):
        block = columns_of(dmix_out, head * HEAD_DIM, 272, QKV_COLS - 768)
        if head == 16:
            dlast[...] = block
        else:
            dmsg[head, :, 0:64] = block[0:64]
            dmsg[head, :, 64:128] = block[64:128]
    for copy in stores:
        copy.wait()
    for copy in sent:
        copy.wait_send()


def middle_call(x, a0, w0, w1, w2, g4, perm, vec):
    packed = jax.ShapeDtypeStruct((2, MAIN, PACK), BF16)
    weights = pltpu.VMEM((2, MAIN, PACK), BF16)
    row_f, row_b = pltpu.VMEM((PAIR, WIDE), F32), pltpu.VMEM((PAIR, WIDE), BF16)
    turn_f, turn_b = pltpu.VMEM((WIDE, PAIR), F32), pltpu.VMEM((WIDE, PAIR), BF16)
    tile, tail = pltpu.VMEM((MAIN, 128), F32), pltpu.VMEM((128, WIDE), BF16)
    half = pltpu.VMEM((WIDE, QUARTER), BF16)
    return pl.pallas_call(
        middle_kernel,
        out_shape=(
            jax.ShapeDtypeStruct((4, 272, QUARTER), BF16), jax.ShapeDtypeStruct((PAIR, WIDE), F32),
            jax.ShapeDtypeStruct((PAIR, WIDE), BF16), packed, packed,
            jax.ShapeDtypeStruct((16, 64, 128), BF16), jax.ShapeDtypeStruct((QUARTER, 64), BF16),
            jax.ShapeDtypeStruct((8, WIDE), F32),
        ),
        in_specs=[VMEM_SPEC, VMEM_SPEC, ANY, ANY, ANY, VMEM_SPEC, VMEM_SPEC, VMEM_SPEC],
        out_specs=(VMEM_SPEC, VMEM_SPEC, VMEM_SPEC, ANY, ANY, VMEM_SPEC, VMEM_SPEC, VMEM_SPEC),
        scratch_shapes=[
            weights, weights, weights, weights, weights, row_f, row_f, pltpu.VMEM((PAIR, 128), F32), row_b, turn_b,
            row_b, turn_b, turn_f, turn_f, row_b, row_b, turn_b, turn_b, pltpu.VMEM((2, PAIR, 384), BF16),
            tile, tile, tail, tail, pltpu.VMEM((128, WIDE), F32), turn_b, turn_b, turn_b, turn_b, half, half,
            pltpu.VMEM((2, 2, QUARTER, 384), BF16),
            pltpu.SemaphoreType.DMA((3, 2)), pltpu.SemaphoreType.DMA((2, 2)), pltpu.SemaphoreType.DMA((5,)),
            pltpu.SemaphoreType.DMA((5,)), pltpu.SemaphoreType.DMA((2,)),
        ],
        compiler_params=pltpu.CompilerParams(
            collective_id=5, has_side_effects=True, vmem_limit_bytes=VMEM_LIMIT
        ),
        name="feed_forward",
    )(x, a0, w0, w1, w2, g4, perm, vec)


def first_kernel(
    x_ref, n1, dresb, dres, dq_ref, a0, w0_ref, perm, vec, vec2,
    gin4, gr0_out, sums,
    w0, gr0, dq, n1_t, dres_t, turn, dn1_t, tiles, out_tiles, tail, tail_sum, mine, theirs,
    load, store, send, recv, local,
):
    me = Place()
    partner = me.partner()
    loads = load_weights(w0_ref, w0, load)
    greet([partner])
    mine_rows = own_half(me.core)
    copy = remote(dq_ref.at[1 - me.core], dq.at[:, mine_rows, :], send.at[0], recv.at[0], partner)
    copy.start()
    own = pltpu.make_async_copy(dq_ref.at[me.core], dq.at[:, mine_rows, :], local)
    own.start()
    for buffer in (tail, out_tiles, dn1_t):
        buffer[...] = jnp.zeros_like(buffer)
    n1_t[...] = turned(n1[...])
    dres_t[...] = turned(dresb[...])
    normed, inverse, _ = norm_forward(x_ref[...].astype(F32), vec[0:1], vec[1:2])
    own.wait()
    remote(
        dq_ref.at[me.core], dq.at[:, own_half(1 - me.core), :], send.at[0], recv.at[0], partner
    ).wait_recv()
    for j in range(2):
        loads[j].wait()
        unpack_tail(w0.at[j], tiles, tail_sum, tail)
        turn[...] = turned(dq[j])
        add_to_features(dn1_t, turn, w0.at[j], tail)
    swap = swap_start(dn1_t, mine, theirs, send.at[1], recv.at[1], partner)
    stores = []
    for j in range(2):
        packed = gr0.at[j]

        @pl.loop(0, 4)
        def _(b):
            rows = pl.ds(pl.multiple_of(b * 256, 256), 256)
            packed[rows, :768] = dot_nn(n1_t[rows, :], dq[j, :, :768]).astype(BF16)
            packed[rows, 768:WIDE] = (
                dot_nn(n1_t[rows, :], dq[j, :, 768:]) + dot_nn(dres_t[rows, :], a0[j, :, 768:])
            ).astype(BF16)

        tail_sum[:, :768] = dot_nn(n1_t[MAIN:, :], dq[j, :, :768])
        tail_sum[:, 768:] = dot_nn(n1_t[MAIN:, :], dq[j, :, 768:]) + dot_nn(dres_t[MAIN:, :], a0[j, :, 768:])
        pack_tail(tail_sum, out_tiles, packed)
        out = pltpu.make_async_copy(packed, gr0_out.at[j], store.at[j])
        out.start()
        stores.append(out)
    grad = swap_end(swap, mine, theirs).T
    sums[...] = vec2[...]
    sums[4:5, :] = jnp.sum(grad * normed, axis=0, keepdims=True)
    sums[5:6, :] = jnp.sum(grad, axis=0, keepdims=True)
    back = dres[...] + norm_reverse(grad, normed, inverse, vec[0:1])
    dn1_t[...] = real_features(back).T
    back = dn1_t[:, mine_rows].astype(BF16)
    for c in range(4):
        gin4[c] = dot_nn(perm[c], back).astype(BF16)
    for out in stores:
        out.wait()
    copy.wait_send()
    swap.wait_send()


def first_call(x, n1, dresb, dres, dq, a0, w0, perm, vec, vec2):
    weights = pltpu.VMEM((2, MAIN, PACK), BF16)
    turn_b = pltpu.VMEM((WIDE, PAIR), BF16)
    tile = pltpu.VMEM((MAIN, 128), F32)
    return pl.pallas_call(
        first_kernel,
        out_shape=(
            jax.ShapeDtypeStruct((4, 272, QUARTER), BF16), jax.ShapeDtypeStruct((2, MAIN, PACK), BF16),
            jax.ShapeDtypeStruct((8, WIDE), F32),
        ),
        in_specs=[VMEM_SPEC] * 4 + [ANY, VMEM_SPEC, ANY] + [VMEM_SPEC] * 3,
        out_specs=(VMEM_SPEC, ANY, VMEM_SPEC),
        scratch_shapes=[
            weights, weights, pltpu.VMEM((2, PAIR, WIDE), BF16), turn_b, turn_b, turn_b,
            pltpu.VMEM((WIDE, PAIR), F32), tile, tile, pltpu.VMEM((128, WIDE), BF16), pltpu.VMEM((128, WIDE), F32),
            turn_b, turn_b,
            pltpu.SemaphoreType.DMA((2,)), pltpu.SemaphoreType.DMA((2,)), pltpu.SemaphoreType.DMA((2,)),
            pltpu.SemaphoreType.DMA((2,)), pltpu.SemaphoreType.DMA,
        ],
        compiler_params=pltpu.CompilerParams(
            collective_id=6, has_side_effects=True, vmem_limit_bytes=VMEM_LIMIT
        ),
        name="first_norm_back",
    )(x, n1, dresb, dres, dq, a0, w0, perm, vec, vec2)


def allowed_pairs(shape, key_start, query_start):
    key = key_start + lax.broadcasted_iota(jnp.int32, shape, 0)
    query = query_start + lax.broadcasted_iota(jnp.int32, shape, 1)
    return key <= query


def transposed(values):
    return values.astype(F32).T


def spread(block, target, row, rows=64):
    target[pl.ds(row, 64), :] = block[:, 0:64]
    target[pl.ds(row + 64, 64), :] = block[:, 64:128]


def attend_kernel(info, r_ref, kv16, q16, dense_out, o_out, o16_out, l_out, l16_out, query, key, value, value_t, value16_t):
    rank, wraps = info[0], info[1]

    @pl.loop(0, 16)
    def _(b):
        row = pl.multiple_of(b * 128, 128)
        spread(r_ref[b, 0:64, :] * jnp.asarray(0.125, BF16), query, row)
        spread(r_ref[b, 64:128, :], key, row)
        spread(r_ref[b, 128:192, :], value, row)

    @pl.loop(0, 4)
    def _(b):
        rows = pl.ds(pl.multiple_of(b * KEYS, KEYS), KEYS)
        value_t[:, rows] = transposed(value[rows, :]).astype(BF16)
        value16_t[:, rows] = transposed(kv16[rows, :])[64:128].astype(BF16)

    def step(q, k_ref, v_t, j, carry, query_start=None):
        peak, running, mixed = carry
        rows = pl.ds(pl.multiple_of(j * KEYS, KEYS), KEYS)
        scores = dot_nt(k_ref[rows, 0:64], q)
        if query_start is not None:
            scores = jnp.where(allowed_pairs(scores.shape, j * KEYS, query_start), scores, masked_score)
        new_peak = jnp.maximum(peak, jnp.max(scores, axis=0, keepdims=True))
        shrink = jnp.exp(peak - new_peak)
        weights = jnp.exp(scores - new_peak)
        running = running * shrink + jnp.sum(weights, axis=0, keepdims=True)
        mixed = mixed * shrink + dot_nn(v_t[:, rows], weights.astype(BF16))
        return new_peak, running, mixed

    def empty(width):
        return (
            jnp.full((1, width), masked_score, F32), jnp.zeros((1, width), F32), jnp.zeros((64, width), F32)
        )

    @pl.loop(0, 4)
    def _(i):
        rows = pl.ds(pl.multiple_of(i * KEYS, KEYS), KEYS)
        q = query[rows, :]
        start = jnp.where((wraps == 1) & (i >= 2), 2, 0)
        carry = lax.fori_loop(
            start, i, lambda j, carry: step(q, key, value_t, j, carry), empty(KEYS)
        )
        peak, running, mixed = step(q, key, value_t, i, carry, i * KEYS)
        result = (mixed / running).T.astype(BF16)
        o_out[rows, :] = result
        for n in range(4):
            dense_out[2 * i + n // 2, :, 64 * (n % 2) : 64 * (n % 2) + 64] = result[128 * n : 128 * n + 128]
        l_out[:, rows] = peak + jnp.log(running)

    q = q16[...] * jnp.asarray(0.125, BF16)
    start = jnp.where((wraps == 1) & (rank >= 8), 2, 0)
    peak, running, mixed = lax.fori_loop(
        start, rank // 4 + 1,
        lambda j, carry: step(q, kv16, value16_t, j, carry, rank * QUARTER), empty(QUARTER),
    )
    o16_out[...] = (mixed / running).T.astype(BF16)
    l16_out[...] = peak + jnp.log(running)


def attend_call(info, r, kv16, q16):
    tokens = jax.ShapeDtypeStruct((SEQ, 64), BF16)
    return pl.pallas_call(
        attend_kernel,
        out_shape=(
            jax.ShapeDtypeStruct((8, 128, 128), BF16), tokens, jax.ShapeDtypeStruct((QUARTER, 64), BF16),
            jax.ShapeDtypeStruct((1, SEQ), F32), jax.ShapeDtypeStruct((1, QUARTER), F32), tokens, tokens, tokens,
        ),
        in_specs=[SMEM_SPEC, VMEM_SPEC, VMEM_SPEC, VMEM_SPEC],
        out_specs=(VMEM_SPEC,) * 8,
        scratch_shapes=[pltpu.VMEM((64, SEQ), BF16), pltpu.VMEM((64, SEQ), BF16)],
        compiler_params=pltpu.CompilerParams(vmem_limit_bytes=VMEM_LIMIT),
        name="attend_forward",
    )(info, r, kv16, q16)


def attend_back_kernel(
    info, query, key, value, kv16, q16, o_ref, o16, do_dense, do16, l_ref, l16,
    msg, part16, dq16_out, do_ref, key_t, key16_t, delta, dq_t,
):
    rank, wraps = info[0], info[1]

    @pl.loop(0, 16)
    def _(b):
        spread(do_dense[b], do_ref, pl.multiple_of(b * 128, 128))

    @pl.loop(0, 4)
    def _(b):
        rows = pl.ds(pl.multiple_of(b * KEYS, KEYS), KEYS)
        key_t[:, rows] = transposed(key[rows, :]).astype(BF16)
        key16_t[:, rows] = transposed(kv16[rows, :])[0:64].astype(BF16)
        product = do_ref[rows, :].astype(F32) * o_ref[rows, :].astype(F32)
        delta[:, rows] = jnp.sum(product.T, axis=0, keepdims=True)
        dq_t[:, rows] = jnp.zeros((64, KEYS), F32)

    def put(section, j, result):
        for n in range(4):
            for half in range(2):
                msg[4 * j + n, 64 * section : 64 * section + 64, 64 * half : 64 * half + 64] = result[
                    128 * n + 64 * half : 128 * n + 64 * half + 64
                ]

    def pair(keys, values, q, d_out, log_total, delta_row, mask):
        scores = dot_nt(keys, q)
        probs = jnp.exp(scores - log_total)
        if mask is not None:
            probs = jnp.where(mask(scores.shape), probs, 0.0)
        probs = probs.astype(BF16)
        d_prob = dot_nt(values, d_out)
        d_scores = (probs.astype(F32) * (d_prob - delta_row)).astype(BF16)
        return dot_nn(d_scores, q), dot_nn(probs, d_out), d_scores

    @pl.loop(0, 4)
    def _(j):
        rows = pl.ds(pl.multiple_of(j * KEYS, KEYS), KEYS)
        keys, values = key[rows, :], value[rows, :]

        def step(i, carry, mask=None):
            d_key, d_value = carry
            at = pl.ds(pl.multiple_of(i * KEYS, KEYS), KEYS)
            more_key, more_value, d_scores = pair(
                keys, values, query[at, :], do_ref[at, :], l_ref[:, at], delta[:, at], mask
            )
            dq_t[:, at] += dot_nn(key_t[:, rows], d_scores)
            return d_key + more_key, d_value + more_value

        zero = jnp.zeros((KEYS, 64), F32)
        carry = step(j, (zero, zero), lambda shape: allowed_pairs(shape, 0, 0))
        end = jnp.where((wraps == 1) & (j < 2), 2, 4)
        d_key, d_value = lax.fori_loop(j + 1, end, step, carry)
        put(1, j, d_key.astype(BF16))
        put(2, j, d_value.astype(BF16))

    q = q16[...] * jnp.asarray(0.125, BF16)
    d_out16 = do16[...]
    delta16 = jnp.sum((d_out16.astype(F32) * o16[...].astype(F32)).T, axis=0, keepdims=True)
    start = jnp.where((wraps == 1) & (rank >= 8), 2, 0)

    def last_step(j, dq):
        rows = pl.ds(pl.multiple_of(j * KEYS, KEYS), KEYS)
        d_key, d_value, d_scores = pair(
            kv16[rows, 0:64], kv16[rows, 64:128], q, d_out16, l16[...], delta16,
            lambda shape: allowed_pairs(shape, j * KEYS, rank * QUARTER),
        )
        part16[rows, 0:64] = d_key.astype(BF16)
        part16[rows, 64:128] = d_value.astype(BF16)
        return dq + dot_nn(key16_t[:, rows], d_scores)

    @pl.loop(0, 4)
    def _(j):
        rows = pl.ds(pl.multiple_of(j * KEYS, KEYS), KEYS)
        part16[rows, :] = jnp.zeros((KEYS, 128), BF16)
        put(0, j, (dq_t[:, rows] * 0.125).T.astype(BF16))

    dq = lax.fori_loop(start, rank // 4 + 1, last_step, jnp.zeros((64, QUARTER), F32))
    dq16_out[...] = (dq * 0.125).T.astype(BF16)


def attend_back_call(info, *args):
    return pl.pallas_call(
        attend_back_kernel,
        out_shape=(
            jax.ShapeDtypeStruct((16, 192, 128), BF16), jax.ShapeDtypeStruct((SEQ, 128), BF16),
            jax.ShapeDtypeStruct((QUARTER, 64), BF16),
        ),
        in_specs=[SMEM_SPEC] + [VMEM_SPEC] * 11,
        out_specs=(VMEM_SPEC,) * 3,
        scratch_shapes=[
            pltpu.VMEM((SEQ, 64), BF16), pltpu.VMEM((64, SEQ), BF16), pltpu.VMEM((64, SEQ), BF16),
            pltpu.VMEM((1, SEQ), F32), pltpu.VMEM((64, SEQ), F32),
        ],
        compiler_params=pltpu.CompilerParams(vmem_limit_bytes=VMEM_LIMIT),
        name="attend_backward",
    )(info, *args)


def packed_block(block):
    tail = jnp.pad(block[32:34], ((0, 0), (0, WIDE - D))).reshape(18, 128)
    return jnp.concatenate(
        [jnp.pad(block[:32], ((0, 0), (0, WIDE - D))), jnp.pad(tail, ((0, 14), (0, 0)))], axis=1
    )


def unpacked_block(packed):
    tail = packed[:18, WIDE:].reshape(2, WIDE)[:, :D]
    return jnp.concatenate([packed[:, :D], tail], axis=0)


def permutation():
    feature = jnp.arange(D, dtype=jnp.int32)
    block, inside = feature // 34, feature % 34
    place = jnp.where(inside < 32, 32 * block + inside, MAIN + 32 * (inside - 32) + block)
    chosen = place[:, None] == jnp.arange(WIDE, dtype=jnp.int32)[None, :]
    return chosen.astype(BF16).reshape(4, 272, WIDE)


def per_device(
    layer_input,
    first_norm_gain,
    first_norm_bias,
    w_qkv,
    w_out,
    second_norm_gain,
    second_norm_bias,
    w_up,
    w_down,
    gradient_of_output,
):
    row, col = lax.axis_index("row"), lax.axis_index("col")
    rank, core = (row + 2) % 4 * 4 + col, col % 2
    wraps = ((row < 2) | (row >= 30)).astype(jnp.int32)
    info = jnp.stack([rank, wraps]).astype(jnp.int32)
    perm = permutation()
    vectors = jnp.concatenate(
        [
            jnp.stack([first_norm_gain, first_norm_bias, second_norm_gain, second_norm_bias]),
            jnp.zeros((4, 272), F32),
        ]
    )
    blocks = (
        packed_block(jnp.concatenate([w_qkv, w_out.T], axis=1)),
        packed_block(w_up),
        packed_block(w_down.T),
    )
    w0, w1, w2, x4, g4, v4 = gather_all(blocks, layer_input.T, gradient_of_output.T, vectors)
    w0, w1, w2 = (w.reshape(2, MAIN, PACK) for w in (w0, w1, w2))
    x, n1, vec, message, last, q16 = qkv_call(x4, v4, perm, w0)
    heads, kv16 = qkv_exchange(message, last)
    kv16 = kv16.reshape(SEQ, 128)
    dense, o, o16, log_total, log16, query, key, value = attend_call(info, heads, kv16, q16)
    mixed, both16 = mixed_exchange(dense, o16)
    attn = jnp.concatenate(
        [
            mixed.reshape(16, QUARTER, 2, HEAD_DIM).transpose(2, 1, 0, 3).reshape(PAIR, 1024),
            both16.reshape(PAIR, HEAD_DIM),
        ],
        axis=1,
    ).reshape(PAIR, 2, 2, 272)
    attn = lax.dynamic_index_in_dim(attn, core, 2, keepdims=False)
    a0 = jnp.pad(attn.transpose(1, 0, 2), ((0, 0), (0, 0), (QKV_COLS, WIDE - D)))
    y4, dres, dresb, gr1, gr2, dmsg, do16, vec2 = middle_call(x, a0, w0, w1, w2, g4, perm, vec)
    do = grad_exchange(dmsg)
    back, part16, dq16 = attend_back_call(
        info, query, key, value, kv16, q16, o, o16, do, do16, log_total, log16
    )
    back, sums16 = back_exchange(back, part16.reshape(8, 2, QUARTER, 128))
    last_sums = jnp.sum(sums16.astype(F32), axis=0).astype(BF16)
    back = back.reshape(16, 3, 64, 2, HEAD_DIM).transpose(1, 3, 2, 0, 4).reshape(3, QUARTER, 1024)
    d_qkv = jnp.concatenate(
        [back[0], dq16, back[1], last_sums[:, :64], back[2], last_sums[:, 64:]], axis=1
    )
    dq0 = jnp.pad(
        d_qkv.reshape(QUARTER, 2, 2, QKV_COLS).transpose(2, 1, 0, 3), ((0, 0), (0, 0), (0, 0), (0, WIDE - QKV_COLS))
    )
    gin4, gr0, sums4 = first_call(x, n1, dresb, dres, dq0, a0, w0, perm, vec, vec2)
    grouped = tuple(g.reshape(2, 2, 4, 4, 32, PACK) for g in (gr0, gr1, gr2))
    sums, layer_output, gin, sums4 = scatter_all(grouped, y4, gin4, sums4)
    own_perm = lax.dynamic_index_in_dim(perm, col, 0, keepdims=False).astype(F32)
    vg = lax.dot_general(
        sums4, own_perm, (((1,), (1,)), ((), ())),
        preferred_element_type=F32, precision=lax.Precision.HIGHEST,
    )
    s0, s1, s2 = (unpacked_block(sums[n]) for n in range(3))
    return (
        layer_output.T,
        gin.T.astype(F32),
        vg[4],
        vg[5],
        s0[:, :QKV_COLS],
        s0[:, QKV_COLS:].T,
        vg[0],
        vg[1],
        s1,
        s2.T,
    )


def solution(mesh):
    placed = (
        P("row", "col"),
        P("col"),
        P("col"),
        P("row", "col"),
        P("col", "row"),
        P("col"),
        P("col"),
        P("row", "col"),
        P("col", "row"),
        P("row", "col"),
    )
    return jax.shard_map(
        per_device,
        mesh=mesh,
        in_specs=placed,
        out_specs=(
            P("row", "col"),
            P("row", "col"),
            P("col"),
            P("col"),
            P("row", "col"),
            P("col", "row"),
            P("col"),
            P("col"),
            P("row", "col"),
            P("col", "row"),
        ),
        check_vma=False,
    )
```

```python
import math

import jax
import jax.numpy as jnp
from jax import lax
from jax.experimental import pallas as pl
from jax.experimental.pallas import tpu as pltpu
from jax.sharding import PartitionSpec as P

HEADS = 17
HEAD_DIM = 64
D = 1088
SEQ = 2048
MAIN = 1024
WIDE = 1152
PACK = 1280
QKV_COLS = 816
QUARTER = 128
PAIR = 256
KEYS = 512

gelu_coef = math.sqrt(2.0 / math.pi)
norm_epsilon = 1e-05
masked_score = -1e30
MESH = pl.DeviceIdType.MESH
F32 = jnp.float32
BF16 = jnp.bfloat16
VMEM_LIMIT = 60 * 1024 * 1024
ANY = pl.BlockSpec(memory_space=pl.ANY)
VMEM_SPEC = pl.BlockSpec(memory_space=pltpu.VMEM)
SMEM_SPEC = pl.BlockSpec(memory_space=pltpu.SMEM)

GATHER_ORDERS = (("x", "y", "z"), ("y", "z", "x"), ("z", "x", "y"))
SCATTER_ORDERS = (("z", "y", "x"), ("x", "z", "y"), ("y", "x", "z"))


def dot_nn(a, b):
    return lax.dot_general(a, b, (((1,), (0,)), ((), ())), preferred_element_type=F32)


def dot_nt(a, b):
    return lax.dot_general(a, b, (((1,), (1,)), ((), ())), preferred_element_type=F32)


class Place:
    def __init__(self):
        self.row = lax.axis_index("row")
        self.col = lax.axis_index("col")
        self.at = {
            "x": lax.rem(self.row, 4),
            "z": lax.rem(self.row // 4, 4),
            "y": (self.row // 16) * 2 + self.col // 2,
        }
        self.core = lax.rem(self.col, 2)

    def device(self, at, core):
        return ((at["y"] // 2) * 16 + at["z"] * 4 + at["x"], lax.rem(at["y"], 2) * 2 + core)

    def step(self, axis, distance):
        at = dict(self.at)
        at[axis] = lax.rem(at[axis] + distance + 4, 4)
        return self.device(at, self.core)

    def partner(self):
        return (self.row, self.col + 1 - 2 * self.core)

    def beside(self, distance):
        return (self.row, lax.rem(self.col + distance, 4))

    def neighbours(self):
        found = [self.step(axis, d) for axis in ("x", "y", "z") for d in (1, -1)]
        found.append(self.partner())
        other = lax.rem(self.col // 2 + 1, 2)
        found.append((self.row, other * 2 + 1 - self.core))
        return found


def greet(devices):
    barrier = pltpu.get_barrier_semaphore()
    for device in devices:
        pl.semaphore_signal(barrier, inc=1, device_id=device, device_id_type=MESH)
    pl.semaphore_wait(barrier, len(devices))


def everything():
    return slice(None)


def place_index(fixed):
    if "y" in fixed:
        y_lo, y_hi = lax.rem(fixed["y"], 2), fixed["y"] // 2
    else:
        y_lo, y_hi = everything(), everything()
    return (y_lo, y_hi, fixed.get("z", everything()), fixed.get("x", everything()))


def remote(source, target, ssem, rsem, device):
    return pltpu.make_async_remote_copy(
        src_ref=source, dst_ref=target, send_sem=ssem, recv_sem=rsem,
        device_id=device, device_id_type=MESH,
    )


def gather_kernel(
    block0, block1, block2, x_ref, g_ref, v_ref,
    all0, all1, all2, x_out, g_out, v_out,
    send, recv, last_send, last_recv, local, in_send, in_recv, in_local,
):
    me = Place()
    blocks = (block0, block1, block2)
    wholes = (all0, all1, all2)
    greet(me.neighbours())

    def region(piece, fixed, rows=None):
        index = place_index(fixed) + ((everything(),) if rows is None else (pl.ds(rows, 16),))
        return wholes[piece].at[index]

    def around(piece, stage, value):
        order = GATHER_ORDERS[piece]
        fixed = {order[stage]: value}
        for axis in order[stage + 1 :]:
            fixed[axis] = me.at[axis]
        return fixed

    sent = []
    pairs = ((x_ref, x_out), (g_ref, g_out))
    waits, arrivals, own_copies = [], [], []
    for piece in range(3):
        copy = pltpu.make_async_copy(
            blocks[piece], region(piece, around(piece, 0, me.at[GATHER_ORDERS[piece][0]])), local.at[piece]
        )
        copy.start()
        own_copies.append(copy)

    def semaphores(piece, stage, n, u):
        if stage == 2:
            return last_send.at[piece, u, n], last_recv.at[piece, u, n]
        return send.at[piece, stage, n], recv.at[piece, stage, n]

    def part(piece, stage, value, u, rows=None):
        fixed = around(piece, stage, value)
        if stage == 2:
            axis = GATHER_ORDERS[piece][1]
            fixed[axis] = lax.rem(me.at[axis] + (0, 3, 1, 2)[u], 4)
        return region(piece, fixed, rows)

    def begin(piece, stage, u=0):
        axis = GATHER_ORDERS[piece][stage]
        mine = part(piece, stage, me.at[axis], u)
        source = blocks[piece] if stage == 0 else mine
        for n, distance in enumerate((1, -1)):
            copy = remote(source, mine, *semaphores(piece, stage, n, u), me.step(axis, distance))
            copy.start()
            sent.append(copy)

    def arrived(piece, stage, n, u=0):
        axis = GATHER_ORDERS[piece][stage]
        value = lax.rem(me.at[axis] + (3, 1, 2, 2)[n], 4)
        there = part(piece, stage, value, u, (None, None, 0, 16)[n])
        remote(there, there, *semaphores(piece, stage, n, u), me.step(axis, 1)).wait_recv()
        if n < 2:
            half = part(piece, stage, value, u, (0, 16)[n])
            copy = remote(half, half, *semaphores(piece, stage, 2 + n, u), me.step(axis, (1, -1)[n]))
            copy.start()
            sent.append(copy)

    for piece in range(3):
        begin(piece, 0)
    partner, across = me.partner(), me.beside(2)

    def tokens_of(ref, col):
        return ref.at[:, pl.ds(pl.multiple_of(col // 2 * PAIR, PAIR), PAIR)]

    relays = []
    for n, (source, target) in enumerate(pairs + ((v_ref, v_out),)):
        here, there = (v_ref, v_ref) if n == 2 else (tokens_of(source, me.col), tokens_of(source, across[1]))
        own = pltpu.make_async_copy(here, target.at[me.col], in_local.at[n])
        own.start()
        waits.append(own)
        for k, (part_ref, device) in enumerate(((there, across), (here, partner))):
            copy = remote(part_ref, target.at[me.col], in_send.at[n, k], in_recv.at[n, k], device)
            copy.start()
            sent.append(copy)
        relays.append(remote(there, target.at[across[1]], in_send.at[n, 0], in_recv.at[n, 0], across))
        arrivals.append(remote(here, target.at[partner[1]], in_send.at[n, 1], in_recv.at[n, 1], partner))
    for copy in own_copies:
        copy.wait()
    for n in range(4):
        for piece in range(3):
            arrived(piece, 0, n)
    for piece in range(3):
        begin(piece, 1)
    for n, (_, target) in enumerate(pairs + ((v_ref, v_out),)):
        relays[n].wait_recv()
        block = target.at[across[1]]
        copy = remote(block, block, in_send.at[n, 2], in_recv.at[n, 2], partner)
        copy.start()
        sent.append(copy)
        far = target.at[lax.rem(partner[1] + 2, 4)]
        arrivals.append(remote(far, far, in_send.at[n, 2], in_recv.at[n, 2], partner))
    for piece in range(3):
        begin(piece, 2, 0)
    for n in range(4):
        for piece in range(3):
            arrived(piece, 1, n)
            if n < 2:
                begin(piece, 2, n + 1)
            elif n == 3:
                begin(piece, 2, 3)
    for n in (0, 1):
        for piece in range(3):
            arrived(piece, 2, n, 0)
    for u in range(1, 4):
        for n in (0, 1):
            for piece in range(3):
                arrived(piece, 2, n, u)
    for u in range(4):
        for n in (2, 3):
            for piece in range(3):
                arrived(piece, 2, n, u)
    for copy in arrivals:
        copy.wait_recv()
    for copy in waits:
        copy.wait()
    for copy in sent:
        copy.wait_send()


def gather_all(blocks, x, g, v):
    whole = jax.ShapeDtypeStruct((2, 2, 4, 4, 32, PACK), BF16)
    tokens = jax.ShapeDtypeStruct((4, 272, PAIR), BF16)
    return pl.pallas_call(
        gather_kernel,
        out_shape=(whole, whole, whole, tokens, tokens, jax.ShapeDtypeStruct((4, 8, 272), F32)),
        in_specs=[ANY] * 6,
        out_specs=(ANY,) * 6,
        scratch_shapes=[
            pltpu.SemaphoreType.DMA((3, 2, 4)),
            pltpu.SemaphoreType.DMA((3, 2, 4)),
            pltpu.SemaphoreType.DMA((3, 4, 4)),
            pltpu.SemaphoreType.DMA((3, 4, 4)),
            pltpu.SemaphoreType.DMA((3,)),
            pltpu.SemaphoreType.DMA((3, 3)),
            pltpu.SemaphoreType.DMA((3, 3)),
            pltpu.SemaphoreType.DMA((3,)),
        ],
        compiler_params=pltpu.CompilerParams(collective_id=0, has_side_effects=True),
        name="gather_weights",
    )(*blocks, x, g, v)


class Group:
    def __init__(self):
        self.row, self.col = lax.axis_index("row"), lax.axis_index("col")
        self.in_group = lax.rem(self.row + 2, 4)
        self.rank = self.in_group * 4 + self.col
        self.pair, self.core = self.rank // 2, lax.rem(self.col, 2)
        self.partner = (self.row, self.col + 1 - 2 * self.core)

    def device(self, other):
        return (lax.rem(self.row - self.in_group + other // 4 + 32, 32), lax.rem(other, 4))

    def greet(self):
        greet([self.device(lax.rem(self.rank + d, 16)) for d in range(1, 16)])

    def all_to_all(self, source, target, send, recv, local):
        own = pltpu.make_async_copy(source.at[self.rank], target.at[self.rank], local)
        own.start()
        sent, arrivals = [], []
        for d in range(1, 16):
            other = lax.rem(self.rank + d, 16)
            copy = remote(source.at[other], target.at[self.rank], send.at[d], recv.at[d], self.device(other))
            copy.start()
            sent.append(copy)
            origin = lax.rem(self.rank + 16 - d, 16)
            arrivals.append(remote(source.at[other], target.at[origin], send.at[d], recv.at[d], self.device(origin)))
        return own, sent, arrivals

    def finish(self, own, sent, arrivals):
        for copy in arrivals:
            copy.wait_recv()
        for copy in sent:
            copy.wait_send()
        own.wait()

    def relay(self, source_of, target, send, recv, local):
        own = pltpu.make_async_copy(source_of(self.pair), target.at[self.rank], local)
        own.start()
        beside = remote(source_of(self.pair), target.at[self.rank], send.at[0, 0], recv.at[0, 0], self.partner)
        beside.start()
        sent = [beside]
        for e in range(1, 8):
            other = lax.rem(self.pair + e, 8)
            copy = remote(
                source_of(other), target.at[self.rank], send.at[0, e], recv.at[0, e], self.device(other * 2 + self.core)
            )
            copy.start()
            sent.append(copy)
        return own, sent

    def pass_on(self, own, sent, target, send, recv):
        for e in range(1, 8):
            origin = lax.rem(self.pair + 8 - e, 8) * 2 + self.core
            block = target.at[origin]
            remote(block, block, send.at[0, e], recv.at[0, e], self.device(origin)).wait_recv()
            copy = remote(block, block, send.at[1, e], recv.at[1, e], self.partner)
            copy.start()
            sent.append(copy)
        for e in range(0, 8):
            block = target.at[lax.rem(self.pair + 8 - e, 8) * 2 + 1 - self.core]
            n = 0 if e == 0 else 1
            remote(block, block, send.at[n, e], recv.at[n, e], self.partner).wait_recv()
        for copy in sent:
            copy.wait_send()
        own.wait()


RELAY = [pltpu.SemaphoreType.DMA((2, 8)), pltpu.SemaphoreType.DMA((2, 8)), pltpu.SemaphoreType.DMA]
DIRECT = [pltpu.SemaphoreType.DMA((16,)), pltpu.SemaphoreType.DMA((16,)), pltpu.SemaphoreType.DMA]


def exchange_call(kernel, name, collective_id, outs, scratch, *args, in_specs=None):
    return pl.pallas_call(
        kernel,
        out_shape=outs,
        in_specs=in_specs or [ANY] * len(args),
        out_specs=(ANY,) * len(outs),
        scratch_shapes=scratch,
        compiler_params=pltpu.CompilerParams(collective_id=collective_id, has_side_effects=True),
        name=name,
    )(*args)


def qkv_exchange_kernel(source, last, target, last_out, send, recv, local, rsend, rrecv, rlocal):
    group = Group()
    group.greet()
    relayed = group.relay(lambda p: last, last_out, rsend, rrecv, rlocal)
    direct = group.all_to_all(source, target, send, recv, local)
    group.pass_on(*relayed, last_out, rsend, rrecv)
    group.finish(*direct)


def qkv_exchange(source, last):
    outs = (jax.ShapeDtypeStruct((16, 192, 128), BF16), jax.ShapeDtypeStruct((16, QUARTER, 128), BF16))
    return exchange_call(qkv_exchange_kernel, "exchange_qkv", 1, outs, DIRECT + RELAY, source, last)


def mixed_exchange_kernel(source, last, target, last_out, send, recv, local, last_send, last_recv, last_local):
    group = Group()
    group.greet()
    relayed = group.relay(lambda p: source.at[p], target, send, recv, local)
    own = pltpu.make_async_copy(last, last_out.at[group.core], last_local)
    own.start()
    copy = remote(last, last_out.at[group.core], last_send, last_recv, group.partner)
    copy.start()
    group.pass_on(*relayed, target, send, recv)
    remote(last, last_out.at[1 - group.core], last_send, last_recv, group.partner).wait_recv()
    copy.wait_send()
    own.wait()


def mixed_exchange(source, last):
    outs = (jax.ShapeDtypeStruct((16, 128, 128), BF16), jax.ShapeDtypeStruct((2, QUARTER, 64), BF16))
    return exchange_call(
        mixed_exchange_kernel, "exchange_mixed", 2, outs, RELAY + [pltpu.SemaphoreType.DMA] * 3, source, last
    )


def free_axes(fixed):
    return [axis for axis in ("y", "z", "x") if axis not in fixed]


def buffer_shape(fixed, rows, width):
    shape = ()
    for axis in free_axes(fixed):
        shape = shape + ((2, 2) if axis == "y" else (4,))
    return shape + (rows, width)


def buffer_index(at):
    index = ()
    for axis in ("y", "z", "x"):
        if axis in at:
            index = index + ((lax.rem(at[axis], 2), at[axis] // 2) if axis == "y" else (at[axis],))
    return index


VECTOR_AXES = ("z", "x", "y")
CHUNKS = (2, 1, 3, 0)


class Reduction:
    def __init__(self, me, source, widths, scratch, out):
        self.me, self.source, self.widths, self.out = me, source, widths, out
        self.offsets = (0, widths[0], widths[0] + widths[1])
        self.sums = scratch[0:3]
        self.halves, self.fulls = {}, {}
        position = 3
        for piece in range(3):
            for stage in range(3):
                self.halves[piece, stage] = scratch[position : position + 2]
                self.fulls[piece, stage] = scratch[position + 2 : position + 4]
                position += 4
        self.local, self.big_send, self.big_recv, self.send, self.recv = scratch[position : position + 5]
        self.sent, self.loads = [], {}

    @staticmethod
    def scratch(widths):
        found = [pltpu.VMEM((2, 2, 4, 4, 32, width), BF16) for width in widths]
        for piece in range(3):
            order = SCATTER_ORDERS[piece]
            for stage in range(3):
                fixed = order[: stage + 1]
                found += [pltpu.VMEM(buffer_shape(fixed, 16, widths[piece]), BF16) for _ in range(2)]
                found += [pltpu.VMEM(buffer_shape(fixed, 32, widths[piece]), BF16) for _ in range(2)]
        found += [pltpu.SemaphoreType.DMA((3, 4, 4))] * 3 + [pltpu.SemaphoreType.DMA((3, 2, 4))] * 2
        return found

    def shifted(self, axis, distance):
        return lax.rem(self.me.at[axis] + distance, 4)

    def load_all(self):
        for k in range(4):
            for u in range(4):
                for piece in range(3):
                    first, second = SCATTER_ORDERS[piece][:2]
                    index = place_index(
                        {first: self.shifted(first, CHUNKS[k]), second: self.shifted(second, CHUNKS[u])}
                    )
                    lanes = pl.ds(self.offsets[piece], self.widths[piece])
                    load = pltpu.make_async_copy(
                        self.source.at[index + (everything(), lanes)], self.sums[piece].at[index],
                        self.local.at[piece, k, u],
                    )
                    load.start()
                    self.loads[piece, k, u] = load

    def stage_fixed(self, piece, stage):
        return {axis: self.me.at[axis] for axis in SCATTER_ORDERS[piece][:stage]}

    def each_tile(self, fixed, body):
        axes = free_axes(fixed)
        count = 4 ** len(axes)
        if count == 1:
            body({})
            return

        @pl.loop(0, count)
        def _(t):
            body({axes[0]: t})

    def chunk(self, piece, stage, u):
        if stage > 0:
            return {}
        axis = SCATTER_ORDERS[piece][1]
        return {axis: self.shifted(axis, CHUNKS[u])}

    def sems(self, piece, stage, n, u):
        if stage == 0:
            return self.big_send.at[piece, u, n], self.big_recv.at[piece, u, n]
        return self.send.at[piece, stage - 1, n], self.recv.at[piece, stage - 1, n]

    def part_of(self, buffer, piece, stage, u):
        if stage > 0:
            return buffer
        axis = SCATTER_ORDERS[piece][1]
        value = self.shifted(axis, CHUNKS[u])
        index = ()
        for name in free_axes({SCATTER_ORDERS[piece][0]: 0}):
            if name == "y":
                index += (lax.rem(value, 2), value // 2) if name == axis else (everything(), everything())
            else:
                index += (value,) if name == axis else (everything(),)
        return buffer.at[index]

    def start(self, source, target, semaphores, axis, n):
        copy = remote(source, target, *semaphores, self.me.step(axis, (1, -1)[n]))
        copy.start()
        self.sent.append(copy)

    def wait(self, there, semaphores, axis):
        remote(there, there, *semaphores, self.me.step(axis, 1)).wait_recv()

    def begin(self, piece, stage, u=0):
        if stage == 0:
            self.loads[piece, 0, u].wait()
        axis = SCATTER_ORDERS[piece][stage]
        fixed = {**self.stage_fixed(piece, stage), axis: self.shifted(axis, 2), **self.chunk(piece, stage, u)}
        for n in range(2):
            self.start(
                self.sums[piece].at[place_index(fixed) + (pl.ds(16 * n, 16),)],
                self.part_of(self.halves[piece, stage][n], piece, stage, u), self.sems(piece, stage, n, u), axis, n,
            )

    def middle(self, piece, stage, n, u=0):
        if stage == 0:
            self.loads[piece, 1 + n, u].wait()
        axis = SCATTER_ORDERS[piece][stage]
        more = self.chunk(piece, stage, u)
        fixed = {**self.stage_fixed(piece, stage), axis: self.shifted(axis, (1, 3)[n]), **more}
        half, sums = self.halves[piece, stage][n], self.sums[piece]
        self.wait(self.part_of(half, piece, stage, u), self.sems(piece, stage, n, u), axis)

        def body(at):
            index = place_index({**fixed, **at}) + (pl.ds(16 * n, 16),)
            total = sums[index].astype(F32) + half[buffer_index({**more, **at})].astype(F32)
            sums[index] = total.astype(BF16)

        self.each_tile(fixed, body)
        self.start(
            sums.at[place_index(fixed)], self.part_of(self.fulls[piece, stage][n], piece, stage, u),
            self.sems(piece, stage, 2 + n, u), axis, n,
        )

    def finish(self, piece, stage, u=0):
        if stage == 0:
            self.loads[piece, 3, u].wait()
        axis = SCATTER_ORDERS[piece][stage]
        more = self.chunk(piece, stage, u)
        fixed = {**self.stage_fixed(piece, stage), axis: self.me.at[axis], **more}
        first, second = self.fulls[piece, stage]
        sums = self.sums[piece]
        for n, buffer in enumerate((first, second)):
            self.wait(self.part_of(buffer, piece, stage, u), self.sems(piece, stage, 2 + n, u), axis)

        def body(at):
            index = place_index({**fixed, **at})
            if stage == 2:
                total = sums[index].astype(F32) + (first[...].astype(F32) + second[...].astype(F32))
                self.out[:, self.offsets[piece] : self.offsets[piece] + self.widths[piece]] = total
            else:
                place = buffer_index({**more, **at})
                total = sums[index].astype(F32) + (first[place].astype(F32) + second[place].astype(F32))
                sums[index] = total.astype(BF16)

        self.each_tile(fixed, body)

    def begin_chunk(self, u):
        for piece in range(3):
            self.begin(piece, 0, u)

    def middle_chunk(self, u):
        for n in range(2):
            for piece in range(3):
                self.middle(piece, 0, n, u)

    def finish_chunk(self, u):
        for piece in range(3):
            self.finish(piece, 0, u)
            if u == 0:
                self.begin(piece, 1)
            elif u < 3:
                self.middle(piece, 1, u - 1)
            else:
                self.finish(piece, 1)
                self.begin(piece, 2)

    def finish_all(self):
        for n in range(2):
            for piece in range(3):
                self.middle(piece, 2, n)
        for piece in range(3):
            self.finish(piece, 2)

    def wait_sent(self):
        for copy in self.sent:
            copy.wait_send()


LATE_WIDTHS = (512, 384, 384)
EARLY_WIDTHS = (896, 896, 768)


def scatter_kernel(source, y_ref, gin_ref, v_ref, out_ref, y_out, gin_out, v_out, *scratch):
    me = Place()
    vectors = scratch[0:3]
    out_send, out_recv, out_local, v_send, v_recv = scratch[3:8]
    reduction = Reduction(me, source, LATE_WIDTHS, scratch[8:], out_ref)
    greet(me.neighbours() + [me.step(axis, 2) for axis in VECTOR_AXES])
    sent = []
    reduction.load_all()

    def vectors_begin(phase, value):
        axis = VECTOR_AXES[phase]
        mine = vectors[phase].at[me.at[axis]]
        mine[...] = value
        for distance in (1, 2, 3):
            copy = remote(
                mine, mine, v_send.at[phase, distance - 1], v_recv.at[phase, distance - 1], me.step(axis, distance)
            )
            copy.start()
            sent.append(copy)

    def vectors_end(phase):
        axis = VECTOR_AXES[phase]
        for distance in (1, 2, 3):
            there = vectors[phase].at[lax.rem(me.at[axis] + 4 - distance, 4)]
            remote(
                there, there, v_send.at[phase, distance - 1], v_recv.at[phase, distance - 1], me.step(axis, distance)
            ).wait_recv()
        buffer = vectors[phase]
        return (buffer[0] + buffer[1]) + (buffer[2] + buffer[3])

    reduction.begin_chunk(0)
    vectors_begin(0, v_ref[...])
    reduction.begin_chunk(1)
    pairs = ((y_ref, y_out), (gin_ref, gin_out))
    arrivals, own_copies = [], []
    for n, (source, target) in enumerate(pairs):
        rows = pl.ds(pl.multiple_of(me.col * QUARTER, QUARTER), QUARTER)
        own = pltpu.make_async_copy(source.at[me.col], target.at[:, rows], out_local.at[n])
        own.start()
        own_copies.append(own)
        for distance in (1, 2, 3):
            peer = me.beside(distance)
            semaphore = (out_send.at[n, distance - 1], out_recv.at[n, distance - 1])
            copy = remote(source.at[peer[1]], target.at[:, rows], *semaphore, peer)
            copy.start()
            sent.append(copy)
            origin = pl.ds(pl.multiple_of(lax.rem(me.col + 4 - distance, 4) * QUARTER, QUARTER), QUARTER)
            arrivals.append(remote(source.at[me.col], target.at[:, origin], *semaphore, peer))
    for u in range(4):
        reduction.middle_chunk(u)
        if u < 2:
            reduction.begin_chunk(u + 2)
            vectors_begin(u + 1, vectors_end(u))
        if u == 3:
            v_out[...] = vectors_end(2)
        if u > 0:
            reduction.finish_chunk(u - 1)
    reduction.finish_chunk(3)
    reduction.finish_all()
    for copy in arrivals:
        copy.wait_recv()
    for copy in own_copies:
        copy.wait()
    for copy in sent:
        copy.wait_send()
    reduction.wait_sent()


def scatter_all(part, y4, gin4, vectors):
    scratch = [pltpu.VMEM((4, 8, WIDE), F32) for _ in range(3)]
    scratch += [
        pltpu.SemaphoreType.DMA((2, 3)),
        pltpu.SemaphoreType.DMA((2, 3)),
        pltpu.SemaphoreType.DMA((2,)),
        pltpu.SemaphoreType.DMA((3, 3)),
        pltpu.SemaphoreType.DMA((3, 3)),
    ]
    back = jax.ShapeDtypeStruct((272, 512), BF16)
    return pl.pallas_call(
        scatter_kernel,
        out_shape=(jax.ShapeDtypeStruct((32, PACK), F32), back, back, jax.ShapeDtypeStruct((8, WIDE), F32)),
        in_specs=[ANY] * 3 + [VMEM_SPEC],
        out_specs=(VMEM_SPEC, ANY, ANY, VMEM_SPEC),
        scratch_shapes=scratch + Reduction.scratch(LATE_WIDTHS),
        compiler_params=pltpu.CompilerParams(
            collective_id=3, has_side_effects=True, vmem_limit_bytes=VMEM_LIMIT
        ),
        name="scatter_gradients",
    )(part, y4, gin4, vectors)


def unpack_tail(packed, tiles, wide, tail):
    tiles[...] = packed[:, WIDE:PACK].astype(F32)
    for j in range(2):
        for s in range(9):
            wide[pl.ds(32 * j, 32), pl.ds(128 * s, 128)] = tiles[pl.ds(9 * j + s, 32, stride=32), :]
    tail[0:64, :] = wide[0:64, :].astype(BF16)


def pack_tail(tail, tiles, packed):
    for j in range(2):
        for s in range(9):
            tiles[pl.ds(9 * j + s, 32, stride=32), :] = tail[32 * j : 32 * j + 32, 128 * s : 128 * s + 128]
    packed[:, WIDE:PACK] = tiles[...].astype(BF16)


def in_features(values, packed, tail, columns):
    return dot_nn(values[:, :MAIN], packed[:, columns]) + dot_nn(values[:, MAIN:], tail[:, columns])


def add_to_features(total_t, values_t, packed, tail):
    @pl.loop(0, 4)
    def _(b):
        rows = pl.ds(pl.multiple_of(b * 256, 256), 256)
        total_t[rows, :] += dot_nn(packed[rows, :WIDE], values_t[...])

    total_t[MAIN:, :] += dot_nn(tail[...], values_t[...])


def norm_forward(x, gain, bias):
    mean = jnp.sum(x, axis=1, keepdims=True) / D
    square = jnp.sum(x * x, axis=1, keepdims=True) / D
    inverse = lax.rsqrt(square - mean * mean + norm_epsilon)
    normed = (x - mean) * inverse
    return normed, inverse, (normed * gain + bias).astype(BF16)


def norm_reverse(grad, normed, inverse, gain):
    scaled = grad * gain
    first = jnp.sum(scaled, axis=1, keepdims=True) / D
    second = jnp.sum(scaled * normed, axis=1, keepdims=True) / D
    return inverse * (scaled - first - normed * second)


def permuted(pieces, perm):
    total = dot_nn(pieces[0].astype(F32).T.astype(BF16), perm[0])
    for c in range(1, 4):
        total += dot_nn(pieces[c].astype(F32).T.astype(BF16), perm[c])
    return total


def permuted_exact(pieces, perm):
    total = jnp.zeros((8, WIDE), F32)
    for c in range(4):
        left = pieces[c]
        for _ in range(3):
            part = left.astype(BF16)
            left = left - part.astype(F32)
            total += dot_nn(part, perm[c])
    return total


def real_features(values):
    lane = lax.broadcasted_iota(jnp.int32, values.shape, 1)
    return jnp.where(lane < D, values, 0.0)


def turned(values):
    return values.astype(F32).T.astype(BF16)


def own_half(core):
    return pl.ds(pl.multiple_of(core * QUARTER, QUARTER), QUARTER)


def load_weights(source, target, semaphores):
    copies = []
    for j in range(2):
        copy = pltpu.make_async_copy(source.at[j], target.at[j], semaphores.at[j])
        copy.start()
        copies.append(copy)
    return copies


def qkv_kernel(
    x4, v4, perm, w_ref, x_out, n1_out, v_out, msg, last, q16, w, qkv, qkv_out, tiles, wide, tail, load, send, recv, local
):
    me = Place()
    partner = me.partner()
    copies = load_weights(w_ref, w, load)
    greet([partner])
    x = permuted(x4, perm)
    vectors = permuted_exact(v4, perm)
    v_out[...] = vectors
    x_out[...] = x.astype(BF16)
    _, _, normed = norm_forward(x, vectors[0:1], vectors[1:2])
    n1_out[...] = normed
    tail[...] = jnp.zeros_like(tail)
    mine, theirs = own_half(me.core), own_half(1 - me.core)
    sent, own_copies, arrivals = [], [], []
    for j in range(2):
        copies[j].wait()
        packed = w.at[j]
        unpack_tail(packed, tiles, wide, tail)

        @pl.loop(0, 3)
        def _(b):
            columns = pl.ds(pl.multiple_of(b * 384, 128), 384)
            qkv[j, :, columns] = in_features(n1_out[...], packed, tail, columns).astype(BF16)

        own = pltpu.make_async_copy(qkv.at[j, mine, :], qkv_out.at[j, me.core], local.at[j])
        own.start()
        own_copies.append(own)
        copy = remote(qkv.at[j, theirs, :], qkv_out.at[j, me.core], send.at[j], recv.at[j], partner)
        copy.start()
        sent.append(copy)
        arrivals.append(
            remote(qkv.at[j, theirs, :], qkv_out.at[j, 1 - me.core], send.at[j], recv.at[j], partner)
        )
    for copy in arrivals:
        copy.wait_recv()
    for copy in own_copies:
        copy.wait()
    for n in range(3):
        for head in range(HEADS):
            block = columns_of(qkv_out, n * D + head * HEAD_DIM, QKV_COLS, 0)
            if head == 16:
                if n == 0:
                    q16[...] = block
                else:
                    last[:, 64 * (n - 1) : 64 * n] = block
            else:
                msg[head, 64 * n : 64 * n + 64, 0:64] = block[0:64]
                msg[head, 64 * n : 64 * n + 64, 64:128] = block[64:128]
    for copy in sent:
        copy.wait_send()


def columns_of(blocks, start, width, offset):
    pieces = []
    position = start
    while position < start + HEAD_DIM:
        c = position // width
        end = min(start + HEAD_DIM, (c + 1) * width)
        first = position - c * width + offset
        pieces.append(blocks[c // 2, c % 2, :, first : first + end - position])
        position = end
    return pieces[0] if len(pieces) == 1 else jnp.concatenate(pieces, axis=1)


def qkv_call(x4, v4, perm, weights):
    row = jax.ShapeDtypeStruct((PAIR, WIDE), BF16)
    return pl.pallas_call(
        qkv_kernel,
        out_shape=(
            row, row, jax.ShapeDtypeStruct((8, WIDE), F32), jax.ShapeDtypeStruct((16, 192, 128), BF16),
            jax.ShapeDtypeStruct((QUARTER, 128), BF16), jax.ShapeDtypeStruct((QUARTER, 64), BF16),
        ),
        in_specs=[VMEM_SPEC, VMEM_SPEC, VMEM_SPEC, ANY],
        out_specs=(VMEM_SPEC,) * 6,
        scratch_shapes=[
            pltpu.VMEM((2, MAIN, PACK), BF16), pltpu.VMEM((2, PAIR, WIDE), BF16),
            pltpu.VMEM((2, 2, QUARTER, WIDE), BF16),
            pltpu.VMEM((MAIN, 128), F32), pltpu.VMEM((128, WIDE), F32), pltpu.VMEM((128, WIDE), BF16),
            pltpu.SemaphoreType.DMA((2,)), pltpu.SemaphoreType.DMA((2,)), pltpu.SemaphoreType.DMA((2,)),
            pltpu.SemaphoreType.DMA((2,)),
        ],
        compiler_params=pltpu.CompilerParams(
            collective_id=4, has_side_effects=True, vmem_limit_bytes=VMEM_LIMIT
        ),
        name="norm_and_qkv",
    )(x4, v4, perm, weights)


def gelu_both(v):
    square = v * v
    tanh_value = jnp.tanh(gelu_coef * (v + 0.044715 * v * square))
    half = 0.5 * (1.0 + tanh_value)
    value = v * half
    slope = half + 0.5 * v * (1.0 - tanh_value * tanh_value) * gelu_coef * (1.0 + 0.134145 * square)
    return value, slope


def weight_gradient(rows_t, values, tiles, tail_sum, packed):
    @pl.loop(0, 4)
    def _(b):
        rows = pl.ds(pl.multiple_of(b * 256, 256), 256)
        packed[rows, :WIDE] = dot_nn(rows_t[rows, :], values[...]).astype(BF16)

    tail_sum[...] = dot_nn(rows_t[MAIN:, :], values[...])
    pack_tail(tail_sum, tiles, packed)


def swap_start(total_t, mine, theirs, ssem, rsem, partner):
    mine[...] = total_t[...].astype(BF16)
    copy = remote(mine, theirs, ssem, rsem, partner)
    copy.start()
    return copy


def swap_end(copy, mine, theirs):
    copy.wait_recv()
    return mine[...].astype(F32) + theirs[...].astype(F32)


def middle_kernel(
    x_ref, a0, w0_ref, w1_ref, w2_ref, g4, perm, vec,
    y4, dres_out, dresb_out, gr12_out, dmsg, dlast, vec_out,
    w0, w1, w2, gr1, gr2, resid, normed2, inverse2, n2, n2_t, cot, cot_t, total_t, dn2_t, hidden, dpre, turn1, turn2,
    dmix, tiles, out_tiles, tail1, tail2, tail_sum, mine1, theirs1, mine2, theirs2, mine_y, theirs_y, dmix_out,
    load, store, send, recv, local,
):
    me = Place()
    partner = me.partner()
    loads = [load_weights(source, target, load.at[n]) for n, (source, target) in enumerate(
        ((w0_ref, w0), (w1_ref, w1), (w2_ref, w2))
    )]
    greet([partner])
    for buffer in (tail1, tail2, out_tiles, total_t, dn2_t):
        buffer[...] = jnp.zeros_like(buffer)
    for j in range(2):
        turn1[...] = turned(a0[j])
        loads[0][j].wait()
        unpack_tail(w0.at[j], tiles, tail_sum, tail1)
        add_to_features(total_t, turn1, w0.at[j], tail1)
    first = swap_start(total_t, mine1, theirs1, send.at[0], recv.at[0], partner)
    cot_value = permuted(g4, perm)
    cot[...] = cot_value.astype(BF16)
    cot_t[...] = cot_value.T.astype(BF16)
    total_t[...] = jnp.zeros_like(total_t)
    attended = swap_end(first, mine1, theirs1)
    resid[...] = x_ref[...].astype(F32) + attended.T
    normed, inverse, n2_value = norm_forward(resid[...], vec[2:3], vec[3:4])
    normed2[...] = normed
    inverse2[...] = jnp.broadcast_to(inverse, inverse2.shape)
    n2[...] = n2_value
    n2_t[...] = turned(n2_value)
    stores = []
    for j in range(2):
        loads[1][j].wait()
        loads[2][j].wait()
        up, down = w1.at[j], w2.at[j]
        unpack_tail(up, tiles, tail_sum, tail1)
        unpack_tail(down, tiles, tail_sum, tail2)

        @pl.loop(0, 3)
        def _(b):
            columns = pl.ds(pl.multiple_of(b * 384, 128), 384)
            pre = in_features(n2[...], up, tail1, columns)
            d_hidden = in_features(cot[...], down, tail2, columns)
            value, slope = gelu_both(pre)
            hidden[:, columns] = value.astype(BF16)
            dpre[:, columns] = (d_hidden * slope).astype(BF16)

        turn1[...] = turned(hidden[...])
        turn2[...] = turned(dpre[...])
        add_to_features(total_t, turn1, down, tail2)
        add_to_features(dn2_t, turn2, up, tail1)
        if j == 1:
            second = swap_start(dn2_t, mine2, theirs2, send.at[1], recv.at[1], partner)
            half = own_half(1 - me.core)
            mine_y[...] = total_t[:, half].astype(BF16)
            third = remote(mine_y, theirs_y, send.at[2], recv.at[2], partner)
            third.start()
        weight_gradient(n2_t, dpre, out_tiles, tail_sum, gr1.at[j])
        weight_gradient(cot_t, hidden, out_tiles, tail_sum, gr2.at[j])
        for n, source in enumerate((gr1, gr2)):
            copy = pltpu.make_async_copy(source.at[j], gr12_out.at[j, :, pl.ds(PACK * n, PACK)], store.at[n, j])
            copy.start()
            stores.append(copy)
    grad = swap_end(second, mine2, theirs2).T
    normed = normed2[...]
    vec_out[...] = jnp.zeros_like(vec_out)
    vec_out[0:1, :] = jnp.sum(grad * normed, axis=0, keepdims=True)
    vec_out[1:2, :] = jnp.sum(grad, axis=0, keepdims=True)
    back = cot[...].astype(F32) + norm_reverse(grad, normed, inverse2[:, 0:1], vec[2:3])
    back = real_features(back)
    dres_out[...] = back
    dresb_out[...] = back.astype(BF16)
    sent, own_copies, arrivals = [first, second, third], [], []
    columns = slice(768, WIDE)
    for j in range(2):
        unpack_tail(w0.at[j], tiles, tail_sum, tail1)
        dmix[j] = in_features(dresb_out[...], w0.at[j], tail1, columns).astype(BF16)
        own = pltpu.make_async_copy(dmix.at[j, own_half(me.core), :], dmix_out.at[j, me.core], local.at[j])
        own.start()
        own_copies.append(own)
        theirs = dmix.at[j, own_half(1 - me.core), :]
        copy = remote(theirs, dmix_out.at[j, me.core], send.at[3 + j], recv.at[3 + j], partner)
        copy.start()
        sent.append(copy)
        arrivals.append(remote(theirs, dmix_out.at[j, 1 - me.core], send.at[3 + j], recv.at[3 + j], partner))
    half = own_half(me.core)
    third.wait_recv()
    y = (resid[half, :].T + (total_t[:, half] + theirs_y[...].astype(F32))).astype(BF16)
    for c in range(4):
        y4[c] = dot_nn(perm[c], y).astype(BF16)
    for copy in arrivals:
        copy.wait_recv()
    for copy in own_copies:
        copy.wait()
    for head in range(HEADS):
        block = columns_of(dmix_out, head * HEAD_DIM, 272, QKV_COLS - 768)
        if head == 16:
            dlast[...] = block
        else:
            dmsg[head, :, 0:64] = block[0:64]
            dmsg[head, :, 64:128] = block[64:128]
    for copy in stores:
        copy.wait()
    for copy in sent:
        copy.wait_send()


def middle_call(x, a0, w0, w1, w2, g4, perm, vec):
    weights = pltpu.VMEM((2, MAIN, PACK), BF16)
    row_f, row_b = pltpu.VMEM((PAIR, WIDE), F32), pltpu.VMEM((PAIR, WIDE), BF16)
    turn_f, turn_b = pltpu.VMEM((WIDE, PAIR), F32), pltpu.VMEM((WIDE, PAIR), BF16)
    tile, tail = pltpu.VMEM((MAIN, 128), F32), pltpu.VMEM((128, WIDE), BF16)
    half = pltpu.VMEM((WIDE, QUARTER), BF16)
    return pl.pallas_call(
        middle_kernel,
        out_shape=(
            jax.ShapeDtypeStruct((4, 272, QUARTER), BF16), jax.ShapeDtypeStruct((PAIR, WIDE), F32),
            jax.ShapeDtypeStruct((PAIR, WIDE), BF16), jax.ShapeDtypeStruct((2, MAIN, 2 * PACK), BF16),
            jax.ShapeDtypeStruct((16, 64, 128), BF16), jax.ShapeDtypeStruct((QUARTER, 64), BF16),
            jax.ShapeDtypeStruct((8, WIDE), F32),
        ),
        in_specs=[VMEM_SPEC, VMEM_SPEC, ANY, ANY, ANY, VMEM_SPEC, VMEM_SPEC, VMEM_SPEC],
        out_specs=(VMEM_SPEC, VMEM_SPEC, VMEM_SPEC, ANY, VMEM_SPEC, VMEM_SPEC, VMEM_SPEC),
        scratch_shapes=[
            weights, weights, weights, weights, weights, row_f, row_f, pltpu.VMEM((PAIR, 128), F32), row_b, turn_b,
            row_b, turn_b, turn_f, turn_f, row_b, row_b, turn_b, turn_b, pltpu.VMEM((2, PAIR, 384), BF16),
            tile, tile, tail, tail, pltpu.VMEM((128, WIDE), F32), turn_b, turn_b, turn_b, turn_b, half, half,
            pltpu.VMEM((2, 2, QUARTER, 384), BF16),
            pltpu.SemaphoreType.DMA((3, 2)), pltpu.SemaphoreType.DMA((2, 2)), pltpu.SemaphoreType.DMA((5,)),
            pltpu.SemaphoreType.DMA((5,)), pltpu.SemaphoreType.DMA((2,)),
        ],
        compiler_params=pltpu.CompilerParams(
            collective_id=5, has_side_effects=True, vmem_limit_bytes=VMEM_LIMIT
        ),
        name="feed_forward",
    )(x, a0, w0, w1, w2, g4, perm, vec)


def first_kernel(
    x_ref, n1, dresb, dres, dq_ref, a0, w0_ref, perm, vec, vec2,
    gin4, gr0_out, sums,
    w0, gr0, dq, n1_t, dres_t, turn, dn1_t, tiles, out_tiles, tail, tail_sum, mine, theirs,
    load, store, send, recv, local,
):
    me = Place()
    partner = me.partner()
    loads = load_weights(w0_ref, w0, load)
    greet([partner])
    mine_rows = own_half(me.core)
    copy = remote(dq_ref.at[1 - me.core], dq.at[:, mine_rows, :], send.at[0], recv.at[0], partner)
    copy.start()
    own = pltpu.make_async_copy(dq_ref.at[me.core], dq.at[:, mine_rows, :], local)
    own.start()
    for buffer in (tail, out_tiles, dn1_t):
        buffer[...] = jnp.zeros_like(buffer)
    n1_t[...] = turned(n1[...])
    dres_t[...] = turned(dresb[...])
    normed, inverse, _ = norm_forward(x_ref[...].astype(F32), vec[0:1], vec[1:2])
    own.wait()
    remote(
        dq_ref.at[me.core], dq.at[:, own_half(1 - me.core), :], send.at[0], recv.at[0], partner
    ).wait_recv()
    for j in range(2):
        loads[j].wait()
        unpack_tail(w0.at[j], tiles, tail_sum, tail)
        turn[...] = turned(dq[j])
        add_to_features(dn1_t, turn, w0.at[j], tail)
    swap = swap_start(dn1_t, mine, theirs, send.at[1], recv.at[1], partner)
    stores = []
    for j in range(2):
        packed = gr0.at[j]

        @pl.loop(0, 4)
        def _(b):
            rows = pl.ds(pl.multiple_of(b * 256, 256), 256)
            packed[rows, :768] = dot_nn(n1_t[rows, :], dq[j, :, :768]).astype(BF16)
            packed[rows, 768:WIDE] = (
                dot_nn(n1_t[rows, :], dq[j, :, 768:]) + dot_nn(dres_t[rows, :], a0[j, :, 768:])
            ).astype(BF16)

        tail_sum[:, :768] = dot_nn(n1_t[MAIN:, :], dq[j, :, :768])
        tail_sum[:, 768:] = dot_nn(n1_t[MAIN:, :], dq[j, :, 768:]) + dot_nn(dres_t[MAIN:, :], a0[j, :, 768:])
        pack_tail(tail_sum, out_tiles, packed)
        out = pltpu.make_async_copy(packed, gr0_out.at[j], store.at[j])
        out.start()
        stores.append(out)
    grad = swap_end(swap, mine, theirs).T
    sums[...] = vec2[...]
    sums[4:5, :] = jnp.sum(grad * normed, axis=0, keepdims=True)
    sums[5:6, :] = jnp.sum(grad, axis=0, keepdims=True)
    back = dres[...] + norm_reverse(grad, normed, inverse, vec[0:1])
    dn1_t[...] = real_features(back).T
    back = dn1_t[:, mine_rows].astype(BF16)
    for c in range(4):
        gin4[c] = dot_nn(perm[c], back).astype(BF16)
    for out in stores:
        out.wait()
    copy.wait_send()
    swap.wait_send()


def first_call(x, n1, dresb, dres, dq, a0, w0, perm, vec, vec2):
    weights = pltpu.VMEM((2, MAIN, PACK), BF16)
    turn_b = pltpu.VMEM((WIDE, PAIR), BF16)
    tile = pltpu.VMEM((MAIN, 128), F32)
    return pl.pallas_call(
        first_kernel,
        out_shape=(
            jax.ShapeDtypeStruct((4, 272, QUARTER), BF16), jax.ShapeDtypeStruct((2, MAIN, PACK), BF16),
            jax.ShapeDtypeStruct((8, WIDE), F32),
        ),
        in_specs=[VMEM_SPEC] * 4 + [ANY, VMEM_SPEC, ANY] + [VMEM_SPEC] * 3,
        out_specs=(VMEM_SPEC, ANY, VMEM_SPEC),
        scratch_shapes=[
            weights, weights, pltpu.VMEM((2, PAIR, WIDE), BF16), turn_b, turn_b, turn_b,
            pltpu.VMEM((WIDE, PAIR), F32), tile, tile, pltpu.VMEM((128, WIDE), BF16), pltpu.VMEM((128, WIDE), F32),
            turn_b, turn_b,
            pltpu.SemaphoreType.DMA((2,)), pltpu.SemaphoreType.DMA((2,)), pltpu.SemaphoreType.DMA((2,)),
            pltpu.SemaphoreType.DMA((2,)), pltpu.SemaphoreType.DMA,
        ],
        compiler_params=pltpu.CompilerParams(
            collective_id=6, has_side_effects=True, vmem_limit_bytes=VMEM_LIMIT
        ),
        name="first_norm_back",
    )(x, n1, dresb, dres, dq, a0, w0, perm, vec, vec2)


def allowed_pairs(shape, key_start, query_start):
    key = key_start + lax.broadcasted_iota(jnp.int32, shape, 0)
    query = query_start + lax.broadcasted_iota(jnp.int32, shape, 1)
    return key <= query


def transposed(values):
    return values.astype(F32).T


def spread(block, target, row, rows=64):
    target[pl.ds(row, 64), :] = block[:, 0:64]
    target[pl.ds(row + 64, 64), :] = block[:, 64:128]


def attend_kernel(info, r_ref, kv16, q16, dense_out, o_out, o16_out, l_out, l16_out, query, key, value, value_t, value16_t):
    rank, wraps = info[0], info[1]

    @pl.loop(0, 16)
    def _(b):
        row = pl.multiple_of(b * 128, 128)
        spread(r_ref[b, 0:64, :] * jnp.asarray(0.125, BF16), query, row)
        spread(r_ref[b, 64:128, :], key, row)
        spread(r_ref[b, 128:192, :], value, row)

    @pl.loop(0, 4)
    def _(b):
        rows = pl.ds(pl.multiple_of(b * KEYS, KEYS), KEYS)
        value_t[:, rows] = transposed(value[rows, :]).astype(BF16)
        value16_t[:, rows] = transposed(kv16[rows, :])[64:128].astype(BF16)

    def step(q, k_ref, v_t, j, carry, query_start=None):
        peak, running, mixed = carry
        rows = pl.ds(pl.multiple_of(j * KEYS, KEYS), KEYS)
        scores = dot_nt(k_ref[rows, 0:64], q)
        if query_start is not None:
            scores = jnp.where(allowed_pairs(scores.shape, j * KEYS, query_start), scores, masked_score)
        new_peak = jnp.maximum(peak, jnp.max(scores, axis=0, keepdims=True))
        shrink = jnp.exp(peak - new_peak)
        weights = jnp.exp(scores - new_peak)
        running = running * shrink + jnp.sum(weights, axis=0, keepdims=True)
        mixed = mixed * shrink + dot_nn(v_t[:, rows], weights.astype(BF16))
        return new_peak, running, mixed

    def empty(width):
        return (
            jnp.full((1, width), masked_score, F32), jnp.zeros((1, width), F32), jnp.zeros((64, width), F32)
        )

    @pl.loop(0, 4)
    def _(i):
        rows = pl.ds(pl.multiple_of(i * KEYS, KEYS), KEYS)
        q = query[rows, :]
        start = jnp.where((wraps == 1) & (i >= 2), 2, 0)
        carry = lax.fori_loop(
            start, i, lambda j, carry: step(q, key, value_t, j, carry), empty(KEYS)
        )
        peak, running, mixed = step(q, key, value_t, i, carry, i * KEYS)
        result = (mixed / running).T.astype(BF16)
        o_out[rows, :] = result
        for n in range(4):
            dense_out[2 * i + n // 2, :, 64 * (n % 2) : 64 * (n % 2) + 64] = result[128 * n : 128 * n + 128]
        l_out[:, rows] = peak + jnp.log(running)

    q = q16[...] * jnp.asarray(0.125, BF16)
    start = jnp.where((wraps == 1) & (rank >= 8), 2, 0)
    peak, running, mixed = lax.fori_loop(
        start, rank // 4 + 1,
        lambda j, carry: step(q, kv16, value16_t, j, carry, rank * QUARTER), empty(QUARTER),
    )
    o16_out[...] = (mixed / running).T.astype(BF16)
    l16_out[...] = peak + jnp.log(running)


def attend_call(info, r, kv16, q16):
    tokens = jax.ShapeDtypeStruct((SEQ, 64), BF16)
    return pl.pallas_call(
        attend_kernel,
        out_shape=(
            jax.ShapeDtypeStruct((8, 128, 128), BF16), tokens, jax.ShapeDtypeStruct((QUARTER, 64), BF16),
            jax.ShapeDtypeStruct((1, SEQ), F32), jax.ShapeDtypeStruct((1, QUARTER), F32), tokens, tokens, tokens,
        ),
        in_specs=[SMEM_SPEC, VMEM_SPEC, VMEM_SPEC, VMEM_SPEC],
        out_specs=(VMEM_SPEC,) * 8,
        scratch_shapes=[pltpu.VMEM((64, SEQ), BF16), pltpu.VMEM((64, SEQ), BF16)],
        compiler_params=pltpu.CompilerParams(vmem_limit_bytes=VMEM_LIMIT),
        name="attend_forward",
    )(info, r, kv16, q16)


def attend_back_kernel(
    dmsg, gradients, query, key, value, kv16, q16, o_ref, o16, do16, l_ref, l16,
    back_out, sums_out, dq16_out, reduced,
    do_dense, msg, part16, theirs, summed, do_ref, key_t, key16_t, delta, dq_t,
    send1, recv1, local1, send2, recv2, local2, swap_send, swap_recv, psend, precv, plocal, *scratch,
):
    me, group = Place(), Group()
    rank = group.rank
    wraps = (group.row < 2) | (group.row >= 30)
    reduction = Reduction(me, gradients, EARLY_WIDTHS, scratch, reduced)
    greet([group.device(lax.rem(rank + d, 16)) for d in range(1, 16)] + me.neighbours())
    first = group.all_to_all(dmsg, do_dense, send1, recv1, local1)
    reduction.load_all()
    reduction.begin_chunk(0)

    @pl.loop(0, 4)
    def _(b):
        rows = pl.ds(pl.multiple_of(b * KEYS, KEYS), KEYS)
        key_t[:, rows] = transposed(key[rows, :]).astype(BF16)
        key16_t[:, rows] = transposed(kv16[rows, :])[0:64].astype(BF16)
        dq_t[:, rows] = jnp.zeros((64, KEYS), F32)

    group.finish(*first)
    for u in (1, 2, 3):
        reduction.begin_chunk(u)

    @pl.loop(0, 16)
    def _(b):
        spread(do_dense[b], do_ref, pl.multiple_of(b * 128, 128))

    @pl.loop(0, 4)
    def _(b):
        rows = pl.ds(pl.multiple_of(b * KEYS, KEYS), KEYS)
        product = do_ref[rows, :].astype(F32) * o_ref[rows, :].astype(F32)
        delta[:, rows] = jnp.sum(product.T, axis=0, keepdims=True)

    def put(section, j, result):
        for n in range(4):
            for half in range(2):
                msg[4 * j + n, 64 * section : 64 * section + 64, 64 * half : 64 * half + 64] = result[
                    128 * n + 64 * half : 128 * n + 64 * half + 64
                ]

    def pair(keys, values, q, d_out, log_total, delta_row, mask):
        scores = dot_nt(keys, q)
        probs = jnp.exp(scores - log_total)
        if mask is not None:
            probs = jnp.where(mask(scores.shape), probs, 0.0)
        probs = probs.astype(BF16)
        d_prob = dot_nt(values, d_out)
        d_scores = (probs.astype(F32) * (d_prob - delta_row)).astype(BF16)
        return dot_nn(d_scores, q), dot_nn(probs, d_out), d_scores

    def key_block(j):
        rows = pl.ds(pl.multiple_of(j * KEYS, KEYS), KEYS)
        keys, values = key[rows, :], value[rows, :]

        def step(i, carry, mask=None):
            d_key, d_value = carry
            at = pl.ds(pl.multiple_of(i * KEYS, KEYS), KEYS)
            more_key, more_value, d_scores = pair(
                keys, values, query[at, :], do_ref[at, :], l_ref[:, at], delta[:, at], mask
            )
            dq_t[:, at] += dot_nn(key_t[:, rows], d_scores)
            return d_key + more_key, d_value + more_value

        zero = jnp.zeros((KEYS, 64), F32)
        carry = step(j, (zero, zero), lambda shape: allowed_pairs(shape, 0, 0))
        end = jnp.where(wraps & (j < 2), 2, 4)
        d_key, d_value = lax.fori_loop(j + 1, end, step, carry)
        put(1, j, d_key.astype(BF16))
        put(2, j, d_value.astype(BF16))

    q = q16[...] * jnp.asarray(0.125, BF16)
    d_out16 = do16[...]
    delta16 = jnp.sum((d_out16.astype(F32) * o16[...].astype(F32)).T, axis=0, keepdims=True)
    start = jnp.where(wraps & (rank >= 8), 2, 0)

    def last_step(j, dq):
        rows = pl.ds(pl.multiple_of(j * KEYS, KEYS), KEYS)
        d_key, d_value, d_scores = pair(
            kv16[rows, 0:64], kv16[rows, 64:128], q, d_out16, l16[...], delta16,
            lambda shape: allowed_pairs(shape, j * KEYS, rank * QUARTER),
        )
        for n in range(4):
            block = part16.at[2 * j + n // 2, n % 2]
            block[:, 0:64] = d_key[128 * n : 128 * n + 128].astype(BF16)
            block[:, 64:128] = d_value[128 * n : 128 * n + 128].astype(BF16)
        return dq + dot_nn(key16_t[:, rows], d_scores)

    part16[...] = jnp.zeros_like(part16)
    dq = lax.fori_loop(start, rank // 4 + 1, last_step, jnp.zeros((64, QUARTER), F32))
    dq16_out[...] = (dq * 0.125).T.astype(BF16)
    swap = remote(part16.at[:, 1 - group.core], theirs, swap_send, swap_recv, group.partner)
    swap.start()

    @pl.loop(0, 2)
    def _(j):
        key_block(j)

    reduction.middle_chunk(0)

    @pl.loop(2, 4)
    def _(j):
        key_block(j)

    @pl.loop(0, 4)
    def _(j):
        rows = pl.ds(pl.multiple_of(j * KEYS, KEYS), KEYS)
        put(0, j, (dq_t[:, rows] * 0.125).T.astype(BF16))

    second = group.all_to_all(msg, back_out, send2, recv2, local2)
    swap.wait_recv()

    @pl.loop(0, 8)
    def _(p):
        summed[p] = (part16[p, group.core].astype(F32) + theirs[p].astype(F32)).astype(BF16)

    own = pltpu.make_async_copy(summed.at[group.pair], sums_out.at[group.pair], plocal)
    own.start()
    sent = [swap]
    for e in range(1, 8):
        other = lax.rem(group.pair + e, 8)
        copy = remote(
            summed.at[other], sums_out.at[group.pair], psend.at[e], precv.at[e], group.device(other * 2 + group.core)
        )
        copy.start()
        sent.append(copy)
    for u in range(1, 4):
        reduction.middle_chunk(u)
        reduction.finish_chunk(u - 1)
    reduction.finish_chunk(3)
    reduction.finish_all()
    for e in range(1, 8):
        origin = lax.rem(group.pair + 8 - e, 8)
        block = sums_out.at[origin]
        remote(block, block, psend.at[e], precv.at[e], group.device(origin * 2 + group.core)).wait_recv()
    group.finish(*second)
    for copy in sent:
        copy.wait_send()
    own.wait()
    reduction.wait_sent()


def attend_back_call(*args):
    block = pltpu.VMEM((8, QUARTER, 128), BF16)
    eight = pltpu.SemaphoreType.DMA((8,))
    one = pltpu.SemaphoreType.DMA
    return pl.pallas_call(
        attend_back_kernel,
        out_shape=(
            jax.ShapeDtypeStruct((16, 192, 128), BF16), jax.ShapeDtypeStruct((8, QUARTER, 128), BF16),
            jax.ShapeDtypeStruct((QUARTER, 64), BF16), jax.ShapeDtypeStruct((32, 2 * PACK), F32),
        ),
        in_specs=[ANY, ANY] + [VMEM_SPEC] * 10,
        out_specs=(ANY, ANY, VMEM_SPEC, VMEM_SPEC),
        scratch_shapes=[
            pltpu.VMEM((16, 64, 128), BF16), pltpu.VMEM((16, 192, 128), BF16), pltpu.VMEM((8, 2, QUARTER, 128), BF16),
            block, block,
            pltpu.VMEM((SEQ, 64), BF16), pltpu.VMEM((64, SEQ), BF16), pltpu.VMEM((64, SEQ), BF16),
            pltpu.VMEM((1, SEQ), F32), pltpu.VMEM((64, SEQ), F32),
        ] + DIRECT + DIRECT + [one, one, eight, eight, one] + Reduction.scratch(EARLY_WIDTHS),
        compiler_params=pltpu.CompilerParams(
            collective_id=7, has_side_effects=True, vmem_limit_bytes=VMEM_LIMIT
        ),
        name="attend_backward",
    )(*args)


def packed_block(block):
    tail = jnp.pad(block[32:34], ((0, 0), (0, WIDE - D))).reshape(18, 128)
    return jnp.concatenate(
        [jnp.pad(block[:32], ((0, 0), (0, WIDE - D))), jnp.pad(tail, ((0, 14), (0, 0)))], axis=1
    )


def unpacked_block(packed):
    tail = packed[:18, WIDE:].reshape(2, WIDE)[:, :D]
    return jnp.concatenate([packed[:, :D], tail], axis=0)


def permutation():
    feature = jnp.arange(D, dtype=jnp.int32)
    block, inside = feature // 34, feature % 34
    place = jnp.where(inside < 32, 32 * block + inside, MAIN + 32 * (inside - 32) + block)
    chosen = place[:, None] == jnp.arange(WIDE, dtype=jnp.int32)[None, :]
    return chosen.astype(BF16).reshape(4, 272, WIDE)


def per_device(
    layer_input,
    first_norm_gain,
    first_norm_bias,
    w_qkv,
    w_out,
    second_norm_gain,
    second_norm_bias,
    w_up,
    w_down,
    gradient_of_output,
):
    row, col = lax.axis_index("row"), lax.axis_index("col")
    rank, core = (row + 2) % 4 * 4 + col, col % 2
    wraps = ((row < 2) | (row >= 30)).astype(jnp.int32)
    info = jnp.stack([rank, wraps]).astype(jnp.int32)
    perm = permutation()
    vectors = jnp.concatenate(
        [
            jnp.stack([first_norm_gain, first_norm_bias, second_norm_gain, second_norm_bias]),
            jnp.zeros((4, 272), F32),
        ]
    )
    blocks = (
        packed_block(jnp.concatenate([w_qkv, w_out.T], axis=1)),
        packed_block(w_up),
        packed_block(w_down.T),
    )
    w0, w1, w2, x4, g4, v4 = gather_all(blocks, layer_input.T, gradient_of_output.T, vectors)
    w0, w1, w2 = (w.reshape(2, MAIN, PACK) for w in (w0, w1, w2))
    x, n1, vec, message, last, q16 = qkv_call(x4, v4, perm, w0)
    heads, kv16 = qkv_exchange(message, last)
    kv16 = kv16.reshape(SEQ, 128)
    dense, o, o16, log_total, log16, query, key, value = attend_call(info, heads, kv16, q16)
    mixed, both16 = mixed_exchange(dense, o16)
    attn = jnp.concatenate(
        [
            mixed.reshape(16, QUARTER, 2, HEAD_DIM).transpose(2, 1, 0, 3).reshape(PAIR, 1024),
            both16.reshape(PAIR, HEAD_DIM),
        ],
        axis=1,
    ).reshape(PAIR, 2, 2, 272)
    attn = lax.dynamic_index_in_dim(attn, core, 2, keepdims=False)
    a0 = jnp.pad(attn.transpose(1, 0, 2), ((0, 0), (0, 0), (QKV_COLS, WIDE - D)))
    y4, dres, dresb, gr12, dmsg, do16, vec2 = middle_call(x, a0, w0, w1, w2, g4, perm, vec)
    back, sums16, dq16, early = attend_back_call(
        dmsg, gr12.reshape(2, 2, 4, 4, 32, 2 * PACK), query, key, value, kv16, q16, o, o16, do16, log_total, log16
    )
    last_sums = jnp.sum(sums16.astype(F32), axis=0).astype(BF16)
    back = back.reshape(16, 3, 64, 2, HEAD_DIM).transpose(1, 3, 2, 0, 4).reshape(3, QUARTER, 1024)
    d_qkv = jnp.concatenate(
        [back[0], dq16, back[1], last_sums[:, :64], back[2], last_sums[:, 64:]], axis=1
    )
    dq0 = jnp.pad(
        d_qkv.reshape(QUARTER, 2, 2, QKV_COLS).transpose(2, 1, 0, 3), ((0, 0), (0, 0), (0, 0), (0, WIDE - QKV_COLS))
    )
    gin4, gr0, sums4 = first_call(x, n1, dresb, dres, dq0, a0, w0, perm, vec, vec2)
    late, layer_output, gin, sums4 = scatter_all(gr0.reshape(2, 2, 4, 4, 32, PACK), y4, gin4, sums4)
    own_perm = lax.dynamic_index_in_dim(perm, col, 0, keepdims=False).astype(F32)
    vg = lax.dot_general(
        sums4, own_perm, (((1,), (1,)), ((), ())),
        preferred_element_type=F32, precision=lax.Precision.HIGHEST,
    )
    s0, s1, s2 = (unpacked_block(part) for part in (late, early[:, :PACK], early[:, PACK:]))
    return (
        layer_output.T,
        gin.T.astype(F32),
        vg[4],
        vg[5],
        s0[:, :QKV_COLS],
        s0[:, QKV_COLS:].T,
        vg[0],
        vg[1],
        s1,
        s2.T,
    )


def solution(mesh):
    placed = (
        P("row", "col"),
        P("col"),
        P("col"),
        P("row", "col"),
        P("col", "row"),
        P("col"),
        P("col"),
        P("row", "col"),
        P("col", "row"),
        P("row", "col"),
    )
    return jax.shard_map(
        per_device,
        mesh=mesh,
        in_specs=placed,
        out_specs=(
            P("row", "col"),
            P("row", "col"),
            P("col"),
            P("col"),
            P("row", "col"),
            P("col", "row"),
            P("col"),
            P("col"),
            P("row", "col"),
            P("col", "row"),
        ),
        check_vma=False,
    )
```

```python
import math

import jax
import jax.numpy as jnp
import ml_dtypes
import numpy as np
from jax import lax
from jax.experimental import pallas as pl
from jax.experimental.pallas import tpu as pltpu
from jax.sharding import PartitionSpec as P

HEADS = 17
HEAD_DIM = 64
D = 1088
SEQ = 2048
MAIN = 1024
WIDE = 1152
PACK = 1280
QKV_COLS = 816
QUARTER = 128
PAIR = 256
KEYS = 512

gelu_coef = math.sqrt(2.0 / math.pi)
norm_epsilon = 1e-05
masked_score = -1e30
MESH = pl.DeviceIdType.MESH
F32 = jnp.float32
BF16 = jnp.bfloat16
VMEM_LIMIT = 60 * 1024 * 1024
ANY = pl.BlockSpec(memory_space=pl.ANY)
VMEM_SPEC = pl.BlockSpec(memory_space=pltpu.VMEM)
SMEM_SPEC = pl.BlockSpec(memory_space=pltpu.SMEM)

GATHER_ORDERS = (("x", "y", "z"), ("y", "z", "x"), ("z", "x", "y"))
SCATTER_ORDERS = (("z", "y", "x"), ("x", "z", "y"), ("y", "x", "z"))


def dot_nn(a, b):
    return lax.dot_general(a, b, (((1,), (0,)), ((), ())), preferred_element_type=F32)


def dot_nt(a, b):
    return lax.dot_general(a, b, (((1,), (1,)), ((), ())), preferred_element_type=F32)


class Place:
    def __init__(self):
        self.row = lax.axis_index("row")
        self.col = lax.axis_index("col")
        self.at = {
            "x": lax.rem(self.row, 4),
            "z": lax.rem(self.row // 4, 4),
            "y": (self.row // 16) * 2 + self.col // 2,
        }
        self.core = lax.rem(self.col, 2)

    def device(self, at, core):
        return ((at["y"] // 2) * 16 + at["z"] * 4 + at["x"], lax.rem(at["y"], 2) * 2 + core)

    def step(self, axis, distance):
        at = dict(self.at)
        at[axis] = lax.rem(at[axis] + distance + 4, 4)
        return self.device(at, self.core)

    def partner(self):
        return (self.row, self.col + 1 - 2 * self.core)

    def beside(self, distance):
        return (self.row, lax.rem(self.col + distance, 4))

    def neighbours(self):
        found = [self.step(axis, d) for axis in ("x", "y", "z") for d in (1, -1)]
        found.append(self.partner())
        other = lax.rem(self.col // 2 + 1, 2)
        found.append((self.row, other * 2 + 1 - self.core))
        return found


def greet(devices):
    barrier = pltpu.get_barrier_semaphore()
    for device in devices:
        pl.semaphore_signal(barrier, inc=1, device_id=device, device_id_type=MESH)
    pl.semaphore_wait(barrier, len(devices))


def everything():
    return slice(None)


def place_index(fixed):
    if "y" in fixed:
        y_lo, y_hi = lax.rem(fixed["y"], 2), fixed["y"] // 2
    else:
        y_lo, y_hi = everything(), everything()
    return (y_lo, y_hi, fixed.get("z", everything()), fixed.get("x", everything()))


def remote(source, target, ssem, rsem, device):
    return pltpu.make_async_remote_copy(
        src_ref=source, dst_ref=target, send_sem=ssem, recv_sem=rsem,
        device_id=device, device_id_type=MESH,
    )


def gather_kernel(
    w_qkv, w_out_t, w_up, w_down_t, gain1, bias1, gain2, bias2, x_ref, g_ref,
    all0, all1, all2, x_out, g_out, v_out,
    block0, block1, block2, v_ref, full, tile,
    send, recv, last_send, last_recv, local, in_send, in_recv, in_local,
):
    me = Place()
    blocks = (block0, block1, block2)
    wholes = (all0, all1, all2)
    full[...] = jnp.zeros_like(full)
    tile[...] = jnp.zeros_like(tile)
    for piece, sources in enumerate(((w_qkv, w_out_t), (w_up,), (w_down_t,))):
        lane = 0
        for source in sources:
            full[0:34, lane : lane + source.shape[1]] = source[...].astype(F32)
            lane += source.shape[1]
        blocks[piece][:, :WIDE] = full[0:32, :].astype(BF16)
        for j in range(2):
            for n in range(9):
                tile[9 * j + n : 9 * j + n + 1, :] = full[32 + j : 33 + j, 128 * n : 128 * n + 128]
        blocks[piece][:, WIDE:] = tile[...].astype(BF16)
    v_ref[...] = jnp.zeros_like(v_ref)
    for n, source in enumerate((gain1, bias1, gain2, bias2)):
        v_ref[n : n + 1, :] = source[...]
    greet(me.neighbours())

    def region(piece, fixed, rows=None):
        index = place_index(fixed) + ((everything(),) if rows is None else (pl.ds(rows, 16),))
        return wholes[piece].at[index]

    def around(piece, stage, value):
        order = GATHER_ORDERS[piece]
        fixed = {order[stage]: value}
        for axis in order[stage + 1 :]:
            fixed[axis] = me.at[axis]
        return fixed

    sent = []
    pairs = ((x_ref, x_out), (g_ref, g_out))
    waits, arrivals, own_copies = [], [], []
    for piece in range(3):
        copy = pltpu.make_async_copy(
            blocks[piece], region(piece, around(piece, 0, me.at[GATHER_ORDERS[piece][0]])), local.at[piece]
        )
        copy.start()
        own_copies.append(copy)

    def semaphores(piece, stage, n, u):
        if stage == 2:
            return last_send.at[piece, u, n], last_recv.at[piece, u, n]
        return send.at[piece, stage, n], recv.at[piece, stage, n]

    def part(piece, stage, value, u, rows=None):
        fixed = around(piece, stage, value)
        if stage == 2:
            axis = GATHER_ORDERS[piece][1]
            fixed[axis] = lax.rem(me.at[axis] + (0, 3, 1, 2)[u], 4)
        return region(piece, fixed, rows)

    def begin(piece, stage, u=0):
        axis = GATHER_ORDERS[piece][stage]
        mine = part(piece, stage, me.at[axis], u)
        source = blocks[piece] if stage == 0 else mine
        for n, distance in enumerate((1, -1)):
            copy = remote(source, mine, *semaphores(piece, stage, n, u), me.step(axis, distance))
            copy.start()
            sent.append(copy)

    def arrived(piece, stage, n, u=0):
        axis = GATHER_ORDERS[piece][stage]
        value = lax.rem(me.at[axis] + (3, 1, 2, 2)[n], 4)
        there = part(piece, stage, value, u, (None, None, 0, 16)[n])
        remote(there, there, *semaphores(piece, stage, n, u), me.step(axis, 1)).wait_recv()
        if n < 2:
            half = part(piece, stage, value, u, (0, 16)[n])
            copy = remote(half, half, *semaphores(piece, stage, 2 + n, u), me.step(axis, (1, -1)[n]))
            copy.start()
            sent.append(copy)

    for piece in range(3):
        begin(piece, 0)
    partner, across = me.partner(), me.beside(2)

    def tokens_of(ref, col):
        return ref.at[:, pl.ds(pl.multiple_of(col // 2 * PAIR, PAIR), PAIR)]

    relays = []
    for n, (source, target) in enumerate(pairs + ((v_ref, v_out),)):
        here, there = (v_ref, v_ref) if n == 2 else (tokens_of(source, me.col), tokens_of(source, across[1]))
        own = pltpu.make_async_copy(here, target.at[me.col], in_local.at[n])
        own.start()
        waits.append(own)
        for k, (part_ref, device) in enumerate(((there, across), (here, partner))):
            copy = remote(part_ref, target.at[me.col], in_send.at[n, k], in_recv.at[n, k], device)
            copy.start()
            sent.append(copy)
        relays.append(remote(there, target.at[across[1]], in_send.at[n, 0], in_recv.at[n, 0], across))
        arrivals.append(remote(here, target.at[partner[1]], in_send.at[n, 1], in_recv.at[n, 1], partner))
    for copy in own_copies:
        copy.wait()
    for n in range(4):
        for piece in range(3):
            arrived(piece, 0, n)
    for piece in range(3):
        begin(piece, 1)
    for n, (_, target) in enumerate(pairs + ((v_ref, v_out),)):
        relays[n].wait_recv()
        block = target.at[across[1]]
        copy = remote(block, block, in_send.at[n, 2], in_recv.at[n, 2], partner)
        copy.start()
        sent.append(copy)
        far = target.at[lax.rem(partner[1] + 2, 4)]
        arrivals.append(remote(far, far, in_send.at[n, 2], in_recv.at[n, 2], partner))
    for piece in range(3):
        begin(piece, 2, 0)
    for n in range(4):
        for piece in range(3):
            arrived(piece, 1, n)
            if n < 2:
                begin(piece, 2, n + 1)
            elif n == 3:
                begin(piece, 2, 3)
    for n in (0, 1):
        for piece in range(3):
            arrived(piece, 2, n, 0)
    for u in range(1, 4):
        for n in (0, 1):
            for piece in range(3):
                arrived(piece, 2, n, u)
    for u in range(4):
        for n in (2, 3):
            for piece in range(3):
                arrived(piece, 2, n, u)
    for copy in arrivals:
        copy.wait_recv()
    for copy in waits:
        copy.wait()
    for copy in sent:
        copy.wait_send()


def gather_all(*args):
    whole = jax.ShapeDtypeStruct((2, 2, 4, 4, 32, PACK), BF16)
    tokens = jax.ShapeDtypeStruct((4, 272, PAIR), BF16)
    return pl.pallas_call(
        gather_kernel,
        out_shape=(whole, whole, whole, tokens, tokens, jax.ShapeDtypeStruct((4, 8, 272), F32)),
        in_specs=[VMEM_SPEC] * 8 + [ANY] * 2,
        out_specs=(ANY,) * 6,
        scratch_shapes=[
            pltpu.VMEM((32, PACK), BF16), pltpu.VMEM((32, PACK), BF16), pltpu.VMEM((32, PACK), BF16),
            pltpu.VMEM((8, 272), F32), pltpu.VMEM((40, WIDE), F32), pltpu.VMEM((32, 128), F32),
            pltpu.SemaphoreType.DMA((3, 2, 4)),
            pltpu.SemaphoreType.DMA((3, 2, 4)),
            pltpu.SemaphoreType.DMA((3, 4, 4)),
            pltpu.SemaphoreType.DMA((3, 4, 4)),
            pltpu.SemaphoreType.DMA((3,)),
            pltpu.SemaphoreType.DMA((3, 3)),
            pltpu.SemaphoreType.DMA((3, 3)),
            pltpu.SemaphoreType.DMA((3,)),
        ],
        compiler_params=pltpu.CompilerParams(collective_id=0, has_side_effects=True),
        name="gather_weights",
    )(*args)


class Group:
    def __init__(self):
        self.row, self.col = lax.axis_index("row"), lax.axis_index("col")
        self.in_group = lax.rem(self.row + 2, 4)
        self.rank = self.in_group * 4 + self.col
        self.pair, self.core = self.rank // 2, lax.rem(self.col, 2)
        self.partner = (self.row, self.col + 1 - 2 * self.core)

    def device(self, other):
        return (lax.rem(self.row - self.in_group + other // 4 + 32, 32), lax.rem(other, 4))

    def greet(self):
        greet([self.device(lax.rem(self.rank + d, 16)) for d in range(1, 16)])

    def all_to_all(self, source, target, send, recv, local):
        own = pltpu.make_async_copy(source.at[self.rank], target.at[self.rank], local)
        own.start()
        sent, arrivals = [], []
        for d in range(1, 16):
            other = lax.rem(self.rank + d, 16)
            copy = remote(source.at[other], target.at[self.rank], send.at[d], recv.at[d], self.device(other))
            copy.start()
            sent.append(copy)
            origin = lax.rem(self.rank + 16 - d, 16)
            arrivals.append(remote(source.at[other], target.at[origin], send.at[d], recv.at[d], self.device(origin)))
        return own, sent, arrivals

    def finish(self, own, sent, arrivals):
        for copy in arrivals:
            copy.wait_recv()
        for copy in sent:
            copy.wait_send()
        own.wait()

    def relay(self, source_of, target, send, recv, local):
        own = pltpu.make_async_copy(source_of(self.pair), target.at[self.rank], local)
        own.start()
        beside = remote(source_of(self.pair), target.at[self.rank], send.at[0, 0], recv.at[0, 0], self.partner)
        beside.start()
        sent = [beside]
        for e in range(1, 8):
            other = lax.rem(self.pair + e, 8)
            copy = remote(
                source_of(other), target.at[self.rank], send.at[0, e], recv.at[0, e], self.device(other * 2 + self.core)
            )
            copy.start()
            sent.append(copy)
        return own, sent

    def pass_on(self, own, sent, target, send, recv):
        for e in range(1, 8):
            origin = lax.rem(self.pair + 8 - e, 8) * 2 + self.core
            block = target.at[origin]
            remote(block, block, send.at[0, e], recv.at[0, e], self.device(origin)).wait_recv()
            copy = remote(block, block, send.at[1, e], recv.at[1, e], self.partner)
            copy.start()
            sent.append(copy)
        for e in range(0, 8):
            block = target.at[lax.rem(self.pair + 8 - e, 8) * 2 + 1 - self.core]
            n = 0 if e == 0 else 1
            remote(block, block, send.at[n, e], recv.at[n, e], self.partner).wait_recv()
        for copy in sent:
            copy.wait_send()
        own.wait()


RELAY = [pltpu.SemaphoreType.DMA((2, 8)), pltpu.SemaphoreType.DMA((2, 8)), pltpu.SemaphoreType.DMA]
DIRECT = [pltpu.SemaphoreType.DMA((16,)), pltpu.SemaphoreType.DMA((16,)), pltpu.SemaphoreType.DMA]


def exchange_call(kernel, name, collective_id, outs, scratch, *args, in_specs=None):
    return pl.pallas_call(
        kernel,
        out_shape=outs,
        in_specs=in_specs or [ANY] * len(args),
        out_specs=(ANY,) * len(outs),
        scratch_shapes=scratch,
        compiler_params=pltpu.CompilerParams(collective_id=collective_id, has_side_effects=True),
        name=name,
    )(*args)


def qkv_exchange_kernel(source, last, target, last_out, send, recv, local, rsend, rrecv, rlocal):
    group = Group()
    group.greet()
    relayed = group.relay(lambda p: last, last_out, rsend, rrecv, rlocal)
    direct = group.all_to_all(source, target, send, recv, local)
    group.pass_on(*relayed, last_out, rsend, rrecv)
    group.finish(*direct)


def qkv_exchange(source, last):
    outs = (jax.ShapeDtypeStruct((16, 192, 128), BF16), jax.ShapeDtypeStruct((16, QUARTER, 128), BF16))
    return exchange_call(qkv_exchange_kernel, "exchange_qkv", 1, outs, DIRECT + RELAY, source, last)


def mixed_exchange_kernel(source, last, target, last_out, send, recv, local, last_send, last_recv, last_local):
    group = Group()
    group.greet()
    relayed = group.relay(lambda p: source.at[p], target, send, recv, local)
    own = pltpu.make_async_copy(last, last_out.at[group.core], last_local)
    own.start()
    copy = remote(last, last_out.at[group.core], last_send, last_recv, group.partner)
    copy.start()
    group.pass_on(*relayed, target, send, recv)
    remote(last, last_out.at[1 - group.core], last_send, last_recv, group.partner).wait_recv()
    copy.wait_send()
    own.wait()


def mixed_exchange(source, last):
    outs = (jax.ShapeDtypeStruct((16, 128, 128), BF16), jax.ShapeDtypeStruct((2, QUARTER, 64), BF16))
    return exchange_call(
        mixed_exchange_kernel, "exchange_mixed", 2, outs, RELAY + [pltpu.SemaphoreType.DMA] * 3, source, last
    )


def free_axes(fixed):
    return [axis for axis in ("y", "z", "x") if axis not in fixed]


def buffer_shape(fixed, rows, width):
    shape = ()
    for axis in free_axes(fixed):
        shape = shape + ((2, 2) if axis == "y" else (4,))
    return shape + (rows, width)


def buffer_index(at):
    index = ()
    for axis in ("y", "z", "x"):
        if axis in at:
            index = index + ((lax.rem(at[axis], 2), at[axis] // 2) if axis == "y" else (at[axis],))
    return index


VECTOR_AXES = ("z", "x", "y")
CHUNKS = (2, 1, 3, 0)


class Reduction:
    def __init__(self, me, source, widths, scratch, out):
        self.me, self.source, self.widths, self.out = me, source, widths, out
        self.offsets = (0, widths[0], widths[0] + widths[1])
        self.sums = scratch[0:3]
        self.halves, self.fulls = {}, {}
        position = 3
        for piece in range(3):
            for stage in range(3):
                self.halves[piece, stage] = scratch[position : position + 2]
                self.fulls[piece, stage] = scratch[position + 2 : position + 4]
                position += 4
        self.local, self.big_send, self.big_recv, self.send, self.recv = scratch[position : position + 5]
        self.sent, self.loads = [], {}

    @staticmethod
    def scratch(widths):
        found = [pltpu.VMEM((2, 2, 4, 4, 32, width), BF16) for width in widths]
        for piece in range(3):
            order = SCATTER_ORDERS[piece]
            for stage in range(3):
                fixed = order[: stage + 1]
                found += [pltpu.VMEM(buffer_shape(fixed, 16, widths[piece]), BF16) for _ in range(2)]
                found += [pltpu.VMEM(buffer_shape(fixed, 32, widths[piece]), BF16) for _ in range(2)]
        found += [pltpu.SemaphoreType.DMA((3, 4, 4))] * 3 + [pltpu.SemaphoreType.DMA((3, 2, 4))] * 2
        return found

    def shifted(self, axis, distance):
        return lax.rem(self.me.at[axis] + distance, 4)

    def load_all(self):
        for k in range(4):
            for u in range(4):
                for piece in range(3):
                    first, second = SCATTER_ORDERS[piece][:2]
                    index = place_index(
                        {first: self.shifted(first, CHUNKS[k]), second: self.shifted(second, CHUNKS[u])}
                    )
                    lanes = pl.ds(self.offsets[piece], self.widths[piece])
                    load = pltpu.make_async_copy(
                        self.source.at[index + (everything(), lanes)], self.sums[piece].at[index],
                        self.local.at[piece, k, u],
                    )
                    load.start()
                    self.loads[piece, k, u] = load

    def stage_fixed(self, piece, stage):
        return {axis: self.me.at[axis] for axis in SCATTER_ORDERS[piece][:stage]}

    def each_tile(self, fixed, body):
        axes = free_axes(fixed)
        count = 4 ** len(axes)
        if count == 1:
            body({})
            return

        @pl.loop(0, count)
        def _(t):
            body({axes[0]: t})

    def chunk(self, piece, stage, u):
        if stage > 0:
            return {}
        axis = SCATTER_ORDERS[piece][1]
        return {axis: self.shifted(axis, CHUNKS[u])}

    def sems(self, piece, stage, n, u):
        if stage == 0:
            return self.big_send.at[piece, u, n], self.big_recv.at[piece, u, n]
        return self.send.at[piece, stage - 1, n], self.recv.at[piece, stage - 1, n]

    def part_of(self, buffer, piece, stage, u):
        if stage > 0:
            return buffer
        axis = SCATTER_ORDERS[piece][1]
        value = self.shifted(axis, CHUNKS[u])
        index = ()
        for name in free_axes({SCATTER_ORDERS[piece][0]: 0}):
            if name == "y":
                index += (lax.rem(value, 2), value // 2) if name == axis else (everything(), everything())
            else:
                index += (value,) if name == axis else (everything(),)
        return buffer.at[index]

    def start(self, source, target, semaphores, axis, n):
        copy = remote(source, target, *semaphores, self.me.step(axis, (1, -1)[n]))
        copy.start()
        self.sent.append(copy)

    def wait(self, there, semaphores, axis):
        remote(there, there, *semaphores, self.me.step(axis, 1)).wait_recv()

    def begin(self, piece, stage, u=0):
        if stage == 0:
            self.loads[piece, 0, u].wait()
        axis = SCATTER_ORDERS[piece][stage]
        fixed = {**self.stage_fixed(piece, stage), axis: self.shifted(axis, 2), **self.chunk(piece, stage, u)}
        for n in range(2):
            self.start(
                self.sums[piece].at[place_index(fixed) + (pl.ds(16 * n, 16),)],
                self.part_of(self.halves[piece, stage][n], piece, stage, u), self.sems(piece, stage, n, u), axis, n,
            )

    def middle(self, piece, stage, n, u=0):
        if stage == 0:
            self.loads[piece, 1 + n, u].wait()
        axis = SCATTER_ORDERS[piece][stage]
        more = self.chunk(piece, stage, u)
        fixed = {**self.stage_fixed(piece, stage), axis: self.shifted(axis, (1, 3)[n]), **more}
        half, sums = self.halves[piece, stage][n], self.sums[piece]
        self.wait(self.part_of(half, piece, stage, u), self.sems(piece, stage, n, u), axis)

        def body(at):
            index = place_index({**fixed, **at}) + (pl.ds(16 * n, 16),)
            total = sums[index].astype(F32) + half[buffer_index({**more, **at})].astype(F32)
            sums[index] = total.astype(BF16)

        self.each_tile(fixed, body)
        self.start(
            sums.at[place_index(fixed)], self.part_of(self.fulls[piece, stage][n], piece, stage, u),
            self.sems(piece, stage, 2 + n, u), axis, n,
        )

    def finish(self, piece, stage, u=0):
        if stage == 0:
            self.loads[piece, 3, u].wait()
        axis = SCATTER_ORDERS[piece][stage]
        more = self.chunk(piece, stage, u)
        fixed = {**self.stage_fixed(piece, stage), axis: self.me.at[axis], **more}
        first, second = self.fulls[piece, stage]
        sums = self.sums[piece]
        for n, buffer in enumerate((first, second)):
            self.wait(self.part_of(buffer, piece, stage, u), self.sems(piece, stage, 2 + n, u), axis)

        def body(at):
            index = place_index({**fixed, **at})
            if stage == 2:
                total = sums[index].astype(F32) + (first[...].astype(F32) + second[...].astype(F32))
                self.out[:, self.offsets[piece] : self.offsets[piece] + self.widths[piece]] = total
            else:
                place = buffer_index({**more, **at})
                total = sums[index].astype(F32) + (first[place].astype(F32) + second[place].astype(F32))
                sums[index] = total.astype(BF16)

        self.each_tile(fixed, body)

    def begin_chunk(self, u):
        for piece in range(3):
            self.begin(piece, 0, u)

    def middle_chunk(self, u):
        for n in range(2):
            for piece in range(3):
                self.middle(piece, 0, n, u)

    def finish_chunk(self, u):
        for piece in range(3):
            self.finish(piece, 0, u)
            if u == 0:
                self.begin(piece, 1)
            elif u < 3:
                self.middle(piece, 1, u - 1)
            else:
                self.finish(piece, 1)
                self.begin(piece, 2)

    def finish_all(self):
        for n in range(2):
            for piece in range(3):
                self.middle(piece, 2, n)
        for piece in range(3):
            self.finish(piece, 2)

    def wait_sent(self):
        for copy in self.sent:
            copy.wait_send()


def unpack_rows(packed, first, target):
    target[0:32, :] = packed[:, first : first + target.shape[1]]
    for j in range(2):
        for n in range(9):
            width = min(128, target.shape[1] - 128 * n)
            target[32 + j : 33 + j, 128 * n : 128 * n + width] = packed[
                9 * j + n : 9 * j + n + 1, first + WIDE : first + WIDE + width
            ]


LATE_WIDTHS = (512, 512, 256)
EARLY_WIDTHS = (1024, 512, 1024)


def scatter_kernel(source, y_ref, gin_ref, v_ref, qkv_out, out_out, y_out, gin_out, v_out, out_ref, full, *scratch):
    me = Place()
    vectors = scratch[0:3]
    out_send, out_recv, out_local, v_send, v_recv = scratch[3:8]
    reduction = Reduction(me, source, LATE_WIDTHS, scratch[8:], out_ref)
    greet(me.neighbours() + [me.step(axis, 2) for axis in VECTOR_AXES])
    sent = []
    reduction.load_all()

    def vectors_begin(phase, value):
        axis = VECTOR_AXES[phase]
        mine = vectors[phase].at[me.at[axis]]
        mine[...] = value
        for distance in (1, 2, 3):
            copy = remote(
                mine, mine, v_send.at[phase, distance - 1], v_recv.at[phase, distance - 1], me.step(axis, distance)
            )
            copy.start()
            sent.append(copy)

    def vectors_end(phase):
        axis = VECTOR_AXES[phase]
        for distance in (1, 2, 3):
            there = vectors[phase].at[lax.rem(me.at[axis] + 4 - distance, 4)]
            remote(
                there, there, v_send.at[phase, distance - 1], v_recv.at[phase, distance - 1], me.step(axis, distance)
            ).wait_recv()
        buffer = vectors[phase]
        return (buffer[0] + buffer[1]) + (buffer[2] + buffer[3])

    reduction.begin_chunk(0)
    vectors_begin(0, v_ref[...])
    reduction.begin_chunk(1)
    pairs = ((y_ref, y_out), (gin_ref, gin_out))
    arrivals, own_copies = [], []
    for n, (source, target) in enumerate(pairs):
        rows = pl.ds(pl.multiple_of(me.col * QUARTER, QUARTER), QUARTER)
        own = pltpu.make_async_copy(source.at[me.col], target.at[:, rows], out_local.at[n])
        own.start()
        own_copies.append(own)
        for distance in (1, 2, 3):
            peer = me.beside(distance)
            semaphore = (out_send.at[n, distance - 1], out_recv.at[n, distance - 1])
            copy = remote(source.at[peer[1]], target.at[:, rows], *semaphore, peer)
            copy.start()
            sent.append(copy)
            origin = pl.ds(pl.multiple_of(lax.rem(me.col + 4 - distance, 4) * QUARTER, QUARTER), QUARTER)
            arrivals.append(remote(source.at[me.col], target.at[:, origin], *semaphore, peer))
    for u in range(4):
        reduction.middle_chunk(u)
        if u < 2:
            reduction.begin_chunk(u + 2)
            vectors_begin(u + 1, vectors_end(u))
        if u == 3:
            v_out[...] = vectors_end(2)
        if u > 0:
            reduction.finish_chunk(u - 1)
    reduction.finish_chunk(3)
    reduction.finish_all()
    unpack_rows(out_ref, 0, full)
    qkv_out[...] = full[0:34, 0:QKV_COLS]
    out_out[...] = full[0:34, QKV_COLS:D]
    for copy in arrivals:
        copy.wait_recv()
    for copy in own_copies:
        copy.wait()
    for copy in sent:
        copy.wait_send()
    reduction.wait_sent()


def scatter_all(part, y4, gin4, vectors):
    scratch = [pltpu.VMEM((32, PACK), F32), pltpu.VMEM((34, D), F32)]
    scratch += [pltpu.VMEM((4, 8, WIDE), F32) for _ in range(3)]
    scratch += [
        pltpu.SemaphoreType.DMA((2, 3)),
        pltpu.SemaphoreType.DMA((2, 3)),
        pltpu.SemaphoreType.DMA((2,)),
        pltpu.SemaphoreType.DMA((3, 3)),
        pltpu.SemaphoreType.DMA((3, 3)),
    ]
    back = jax.ShapeDtypeStruct((272, 512), BF16)
    return pl.pallas_call(
        scatter_kernel,
        out_shape=(
            jax.ShapeDtypeStruct((34, QKV_COLS), F32), jax.ShapeDtypeStruct((34, D - QKV_COLS), F32), back, back,
            jax.ShapeDtypeStruct((8, WIDE), F32),
        ),
        in_specs=[ANY] * 3 + [VMEM_SPEC],
        out_specs=(VMEM_SPEC, VMEM_SPEC, ANY, ANY, VMEM_SPEC),
        scratch_shapes=scratch + Reduction.scratch(LATE_WIDTHS),
        compiler_params=pltpu.CompilerParams(
            collective_id=3, has_side_effects=True, vmem_limit_bytes=VMEM_LIMIT
        ),
        name="scatter_gradients",
    )(part, y4, gin4, vectors)


def unpack_tail(packed, tiles, wide, tail):
    tiles[...] = packed[:, WIDE:PACK].astype(F32)
    for j in range(2):
        for s in range(9):
            wide[pl.ds(32 * j, 32), pl.ds(128 * s, 128)] = tiles[pl.ds(9 * j + s, 32, stride=32), :]
    tail[0:64, :] = wide[0:64, :].astype(BF16)


def pack_tail(tail, tiles, packed):
    for j in range(2):
        for s in range(9):
            tiles[pl.ds(9 * j + s, 32, stride=32), :] = tail[32 * j : 32 * j + 32, 128 * s : 128 * s + 128]
    packed[:, WIDE:PACK] = tiles[...].astype(BF16)


def in_features(values, packed, tail, columns):
    return dot_nn(values[:, :MAIN], packed[:, columns]) + dot_nn(values[:, MAIN:], tail[:, columns])


def add_to_features(total_t, values_t, packed, tail):
    @pl.loop(0, 4)
    def _(b):
        rows = pl.ds(pl.multiple_of(b * 256, 256), 256)
        total_t[rows, :] += dot_nn(packed[rows, :WIDE], values_t[...])

    total_t[MAIN:, :] += dot_nn(tail[...], values_t[...])


def norm_forward(x, gain, bias):
    mean = jnp.sum(x, axis=1, keepdims=True) / D
    square = jnp.sum(x * x, axis=1, keepdims=True) / D
    inverse = lax.rsqrt(square - mean * mean + norm_epsilon)
    normed = (x - mean) * inverse
    return normed, inverse, (normed * gain + bias).astype(BF16)


def norm_reverse(grad, normed, inverse, gain):
    scaled = grad * gain
    first = jnp.sum(scaled, axis=1, keepdims=True) / D
    second = jnp.sum(scaled * normed, axis=1, keepdims=True) / D
    return inverse * (scaled - first - normed * second)


def permuted(pieces, perm):
    total = dot_nn(pieces[0].astype(F32).T.astype(BF16), perm[0])
    for c in range(1, 4):
        total += dot_nn(pieces[c].astype(F32).T.astype(BF16), perm[c])
    return total


def permuted_exact(pieces, perm):
    total = jnp.zeros((8, WIDE), F32)
    for c in range(4):
        left = pieces[c]
        for _ in range(3):
            part = left.astype(BF16)
            left = left - part.astype(F32)
            total += dot_nn(part, perm[c])
    return total


def real_features(values):
    lane = lax.broadcasted_iota(jnp.int32, values.shape, 1)
    return jnp.where(lane < D, values, 0.0)


def turned(values):
    return values.astype(F32).T.astype(BF16)


def own_half(core):
    return pl.ds(pl.multiple_of(core * QUARTER, QUARTER), QUARTER)


def load_weights(source, target, semaphores):
    copies = []
    for j in range(2):
        copy = pltpu.make_async_copy(source.at[j], target.at[j], semaphores.at[j])
        copy.start()
        copies.append(copy)
    return copies


def qkv_kernel(
    x4, v4, perm, w_ref, x_out, n1_out, v_out, msg, last, q16, w, qkv, qkv_out, tiles, wide, tail, load, send, recv, local
):
    me = Place()
    partner = me.partner()
    copies = load_weights(w_ref, w, load)
    greet([partner])
    x = permuted(x4, perm)
    vectors = permuted_exact(v4, perm)
    v_out[...] = vectors
    x_out[...] = x.astype(BF16)
    _, _, normed = norm_forward(x, vectors[0:1], vectors[1:2])
    n1_out[...] = normed
    tail[...] = jnp.zeros_like(tail)
    mine, theirs = own_half(me.core), own_half(1 - me.core)
    sent, own_copies, arrivals = [], [], []
    for j in range(2):
        copies[j].wait()
        packed = w.at[j]
        unpack_tail(packed, tiles, wide, tail)

        @pl.loop(0, 3)
        def _(b):
            columns = pl.ds(pl.multiple_of(b * 384, 128), 384)
            qkv[j, :, columns] = in_features(n1_out[...], packed, tail, columns).astype(BF16)

        own = pltpu.make_async_copy(qkv.at[j, mine, :], qkv_out.at[j, me.core], local.at[j])
        own.start()
        own_copies.append(own)
        copy = remote(qkv.at[j, theirs, :], qkv_out.at[j, me.core], send.at[j], recv.at[j], partner)
        copy.start()
        sent.append(copy)
        arrivals.append(
            remote(qkv.at[j, theirs, :], qkv_out.at[j, 1 - me.core], send.at[j], recv.at[j], partner)
        )
    for copy in arrivals:
        copy.wait_recv()
    for copy in own_copies:
        copy.wait()
    for n in range(3):
        for head in range(HEADS):
            block = columns_of(qkv_out, n * D + head * HEAD_DIM, QKV_COLS, 0)
            if head == 16:
                if n == 0:
                    q16[...] = block
                else:
                    last[:, 64 * (n - 1) : 64 * n] = block
            else:
                msg[head, 64 * n : 64 * n + 64, 0:64] = block[0:64]
                msg[head, 64 * n : 64 * n + 64, 64:128] = block[64:128]
    for copy in sent:
        copy.wait_send()


def columns_of(blocks, start, width, offset):
    pieces = []
    position = start
    while position < start + HEAD_DIM:
        c = position // width
        end = min(start + HEAD_DIM, (c + 1) * width)
        first = position - c * width + offset
        pieces.append(blocks[c // 2, c % 2, :, first : first + end - position])
        position = end
    return pieces[0] if len(pieces) == 1 else jnp.concatenate(pieces, axis=1)


def qkv_call(x4, v4, perm, weights):
    row = jax.ShapeDtypeStruct((PAIR, WIDE), BF16)
    return pl.pallas_call(
        qkv_kernel,
        out_shape=(
            row, row, jax.ShapeDtypeStruct((8, WIDE), F32), jax.ShapeDtypeStruct((16, 192, 128), BF16),
            jax.ShapeDtypeStruct((QUARTER, 128), BF16), jax.ShapeDtypeStruct((QUARTER, 64), BF16),
        ),
        in_specs=[VMEM_SPEC, VMEM_SPEC, VMEM_SPEC, ANY],
        out_specs=(VMEM_SPEC,) * 6,
        scratch_shapes=[
            pltpu.VMEM((2, MAIN, PACK), BF16), pltpu.VMEM((2, PAIR, WIDE), BF16),
            pltpu.VMEM((2, 2, QUARTER, WIDE), BF16),
            pltpu.VMEM((MAIN, 128), F32), pltpu.VMEM((128, WIDE), F32), pltpu.VMEM((128, WIDE), BF16),
            pltpu.SemaphoreType.DMA((2,)), pltpu.SemaphoreType.DMA((2,)), pltpu.SemaphoreType.DMA((2,)),
            pltpu.SemaphoreType.DMA((2,)),
        ],
        compiler_params=pltpu.CompilerParams(
            collective_id=4, has_side_effects=True, vmem_limit_bytes=VMEM_LIMIT
        ),
        name="norm_and_qkv",
    )(x4, v4, perm, weights)


def gelu_both(v):
    square = v * v
    tanh_value = jnp.tanh(gelu_coef * (v + 0.044715 * v * square))
    half = 0.5 * (1.0 + tanh_value)
    value = v * half
    slope = half + 0.5 * v * (1.0 - tanh_value * tanh_value) * gelu_coef * (1.0 + 0.134145 * square)
    return value, slope


def weight_gradient(rows_t, values, tiles, tail_sum, packed):
    @pl.loop(0, 4)
    def _(b):
        rows = pl.ds(pl.multiple_of(b * 256, 256), 256)
        packed[rows, :WIDE] = dot_nn(rows_t[rows, :], values[...]).astype(BF16)

    tail_sum[...] = dot_nn(rows_t[MAIN:, :], values[...])
    pack_tail(tail_sum, tiles, packed)


def swap_start(total_t, mine, theirs, ssem, rsem, partner):
    mine[...] = total_t[...].astype(BF16)
    copy = remote(mine, theirs, ssem, rsem, partner)
    copy.start()
    return copy


def swap_end(copy, mine, theirs):
    copy.wait_recv()
    return mine[...].astype(F32) + theirs[...].astype(F32)


def middle_kernel(
    x_ref, a0, w0_ref, w1_ref, w2_ref, g4, perm, vec,
    y4, dres_out, dresb_out, gr12_out, dmsg, dlast, vec_out,
    w0, w1, w2, gr1, gr2, resid, normed2, inverse2, n2, n2_t, cot, cot_t, total_t, dn2_t, hidden, dpre, turn1, turn2,
    dmix, tiles, out_tiles, tail1, tail2, tail_sum, mine1, theirs1, mine2, theirs2, mine_y, theirs_y, dmix_out,
    load, store, send, recv, local,
):
    me = Place()
    partner = me.partner()
    loads = [load_weights(source, target, load.at[n]) for n, (source, target) in enumerate(
        ((w0_ref, w0), (w1_ref, w1), (w2_ref, w2))
    )]
    greet([partner])
    for buffer in (tail1, tail2, out_tiles, total_t, dn2_t):
        buffer[...] = jnp.zeros_like(buffer)
    for j in range(2):
        turn1[...] = turned(a0[j])
        loads[0][j].wait()
        unpack_tail(w0.at[j], tiles, tail_sum, tail1)
        add_to_features(total_t, turn1, w0.at[j], tail1)
    first = swap_start(total_t, mine1, theirs1, send.at[0], recv.at[0], partner)
    cot_value = permuted(g4, perm)
    cot[...] = cot_value.astype(BF16)
    cot_t[...] = cot_value.T.astype(BF16)
    total_t[...] = jnp.zeros_like(total_t)
    attended = swap_end(first, mine1, theirs1)
    resid[...] = x_ref[...].astype(F32) + attended.T
    normed, inverse, n2_value = norm_forward(resid[...], vec[2:3], vec[3:4])
    normed2[...] = normed
    inverse2[...] = jnp.broadcast_to(inverse, inverse2.shape)
    n2[...] = n2_value
    n2_t[...] = turned(n2_value)
    stores = []
    for j in range(2):
        loads[1][j].wait()
        loads[2][j].wait()
        up, down = w1.at[j], w2.at[j]
        unpack_tail(up, tiles, tail_sum, tail1)
        unpack_tail(down, tiles, tail_sum, tail2)

        @pl.loop(0, 3)
        def _(b):
            columns = pl.ds(pl.multiple_of(b * 384, 128), 384)
            pre = in_features(n2[...], up, tail1, columns)
            d_hidden = in_features(cot[...], down, tail2, columns)
            value, slope = gelu_both(pre)
            hidden[:, columns] = value.astype(BF16)
            dpre[:, columns] = (d_hidden * slope).astype(BF16)

        turn1[...] = turned(hidden[...])
        turn2[...] = turned(dpre[...])
        add_to_features(total_t, turn1, down, tail2)
        add_to_features(dn2_t, turn2, up, tail1)
        if j == 1:
            second = swap_start(dn2_t, mine2, theirs2, send.at[1], recv.at[1], partner)
            half = own_half(1 - me.core)
            mine_y[...] = total_t[:, half].astype(BF16)
            third = remote(mine_y, theirs_y, send.at[2], recv.at[2], partner)
            third.start()
        weight_gradient(n2_t, dpre, out_tiles, tail_sum, gr1.at[j])
        weight_gradient(cot_t, hidden, out_tiles, tail_sum, gr2.at[j])
        for n, source in enumerate((gr1, gr2)):
            copy = pltpu.make_async_copy(source.at[j], gr12_out.at[j, :, pl.ds(PACK * n, PACK)], store.at[n, j])
            copy.start()
            stores.append(copy)
    grad = swap_end(second, mine2, theirs2).T
    normed = normed2[...]
    vec_out[...] = jnp.zeros_like(vec_out)
    vec_out[0:1, :] = jnp.sum(grad * normed, axis=0, keepdims=True)
    vec_out[1:2, :] = jnp.sum(grad, axis=0, keepdims=True)
    back = cot[...].astype(F32) + norm_reverse(grad, normed, inverse2[:, 0:1], vec[2:3])
    back = real_features(back)
    dres_out[...] = back
    dresb_out[...] = back.astype(BF16)
    sent, own_copies, arrivals = [first, second, third], [], []
    columns = slice(768, WIDE)
    for j in range(2):
        unpack_tail(w0.at[j], tiles, tail_sum, tail1)
        dmix[j] = in_features(dresb_out[...], w0.at[j], tail1, columns).astype(BF16)
        own = pltpu.make_async_copy(dmix.at[j, own_half(me.core), :], dmix_out.at[j, me.core], local.at[j])
        own.start()
        own_copies.append(own)
        theirs = dmix.at[j, own_half(1 - me.core), :]
        copy = remote(theirs, dmix_out.at[j, me.core], send.at[3 + j], recv.at[3 + j], partner)
        copy.start()
        sent.append(copy)
        arrivals.append(remote(theirs, dmix_out.at[j, 1 - me.core], send.at[3 + j], recv.at[3 + j], partner))
    half = own_half(me.core)
    third.wait_recv()
    y = (resid[half, :].T + (total_t[:, half] + theirs_y[...].astype(F32))).astype(BF16)
    for c in range(4):
        y4[c] = dot_nn(perm[c], y).astype(BF16)
    for copy in arrivals:
        copy.wait_recv()
    for copy in own_copies:
        copy.wait()
    for head in range(HEADS):
        block = columns_of(dmix_out, head * HEAD_DIM, 272, QKV_COLS - 768)
        if head == 16:
            dlast[...] = block
        else:
            dmsg[head, :, 0:64] = block[0:64]
            dmsg[head, :, 64:128] = block[64:128]
    for copy in stores:
        copy.wait()
    for copy in sent:
        copy.wait_send()


def middle_call(x, a0, w0, w1, w2, g4, perm, vec):
    weights = pltpu.VMEM((2, MAIN, PACK), BF16)
    row_f, row_b = pltpu.VMEM((PAIR, WIDE), F32), pltpu.VMEM((PAIR, WIDE), BF16)
    turn_f, turn_b = pltpu.VMEM((WIDE, PAIR), F32), pltpu.VMEM((WIDE, PAIR), BF16)
    tile, tail = pltpu.VMEM((MAIN, 128), F32), pltpu.VMEM((128, WIDE), BF16)
    half = pltpu.VMEM((WIDE, QUARTER), BF16)
    return pl.pallas_call(
        middle_kernel,
        out_shape=(
            jax.ShapeDtypeStruct((4, 272, QUARTER), BF16), jax.ShapeDtypeStruct((PAIR, WIDE), F32),
            jax.ShapeDtypeStruct((PAIR, WIDE), BF16), jax.ShapeDtypeStruct((2, MAIN, 2 * PACK), BF16),
            jax.ShapeDtypeStruct((16, 64, 128), BF16), jax.ShapeDtypeStruct((QUARTER, 64), BF16),
            jax.ShapeDtypeStruct((8, WIDE), F32),
        ),
        in_specs=[VMEM_SPEC, VMEM_SPEC, ANY, ANY, ANY, VMEM_SPEC, VMEM_SPEC, VMEM_SPEC],
        out_specs=(VMEM_SPEC, VMEM_SPEC, VMEM_SPEC, ANY, VMEM_SPEC, VMEM_SPEC, VMEM_SPEC),
        scratch_shapes=[
            weights, weights, weights, weights, weights, row_f, row_f, pltpu.VMEM((PAIR, 128), F32), row_b, turn_b,
            row_b, turn_b, turn_f, turn_f, row_b, row_b, turn_b, turn_b, pltpu.VMEM((2, PAIR, 384), BF16),
            tile, tile, tail, tail, pltpu.VMEM((128, WIDE), F32), turn_b, turn_b, turn_b, turn_b, half, half,
            pltpu.VMEM((2, 2, QUARTER, 384), BF16),
            pltpu.SemaphoreType.DMA((3, 2)), pltpu.SemaphoreType.DMA((2, 2)), pltpu.SemaphoreType.DMA((5,)),
            pltpu.SemaphoreType.DMA((5,)), pltpu.SemaphoreType.DMA((2,)),
        ],
        compiler_params=pltpu.CompilerParams(
            collective_id=5, has_side_effects=True, vmem_limit_bytes=VMEM_LIMIT
        ),
        name="feed_forward",
    )(x, a0, w0, w1, w2, g4, perm, vec)


def first_kernel(
    x_ref, n1, dresb, dres, back_ref, sums16, dq16, a0, w0_ref, perm, vec, vec2,
    gin4, gr0_out, sums,
    dq_ref, w0, gr0, dq, n1_t, dres_t, turn, dn1_t, tiles, out_tiles, tail, tail_sum, mine, theirs,
    load, store, send, recv, local,
):
    me = Place()
    partner = me.partner()
    loads = load_weights(w0_ref, w0, load)
    greet([partner])
    mine_rows = own_half(me.core)
    dq_ref[...] = jnp.zeros_like(dq_ref)
    last = jnp.zeros((QUARTER, 128), F32)
    for p in range(8):
        last += sums16[p].astype(F32)
    last = last.astype(BF16)
    for n in range(3):
        for head in range(HEADS):
            if head == 16:
                parts = ((0, QUARTER, dq16[...] if n == 0 else last[:, 64 * (n - 1) : 64 * n]),)
            else:
                block = back_ref[head, 64 * n : 64 * n + 64, :]
                parts = ((0, 64, block[:, 0:64]), (64, 64, block[:, 64:128]))
            start = n * D + head * HEAD_DIM
            position = start
            while position < start + HEAD_DIM:
                c = position // QKV_COLS
                end = min(start + HEAD_DIM, (c + 1) * QKV_COLS)
                lane = position - c * QKV_COLS
                for row, rows, value in parts:
                    dq_ref[c % 2, c // 2, row : row + rows, lane : lane + end - position] = value[
                        :, position - start : end - start
                    ]
                position = end
    copy = remote(dq_ref.at[1 - me.core], dq.at[:, mine_rows, :], send.at[0], recv.at[0], partner)
    copy.start()
    own = pltpu.make_async_copy(dq_ref.at[me.core], dq.at[:, mine_rows, :], local)
    own.start()
    for buffer in (tail, out_tiles, dn1_t):
        buffer[...] = jnp.zeros_like(buffer)
    n1_t[...] = turned(n1[...])
    dres_t[...] = turned(dresb[...])
    normed, inverse, _ = norm_forward(x_ref[...].astype(F32), vec[0:1], vec[1:2])
    own.wait()
    remote(
        dq_ref.at[me.core], dq.at[:, own_half(1 - me.core), :], send.at[0], recv.at[0], partner
    ).wait_recv()
    for j in range(2):
        loads[j].wait()
        unpack_tail(w0.at[j], tiles, tail_sum, tail)
        turn[...] = turned(dq[j])
        add_to_features(dn1_t, turn, w0.at[j], tail)
    swap = swap_start(dn1_t, mine, theirs, send.at[1], recv.at[1], partner)
    stores = []
    for j in range(2):
        packed = gr0.at[j]

        @pl.loop(0, 4)
        def _(b):
            rows = pl.ds(pl.multiple_of(b * 256, 256), 256)
            packed[rows, :768] = dot_nn(n1_t[rows, :], dq[j, :, :768]).astype(BF16)
            packed[rows, 768:WIDE] = (
                dot_nn(n1_t[rows, :], dq[j, :, 768:]) + dot_nn(dres_t[rows, :], a0[j, :, 768:])
            ).astype(BF16)

        tail_sum[:, :768] = dot_nn(n1_t[MAIN:, :], dq[j, :, :768])
        tail_sum[:, 768:] = dot_nn(n1_t[MAIN:, :], dq[j, :, 768:]) + dot_nn(dres_t[MAIN:, :], a0[j, :, 768:])
        pack_tail(tail_sum, out_tiles, packed)
        out = pltpu.make_async_copy(packed, gr0_out.at[j], store.at[j])
        out.start()
        stores.append(out)
    grad = swap_end(swap, mine, theirs).T
    sums[...] = vec2[...]
    sums[4:5, :] = jnp.sum(grad * normed, axis=0, keepdims=True)
    sums[5:6, :] = jnp.sum(grad, axis=0, keepdims=True)
    back = dres[...] + norm_reverse(grad, normed, inverse, vec[0:1])
    dn1_t[...] = real_features(back).T
    back = dn1_t[:, mine_rows].astype(BF16)
    for c in range(4):
        gin4[c] = dot_nn(perm[c], back).astype(BF16)
    for out in stores:
        out.wait()
    copy.wait_send()
    swap.wait_send()


def first_call(*args):
    weights = pltpu.VMEM((2, MAIN, PACK), BF16)
    turn_b = pltpu.VMEM((WIDE, PAIR), BF16)
    tile = pltpu.VMEM((MAIN, 128), F32)
    return pl.pallas_call(
        first_kernel,
        out_shape=(
            jax.ShapeDtypeStruct((4, 272, QUARTER), BF16), jax.ShapeDtypeStruct((2, MAIN, PACK), BF16),
            jax.ShapeDtypeStruct((8, WIDE), F32),
        ),
        in_specs=[VMEM_SPEC] * 8 + [ANY] + [VMEM_SPEC] * 3,
        out_specs=(VMEM_SPEC, ANY, VMEM_SPEC),
        scratch_shapes=[
            pltpu.VMEM((2, 2, QUARTER, WIDE), BF16),
            weights, weights, pltpu.VMEM((2, PAIR, WIDE), BF16), turn_b, turn_b, turn_b,
            pltpu.VMEM((WIDE, PAIR), F32), tile, tile, pltpu.VMEM((128, WIDE), BF16), pltpu.VMEM((128, WIDE), F32),
            turn_b, turn_b,
            pltpu.SemaphoreType.DMA((2,)), pltpu.SemaphoreType.DMA((2,)), pltpu.SemaphoreType.DMA((2,)),
            pltpu.SemaphoreType.DMA((2,)), pltpu.SemaphoreType.DMA,
        ],
        compiler_params=pltpu.CompilerParams(
            collective_id=6, has_side_effects=True, vmem_limit_bytes=VMEM_LIMIT
        ),
        name="first_norm_back",
    )(*args)


def allowed_pairs(shape, key_start, query_start):
    key = key_start + lax.broadcasted_iota(jnp.int32, shape, 0)
    query = query_start + lax.broadcasted_iota(jnp.int32, shape, 1)
    return key <= query


def transposed(values):
    return values.astype(F32).T


def spread(block, target, row, rows=64):
    target[pl.ds(row, 64), :] = block[:, 0:64]
    target[pl.ds(row + 64, 64), :] = block[:, 64:128]


def attend_kernel(info, r_ref, kv16, q16, dense_out, o_out, o16_out, l_out, l16_out, query, key, value, value_t, value16_t):
    rank, wraps = info[0], info[1]

    @pl.loop(0, 16)
    def _(b):
        row = pl.multiple_of(b * 128, 128)
        spread(r_ref[b, 0:64, :] * jnp.asarray(0.125, BF16), query, row)
        spread(r_ref[b, 64:128, :], key, row)
        spread(r_ref[b, 128:192, :], value, row)

    @pl.loop(0, 4)
    def _(b):
        rows = pl.ds(pl.multiple_of(b * KEYS, KEYS), KEYS)
        value_t[:, rows] = transposed(value[rows, :]).astype(BF16)
        value16_t[:, rows] = transposed(kv16[rows, :])[64:128].astype(BF16)

    def step(q, k_ref, v_t, j, carry, query_start=None):
        peak, running, mixed = carry
        rows = pl.ds(pl.multiple_of(j * KEYS, KEYS), KEYS)
        scores = dot_nt(k_ref[rows, 0:64], q)
        if query_start is not None:
            scores = jnp.where(allowed_pairs(scores.shape, j * KEYS, query_start), scores, masked_score)
        new_peak = jnp.maximum(peak, jnp.max(scores, axis=0, keepdims=True))
        shrink = jnp.exp(peak - new_peak)
        weights = jnp.exp(scores - new_peak)
        running = running * shrink + jnp.sum(weights, axis=0, keepdims=True)
        mixed = mixed * shrink + dot_nn(v_t[:, rows], weights.astype(BF16))
        return new_peak, running, mixed

    def empty(width):
        return (
            jnp.full((1, width), masked_score, F32), jnp.zeros((1, width), F32), jnp.zeros((64, width), F32)
        )

    @pl.loop(0, 4)
    def _(i):
        rows = pl.ds(pl.multiple_of(i * KEYS, KEYS), KEYS)
        q = query[rows, :]
        start = jnp.where((wraps == 1) & (i >= 2), 2, 0)
        carry = lax.fori_loop(
            start, i, lambda j, carry: step(q, key, value_t, j, carry), empty(KEYS)
        )
        peak, running, mixed = step(q, key, value_t, i, carry, i * KEYS)
        result = (mixed / running).T.astype(BF16)
        o_out[rows, :] = result
        for n in range(4):
            dense_out[2 * i + n // 2, :, 64 * (n % 2) : 64 * (n % 2) + 64] = result[128 * n : 128 * n + 128]
        l_out[:, rows] = peak + jnp.log(running)

    q = q16[...] * jnp.asarray(0.125, BF16)
    start = jnp.where((wraps == 1) & (rank >= 8), 2, 0)
    peak, running, mixed = lax.fori_loop(
        start, rank // 4 + 1,
        lambda j, carry: step(q, kv16, value16_t, j, carry, rank * QUARTER), empty(QUARTER),
    )
    o16_out[...] = (mixed / running).T.astype(BF16)
    l16_out[...] = peak + jnp.log(running)


def attend_call(info, r, kv16, q16):
    tokens = jax.ShapeDtypeStruct((SEQ, 64), BF16)
    return pl.pallas_call(
        attend_kernel,
        out_shape=(
            jax.ShapeDtypeStruct((8, 128, 128), BF16), tokens, jax.ShapeDtypeStruct((QUARTER, 64), BF16),
            jax.ShapeDtypeStruct((1, SEQ), F32), jax.ShapeDtypeStruct((1, QUARTER), F32), tokens, tokens, tokens,
        ),
        in_specs=[SMEM_SPEC, VMEM_SPEC, VMEM_SPEC, VMEM_SPEC],
        out_specs=(VMEM_SPEC,) * 8,
        scratch_shapes=[pltpu.VMEM((64, SEQ), BF16), pltpu.VMEM((64, SEQ), BF16)],
        compiler_params=pltpu.CompilerParams(vmem_limit_bytes=VMEM_LIMIT),
        name="attend_forward",
    )(info, r, kv16, q16)


def attend_back_kernel(
    dmsg, gradients, query, key, value, kv16, q16, o_ref, o16, do16, l_ref, l16,
    back_out, sums_out, dq16_out, up_out, down_out,
    reduced, do_dense, msg, part16, theirs, summed, do_ref, key_t, key16_t, delta, dq_t,
    send1, recv1, local1, send2, recv2, local2, swap_send, swap_recv, psend, precv, plocal, *scratch,
):
    me, group = Place(), Group()
    rank = group.rank
    wraps = (group.row < 2) | (group.row >= 30)
    reduction = Reduction(me, gradients, EARLY_WIDTHS, scratch, reduced)
    greet([group.device(lax.rem(rank + d, 16)) for d in range(1, 16)] + me.neighbours())
    first = group.all_to_all(dmsg, do_dense, send1, recv1, local1)
    reduction.load_all()
    reduction.begin_chunk(0)

    @pl.loop(0, 4)
    def _(b):
        rows = pl.ds(pl.multiple_of(b * KEYS, KEYS), KEYS)
        key_t[:, rows] = transposed(key[rows, :]).astype(BF16)
        key16_t[:, rows] = transposed(kv16[rows, :])[0:64].astype(BF16)
        dq_t[:, rows] = jnp.zeros((64, KEYS), F32)

    group.finish(*first)
    for u in (1, 2, 3):
        reduction.begin_chunk(u)

    @pl.loop(0, 16)
    def _(b):
        spread(do_dense[b], do_ref, pl.multiple_of(b * 128, 128))

    @pl.loop(0, 4)
    def _(b):
        rows = pl.ds(pl.multiple_of(b * KEYS, KEYS), KEYS)
        product = do_ref[rows, :].astype(F32) * o_ref[rows, :].astype(F32)
        delta[:, rows] = jnp.sum(product.T, axis=0, keepdims=True)

    def put(section, j, result):
        for n in range(4):
            for half in range(2):
                msg[4 * j + n, 64 * section : 64 * section + 64, 64 * half : 64 * half + 64] = result[
                    128 * n + 64 * half : 128 * n + 64 * half + 64
                ]

    def pair(keys, values, q, d_out, log_total, delta_row, mask):
        scores = dot_nt(keys, q)
        probs = jnp.exp(scores - log_total)
        if mask is not None:
            probs = jnp.where(mask(scores.shape), probs, 0.0)
        probs = probs.astype(BF16)
        d_prob = dot_nt(values, d_out)
        d_scores = (probs.astype(F32) * (d_prob - delta_row)).astype(BF16)
        return dot_nn(d_scores, q), dot_nn(probs, d_out), d_scores

    def key_block(j):
        rows = pl.ds(pl.multiple_of(j * KEYS, KEYS), KEYS)
        keys, values = key[rows, :], value[rows, :]

        def step(i, carry, mask=None):
            d_key, d_value = carry
            at = pl.ds(pl.multiple_of(i * KEYS, KEYS), KEYS)
            more_key, more_value, d_scores = pair(
                keys, values, query[at, :], do_ref[at, :], l_ref[:, at], delta[:, at], mask
            )
            dq_t[:, at] += dot_nn(key_t[:, rows], d_scores)
            return d_key + more_key, d_value + more_value

        zero = jnp.zeros((KEYS, 64), F32)
        carry = step(j, (zero, zero), lambda shape: allowed_pairs(shape, 0, 0))
        end = jnp.where(wraps & (j < 2), 2, 4)
        d_key, d_value = lax.fori_loop(j + 1, end, step, carry)
        put(1, j, d_key.astype(BF16))
        put(2, j, d_value.astype(BF16))

    q = q16[...] * jnp.asarray(0.125, BF16)
    d_out16 = do16[...]
    delta16 = jnp.sum((d_out16.astype(F32) * o16[...].astype(F32)).T, axis=0, keepdims=True)
    start = jnp.where(wraps & (rank >= 8), 2, 0)

    def last_step(j, dq):
        rows = pl.ds(pl.multiple_of(j * KEYS, KEYS), KEYS)
        d_key, d_value, d_scores = pair(
            kv16[rows, 0:64], kv16[rows, 64:128], q, d_out16, l16[...], delta16,
            lambda shape: allowed_pairs(shape, j * KEYS, rank * QUARTER),
        )
        for n in range(4):
            block = part16.at[2 * j + n // 2, n % 2]
            block[:, 0:64] = d_key[128 * n : 128 * n + 128].astype(BF16)
            block[:, 64:128] = d_value[128 * n : 128 * n + 128].astype(BF16)
        return dq + dot_nn(key16_t[:, rows], d_scores)

    part16[...] = jnp.zeros_like(part16)
    dq = lax.fori_loop(start, rank // 4 + 1, last_step, jnp.zeros((64, QUARTER), F32))
    dq16_out[...] = (dq * 0.125).T.astype(BF16)
    swap = remote(part16.at[:, 1 - group.core], theirs, swap_send, swap_recv, group.partner)
    swap.start()

    @pl.loop(0, 2)
    def _(j):
        key_block(j)

    reduction.middle_chunk(0)

    @pl.loop(2, 4)
    def _(j):
        key_block(j)

    @pl.loop(0, 4)
    def _(j):
        rows = pl.ds(pl.multiple_of(j * KEYS, KEYS), KEYS)
        put(0, j, (dq_t[:, rows] * 0.125).T.astype(BF16))

    second = group.all_to_all(msg, back_out, send2, recv2, local2)
    swap.wait_recv()

    @pl.loop(0, 8)
    def _(p):
        summed[p] = (part16[p, group.core].astype(F32) + theirs[p].astype(F32)).astype(BF16)

    own = pltpu.make_async_copy(summed.at[group.pair], sums_out.at[group.pair], plocal)
    own.start()
    sent = [swap]
    for e in range(1, 8):
        other = lax.rem(group.pair + e, 8)
        copy = remote(
            summed.at[other], sums_out.at[group.pair], psend.at[e], precv.at[e], group.device(other * 2 + group.core)
        )
        copy.start()
        sent.append(copy)
    for u in range(1, 4):
        reduction.middle_chunk(u)
        reduction.finish_chunk(u - 1)
    reduction.finish_chunk(3)
    reduction.finish_all()
    unpack_rows(reduced, 0, up_out)
    unpack_rows(reduced, PACK, down_out)
    for e in range(1, 8):
        origin = lax.rem(group.pair + 8 - e, 8)
        block = sums_out.at[origin]
        remote(block, block, psend.at[e], precv.at[e], group.device(origin * 2 + group.core)).wait_recv()
    group.finish(*second)
    for copy in sent:
        copy.wait_send()
    own.wait()
    reduction.wait_sent()


def attend_back_call(*args):
    block = pltpu.VMEM((8, QUARTER, 128), BF16)
    eight = pltpu.SemaphoreType.DMA((8,))
    one = pltpu.SemaphoreType.DMA
    return pl.pallas_call(
        attend_back_kernel,
        out_shape=(
            jax.ShapeDtypeStruct((16, 192, 128), BF16), jax.ShapeDtypeStruct((8, QUARTER, 128), BF16),
            jax.ShapeDtypeStruct((QUARTER, 64), BF16), jax.ShapeDtypeStruct((34, D), F32),
            jax.ShapeDtypeStruct((34, D), F32),
        ),
        in_specs=[ANY, ANY] + [VMEM_SPEC] * 10,
        out_specs=(ANY, ANY, VMEM_SPEC, VMEM_SPEC, VMEM_SPEC),
        scratch_shapes=[
            pltpu.VMEM((32, 2 * PACK), F32),
            pltpu.VMEM((16, 64, 128), BF16), pltpu.VMEM((16, 192, 128), BF16), pltpu.VMEM((8, 2, QUARTER, 128), BF16),
            block, block,
            pltpu.VMEM((SEQ, 64), BF16), pltpu.VMEM((64, SEQ), BF16), pltpu.VMEM((64, SEQ), BF16),
            pltpu.VMEM((1, SEQ), F32), pltpu.VMEM((64, SEQ), F32),
        ] + DIRECT + DIRECT + [one, one, eight, eight, one] + Reduction.scratch(EARLY_WIDTHS),
        compiler_params=pltpu.CompilerParams(
            collective_id=7, has_side_effects=True, vmem_limit_bytes=VMEM_LIMIT
        ),
        name="attend_backward",
    )(*args)


def permutation():
    feature = np.arange(D)
    block, inside = feature // 34, feature % 34
    place = np.where(inside < 32, 32 * block + inside, MAIN + 32 * (inside - 32) + block)
    chosen = np.zeros((D, WIDE), np.float32)
    chosen[feature, place] = 1.0
    return jnp.asarray(chosen.reshape(4, 272, WIDE).astype(ml_dtypes.bfloat16))


def per_device(
    layer_input,
    first_norm_gain,
    first_norm_bias,
    w_qkv,
    w_out,
    second_norm_gain,
    second_norm_bias,
    w_up,
    w_down,
    gradient_of_output,
):
    row, col = lax.axis_index("row"), lax.axis_index("col")
    rank, core = (row + 2) % 4 * 4 + col, col % 2
    wraps = ((row < 2) | (row >= 30)).astype(jnp.int32)
    info = jnp.stack([rank, wraps]).astype(jnp.int32)
    perm = permutation()
    vectors = (v.reshape(1, 272) for v in (first_norm_gain, first_norm_bias, second_norm_gain, second_norm_bias))
    w0, w1, w2, x4, g4, v4 = gather_all(
        w_qkv, w_out.T, w_up, w_down.T, *vectors, layer_input.T, gradient_of_output.T
    )
    w0, w1, w2 = (w.reshape(2, MAIN, PACK) for w in (w0, w1, w2))
    x, n1, vec, message, last, q16 = qkv_call(x4, v4, perm, w0)
    heads, kv16 = qkv_exchange(message, last)
    kv16 = kv16.reshape(SEQ, 128)
    dense, o, o16, log_total, log16, query, key, value = attend_call(info, heads, kv16, q16)
    mixed, both16 = mixed_exchange(dense, o16)
    attn = jnp.concatenate(
        [
            mixed.reshape(16, QUARTER, 2, HEAD_DIM).transpose(2, 1, 0, 3).reshape(PAIR, 1024),
            both16.reshape(PAIR, HEAD_DIM),
        ],
        axis=1,
    ).reshape(PAIR, 2, 2, 272)
    attn = lax.dynamic_index_in_dim(attn, core, 2, keepdims=False)
    a0 = jnp.pad(attn.transpose(1, 0, 2), ((0, 0), (0, 0), (QKV_COLS, WIDE - D)))
    y4, dres, dresb, gr12, dmsg, do16, vec2 = middle_call(x, a0, w0, w1, w2, g4, perm, vec)
    back, sums16, dq16, up_sum, down_sum = attend_back_call(
        dmsg, gr12.reshape(2, 2, 4, 4, 32, 2 * PACK), query, key, value, kv16, q16, o, o16, do16, log_total, log16
    )
    gin4, gr0, sums4 = first_call(x, n1, dresb, dres, back, sums16, dq16, a0, w0, perm, vec, vec2)
    qkv_sum, out_sum, layer_output, gin, sums4 = scatter_all(gr0.reshape(2, 2, 4, 4, 32, PACK), y4, gin4, sums4)
    own_perm = lax.dynamic_index_in_dim(perm, col, 0, keepdims=False).astype(F32)
    vg = lax.dot_general(
        sums4, own_perm, (((1,), (1,)), ((), ())),
        preferred_element_type=F32, precision=lax.Precision.HIGHEST,
    )
    return (
        layer_output.T,
        gin.T.astype(F32),
        vg[4],
        vg[5],
        qkv_sum,
        out_sum.T,
        vg[0],
        vg[1],
        up_sum,
        down_sum.T,
    )


def solution(mesh):
    placed = (
        P("row", "col"),
        P("col"),
        P("col"),
        P("row", "col"),
        P("col", "row"),
        P("col"),
        P("col"),
        P("row", "col"),
        P("col", "row"),
        P("row", "col"),
    )
    return jax.shard_map(
        per_device,
        mesh=mesh,
        in_specs=placed,
        out_specs=(
            P("row", "col"),
            P("row", "col"),
            P("col"),
            P("col"),
            P("row", "col"),
            P("col", "row"),
            P("col"),
            P("col"),
            P("row", "col"),
            P("col", "row"),
        ),
        check_vma=False,
    )
```

```python
import math

import jax
import jax.numpy as jnp
import ml_dtypes
import numpy as np
from jax import lax
from jax.experimental import pallas as pl
from jax.experimental.pallas import tpu as pltpu
from jax.sharding import PartitionSpec as P

HEADS = 17
HEAD_DIM = 64
D = 1088
SEQ = 2048
MAIN = 1024
WIDE = 1152
PACK = 1280
QKV_COLS = 816
QUARTER = 128
PAIR = 256
KEYS = 512

gelu_coef = math.sqrt(2.0 / math.pi)
norm_epsilon = 1e-05
masked_score = -1e30
MESH = pl.DeviceIdType.MESH
F32 = jnp.float32
BF16 = jnp.bfloat16
VMEM_LIMIT = 60 * 1024 * 1024
ANY = pl.BlockSpec(memory_space=pl.ANY)
VMEM_SPEC = pl.BlockSpec(memory_space=pltpu.VMEM)
SMEM_SPEC = pl.BlockSpec(memory_space=pltpu.SMEM)

GATHER_ORDERS = (("x", "y", "z"), ("y", "z", "x"), ("z", "x", "y"))
SCATTER_ORDERS = (("z", "y", "x"), ("x", "z", "y"), ("y", "x", "z"))


def dot_nn(a, b):
    return lax.dot_general(a, b, (((1,), (0,)), ((), ())), preferred_element_type=F32)


def dot_nt(a, b):
    return lax.dot_general(a, b, (((1,), (1,)), ((), ())), preferred_element_type=F32)


class Place:
    def __init__(self):
        self.row = lax.axis_index("row")
        self.col = lax.axis_index("col")
        self.at = {
            "x": lax.rem(self.row, 4),
            "z": lax.rem(self.row // 4, 4),
            "y": (self.row // 16) * 2 + self.col // 2,
        }
        self.core = lax.rem(self.col, 2)

    def device(self, at, core):
        return ((at["y"] // 2) * 16 + at["z"] * 4 + at["x"], lax.rem(at["y"], 2) * 2 + core)

    def step(self, axis, distance):
        at = dict(self.at)
        at[axis] = lax.rem(at[axis] + distance + 4, 4)
        return self.device(at, self.core)

    def partner(self):
        return (self.row, self.col + 1 - 2 * self.core)

    def beside(self, distance):
        return (self.row, lax.rem(self.col + distance, 4))

    def neighbours(self):
        found = [self.step(axis, d) for axis in ("x", "y", "z") for d in (1, -1)]
        found.append(self.partner())
        other = lax.rem(self.col // 2 + 1, 2)
        found.append((self.row, other * 2 + 1 - self.core))
        return found


def greet(devices):
    barrier = pltpu.get_barrier_semaphore()
    for device in devices:
        pl.semaphore_signal(barrier, inc=1, device_id=device, device_id_type=MESH)
    pl.semaphore_wait(barrier, len(devices))


def everything():
    return slice(None)


def place_index(fixed):
    if "y" in fixed:
        y_lo, y_hi = lax.rem(fixed["y"], 2), fixed["y"] // 2
    else:
        y_lo, y_hi = everything(), everything()
    return (y_lo, y_hi, fixed.get("z", everything()), fixed.get("x", everything()))


def remote(source, target, ssem, rsem, device):
    return pltpu.make_async_remote_copy(
        src_ref=source, dst_ref=target, send_sem=ssem, recv_sem=rsem,
        device_id=device, device_id_type=MESH,
    )


def gather_kernel(
    w_qkv, w_out_t, w_up, w_down_t, v_ref, x_ref, g_ref,
    all0, all1, all2, x_out, g_out, v_out,
    block0, block1, block2, full, tile,
    send, recv, last_send, last_recv, local, in_send, in_recv, in_local,
):
    me = Place()
    blocks = (block0, block1, block2)
    wholes = (all0, all1, all2)
    full[...] = jnp.zeros_like(full)
    tile[...] = jnp.zeros_like(tile)
    for piece, sources in enumerate(((w_qkv, w_out_t), (w_up,), (w_down_t,))):
        lane = 0
        for source in sources:
            full[0:34, lane : lane + source.shape[1]] = source[...].astype(F32)
            lane += source.shape[1]
        blocks[piece][:, :WIDE] = full[0:32, :].astype(BF16)
        for j in range(2):
            for n in range(9):
                tile[9 * j + n : 9 * j + n + 1, :] = full[32 + j : 33 + j, 128 * n : 128 * n + 128]
        blocks[piece][:, WIDE:] = tile[...].astype(BF16)
    greet(me.neighbours())

    def region(piece, fixed, rows=None):
        index = place_index(fixed) + ((everything(),) if rows is None else (pl.ds(rows, 16),))
        return wholes[piece].at[index]

    def around(piece, stage, value):
        order = GATHER_ORDERS[piece]
        fixed = {order[stage]: value}
        for axis in order[stage + 1 :]:
            fixed[axis] = me.at[axis]
        return fixed

    sent = []
    pairs = ((x_ref, x_out), (g_ref, g_out))
    waits, arrivals, own_copies = [], [], []
    for piece in range(3):
        copy = pltpu.make_async_copy(
            blocks[piece], region(piece, around(piece, 0, me.at[GATHER_ORDERS[piece][0]])), local.at[piece]
        )
        copy.start()
        own_copies.append(copy)

    def semaphores(piece, stage, n, u):
        if stage == 2:
            return last_send.at[piece, u, n], last_recv.at[piece, u, n]
        return send.at[piece, stage, n], recv.at[piece, stage, n]

    def part(piece, stage, value, u, rows=None):
        fixed = around(piece, stage, value)
        if stage == 2:
            axis = GATHER_ORDERS[piece][1]
            fixed[axis] = lax.rem(me.at[axis] + (0, 3, 1, 2)[u], 4)
        return region(piece, fixed, rows)

    def begin(piece, stage, u=0):
        axis = GATHER_ORDERS[piece][stage]
        mine = part(piece, stage, me.at[axis], u)
        source = blocks[piece] if stage == 0 else mine
        for n, distance in enumerate((1, -1)):
            copy = remote(source, mine, *semaphores(piece, stage, n, u), me.step(axis, distance))
            copy.start()
            sent.append(copy)

    def arrived(piece, stage, n, u=0):
        axis = GATHER_ORDERS[piece][stage]
        value = lax.rem(me.at[axis] + (3, 1, 2, 2)[n], 4)
        there = part(piece, stage, value, u, (None, None, 0, 16)[n])
        remote(there, there, *semaphores(piece, stage, n, u), me.step(axis, 1)).wait_recv()
        if n < 2:
            half = part(piece, stage, value, u, (0, 16)[n])
            copy = remote(half, half, *semaphores(piece, stage, 2 + n, u), me.step(axis, (1, -1)[n]))
            copy.start()
            sent.append(copy)

    for piece in range(3):
        begin(piece, 0)
    partner, across = me.partner(), me.beside(2)

    def tokens_of(ref, col):
        return ref.at[:, pl.ds(pl.multiple_of(col // 2 * PAIR, PAIR), PAIR)]

    relays = []
    for n, (source, target) in enumerate(pairs + ((v_ref, v_out),)):
        here, there = (v_ref, v_ref) if n == 2 else (tokens_of(source, me.col), tokens_of(source, across[1]))
        own = pltpu.make_async_copy(here, target.at[me.col], in_local.at[n])
        own.start()
        waits.append(own)
        for k, (part_ref, device) in enumerate(((there, across), (here, partner))):
            copy = remote(part_ref, target.at[me.col], in_send.at[n, k], in_recv.at[n, k], device)
            copy.start()
            sent.append(copy)
        relays.append(remote(there, target.at[across[1]], in_send.at[n, 0], in_recv.at[n, 0], across))
        arrivals.append(remote(here, target.at[partner[1]], in_send.at[n, 1], in_recv.at[n, 1], partner))
    for copy in own_copies:
        copy.wait()
    for n in range(4):
        for piece in range(3):
            arrived(piece, 0, n)
    for piece in range(3):
        begin(piece, 1)
    for n, (_, target) in enumerate(pairs + ((v_ref, v_out),)):
        relays[n].wait_recv()
        block = target.at[across[1]]
        copy = remote(block, block, in_send.at[n, 2], in_recv.at[n, 2], partner)
        copy.start()
        sent.append(copy)
        far = target.at[lax.rem(partner[1] + 2, 4)]
        arrivals.append(remote(far, far, in_send.at[n, 2], in_recv.at[n, 2], partner))
    for piece in range(3):
        begin(piece, 2, 0)
    for n in range(4):
        for piece in range(3):
            arrived(piece, 1, n)
            if n < 2:
                begin(piece, 2, n + 1)
            elif n == 3:
                begin(piece, 2, 3)
    for n in (0, 1):
        for piece in range(3):
            arrived(piece, 2, n, 0)
    for u in range(1, 4):
        for n in (0, 1):
            for piece in range(3):
                arrived(piece, 2, n, u)
    for u in range(4):
        for n in (2, 3):
            for piece in range(3):
                arrived(piece, 2, n, u)
    for copy in arrivals:
        copy.wait_recv()
    for copy in waits:
        copy.wait()
    for copy in sent:
        copy.wait_send()


def gather_all(*args):
    whole = jax.ShapeDtypeStruct((2, 2, 4, 4, 32, PACK), BF16)
    tokens = jax.ShapeDtypeStruct((4, 272, PAIR), BF16)
    return pl.pallas_call(
        gather_kernel,
        out_shape=(whole, whole, whole, tokens, tokens, jax.ShapeDtypeStruct((4, 8, 272), F32)),
        in_specs=[VMEM_SPEC] * 5 + [ANY] * 2,
        out_specs=(ANY,) * 6,
        scratch_shapes=[
            pltpu.VMEM((32, PACK), BF16), pltpu.VMEM((32, PACK), BF16), pltpu.VMEM((32, PACK), BF16),
            pltpu.VMEM((40, WIDE), F32), pltpu.VMEM((32, 128), F32),
            pltpu.SemaphoreType.DMA((3, 2, 4)),
            pltpu.SemaphoreType.DMA((3, 2, 4)),
            pltpu.SemaphoreType.DMA((3, 4, 4)),
            pltpu.SemaphoreType.DMA((3, 4, 4)),
            pltpu.SemaphoreType.DMA((3,)),
            pltpu.SemaphoreType.DMA((3, 3)),
            pltpu.SemaphoreType.DMA((3, 3)),
            pltpu.SemaphoreType.DMA((3,)),
        ],
        compiler_params=pltpu.CompilerParams(collective_id=0, has_side_effects=True),
        name="gather_weights",
    )(*args)


class Group:
    def __init__(self):
        self.row, self.col = lax.axis_index("row"), lax.axis_index("col")
        self.in_group = lax.rem(self.row + 2, 4)
        self.rank = self.in_group * 4 + self.col
        self.pair, self.core = self.rank // 2, lax.rem(self.col, 2)
        self.partner = (self.row, self.col + 1 - 2 * self.core)

    def device(self, other):
        return (lax.rem(self.row - self.in_group + other // 4 + 32, 32), lax.rem(other, 4))

    def greet(self):
        greet([self.device(lax.rem(self.rank + d, 16)) for d in range(1, 16)])

    def all_to_all(self, source, target, send, recv, local):
        own = pltpu.make_async_copy(source.at[self.rank], target.at[self.rank], local)
        own.start()
        sent, arrivals = [], []
        for d in range(1, 16):
            other = lax.rem(self.rank + d, 16)
            copy = remote(source.at[other], target.at[self.rank], send.at[d], recv.at[d], self.device(other))
            copy.start()
            sent.append(copy)
            origin = lax.rem(self.rank + 16 - d, 16)
            arrivals.append(remote(source.at[other], target.at[origin], send.at[d], recv.at[d], self.device(origin)))
        return own, sent, arrivals

    def finish(self, own, sent, arrivals):
        for copy in arrivals:
            copy.wait_recv()
        for copy in sent:
            copy.wait_send()
        own.wait()

    def relay(self, source_of, target, send, recv, local):
        own = pltpu.make_async_copy(source_of(self.pair), target.at[self.rank], local)
        own.start()
        beside = remote(source_of(self.pair), target.at[self.rank], send.at[0, 0], recv.at[0, 0], self.partner)
        beside.start()
        sent = [beside]
        for e in range(1, 8):
            other = lax.rem(self.pair + e, 8)
            copy = remote(
                source_of(other), target.at[self.rank], send.at[0, e], recv.at[0, e], self.device(other * 2 + self.core)
            )
            copy.start()
            sent.append(copy)
        return own, sent

    def pass_on(self, own, sent, target, send, recv):
        for e in range(1, 8):
            origin = lax.rem(self.pair + 8 - e, 8) * 2 + self.core
            block = target.at[origin]
            remote(block, block, send.at[0, e], recv.at[0, e], self.device(origin)).wait_recv()
            copy = remote(block, block, send.at[1, e], recv.at[1, e], self.partner)
            copy.start()
            sent.append(copy)
        for e in range(0, 8):
            block = target.at[lax.rem(self.pair + 8 - e, 8) * 2 + 1 - self.core]
            n = 0 if e == 0 else 1
            remote(block, block, send.at[n, e], recv.at[n, e], self.partner).wait_recv()
        for copy in sent:
            copy.wait_send()
        own.wait()


RELAY = [pltpu.SemaphoreType.DMA((2, 8)), pltpu.SemaphoreType.DMA((2, 8)), pltpu.SemaphoreType.DMA]
DIRECT = [pltpu.SemaphoreType.DMA((16,)), pltpu.SemaphoreType.DMA((16,)), pltpu.SemaphoreType.DMA]


def exchange_call(kernel, name, collective_id, outs, scratch, *args, in_specs=None):
    return pl.pallas_call(
        kernel,
        out_shape=outs,
        in_specs=in_specs or [ANY] * len(args),
        out_specs=(ANY,) * len(outs),
        scratch_shapes=scratch,
        compiler_params=pltpu.CompilerParams(collective_id=collective_id, has_side_effects=True),
        name=name,
    )(*args)


def qkv_exchange_kernel(source, last, target, last_out, send, recv, local, rsend, rrecv, rlocal):
    group = Group()
    group.greet()
    relayed = group.relay(lambda p: last, last_out, rsend, rrecv, rlocal)
    direct = group.all_to_all(source, target, send, recv, local)
    group.pass_on(*relayed, last_out, rsend, rrecv)
    group.finish(*direct)


def qkv_exchange(source, last):
    outs = (jax.ShapeDtypeStruct((16, 192, 128), BF16), jax.ShapeDtypeStruct((16, QUARTER, 128), BF16))
    return exchange_call(qkv_exchange_kernel, "exchange_qkv", 1, outs, DIRECT + RELAY, source, last)


def mixed_exchange_kernel(source, last, target, last_out, send, recv, local, last_send, last_recv, last_local):
    group = Group()
    group.greet()
    relayed = group.relay(lambda p: source.at[p], target, send, recv, local)
    own = pltpu.make_async_copy(last, last_out.at[group.core], last_local)
    own.start()
    copy = remote(last, last_out.at[group.core], last_send, last_recv, group.partner)
    copy.start()
    group.pass_on(*relayed, target, send, recv)
    remote(last, last_out.at[1 - group.core], last_send, last_recv, group.partner).wait_recv()
    copy.wait_send()
    own.wait()


def mixed_exchange(source, last):
    outs = (jax.ShapeDtypeStruct((16, 128, 128), BF16), jax.ShapeDtypeStruct((2, QUARTER, 64), BF16))
    return exchange_call(
        mixed_exchange_kernel, "exchange_mixed", 2, outs, RELAY + [pltpu.SemaphoreType.DMA] * 3, source, last
    )


def free_axes(fixed):
    return [axis for axis in ("y", "z", "x") if axis not in fixed]


def buffer_shape(fixed, rows, width):
    shape = ()
    for axis in free_axes(fixed):
        shape = shape + ((2, 2) if axis == "y" else (4,))
    return shape + (rows, width)


def buffer_index(at):
    index = ()
    for axis in ("y", "z", "x"):
        if axis in at:
            index = index + ((lax.rem(at[axis], 2), at[axis] // 2) if axis == "y" else (at[axis],))
    return index


VECTOR_AXES = ("z", "x", "y")
CHUNKS = (2, 1, 3, 0)


class Reduction:
    def __init__(self, me, source, widths, scratch, out):
        self.me, self.source, self.widths, self.out = me, source, widths, out
        self.offsets = (0, widths[0], widths[0] + widths[1])
        self.sums = scratch[0:3]
        self.halves, self.fulls = {}, {}
        position = 3
        for piece in range(3):
            for stage in range(3):
                self.halves[piece, stage] = scratch[position : position + 2]
                self.fulls[piece, stage] = scratch[position + 2 : position + 4]
                position += 4
        self.local, self.big_send, self.big_recv, self.send, self.recv = scratch[position : position + 5]
        self.sent, self.loads = [], {}

    @staticmethod
    def scratch(widths):
        found = [pltpu.VMEM((2, 2, 4, 4, 32, width), BF16) for width in widths]
        for piece in range(3):
            order = SCATTER_ORDERS[piece]
            for stage in range(3):
                fixed = order[: stage + 1]
                found += [pltpu.VMEM(buffer_shape(fixed, 16, widths[piece]), BF16) for _ in range(2)]
                found += [pltpu.VMEM(buffer_shape(fixed, 32, widths[piece]), BF16) for _ in range(2)]
        found += [pltpu.SemaphoreType.DMA((3, 4, 4))] * 3 + [pltpu.SemaphoreType.DMA((3, 2, 4))] * 2
        return found

    def shifted(self, axis, distance):
        return lax.rem(self.me.at[axis] + distance, 4)

    def load_all(self):
        for k in range(4):
            for u in range(4):
                for piece in range(3):
                    first, second = SCATTER_ORDERS[piece][:2]
                    index = place_index(
                        {first: self.shifted(first, CHUNKS[k]), second: self.shifted(second, CHUNKS[u])}
                    )
                    lanes = pl.ds(self.offsets[piece], self.widths[piece])
                    load = pltpu.make_async_copy(
                        self.source.at[index + (everything(), lanes)], self.sums[piece].at[index],
                        self.local.at[piece, k, u],
                    )
                    load.start()
                    self.loads[piece, k, u] = load

    def stage_fixed(self, piece, stage):
        return {axis: self.me.at[axis] for axis in SCATTER_ORDERS[piece][:stage]}

    def each_tile(self, fixed, body):
        axes = free_axes(fixed)
        count = 4 ** len(axes)
        if count == 1:
            body({})
            return

        @pl.loop(0, count)
        def _(t):
            body({axes[0]: t})

    def chunk(self, piece, stage, u):
        if stage > 0:
            return {}
        axis = SCATTER_ORDERS[piece][1]
        return {axis: self.shifted(axis, CHUNKS[u])}

    def sems(self, piece, stage, n, u):
        if stage == 0:
            return self.big_send.at[piece, u, n], self.big_recv.at[piece, u, n]
        return self.send.at[piece, stage - 1, n], self.recv.at[piece, stage - 1, n]

    def part_of(self, buffer, piece, stage, u):
        if stage > 0:
            return buffer
        axis = SCATTER_ORDERS[piece][1]
        value = self.shifted(axis, CHUNKS[u])
        index = ()
        for name in free_axes({SCATTER_ORDERS[piece][0]: 0}):
            if name == "y":
                index += (lax.rem(value, 2), value // 2) if name == axis else (everything(), everything())
            else:
                index += (value,) if name == axis else (everything(),)
        return buffer.at[index]

    def start(self, source, target, semaphores, axis, n):
        copy = remote(source, target, *semaphores, self.me.step(axis, (1, -1)[n]))
        copy.start()
        self.sent.append(copy)

    def wait(self, there, semaphores, axis):
        remote(there, there, *semaphores, self.me.step(axis, 1)).wait_recv()

    def begin(self, piece, stage, u=0):
        if stage == 0:
            self.loads[piece, 0, u].wait()
        axis = SCATTER_ORDERS[piece][stage]
        fixed = {**self.stage_fixed(piece, stage), axis: self.shifted(axis, 2), **self.chunk(piece, stage, u)}
        for n in range(2):
            self.start(
                self.sums[piece].at[place_index(fixed) + (pl.ds(16 * n, 16),)],
                self.part_of(self.halves[piece, stage][n], piece, stage, u), self.sems(piece, stage, n, u), axis, n,
            )

    def middle(self, piece, stage, n, u=0):
        if stage == 0:
            self.loads[piece, 1 + n, u].wait()
        axis = SCATTER_ORDERS[piece][stage]
        more = self.chunk(piece, stage, u)
        fixed = {**self.stage_fixed(piece, stage), axis: self.shifted(axis, (1, 3)[n]), **more}
        half, sums = self.halves[piece, stage][n], self.sums[piece]
        self.wait(self.part_of(half, piece, stage, u), self.sems(piece, stage, n, u), axis)

        def body(at):
            index = place_index({**fixed, **at}) + (pl.ds(16 * n, 16),)
            total = sums[index].astype(F32) + half[buffer_index({**more, **at})].astype(F32)
            sums[index] = total.astype(BF16)

        self.each_tile(fixed, body)
        self.start(
            sums.at[place_index(fixed)], self.part_of(self.fulls[piece, stage][n], piece, stage, u),
            self.sems(piece, stage, 2 + n, u), axis, n,
        )

    def finish(self, piece, stage, u=0):
        if stage == 0:
            self.loads[piece, 3, u].wait()
        axis = SCATTER_ORDERS[piece][stage]
        more = self.chunk(piece, stage, u)
        fixed = {**self.stage_fixed(piece, stage), axis: self.me.at[axis], **more}
        first, second = self.fulls[piece, stage]
        sums = self.sums[piece]
        for n, buffer in enumerate((first, second)):
            self.wait(self.part_of(buffer, piece, stage, u), self.sems(piece, stage, 2 + n, u), axis)

        def body(at):
            index = place_index({**fixed, **at})
            if stage == 2:
                total = sums[index].astype(F32) + (first[...].astype(F32) + second[...].astype(F32))
                self.out[:, self.offsets[piece] : self.offsets[piece] + self.widths[piece]] = total
            else:
                place = buffer_index({**more, **at})
                total = sums[index].astype(F32) + (first[place].astype(F32) + second[place].astype(F32))
                sums[index] = total.astype(BF16)

        self.each_tile(fixed, body)

    def begin_chunk(self, u):
        for piece in range(3):
            self.begin(piece, 0, u)

    def middle_chunk(self, u):
        for n in range(2):
            for piece in range(3):
                self.middle(piece, 0, n, u)

    def own_part(self, piece):
        first = SCATTER_ORDERS[piece][0]
        return self.sums[piece].at[place_index({first: self.me.at[first]})]

    def store_first_stage(self, targets):
        copies = []
        for piece in range(3):
            copy = pltpu.make_async_copy(self.own_part(piece), targets[piece], self.local.at[piece, 0, 0])
            copy.start()
            copies.append(copy)
        for copy in copies:
            copy.wait()

    def load_first_stage(self, sources):
        for piece in range(3):
            load = pltpu.make_async_copy(sources[piece], self.own_part(piece), self.local.at[piece, 0, 0])
            load.start()
            self.loads[piece] = load

    def second_stage(self, step):
        for piece in range(3):
            if step == 0:
                self.loads[piece].wait()
                self.begin(piece, 1)
            elif step < 3:
                self.middle(piece, 1, step - 1)
            else:
                self.finish(piece, 1)
                self.begin(piece, 2)

    def finish_chunk(self, u):
        for piece in range(3):
            self.finish(piece, 0, u)
            if u == 0:
                self.begin(piece, 1)
            elif u < 3:
                self.middle(piece, 1, u - 1)
            else:
                self.finish(piece, 1)
                self.begin(piece, 2)

    def finish_all(self):
        for n in range(2):
            for piece in range(3):
                self.middle(piece, 2, n)
        for piece in range(3):
            self.finish(piece, 2)

    def wait_sent(self):
        for copy in self.sent:
            copy.wait_send()


def unpack_rows(packed, first, target):
    target[0:32, :] = packed[:, first : first + target.shape[1]]
    for j in range(2):
        for n in range(9):
            width = min(128, target.shape[1] - 128 * n)
            target[32 + j : 33 + j, 128 * n : 128 * n + width] = packed[
                9 * j + n : 9 * j + n + 1, first + WIDE : first + WIDE + width
            ]


LATE_WIDTHS = (512, 512, 256)
EARLY_WIDTHS = (1024, 512, 1024)


def scatter_kernel(
    source, early0, early1, early2, y_ref, gin_ref, v_ref, out_ref, early_out, y_out, gin_out, v_out, *scratch
):
    me = Place()
    vectors = scratch[0:3]
    out_send, out_recv, out_local, v_send, v_recv = scratch[3:8]
    count = len(Reduction.scratch(LATE_WIDTHS))
    reduction = Reduction(me, source, LATE_WIDTHS, scratch[8 : 8 + count], out_ref)
    early = Reduction(me, None, EARLY_WIDTHS, scratch[8 + count :], early_out)
    greet(me.neighbours() + [me.step(axis, 2) for axis in VECTOR_AXES])
    sent = []
    early.load_first_stage((early0, early1, early2))
    reduction.load_all()

    def vectors_begin(phase, value):
        axis = VECTOR_AXES[phase]
        mine = vectors[phase].at[me.at[axis]]
        mine[...] = value
        for distance in (1, 2, 3):
            copy = remote(
                mine, mine, v_send.at[phase, distance - 1], v_recv.at[phase, distance - 1], me.step(axis, distance)
            )
            copy.start()
            sent.append(copy)

    def vectors_end(phase):
        axis = VECTOR_AXES[phase]
        for distance in (1, 2, 3):
            there = vectors[phase].at[lax.rem(me.at[axis] + 4 - distance, 4)]
            remote(
                there, there, v_send.at[phase, distance - 1], v_recv.at[phase, distance - 1], me.step(axis, distance)
            ).wait_recv()
        buffer = vectors[phase]
        return (buffer[0] + buffer[1]) + (buffer[2] + buffer[3])

    early.second_stage(0)
    reduction.begin_chunk(0)
    vectors_begin(0, v_ref[...])
    reduction.begin_chunk(1)
    pairs = ((y_ref, y_out), (gin_ref, gin_out))
    arrivals, own_copies = [], []
    for n, (source, target) in enumerate(pairs):
        rows = pl.ds(pl.multiple_of(me.col * QUARTER, QUARTER), QUARTER)
        own = pltpu.make_async_copy(source.at[me.col], target.at[:, rows], out_local.at[n])
        own.start()
        own_copies.append(own)
        for distance in (1, 2, 3):
            peer = me.beside(distance)
            semaphore = (out_send.at[n, distance - 1], out_recv.at[n, distance - 1])
            copy = remote(source.at[peer[1]], target.at[:, rows], *semaphore, peer)
            copy.start()
            sent.append(copy)
            origin = pl.ds(pl.multiple_of(lax.rem(me.col + 4 - distance, 4) * QUARTER, QUARTER), QUARTER)
            arrivals.append(remote(source.at[me.col], target.at[:, origin], *semaphore, peer))
    early.second_stage(1)
    early.second_stage(2)
    for u in range(4):
        reduction.middle_chunk(u)
        if u == 2:
            early.second_stage(3)
        if u < 2:
            reduction.begin_chunk(u + 2)
            vectors_begin(u + 1, vectors_end(u))
        if u == 3:
            v_out[...] = vectors_end(2)
        if u > 0:
            reduction.finish_chunk(u - 1)
    for n in range(2):
        for piece in range(3):
            early.middle(piece, 2, n)
    reduction.finish_chunk(3)
    for piece in range(3):
        early.finish(piece, 2)
    reduction.finish_all()
    early.wait_sent()
    for copy in arrivals:
        copy.wait_recv()
    for copy in own_copies:
        copy.wait()
    for copy in sent:
        copy.wait_send()
    reduction.wait_sent()


def scatter_all(part, early, y4, gin4, vectors):
    scratch = [pltpu.VMEM((4, 8, WIDE), F32) for _ in range(3)]
    scratch += [
        pltpu.SemaphoreType.DMA((2, 3)),
        pltpu.SemaphoreType.DMA((2, 3)),
        pltpu.SemaphoreType.DMA((2,)),
        pltpu.SemaphoreType.DMA((3, 3)),
        pltpu.SemaphoreType.DMA((3, 3)),
    ]
    back = jax.ShapeDtypeStruct((272, 512), BF16)
    return pl.pallas_call(
        scatter_kernel,
        out_shape=(
            jax.ShapeDtypeStruct((32, PACK), F32), jax.ShapeDtypeStruct((32, 2 * PACK), F32), back, back,
            jax.ShapeDtypeStruct((8, WIDE), F32),
        ),
        in_specs=[ANY] * 6 + [VMEM_SPEC],
        out_specs=(VMEM_SPEC, VMEM_SPEC, ANY, ANY, VMEM_SPEC),
        scratch_shapes=scratch + Reduction.scratch(LATE_WIDTHS) + Reduction.scratch(EARLY_WIDTHS),
        compiler_params=pltpu.CompilerParams(
            collective_id=3, has_side_effects=True, vmem_limit_bytes=VMEM_LIMIT
        ),
        name="scatter_gradients",
    )(part, *early, y4, gin4, vectors)


def results_kernel(
    info, late, early, y_ref, gin_ref, sums, perm, qkv_out, out_out, up_out, down_out, y_out, gin_out, v_out, full
):
    unpack_rows(late, 0, full)
    qkv_out[...] = full[:, 0:QKV_COLS]
    out_out[...] = full[:, QKV_COLS:D]
    unpack_rows(early, 0, up_out)
    unpack_rows(early, PACK, down_out)
    y_out[...] = y_ref[...]
    gin_out[...] = gin_ref[...].astype(F32)
    own = perm[lax.rem(info[0], 4)]
    left = sums[...]
    total = jnp.zeros((8, 272), F32)
    for _ in range(3):
        part = left.astype(BF16)
        left = left - part.astype(F32)
        total += dot_nt(part, own)
    v_out[...] = total


def results_call(*args):
    return pl.pallas_call(
        results_kernel,
        out_shape=(
            jax.ShapeDtypeStruct((34, QKV_COLS), F32), jax.ShapeDtypeStruct((34, D - QKV_COLS), F32),
            jax.ShapeDtypeStruct((34, D), F32), jax.ShapeDtypeStruct((34, D), F32),
            jax.ShapeDtypeStruct((272, 512), BF16), jax.ShapeDtypeStruct((272, 512), F32),
            jax.ShapeDtypeStruct((8, 272), F32),
        ),
        in_specs=[SMEM_SPEC] + [VMEM_SPEC] * 6,
        out_specs=(VMEM_SPEC,) * 7,
        scratch_shapes=[pltpu.VMEM((34, D), F32)],
        compiler_params=pltpu.CompilerParams(vmem_limit_bytes=VMEM_LIMIT),
        name="write_results",
    )(*args)


def unpack_tail(packed, tiles, wide, tail):
    tiles[...] = packed[:, WIDE:PACK].astype(F32)
    for j in range(2):
        for s in range(9):
            wide[pl.ds(32 * j, 32), pl.ds(128 * s, 128)] = tiles[pl.ds(9 * j + s, 32, stride=32), :]
    tail[0:64, :] = wide[0:64, :].astype(BF16)


def pack_tail(tail, tiles, packed):
    for j in range(2):
        for s in range(9):
            tiles[pl.ds(9 * j + s, 32, stride=32), :] = tail[32 * j : 32 * j + 32, 128 * s : 128 * s + 128]
    packed[:, WIDE:PACK] = tiles[...].astype(BF16)


def in_features(values, packed, tail, columns):
    return dot_nn(values[:, :MAIN], packed[:, columns]) + dot_nn(values[:, MAIN:], tail[:, columns])


def add_to_features(total_t, values_t, packed, tail):
    @pl.loop(0, 4)
    def _(b):
        rows = pl.ds(pl.multiple_of(b * 256, 256), 256)
        total_t[rows, :] += dot_nn(packed[rows, :WIDE], values_t[...])

    total_t[MAIN:, :] += dot_nn(tail[...], values_t[...])


def norm_forward(x, gain, bias):
    mean = jnp.sum(x, axis=1, keepdims=True) / D
    square = jnp.sum(x * x, axis=1, keepdims=True) / D
    inverse = lax.rsqrt(square - mean * mean + norm_epsilon)
    normed = (x - mean) * inverse
    return normed, inverse, (normed * gain + bias).astype(BF16)


def norm_reverse(grad, normed, inverse, gain):
    scaled = grad * gain
    first = jnp.sum(scaled, axis=1, keepdims=True) / D
    second = jnp.sum(scaled * normed, axis=1, keepdims=True) / D
    return inverse * (scaled - first - normed * second)


def permuted(pieces, perm):
    total = dot_nn(pieces[0].astype(F32).T.astype(BF16), perm[0])
    for c in range(1, 4):
        total += dot_nn(pieces[c].astype(F32).T.astype(BF16), perm[c])
    return total


def permuted_exact(pieces, perm):
    total = jnp.zeros((8, WIDE), F32)
    for c in range(4):
        left = pieces[c]
        for _ in range(3):
            part = left.astype(BF16)
            left = left - part.astype(F32)
            total += dot_nn(part, perm[c])
    return total


def real_features(values):
    lane = lax.broadcasted_iota(jnp.int32, values.shape, 1)
    return jnp.where(lane < D, values, 0.0)


def turned(values):
    return values.astype(F32).T.astype(BF16)


def own_half(core):
    return pl.ds(pl.multiple_of(core * QUARTER, QUARTER), QUARTER)


def load_weights(source, target, semaphores):
    copies = []
    for j in range(2):
        copy = pltpu.make_async_copy(source.at[j], target.at[j], semaphores.at[j])
        copy.start()
        copies.append(copy)
    return copies


def qkv_kernel(
    x4, v4, perm, w_ref, x_out, n1_out, v_out, msg, last, q16, w, qkv, qkv_out, tiles, wide, tail, load, send, recv, local
):
    me = Place()
    partner = me.partner()
    copies = load_weights(w_ref, w, load)
    greet([partner])
    x = permuted(x4, perm)
    vectors = permuted_exact(v4, perm)
    v_out[...] = vectors
    x_out[...] = x.astype(BF16)
    _, _, normed = norm_forward(x, vectors[0:1], vectors[1:2])
    n1_out[...] = normed
    tail[...] = jnp.zeros_like(tail)
    mine, theirs = own_half(me.core), own_half(1 - me.core)
    sent, own_copies, arrivals = [], [], []
    for j in range(2):
        copies[j].wait()
        packed = w.at[j]
        unpack_tail(packed, tiles, wide, tail)

        @pl.loop(0, 3)
        def _(b):
            columns = pl.ds(pl.multiple_of(b * 384, 128), 384)
            qkv[j, :, columns] = in_features(n1_out[...], packed, tail, columns).astype(BF16)

        own = pltpu.make_async_copy(qkv.at[j, mine, :], qkv_out.at[j, me.core], local.at[j])
        own.start()
        own_copies.append(own)
        copy = remote(qkv.at[j, theirs, :], qkv_out.at[j, me.core], send.at[j], recv.at[j], partner)
        copy.start()
        sent.append(copy)
        arrivals.append(
            remote(qkv.at[j, theirs, :], qkv_out.at[j, 1 - me.core], send.at[j], recv.at[j], partner)
        )
    for copy in arrivals:
        copy.wait_recv()
    for copy in own_copies:
        copy.wait()
    for n in range(3):
        for head in range(HEADS):
            block = columns_of(qkv_out, n * D + head * HEAD_DIM, QKV_COLS, 0)
            if head == 16:
                if n == 0:
                    q16[...] = block
                else:
                    last[:, 64 * (n - 1) : 64 * n] = block
            else:
                msg[head, 64 * n : 64 * n + 64, 0:64] = block[0:64]
                msg[head, 64 * n : 64 * n + 64, 64:128] = block[64:128]
    for copy in sent:
        copy.wait_send()


def columns_of(blocks, start, width, offset):
    pieces = []
    position = start
    while position < start + HEAD_DIM:
        c = position // width
        end = min(start + HEAD_DIM, (c + 1) * width)
        first = position - c * width + offset
        pieces.append(blocks[c // 2, c % 2, :, first : first + end - position])
        position = end
    return pieces[0] if len(pieces) == 1 else jnp.concatenate(pieces, axis=1)


def qkv_call(x4, v4, perm, weights):
    row = jax.ShapeDtypeStruct((PAIR, WIDE), BF16)
    return pl.pallas_call(
        qkv_kernel,
        out_shape=(
            row, row, jax.ShapeDtypeStruct((8, WIDE), F32), jax.ShapeDtypeStruct((16, 192, 128), BF16),
            jax.ShapeDtypeStruct((QUARTER, 128), BF16), jax.ShapeDtypeStruct((QUARTER, 64), BF16),
        ),
        in_specs=[VMEM_SPEC, VMEM_SPEC, VMEM_SPEC, ANY],
        out_specs=(VMEM_SPEC,) * 6,
        scratch_shapes=[
            pltpu.VMEM((2, MAIN, PACK), BF16), pltpu.VMEM((2, PAIR, WIDE), BF16),
            pltpu.VMEM((2, 2, QUARTER, WIDE), BF16),
            pltpu.VMEM((MAIN, 128), F32), pltpu.VMEM((128, WIDE), F32), pltpu.VMEM((128, WIDE), BF16),
            pltpu.SemaphoreType.DMA((2,)), pltpu.SemaphoreType.DMA((2,)), pltpu.SemaphoreType.DMA((2,)),
            pltpu.SemaphoreType.DMA((2,)),
        ],
        compiler_params=pltpu.CompilerParams(
            collective_id=4, has_side_effects=True, vmem_limit_bytes=VMEM_LIMIT
        ),
        name="norm_and_qkv",
    )(x4, v4, perm, weights)


def gelu_both(v):
    square = v * v
    tanh_value = jnp.tanh(gelu_coef * (v + 0.044715 * v * square))
    half = 0.5 * (1.0 + tanh_value)
    value = v * half
    slope = half + 0.5 * v * (1.0 - tanh_value * tanh_value) * gelu_coef * (1.0 + 0.134145 * square)
    return value, slope


def weight_gradient(rows_t, values, tiles, tail_sum, packed):
    @pl.loop(0, 4)
    def _(b):
        rows = pl.ds(pl.multiple_of(b * 256, 256), 256)
        packed[rows, :WIDE] = dot_nn(rows_t[rows, :], values[...]).astype(BF16)

    tail_sum[...] = dot_nn(rows_t[MAIN:, :], values[...])
    pack_tail(tail_sum, tiles, packed)


def swap_start(total_t, mine, theirs, ssem, rsem, partner):
    mine[...] = total_t[...].astype(BF16)
    copy = remote(mine, theirs, ssem, rsem, partner)
    copy.start()
    return copy


def swap_end(copy, mine, theirs):
    copy.wait_recv()
    return mine[...].astype(F32) + theirs[...].astype(F32)


def middle_kernel(
    x_ref, a0, w0_ref, w1_ref, w2_ref, g4, perm, vec,
    y4, dres_out, dresb_out, gr12_out, dmsg, dlast, vec_out,
    w0, w1, w2, gr1, gr2, resid, normed2, inverse2, n2, n2_t, cot, cot_t, total_t, dn2_t, hidden, dpre, turn1, turn2,
    dmix, tiles, out_tiles, tail1, tail2, tail_sum, mine1, theirs1, mine2, theirs2, mine_y, theirs_y, dmix_out,
    load, store, send, recv, local,
):
    me = Place()
    partner = me.partner()
    loads = [load_weights(source, target, load.at[n]) for n, (source, target) in enumerate(
        ((w0_ref, w0), (w1_ref, w1), (w2_ref, w2))
    )]
    greet([partner])
    for buffer in (tail1, tail2, out_tiles, total_t, dn2_t):
        buffer[...] = jnp.zeros_like(buffer)
    for j in range(2):
        turn1[...] = turned(a0[j])
        loads[0][j].wait()
        unpack_tail(w0.at[j], tiles, tail_sum, tail1)
        add_to_features(total_t, turn1, w0.at[j], tail1)
    first = swap_start(total_t, mine1, theirs1, send.at[0], recv.at[0], partner)
    cot_value = permuted(g4, perm)
    cot[...] = cot_value.astype(BF16)
    cot_t[...] = cot_value.T.astype(BF16)
    total_t[...] = jnp.zeros_like(total_t)
    attended = swap_end(first, mine1, theirs1)
    resid[...] = x_ref[...].astype(F32) + attended.T
    normed, inverse, n2_value = norm_forward(resid[...], vec[2:3], vec[3:4])
    normed2[...] = normed
    inverse2[...] = jnp.broadcast_to(inverse, inverse2.shape)
    n2[...] = n2_value
    n2_t[...] = turned(n2_value)
    stores = []
    for j in range(2):
        loads[1][j].wait()
        loads[2][j].wait()
        up, down = w1.at[j], w2.at[j]
        unpack_tail(up, tiles, tail_sum, tail1)
        unpack_tail(down, tiles, tail_sum, tail2)

        @pl.loop(0, 3)
        def _(b):
            columns = pl.ds(pl.multiple_of(b * 384, 128), 384)
            pre = in_features(n2[...], up, tail1, columns)
            d_hidden = in_features(cot[...], down, tail2, columns)
            value, slope = gelu_both(pre)
            hidden[:, columns] = value.astype(BF16)
            dpre[:, columns] = (d_hidden * slope).astype(BF16)

        turn1[...] = turned(hidden[...])
        turn2[...] = turned(dpre[...])
        add_to_features(total_t, turn1, down, tail2)
        add_to_features(dn2_t, turn2, up, tail1)
        if j == 1:
            second = swap_start(dn2_t, mine2, theirs2, send.at[1], recv.at[1], partner)
            half = own_half(1 - me.core)
            mine_y[...] = total_t[:, half].astype(BF16)
            third = remote(mine_y, theirs_y, send.at[2], recv.at[2], partner)
            third.start()
        weight_gradient(n2_t, dpre, out_tiles, tail_sum, gr1.at[j])
        weight_gradient(cot_t, hidden, out_tiles, tail_sum, gr2.at[j])
        for n, source in enumerate((gr1, gr2)):
            copy = pltpu.make_async_copy(source.at[j], gr12_out.at[j, :, pl.ds(PACK * n, PACK)], store.at[n, j])
            copy.start()
            stores.append(copy)
    grad = swap_end(second, mine2, theirs2).T
    normed = normed2[...]
    vec_out[...] = jnp.zeros_like(vec_out)
    vec_out[0:1, :] = jnp.sum(grad * normed, axis=0, keepdims=True)
    vec_out[1:2, :] = jnp.sum(grad, axis=0, keepdims=True)
    back = cot[...].astype(F32) + norm_reverse(grad, normed, inverse2[:, 0:1], vec[2:3])
    back = real_features(back)
    dres_out[...] = back
    dresb_out[...] = back.astype(BF16)
    sent, own_copies, arrivals = [first, second, third], [], []
    columns = slice(768, WIDE)
    for j in range(2):
        unpack_tail(w0.at[j], tiles, tail_sum, tail1)
        dmix[j] = in_features(dresb_out[...], w0.at[j], tail1, columns).astype(BF16)
        own = pltpu.make_async_copy(dmix.at[j, own_half(me.core), :], dmix_out.at[j, me.core], local.at[j])
        own.start()
        own_copies.append(own)
        theirs = dmix.at[j, own_half(1 - me.core), :]
        copy = remote(theirs, dmix_out.at[j, me.core], send.at[3 + j], recv.at[3 + j], partner)
        copy.start()
        sent.append(copy)
        arrivals.append(remote(theirs, dmix_out.at[j, 1 - me.core], send.at[3 + j], recv.at[3 + j], partner))
    half = own_half(me.core)
    third.wait_recv()
    y = (resid[half, :].T + (total_t[:, half] + theirs_y[...].astype(F32))).astype(BF16)
    for c in range(4):
        y4[c] = dot_nn(perm[c], y).astype(BF16)
    for copy in arrivals:
        copy.wait_recv()
    for copy in own_copies:
        copy.wait()
    for head in range(HEADS):
        block = columns_of(dmix_out, head * HEAD_DIM, 272, QKV_COLS - 768)
        if head == 16:
            dlast[...] = block
        else:
            dmsg[head, :, 0:64] = block[0:64]
            dmsg[head, :, 64:128] = block[64:128]
    for copy in stores:
        copy.wait()
    for copy in sent:
        copy.wait_send()


def middle_call(x, a0, w0, w1, w2, g4, perm, vec):
    weights = pltpu.VMEM((2, MAIN, PACK), BF16)
    row_f, row_b = pltpu.VMEM((PAIR, WIDE), F32), pltpu.VMEM((PAIR, WIDE), BF16)
    turn_f, turn_b = pltpu.VMEM((WIDE, PAIR), F32), pltpu.VMEM((WIDE, PAIR), BF16)
    tile, tail = pltpu.VMEM((MAIN, 128), F32), pltpu.VMEM((128, WIDE), BF16)
    half = pltpu.VMEM((WIDE, QUARTER), BF16)
    return pl.pallas_call(
        middle_kernel,
        out_shape=(
            jax.ShapeDtypeStruct((4, 272, QUARTER), BF16), jax.ShapeDtypeStruct((PAIR, WIDE), F32),
            jax.ShapeDtypeStruct((PAIR, WIDE), BF16), jax.ShapeDtypeStruct((2, MAIN, 2 * PACK), BF16),
            jax.ShapeDtypeStruct((16, 64, 128), BF16), jax.ShapeDtypeStruct((QUARTER, 64), BF16),
            jax.ShapeDtypeStruct((8, WIDE), F32),
        ),
        in_specs=[VMEM_SPEC, VMEM_SPEC, ANY, ANY, ANY, VMEM_SPEC, VMEM_SPEC, VMEM_SPEC],
        out_specs=(VMEM_SPEC, VMEM_SPEC, VMEM_SPEC, ANY, VMEM_SPEC, VMEM_SPEC, VMEM_SPEC),
        scratch_shapes=[
            weights, weights, weights, weights, weights, row_f, row_f, pltpu.VMEM((PAIR, 128), F32), row_b, turn_b,
            row_b, turn_b, turn_f, turn_f, row_b, row_b, turn_b, turn_b, pltpu.VMEM((2, PAIR, 384), BF16),
            tile, tile, tail, tail, pltpu.VMEM((128, WIDE), F32), turn_b, turn_b, turn_b, turn_b, half, half,
            pltpu.VMEM((2, 2, QUARTER, 384), BF16),
            pltpu.SemaphoreType.DMA((3, 2)), pltpu.SemaphoreType.DMA((2, 2)), pltpu.SemaphoreType.DMA((5,)),
            pltpu.SemaphoreType.DMA((5,)), pltpu.SemaphoreType.DMA((2,)),
        ],
        compiler_params=pltpu.CompilerParams(
            collective_id=5, has_side_effects=True, vmem_limit_bytes=VMEM_LIMIT
        ),
        name="feed_forward",
    )(x, a0, w0, w1, w2, g4, perm, vec)


def first_kernel(
    x_ref, n1, dresb, dres, back_ref, sums16, dq16, a0, w0_ref, perm, vec, vec2,
    gin4, gr0_out, sums,
    dq_ref, w0, gr0, dq, n1_t, dres_t, turn, dn1_t, tiles, out_tiles, tail, tail_sum, mine, theirs,
    load, store, send, recv, local,
):
    me = Place()
    partner = me.partner()
    loads = load_weights(w0_ref, w0, load)
    greet([partner])
    mine_rows = own_half(me.core)
    dq_ref[...] = jnp.zeros_like(dq_ref)
    last = jnp.zeros((QUARTER, 128), F32)
    for p in range(8):
        last += sums16[p].astype(F32)
    last = last.astype(BF16)
    for n in range(3):
        for head in range(HEADS):
            if head == 16:
                parts = ((0, QUARTER, dq16[...] if n == 0 else last[:, 64 * (n - 1) : 64 * n]),)
            else:
                block = back_ref[head, 64 * n : 64 * n + 64, :]
                parts = ((0, 64, block[:, 0:64]), (64, 64, block[:, 64:128]))
            start = n * D + head * HEAD_DIM
            position = start
            while position < start + HEAD_DIM:
                c = position // QKV_COLS
                end = min(start + HEAD_DIM, (c + 1) * QKV_COLS)
                lane = position - c * QKV_COLS
                for row, rows, value in parts:
                    dq_ref[c % 2, c // 2, row : row + rows, lane : lane + end - position] = value[
                        :, position - start : end - start
                    ]
                position = end
    copy = remote(dq_ref.at[1 - me.core], dq.at[:, mine_rows, :], send.at[0], recv.at[0], partner)
    copy.start()
    own = pltpu.make_async_copy(dq_ref.at[me.core], dq.at[:, mine_rows, :], local)
    own.start()
    for buffer in (tail, out_tiles, dn1_t):
        buffer[...] = jnp.zeros_like(buffer)
    n1_t[...] = turned(n1[...])
    dres_t[...] = turned(dresb[...])
    normed, inverse, _ = norm_forward(x_ref[...].astype(F32), vec[0:1], vec[1:2])
    own.wait()
    remote(
        dq_ref.at[me.core], dq.at[:, own_half(1 - me.core), :], send.at[0], recv.at[0], partner
    ).wait_recv()
    for j in range(2):
        loads[j].wait()
        unpack_tail(w0.at[j], tiles, tail_sum, tail)
        turn[...] = turned(dq[j])
        add_to_features(dn1_t, turn, w0.at[j], tail)
    swap = swap_start(dn1_t, mine, theirs, send.at[1], recv.at[1], partner)
    stores = []
    for j in range(2):
        packed = gr0.at[j]

        @pl.loop(0, 4)
        def _(b):
            rows = pl.ds(pl.multiple_of(b * 256, 256), 256)
            packed[rows, :768] = dot_nn(n1_t[rows, :], dq[j, :, :768]).astype(BF16)
            packed[rows, 768:WIDE] = (
                dot_nn(n1_t[rows, :], dq[j, :, 768:]) + dot_nn(dres_t[rows, :], a0[j, :, 768:])
            ).astype(BF16)

        tail_sum[:, :768] = dot_nn(n1_t[MAIN:, :], dq[j, :, :768])
        tail_sum[:, 768:] = dot_nn(n1_t[MAIN:, :], dq[j, :, 768:]) + dot_nn(dres_t[MAIN:, :], a0[j, :, 768:])
        pack_tail(tail_sum, out_tiles, packed)
        out = pltpu.make_async_copy(packed, gr0_out.at[j], store.at[j])
        out.start()
        stores.append(out)
    grad = swap_end(swap, mine, theirs).T
    sums[...] = vec2[...]
    sums[4:5, :] = jnp.sum(grad * normed, axis=0, keepdims=True)
    sums[5:6, :] = jnp.sum(grad, axis=0, keepdims=True)
    back = dres[...] + norm_reverse(grad, normed, inverse, vec[0:1])
    dn1_t[...] = real_features(back).T
    back = dn1_t[:, mine_rows].astype(BF16)
    for c in range(4):
        gin4[c] = dot_nn(perm[c], back).astype(BF16)
    for out in stores:
        out.wait()
    copy.wait_send()
    swap.wait_send()


def first_call(*args):
    weights = pltpu.VMEM((2, MAIN, PACK), BF16)
    turn_b = pltpu.VMEM((WIDE, PAIR), BF16)
    tile = pltpu.VMEM((MAIN, 128), F32)
    return pl.pallas_call(
        first_kernel,
        out_shape=(
            jax.ShapeDtypeStruct((4, 272, QUARTER), BF16), jax.ShapeDtypeStruct((2, MAIN, PACK), BF16),
            jax.ShapeDtypeStruct((8, WIDE), F32),
        ),
        in_specs=[VMEM_SPEC] * 8 + [ANY] + [VMEM_SPEC] * 3,
        out_specs=(VMEM_SPEC, ANY, VMEM_SPEC),
        scratch_shapes=[
            pltpu.VMEM((2, 2, QUARTER, WIDE), BF16),
            weights, weights, pltpu.VMEM((2, PAIR, WIDE), BF16), turn_b, turn_b, turn_b,
            pltpu.VMEM((WIDE, PAIR), F32), tile, tile, pltpu.VMEM((128, WIDE), BF16), pltpu.VMEM((128, WIDE), F32),
            turn_b, turn_b,
            pltpu.SemaphoreType.DMA((2,)), pltpu.SemaphoreType.DMA((2,)), pltpu.SemaphoreType.DMA((2,)),
            pltpu.SemaphoreType.DMA((2,)), pltpu.SemaphoreType.DMA,
        ],
        compiler_params=pltpu.CompilerParams(
            collective_id=6, has_side_effects=True, vmem_limit_bytes=VMEM_LIMIT
        ),
        name="first_norm_back",
    )(*args)


def allowed_pairs(shape, key_start, query_start):
    key = key_start + lax.broadcasted_iota(jnp.int32, shape, 0)
    query = query_start + lax.broadcasted_iota(jnp.int32, shape, 1)
    return key <= query


def transposed(values):
    return values.astype(F32).T


def spread(block, target, row, rows=64):
    target[pl.ds(row, 64), :] = block[:, 0:64]
    target[pl.ds(row + 64, 64), :] = block[:, 64:128]


def attend_kernel(info, r_ref, kv16, q16, dense_out, o_out, o16_out, l_out, l16_out, query, key, value, value_t, value16_t):
    rank, wraps = info[0], info[1]

    @pl.loop(0, 16)
    def _(b):
        row = pl.multiple_of(b * 128, 128)
        spread(r_ref[b, 0:64, :] * jnp.asarray(0.125, BF16), query, row)
        spread(r_ref[b, 64:128, :], key, row)
        spread(r_ref[b, 128:192, :], value, row)

    @pl.loop(0, 4)
    def _(b):
        rows = pl.ds(pl.multiple_of(b * KEYS, KEYS), KEYS)
        value_t[:, rows] = transposed(value[rows, :]).astype(BF16)
        value16_t[:, rows] = transposed(kv16[rows, :])[64:128].astype(BF16)

    def step(q, k_ref, v_t, j, carry, query_start=None):
        peak, running, mixed = carry
        rows = pl.ds(pl.multiple_of(j * KEYS, KEYS), KEYS)
        scores = dot_nt(k_ref[rows, 0:64], q)
        if query_start is not None:
            scores = jnp.where(allowed_pairs(scores.shape, j * KEYS, query_start), scores, masked_score)
        new_peak = jnp.maximum(peak, jnp.max(scores, axis=0, keepdims=True))
        shrink = jnp.exp(peak - new_peak)
        weights = jnp.exp(scores - new_peak)
        running = running * shrink + jnp.sum(weights, axis=0, keepdims=True)
        mixed = mixed * shrink + dot_nn(v_t[:, rows], weights.astype(BF16))
        return new_peak, running, mixed

    def empty(width):
        return (
            jnp.full((1, width), masked_score, F32), jnp.zeros((1, width), F32), jnp.zeros((64, width), F32)
        )

    @pl.loop(0, 4)
    def _(i):
        rows = pl.ds(pl.multiple_of(i * KEYS, KEYS), KEYS)
        q = query[rows, :]
        start = jnp.where((wraps == 1) & (i >= 2), 2, 0)
        carry = lax.fori_loop(
            start, i, lambda j, carry: step(q, key, value_t, j, carry), empty(KEYS)
        )
        peak, running, mixed = step(q, key, value_t, i, carry, i * KEYS)
        result = (mixed / running).T.astype(BF16)
        o_out[rows, :] = result
        for n in range(4):
            dense_out[2 * i + n // 2, :, 64 * (n % 2) : 64 * (n % 2) + 64] = result[128 * n : 128 * n + 128]
        l_out[:, rows] = peak + jnp.log(running)

    q = q16[...] * jnp.asarray(0.125, BF16)
    start = jnp.where((wraps == 1) & (rank >= 8), 2, 0)
    peak, running, mixed = lax.fori_loop(
        start, rank // 4 + 1,
        lambda j, carry: step(q, kv16, value16_t, j, carry, rank * QUARTER), empty(QUARTER),
    )
    o16_out[...] = (mixed / running).T.astype(BF16)
    l16_out[...] = peak + jnp.log(running)


def attend_call(info, r, kv16, q16):
    tokens = jax.ShapeDtypeStruct((SEQ, 64), BF16)
    return pl.pallas_call(
        attend_kernel,
        out_shape=(
            jax.ShapeDtypeStruct((8, 128, 128), BF16), tokens, jax.ShapeDtypeStruct((QUARTER, 64), BF16),
            jax.ShapeDtypeStruct((1, SEQ), F32), jax.ShapeDtypeStruct((1, QUARTER), F32), tokens, tokens, tokens,
        ),
        in_specs=[SMEM_SPEC, VMEM_SPEC, VMEM_SPEC, VMEM_SPEC],
        out_specs=(VMEM_SPEC,) * 8,
        scratch_shapes=[pltpu.VMEM((64, SEQ), BF16), pltpu.VMEM((64, SEQ), BF16)],
        compiler_params=pltpu.CompilerParams(vmem_limit_bytes=VMEM_LIMIT),
        name="attend_forward",
    )(info, r, kv16, q16)


def attend_back_kernel(
    dmsg, gradients, query, key, value, kv16, q16, o_ref, o16, do16, l_ref, l16,
    back_out, sums_out, dq16_out, early0, early1, early2,
    do_dense, msg, part16, theirs, summed, do_ref, key_t, key16_t, delta, dq_t,
    send1, recv1, local1, send2, recv2, local2, swap_send, swap_recv, psend, precv, plocal, *scratch,
):
    me, group = Place(), Group()
    rank = group.rank
    wraps = (group.row < 2) | (group.row >= 30)
    reduction = Reduction(me, gradients, EARLY_WIDTHS, scratch, None)
    greet([group.device(lax.rem(rank + d, 16)) for d in range(1, 16)] + me.neighbours())
    first = group.all_to_all(dmsg, do_dense, send1, recv1, local1)
    reduction.load_all()
    reduction.begin_chunk(0)

    @pl.loop(0, 4)
    def _(b):
        rows = pl.ds(pl.multiple_of(b * KEYS, KEYS), KEYS)
        key_t[:, rows] = transposed(key[rows, :]).astype(BF16)
        key16_t[:, rows] = transposed(kv16[rows, :])[0:64].astype(BF16)
        dq_t[:, rows] = jnp.zeros((64, KEYS), F32)

    group.finish(*first)
    for u in (1, 2, 3):
        reduction.begin_chunk(u)

    @pl.loop(0, 16)
    def _(b):
        spread(do_dense[b], do_ref, pl.multiple_of(b * 128, 128))

    @pl.loop(0, 4)
    def _(b):
        rows = pl.ds(pl.multiple_of(b * KEYS, KEYS), KEYS)
        product = do_ref[rows, :].astype(F32) * o_ref[rows, :].astype(F32)
        delta[:, rows] = jnp.sum(product.T, axis=0, keepdims=True)

    def put(section, j, result):
        for n in range(4):
            for half in range(2):
                msg[4 * j + n, 64 * section : 64 * section + 64, 64 * half : 64 * half + 64] = result[
                    128 * n + 64 * half : 128 * n + 64 * half + 64
                ]

    def pair(keys, values, q, d_out, log_total, delta_row, mask):
        scores = dot_nt(keys, q)
        probs = jnp.exp(scores - log_total)
        if mask is not None:
            probs = jnp.where(mask(scores.shape), probs, 0.0)
        probs = probs.astype(BF16)
        d_prob = dot_nt(values, d_out)
        d_scores = (probs.astype(F32) * (d_prob - delta_row)).astype(BF16)
        return dot_nn(d_scores, q), dot_nn(probs, d_out), d_scores

    def key_block(j):
        rows = pl.ds(pl.multiple_of(j * KEYS, KEYS), KEYS)
        keys, values = key[rows, :], value[rows, :]

        def step(i, carry, mask=None):
            d_key, d_value = carry
            at = pl.ds(pl.multiple_of(i * KEYS, KEYS), KEYS)
            more_key, more_value, d_scores = pair(
                keys, values, query[at, :], do_ref[at, :], l_ref[:, at], delta[:, at], mask
            )
            dq_t[:, at] += dot_nn(key_t[:, rows], d_scores)
            return d_key + more_key, d_value + more_value

        zero = jnp.zeros((KEYS, 64), F32)
        carry = step(j, (zero, zero), lambda shape: allowed_pairs(shape, 0, 0))
        end = jnp.where(wraps & (j < 2), 2, 4)
        d_key, d_value = lax.fori_loop(j + 1, end, step, carry)
        put(1, j, d_key.astype(BF16))
        put(2, j, d_value.astype(BF16))

    q = q16[...] * jnp.asarray(0.125, BF16)
    d_out16 = do16[...]
    delta16 = jnp.sum((d_out16.astype(F32) * o16[...].astype(F32)).T, axis=0, keepdims=True)
    start = jnp.where(wraps & (rank >= 8), 2, 0)

    def last_step(j, dq):
        rows = pl.ds(pl.multiple_of(j * KEYS, KEYS), KEYS)
        d_key, d_value, d_scores = pair(
            kv16[rows, 0:64], kv16[rows, 64:128], q, d_out16, l16[...], delta16,
            lambda shape: allowed_pairs(shape, j * KEYS, rank * QUARTER),
        )
        for n in range(4):
            block = part16.at[2 * j + n // 2, n % 2]
            block[:, 0:64] = d_key[128 * n : 128 * n + 128].astype(BF16)
            block[:, 64:128] = d_value[128 * n : 128 * n + 128].astype(BF16)
        return dq + dot_nn(key16_t[:, rows], d_scores)

    part16[...] = jnp.zeros_like(part16)
    dq = lax.fori_loop(start, rank // 4 + 1, last_step, jnp.zeros((64, QUARTER), F32))
    dq16_out[...] = (dq * 0.125).T.astype(BF16)
    swap = remote(part16.at[:, 1 - group.core], theirs, swap_send, swap_recv, group.partner)
    swap.start()

    @pl.loop(0, 2)
    def _(j):
        key_block(j)

    reduction.middle_chunk(0)

    @pl.loop(2, 4)
    def _(j):
        key_block(j)

    @pl.loop(0, 4)
    def _(j):
        rows = pl.ds(pl.multiple_of(j * KEYS, KEYS), KEYS)
        put(0, j, (dq_t[:, rows] * 0.125).T.astype(BF16))

    second = group.all_to_all(msg, back_out, send2, recv2, local2)
    swap.wait_recv()

    @pl.loop(0, 8)
    def _(p):
        summed[p] = (part16[p, group.core].astype(F32) + theirs[p].astype(F32)).astype(BF16)

    own = pltpu.make_async_copy(summed.at[group.pair], sums_out.at[group.pair], plocal)
    own.start()
    sent = [swap]
    for e in range(1, 8):
        other = lax.rem(group.pair + e, 8)
        copy = remote(
            summed.at[other], sums_out.at[group.pair], psend.at[e], precv.at[e], group.device(other * 2 + group.core)
        )
        copy.start()
        sent.append(copy)
    for u in range(1, 4):
        reduction.middle_chunk(u)
        for piece in range(3):
            reduction.finish(piece, 0, u - 1)
    for piece in range(3):
        reduction.finish(piece, 0, 3)
    reduction.store_first_stage((early0, early1, early2))
    for e in range(1, 8):
        origin = lax.rem(group.pair + 8 - e, 8)
        block = sums_out.at[origin]
        remote(block, block, psend.at[e], precv.at[e], group.device(origin * 2 + group.core)).wait_recv()
    group.finish(*second)
    for copy in sent:
        copy.wait_send()
    own.wait()
    reduction.wait_sent()


def attend_back_call(*args):
    block = pltpu.VMEM((8, QUARTER, 128), BF16)
    eight = pltpu.SemaphoreType.DMA((8,))
    one = pltpu.SemaphoreType.DMA
    return pl.pallas_call(
        attend_back_kernel,
        out_shape=(
            jax.ShapeDtypeStruct((16, 192, 128), BF16), jax.ShapeDtypeStruct((8, QUARTER, 128), BF16),
            jax.ShapeDtypeStruct((QUARTER, 64), BF16),
            *(
                jax.ShapeDtypeStruct(buffer_shape(SCATTER_ORDERS[n][:1], 32, EARLY_WIDTHS[n]), BF16)
                for n in range(3)
            ),
        ),
        in_specs=[ANY, ANY] + [VMEM_SPEC] * 10,
        out_specs=(ANY, ANY, VMEM_SPEC, ANY, ANY, ANY),
        scratch_shapes=[
            pltpu.VMEM((16, 64, 128), BF16), pltpu.VMEM((16, 192, 128), BF16), pltpu.VMEM((8, 2, QUARTER, 128), BF16),
            block, block,
            pltpu.VMEM((SEQ, 64), BF16), pltpu.VMEM((64, SEQ), BF16), pltpu.VMEM((64, SEQ), BF16),
            pltpu.VMEM((1, SEQ), F32), pltpu.VMEM((64, SEQ), F32),
        ] + DIRECT + DIRECT + [one, one, eight, eight, one] + Reduction.scratch(EARLY_WIDTHS),
        compiler_params=pltpu.CompilerParams(
            collective_id=7, has_side_effects=True, vmem_limit_bytes=VMEM_LIMIT
        ),
        name="attend_backward",
    )(*args)


def permutation():
    feature = np.arange(D)
    block, inside = feature // 34, feature % 34
    place = np.where(inside < 32, 32 * block + inside, MAIN + 32 * (inside - 32) + block)
    chosen = np.zeros((D, WIDE), np.float32)
    chosen[feature, place] = 1.0
    return jnp.asarray(chosen.reshape(4, 272, WIDE).astype(ml_dtypes.bfloat16))


def per_device(
    layer_input,
    first_norm_gain,
    first_norm_bias,
    w_qkv,
    w_out,
    second_norm_gain,
    second_norm_bias,
    w_up,
    w_down,
    gradient_of_output,
):
    row, col = lax.axis_index("row"), lax.axis_index("col")
    rank, core = (row + 2) % 4 * 4 + col, col % 2
    wraps = ((row < 2) | (row >= 30)).astype(jnp.int32)
    info = jnp.stack([rank, wraps]).astype(jnp.int32)
    perm = permutation()
    vectors = jnp.concatenate(
        [
            jnp.stack([first_norm_gain, first_norm_bias, second_norm_gain, second_norm_bias]),
            jnp.zeros((4, 272), F32),
        ]
    )
    w0, w1, w2, x4, g4, v4 = gather_all(
        w_qkv, w_out.T, w_up, w_down.T, vectors, layer_input.T, gradient_of_output.T
    )
    w0, w1, w2 = (w.reshape(2, MAIN, PACK) for w in (w0, w1, w2))
    x, n1, vec, message, last, q16 = qkv_call(x4, v4, perm, w0)
    heads, kv16 = qkv_exchange(message, last)
    kv16 = kv16.reshape(SEQ, 128)
    dense, o, o16, log_total, log16, query, key, value = attend_call(info, heads, kv16, q16)
    mixed, both16 = mixed_exchange(dense, o16)
    attn = jnp.concatenate(
        [
            mixed.reshape(16, QUARTER, 2, HEAD_DIM).transpose(2, 1, 0, 3).reshape(PAIR, 1024),
            both16.reshape(PAIR, HEAD_DIM),
        ],
        axis=1,
    ).reshape(PAIR, 2, 2, 272)
    attn = lax.dynamic_index_in_dim(attn, core, 2, keepdims=False)
    a0 = jnp.pad(attn.transpose(1, 0, 2), ((0, 0), (0, 0), (QKV_COLS, WIDE - D)))
    y4, dres, dresb, gr12, dmsg, do16, vec2 = middle_call(x, a0, w0, w1, w2, g4, perm, vec)
    back, sums16, dq16, *early = attend_back_call(
        dmsg, gr12.reshape(2, 2, 4, 4, 32, 2 * PACK), query, key, value, kv16, q16, o, o16, do16, log_total, log16
    )
    gin4, gr0, sums4 = first_call(x, n1, dresb, dres, back, sums16, dq16, a0, w0, perm, vec, vec2)
    late, early, layer_output, gin, sums4 = scatter_all(
        gr0.reshape(2, 2, 4, 4, 32, PACK), early, y4, gin4, sums4
    )
    qkv_sum, out_sum, up_sum, down_sum, layer_output, gin, vg = results_call(
        info, late, early, layer_output, gin, sums4, perm
    )
    return (
        layer_output.T,
        gin.T,
        vg[4],
        vg[5],
        qkv_sum,
        out_sum.T,
        vg[0],
        vg[1],
        up_sum,
        down_sum.T,
    )


def solution(mesh):
    placed = (
        P("row", "col"),
        P("col"),
        P("col"),
        P("row", "col"),
        P("col", "row"),
        P("col"),
        P("col"),
        P("row", "col"),
        P("col", "row"),
        P("row", "col"),
    )
    return jax.shard_map(
        per_device,
        mesh=mesh,
        in_specs=placed,
        out_specs=(
            P("row", "col"),
            P("row", "col"),
            P("col"),
            P("col"),
            P("row", "col"),
            P("col", "row"),
            P("col"),
            P("col"),
            P("row", "col"),
            P("col", "row"),
        ),
        check_vma=False,
    )
```

```python
import math

import jax
import jax.numpy as jnp
import ml_dtypes
import numpy as np
from jax import lax
from jax.experimental import pallas as pl
from jax.experimental.pallas import tpu as pltpu
from jax.sharding import PartitionSpec as P

HEADS = 17
HEAD_DIM = 64
D = 1088
SEQ = 2048
MAIN = 1024
WIDE = 1152
PACK = 1280
QKV_COLS = 816
QUARTER = 128
PAIR = 256
KEYS = 512

gelu_coef = math.sqrt(2.0 / math.pi)
norm_epsilon = 1e-05
masked_score = -1e30
MESH = pl.DeviceIdType.MESH
F32 = jnp.float32
BF16 = jnp.bfloat16
VMEM_LIMIT = 60 * 1024 * 1024
ANY = pl.BlockSpec(memory_space=pl.ANY)
VMEM_SPEC = pl.BlockSpec(memory_space=pltpu.VMEM)
SMEM_SPEC = pl.BlockSpec(memory_space=pltpu.SMEM)

GATHER_ORDERS = (("x", "y", "z"), ("y", "z", "x"), ("z", "x", "y"))
SCATTER_ORDERS = (("z", "y", "x"), ("x", "z", "y"), ("y", "x", "z"))


def dot_nn(a, b):
    return lax.dot_general(a, b, (((1,), (0,)), ((), ())), preferred_element_type=F32)


def dot_nt(a, b):
    return lax.dot_general(a, b, (((1,), (1,)), ((), ())), preferred_element_type=F32)


class Place:
    def __init__(self):
        self.row = lax.axis_index("row")
        self.col = lax.axis_index("col")
        self.at = {
            "x": lax.rem(self.row, 4),
            "z": lax.rem(self.row // 4, 4),
            "y": (self.row // 16) * 2 + self.col // 2,
        }
        self.core = lax.rem(self.col, 2)

    def device(self, at, core):
        return ((at["y"] // 2) * 16 + at["z"] * 4 + at["x"], lax.rem(at["y"], 2) * 2 + core)

    def step(self, axis, distance):
        at = dict(self.at)
        at[axis] = lax.rem(at[axis] + distance + 4, 4)
        return self.device(at, self.core)

    def partner(self):
        return (self.row, self.col + 1 - 2 * self.core)

    def beside(self, distance):
        return (self.row, lax.rem(self.col + distance, 4))

    def neighbours(self):
        found = [self.step(axis, d) for axis in ("x", "y", "z") for d in (1, -1)]
        found.append(self.partner())
        other = lax.rem(self.col // 2 + 1, 2)
        found.append((self.row, other * 2 + 1 - self.core))
        return found


def greet(devices):
    barrier = pltpu.get_barrier_semaphore()
    for device in devices:
        pl.semaphore_signal(barrier, inc=1, device_id=device, device_id_type=MESH)
    pl.semaphore_wait(barrier, len(devices))


def everything():
    return slice(None)


def place_index(fixed):
    if "y" in fixed:
        y_lo, y_hi = lax.rem(fixed["y"], 2), fixed["y"] // 2
    else:
        y_lo, y_hi = everything(), everything()
    return (y_lo, y_hi, fixed.get("z", everything()), fixed.get("x", everything()))


def remote(source, target, ssem, rsem, device):
    return pltpu.make_async_remote_copy(
        src_ref=source, dst_ref=target, send_sem=ssem, recv_sem=rsem,
        device_id=device, device_id_type=MESH,
    )


def gather_kernel(
    w_qkv, w_out_t, w_up, w_down_t, v_ref, x_ref, g_ref,
    all0, all1, all2, x_out, g_out, v_out,
    block0, block1, block2, full, tile,
    send, recv, last_send, last_recv, local, in_send, in_recv, in_local,
):
    me = Place()
    blocks = (block0, block1, block2)
    wholes = (all0, all1, all2)
    full[...] = jnp.zeros_like(full)
    tile[...] = jnp.zeros_like(tile)
    for piece, sources in enumerate(((w_qkv, w_out_t), (w_up,), (w_down_t,))):
        lane = 0
        for source in sources:
            full[0:34, lane : lane + source.shape[1]] = source[...].astype(F32)
            lane += source.shape[1]
        blocks[piece][:, :WIDE] = full[0:32, :].astype(BF16)
        for j in range(2):
            for n in range(9):
                tile[9 * j + n : 9 * j + n + 1, :] = full[32 + j : 33 + j, 128 * n : 128 * n + 128]
        blocks[piece][:, WIDE:] = tile[...].astype(BF16)
    greet(me.neighbours())

    def region(piece, fixed, rows=None):
        index = place_index(fixed) + ((everything(),) if rows is None else (pl.ds(rows, 16),))
        return wholes[piece].at[index]

    def around(piece, stage, value):
        order = GATHER_ORDERS[piece]
        fixed = {order[stage]: value}
        for axis in order[stage + 1 :]:
            fixed[axis] = me.at[axis]
        return fixed

    sent = []
    pairs = ((x_ref, x_out), (g_ref, g_out))
    waits, arrivals, own_copies = [], [], []
    for piece in range(3):
        copy = pltpu.make_async_copy(
            blocks[piece], region(piece, around(piece, 0, me.at[GATHER_ORDERS[piece][0]])), local.at[piece]
        )
        copy.start()
        own_copies.append(copy)

    def semaphores(piece, stage, n, u):
        if stage == 2:
            return last_send.at[piece, u, n], last_recv.at[piece, u, n]
        return send.at[piece, stage, n], recv.at[piece, stage, n]

    def part(piece, stage, value, u, rows=None):
        fixed = around(piece, stage, value)
        if stage == 2:
            axis = GATHER_ORDERS[piece][1]
            fixed[axis] = lax.rem(me.at[axis] + (0, 3, 1, 2)[u], 4)
        return region(piece, fixed, rows)

    def begin(piece, stage, u=0):
        axis = GATHER_ORDERS[piece][stage]
        mine = part(piece, stage, me.at[axis], u)
        source = blocks[piece] if stage == 0 else mine
        for n, distance in enumerate((1, -1)):
            copy = remote(source, mine, *semaphores(piece, stage, n, u), me.step(axis, distance))
            copy.start()
            sent.append(copy)

    def arrived(piece, stage, n, u=0):
        axis = GATHER_ORDERS[piece][stage]
        value = lax.rem(me.at[axis] + (3, 1, 2, 2)[n], 4)
        there = part(piece, stage, value, u, (None, None, 0, 16)[n])
        remote(there, there, *semaphores(piece, stage, n, u), me.step(axis, 1)).wait_recv()
        if n < 2:
            half = part(piece, stage, value, u, (0, 16)[n])
            copy = remote(half, half, *semaphores(piece, stage, 2 + n, u), me.step(axis, (1, -1)[n]))
            copy.start()
            sent.append(copy)

    for piece in range(3):
        begin(piece, 0)
    partner, across = me.partner(), me.beside(2)

    def tokens_of(ref, col):
        return ref.at[:, pl.ds(pl.multiple_of(col // 2 * PAIR, PAIR), PAIR)]

    relays = []
    for n, (source, target) in enumerate(pairs + ((v_ref, v_out),)):
        here, there = (v_ref, v_ref) if n == 2 else (tokens_of(source, me.col), tokens_of(source, across[1]))
        own = pltpu.make_async_copy(here, target.at[me.col], in_local.at[n])
        own.start()
        waits.append(own)
        for k, (part_ref, device) in enumerate(((there, across), (here, partner))):
            copy = remote(part_ref, target.at[me.col], in_send.at[n, k], in_recv.at[n, k], device)
            copy.start()
            sent.append(copy)
        relays.append(remote(there, target.at[across[1]], in_send.at[n, 0], in_recv.at[n, 0], across))
        arrivals.append(remote(here, target.at[partner[1]], in_send.at[n, 1], in_recv.at[n, 1], partner))
    for copy in own_copies:
        copy.wait()
    for n in range(4):
        for piece in range(3):
            arrived(piece, 0, n)
    for piece in range(3):
        begin(piece, 1)
    for n, (_, target) in enumerate(pairs + ((v_ref, v_out),)):
        relays[n].wait_recv()
        block = target.at[across[1]]
        copy = remote(block, block, in_send.at[n, 2], in_recv.at[n, 2], partner)
        copy.start()
        sent.append(copy)
        far = target.at[lax.rem(partner[1] + 2, 4)]
        arrivals.append(remote(far, far, in_send.at[n, 2], in_recv.at[n, 2], partner))
    for piece in range(3):
        begin(piece, 2, 0)
    for n in range(4):
        for piece in range(3):
            arrived(piece, 1, n)
            if n < 2:
                begin(piece, 2, n + 1)
            elif n == 3:
                begin(piece, 2, 3)
    for n in (0, 1):
        for piece in range(3):
            arrived(piece, 2, n, 0)
    for u in range(1, 4):
        for n in (0, 1):
            for piece in range(3):
                arrived(piece, 2, n, u)
    for u in range(4):
        for n in (2, 3):
            for piece in range(3):
                arrived(piece, 2, n, u)
    for copy in arrivals:
        copy.wait_recv()
    for copy in waits:
        copy.wait()
    for copy in sent:
        copy.wait_send()


def gather_all(*args):
    whole = jax.ShapeDtypeStruct((2, 2, 4, 4, 32, PACK), BF16)
    tokens = jax.ShapeDtypeStruct((4, 272, PAIR), BF16)
    return pl.pallas_call(
        gather_kernel,
        out_shape=(whole, whole, whole, tokens, tokens, jax.ShapeDtypeStruct((4, 8, 272), F32)),
        in_specs=[VMEM_SPEC] * 5 + [ANY] * 2,
        out_specs=(ANY,) * 6,
        scratch_shapes=[
            pltpu.VMEM((32, PACK), BF16), pltpu.VMEM((32, PACK), BF16), pltpu.VMEM((32, PACK), BF16),
            pltpu.VMEM((40, WIDE), F32), pltpu.VMEM((32, 128), F32),
            pltpu.SemaphoreType.DMA((3, 2, 4)),
            pltpu.SemaphoreType.DMA((3, 2, 4)),
            pltpu.SemaphoreType.DMA((3, 4, 4)),
            pltpu.SemaphoreType.DMA((3, 4, 4)),
            pltpu.SemaphoreType.DMA((3,)),
            pltpu.SemaphoreType.DMA((3, 3)),
            pltpu.SemaphoreType.DMA((3, 3)),
            pltpu.SemaphoreType.DMA((3,)),
        ],
        compiler_params=pltpu.CompilerParams(collective_id=0, has_side_effects=True),
        name="gather_weights",
    )(*args)


class Group:
    def __init__(self):
        self.row, self.col = lax.axis_index("row"), lax.axis_index("col")
        self.in_group = lax.rem(self.row + 2, 4)
        self.rank = self.in_group * 4 + self.col
        self.pair, self.core = self.rank // 2, lax.rem(self.col, 2)
        self.partner = (self.row, self.col + 1 - 2 * self.core)

    def device(self, other):
        return (lax.rem(self.row - self.in_group + other // 4 + 32, 32), lax.rem(other, 4))

    def greet(self):
        greet([self.device(lax.rem(self.rank + d, 16)) for d in range(1, 16)])

    def all_to_all(self, source, target, send, recv, local):
        own = pltpu.make_async_copy(source.at[self.rank], target.at[self.rank], local)
        own.start()
        sent, arrivals = [], []
        for d in range(1, 16):
            other = lax.rem(self.rank + d, 16)
            copy = remote(source.at[other], target.at[self.rank], send.at[d], recv.at[d], self.device(other))
            copy.start()
            sent.append(copy)
            origin = lax.rem(self.rank + 16 - d, 16)
            arrivals.append(remote(source.at[other], target.at[origin], send.at[d], recv.at[d], self.device(origin)))
        return own, sent, arrivals

    def finish(self, own, sent, arrivals):
        for copy in arrivals:
            copy.wait_recv()
        for copy in sent:
            copy.wait_send()
        own.wait()

    def relay(self, source_of, target, send, recv, local):
        own = pltpu.make_async_copy(source_of(self.pair), target.at[self.rank], local)
        own.start()
        beside = remote(source_of(self.pair), target.at[self.rank], send.at[0, 0], recv.at[0, 0], self.partner)
        beside.start()
        sent = [beside]
        for e in range(1, 8):
            other = lax.rem(self.pair + e, 8)
            copy = remote(
                source_of(other), target.at[self.rank], send.at[0, e], recv.at[0, e], self.device(other * 2 + self.core)
            )
            copy.start()
            sent.append(copy)
        return own, sent

    def pass_on(self, own, sent, target, send, recv):
        for e in range(1, 8):
            origin = lax.rem(self.pair + 8 - e, 8) * 2 + self.core
            block = target.at[origin]
            remote(block, block, send.at[0, e], recv.at[0, e], self.device(origin)).wait_recv()
            copy = remote(block, block, send.at[1, e], recv.at[1, e], self.partner)
            copy.start()
            sent.append(copy)
        for e in range(0, 8):
            block = target.at[lax.rem(self.pair + 8 - e, 8) * 2 + 1 - self.core]
            n = 0 if e == 0 else 1
            remote(block, block, send.at[n, e], recv.at[n, e], self.partner).wait_recv()
        for copy in sent:
            copy.wait_send()
        own.wait()


RELAY = [pltpu.SemaphoreType.DMA((2, 8)), pltpu.SemaphoreType.DMA((2, 8)), pltpu.SemaphoreType.DMA]
DIRECT = [pltpu.SemaphoreType.DMA((16,)), pltpu.SemaphoreType.DMA((16,)), pltpu.SemaphoreType.DMA]


def exchange_call(kernel, name, collective_id, outs, scratch, *args, in_specs=None):
    return pl.pallas_call(
        kernel,
        out_shape=outs,
        in_specs=in_specs or [ANY] * len(args),
        out_specs=(ANY,) * len(outs),
        scratch_shapes=scratch,
        compiler_params=pltpu.CompilerParams(collective_id=collective_id, has_side_effects=True),
        name=name,
    )(*args)


def qkv_exchange_kernel(source, last, target, last_out, send, recv, local, rsend, rrecv, rlocal):
    group = Group()
    group.greet()
    relayed = group.relay(lambda p: last, last_out, rsend, rrecv, rlocal)
    direct = group.all_to_all(source, target, send, recv, local)
    group.pass_on(*relayed, last_out, rsend, rrecv)
    group.finish(*direct)


def qkv_exchange(source, last):
    outs = (jax.ShapeDtypeStruct((16, 192, 128), BF16), jax.ShapeDtypeStruct((16, QUARTER, 128), BF16))
    return exchange_call(qkv_exchange_kernel, "exchange_qkv", 1, outs, DIRECT + RELAY, source, last)


def mixed_exchange_kernel(source, last, target, last_out, send, recv, local, last_send, last_recv, last_local):
    group = Group()
    group.greet()
    relayed = group.relay(lambda p: source.at[p], target, send, recv, local)
    own = pltpu.make_async_copy(last, last_out.at[group.core], last_local)
    own.start()
    copy = remote(last, last_out.at[group.core], last_send, last_recv, group.partner)
    copy.start()
    group.pass_on(*relayed, target, send, recv)
    remote(last, last_out.at[1 - group.core], last_send, last_recv, group.partner).wait_recv()
    copy.wait_send()
    own.wait()


def mixed_exchange(source, last):
    outs = (jax.ShapeDtypeStruct((16, 128, 128), BF16), jax.ShapeDtypeStruct((2, QUARTER, 64), BF16))
    return exchange_call(
        mixed_exchange_kernel, "exchange_mixed", 2, outs, RELAY + [pltpu.SemaphoreType.DMA] * 3, source, last
    )


def free_axes(fixed):
    return [axis for axis in ("y", "z", "x") if axis not in fixed]


def buffer_shape(fixed, rows, width):
    shape = ()
    for axis in free_axes(fixed):
        shape = shape + ((2, 2) if axis == "y" else (4,))
    return shape + (rows, width)


def buffer_index(at):
    index = ()
    for axis in ("y", "z", "x"):
        if axis in at:
            index = index + ((lax.rem(at[axis], 2), at[axis] // 2) if axis == "y" else (at[axis],))
    return index


VECTOR_AXES = ("z", "x", "y")
CHUNKS = (2, 1, 3, 0)


class Reduction:
    def __init__(self, me, source, widths, scratch, out):
        self.me, self.source, self.widths, self.out = me, source, widths, out
        self.offsets = (0, widths[0], widths[0] + widths[1])
        self.sums = scratch[0:3]
        self.halves, self.fulls = {}, {}
        position = 3
        for piece in range(3):
            for stage in range(3):
                self.halves[piece, stage] = scratch[position : position + 2]
                self.fulls[piece, stage] = scratch[position + 2 : position + 4]
                position += 4
        self.local, self.big_send, self.big_recv, self.send, self.recv = scratch[position : position + 5]
        self.sent, self.loads = [], {}

    @staticmethod
    def scratch(widths, first_stage=0):
        found = [pltpu.VMEM((2, 2, 4, 4, 32, width), BF16) for width in widths]
        for piece in range(3):
            order = SCATTER_ORDERS[piece]
            for stage in range(3):
                if stage < first_stage:
                    found += [pltpu.VMEM((16, 128), BF16)] * 4
                    continue
                fixed = order[: stage + 1]
                found += [pltpu.VMEM(buffer_shape(fixed, 16, widths[piece]), BF16) for _ in range(2)]
                found += [pltpu.VMEM(buffer_shape(fixed, 32, widths[piece]), BF16) for _ in range(2)]
        found += [pltpu.SemaphoreType.DMA((3, 4, 4))] * 3 + [pltpu.SemaphoreType.DMA((3, 2, 4))] * 2
        return found

    def shifted(self, axis, distance):
        return lax.rem(self.me.at[axis] + distance, 4)

    def load_all(self):
        for k in range(4):
            for u in range(4):
                for piece in range(3):
                    first, second = SCATTER_ORDERS[piece][:2]
                    index = place_index(
                        {first: self.shifted(first, CHUNKS[k]), second: self.shifted(second, CHUNKS[u])}
                    )
                    lanes = pl.ds(self.offsets[piece], self.widths[piece])
                    load = pltpu.make_async_copy(
                        self.source.at[index + (everything(), lanes)], self.sums[piece].at[index],
                        self.local.at[piece, k, u],
                    )
                    load.start()
                    self.loads[piece, k, u] = load

    def stage_fixed(self, piece, stage):
        return {axis: self.me.at[axis] for axis in SCATTER_ORDERS[piece][:stage]}

    def each_tile(self, fixed, body):
        axes = free_axes(fixed)
        count = 4 ** len(axes)
        if count == 1:
            body({})
            return

        @pl.loop(0, count)
        def _(t):
            body({axes[0]: t})

    def chunk(self, piece, stage, u):
        if stage > 0:
            return {}
        axis = SCATTER_ORDERS[piece][1]
        return {axis: self.shifted(axis, CHUNKS[u])}

    def sems(self, piece, stage, n, u):
        if stage == 0:
            return self.big_send.at[piece, u, n], self.big_recv.at[piece, u, n]
        return self.send.at[piece, stage - 1, n], self.recv.at[piece, stage - 1, n]

    def part_of(self, buffer, piece, stage, u):
        if stage > 0:
            return buffer
        axis = SCATTER_ORDERS[piece][1]
        value = self.shifted(axis, CHUNKS[u])
        index = ()
        for name in free_axes({SCATTER_ORDERS[piece][0]: 0}):
            if name == "y":
                index += (lax.rem(value, 2), value // 2) if name == axis else (everything(), everything())
            else:
                index += (value,) if name == axis else (everything(),)
        return buffer.at[index]

    def start(self, source, target, semaphores, axis, n):
        copy = remote(source, target, *semaphores, self.me.step(axis, (1, -1)[n]))
        copy.start()
        self.sent.append(copy)

    def wait(self, there, semaphores, axis):
        remote(there, there, *semaphores, self.me.step(axis, 1)).wait_recv()

    def begin(self, piece, stage, u=0):
        if stage == 0:
            self.loads[piece, 0, u].wait()
        axis = SCATTER_ORDERS[piece][stage]
        fixed = {**self.stage_fixed(piece, stage), axis: self.shifted(axis, 2), **self.chunk(piece, stage, u)}
        for n in range(2):
            self.start(
                self.sums[piece].at[place_index(fixed) + (pl.ds(16 * n, 16),)],
                self.part_of(self.halves[piece, stage][n], piece, stage, u), self.sems(piece, stage, n, u), axis, n,
            )

    def middle(self, piece, stage, n, u=0):
        if stage == 0:
            self.loads[piece, 1 + n, u].wait()
        axis = SCATTER_ORDERS[piece][stage]
        more = self.chunk(piece, stage, u)
        fixed = {**self.stage_fixed(piece, stage), axis: self.shifted(axis, (1, 3)[n]), **more}
        half, sums = self.halves[piece, stage][n], self.sums[piece]
        self.wait(self.part_of(half, piece, stage, u), self.sems(piece, stage, n, u), axis)

        def body(at):
            index = place_index({**fixed, **at}) + (pl.ds(16 * n, 16),)
            total = sums[index].astype(F32) + half[buffer_index({**more, **at})].astype(F32)
            sums[index] = total.astype(BF16)

        self.each_tile(fixed, body)
        self.start(
            sums.at[place_index(fixed)], self.part_of(self.fulls[piece, stage][n], piece, stage, u),
            self.sems(piece, stage, 2 + n, u), axis, n,
        )

    def finish(self, piece, stage, u=0):
        if stage == 0:
            self.loads[piece, 3, u].wait()
        axis = SCATTER_ORDERS[piece][stage]
        more = self.chunk(piece, stage, u)
        fixed = {**self.stage_fixed(piece, stage), axis: self.me.at[axis], **more}
        first, second = self.fulls[piece, stage]
        sums = self.sums[piece]
        for n, buffer in enumerate((first, second)):
            self.wait(self.part_of(buffer, piece, stage, u), self.sems(piece, stage, 2 + n, u), axis)

        def body(at):
            index = place_index({**fixed, **at})
            if stage == 2:
                total = sums[index].astype(F32) + (first[...].astype(F32) + second[...].astype(F32))
                self.out[:, self.offsets[piece] : self.offsets[piece] + self.widths[piece]] = total
            else:
                place = buffer_index({**more, **at})
                total = sums[index].astype(F32) + (first[place].astype(F32) + second[place].astype(F32))
                sums[index] = total.astype(BF16)

        self.each_tile(fixed, body)

    def begin_chunk(self, u):
        for piece in range(3):
            self.begin(piece, 0, u)

    def middle_chunk(self, u):
        for n in range(2):
            for piece in range(3):
                self.middle(piece, 0, n, u)

    def own_part(self, piece):
        first = SCATTER_ORDERS[piece][0]
        return self.sums[piece].at[place_index({first: self.me.at[first]})]

    def store_first_stage(self, targets):
        copies = []
        for piece in range(3):
            copy = pltpu.make_async_copy(self.own_part(piece), targets[piece], self.local.at[piece, 0, 0])
            copy.start()
            copies.append(copy)
        for copy in copies:
            copy.wait()

    def load_first_stage(self, sources):
        for piece in range(3):
            load = pltpu.make_async_copy(sources[piece], self.own_part(piece), self.local.at[piece, 0, 0])
            load.start()
            self.loads[piece] = load

    def second_stage(self, step):
        for piece in range(3):
            if step == 0:
                self.loads[piece].wait()
                self.begin(piece, 1)
            elif step < 3:
                self.middle(piece, 1, step - 1)
            else:
                self.finish(piece, 1)
                self.begin(piece, 2)

    def finish_chunk(self, u):
        for piece in range(3):
            self.finish(piece, 0, u)
            if u == 0:
                self.begin(piece, 1)
            elif u < 3:
                self.middle(piece, 1, u - 1)
            else:
                self.finish(piece, 1)
                self.begin(piece, 2)

    def finish_all(self):
        for n in range(2):
            for piece in range(3):
                self.middle(piece, 2, n)
        for piece in range(3):
            self.finish(piece, 2)

    def wait_sent(self):
        for copy in self.sent:
            copy.wait_send()


def unpack_rows(packed, first, target):
    target[0:32, :] = packed[:, first : first + target.shape[1]]
    for j in range(2):
        for n in range(9):
            width = min(128, target.shape[1] - 128 * n)
            target[32 + j : 33 + j, 128 * n : 128 * n + width] = packed[
                9 * j + n : 9 * j + n + 1, first + WIDE : first + WIDE + width
            ]


LATE_WIDTHS = (512, 512, 256)
EARLY_WIDTHS = (1024, 512, 1024)


def scatter_kernel(
    source, y_ref, gin_ref, v_ref, out_ref, y_out, gin_out, v_out, *scratch
):
    me = Place()
    vectors = scratch[0:3]
    out_send, out_recv, out_local, v_send, v_recv = scratch[3:8]
    reduction = Reduction(me, source, LATE_WIDTHS, scratch[8:], out_ref)
    greet(me.neighbours() + [me.step(axis, 2) for axis in VECTOR_AXES])
    sent = []
    reduction.load_all()

    def vectors_begin(phase, value):
        axis = VECTOR_AXES[phase]
        mine = vectors[phase].at[me.at[axis]]
        mine[...] = value
        for distance in (1, 2, 3):
            copy = remote(
                mine, mine, v_send.at[phase, distance - 1], v_recv.at[phase, distance - 1], me.step(axis, distance)
            )
            copy.start()
            sent.append(copy)

    def vectors_end(phase):
        axis = VECTOR_AXES[phase]
        for distance in (1, 2, 3):
            there = vectors[phase].at[lax.rem(me.at[axis] + 4 - distance, 4)]
            remote(
                there, there, v_send.at[phase, distance - 1], v_recv.at[phase, distance - 1], me.step(axis, distance)
            ).wait_recv()
        buffer = vectors[phase]
        return (buffer[0] + buffer[1]) + (buffer[2] + buffer[3])

    reduction.begin_chunk(0)
    vectors_begin(0, v_ref[...])
    reduction.begin_chunk(1)
    pairs = ((y_ref, y_out), (gin_ref, gin_out))
    arrivals, own_copies = [], []
    for n, (source, target) in enumerate(pairs):
        rows = pl.ds(pl.multiple_of(me.col * QUARTER, QUARTER), QUARTER)
        own = pltpu.make_async_copy(source.at[me.col], target.at[:, rows], out_local.at[n])
        own.start()
        own_copies.append(own)
        for distance in (1, 2, 3):
            peer = me.beside(distance)
            semaphore = (out_send.at[n, distance - 1], out_recv.at[n, distance - 1])
            copy = remote(source.at[peer[1]], target.at[:, rows], *semaphore, peer)
            copy.start()
            sent.append(copy)
            origin = pl.ds(pl.multiple_of(lax.rem(me.col + 4 - distance, 4) * QUARTER, QUARTER), QUARTER)
            arrivals.append(remote(source.at[me.col], target.at[:, origin], *semaphore, peer))
    for u in range(4):
        reduction.middle_chunk(u)
        if u < 2:
            reduction.begin_chunk(u + 2)
            vectors_begin(u + 1, vectors_end(u))
        if u == 3:
            v_out[...] = vectors_end(2)
        if u > 0:
            reduction.finish_chunk(u - 1)
    reduction.finish_chunk(3)
    reduction.finish_all()
    for copy in arrivals:
        copy.wait_recv()
    for copy in own_copies:
        copy.wait()
    for copy in sent:
        copy.wait_send()
    reduction.wait_sent()


def scatter_all(part, y4, gin4, vectors):
    scratch = [pltpu.VMEM((4, 8, WIDE), F32) for _ in range(3)]
    scratch += [
        pltpu.SemaphoreType.DMA((2, 3)),
        pltpu.SemaphoreType.DMA((2, 3)),
        pltpu.SemaphoreType.DMA((2,)),
        pltpu.SemaphoreType.DMA((3, 3)),
        pltpu.SemaphoreType.DMA((3, 3)),
    ]
    back = jax.ShapeDtypeStruct((272, 512), BF16)
    return pl.pallas_call(
        scatter_kernel,
        out_shape=(
            jax.ShapeDtypeStruct((32, PACK), F32), back, back,
            jax.ShapeDtypeStruct((8, WIDE), F32),
        ),
        in_specs=[ANY] * 3 + [VMEM_SPEC],
        out_specs=(VMEM_SPEC, ANY, ANY, VMEM_SPEC),
        scratch_shapes=scratch + Reduction.scratch(LATE_WIDTHS),
        compiler_params=pltpu.CompilerParams(
            collective_id=3, has_side_effects=True, vmem_limit_bytes=VMEM_LIMIT
        ),
        name="scatter_gradients",
    )(part, y4, gin4, vectors)


def results_kernel(
    info, late, early, y_ref, gin_ref, sums, perm, qkv_out, out_out, up_out, down_out, y_out, gin_out, v_out, full
):
    unpack_rows(late, 0, full)
    qkv_out[...] = full[:, 0:QKV_COLS]
    out_out[...] = full[:, QKV_COLS:D]
    unpack_rows(early, 0, up_out)
    unpack_rows(early, PACK, down_out)
    y_out[...] = y_ref[...]
    gin_out[...] = gin_ref[...].astype(F32)
    own = perm[lax.rem(info[0], 4)]
    left = sums[...]
    total = jnp.zeros((8, 272), F32)
    for _ in range(3):
        part = left.astype(BF16)
        left = left - part.astype(F32)
        total += dot_nt(part, own)
    v_out[...] = total


def results_call(*args):
    return pl.pallas_call(
        results_kernel,
        out_shape=(
            jax.ShapeDtypeStruct((34, QKV_COLS), F32), jax.ShapeDtypeStruct((34, D - QKV_COLS), F32),
            jax.ShapeDtypeStruct((34, D), F32), jax.ShapeDtypeStruct((34, D), F32),
            jax.ShapeDtypeStruct((272, 512), BF16), jax.ShapeDtypeStruct((272, 512), F32),
            jax.ShapeDtypeStruct((8, 272), F32),
        ),
        in_specs=[SMEM_SPEC] + [VMEM_SPEC] * 6,
        out_specs=(VMEM_SPEC,) * 7,
        scratch_shapes=[pltpu.VMEM((34, D), F32)],
        compiler_params=pltpu.CompilerParams(vmem_limit_bytes=VMEM_LIMIT),
        name="write_results",
    )(*args)


def unpack_tail(packed, tiles, wide, tail):
    tiles[...] = packed[:, WIDE:PACK].astype(F32)
    for j in range(2):
        for s in range(9):
            wide[pl.ds(32 * j, 32), pl.ds(128 * s, 128)] = tiles[pl.ds(9 * j + s, 32, stride=32), :]
    tail[0:64, :] = wide[0:64, :].astype(BF16)


def pack_tail(tail, tiles, packed):
    for j in range(2):
        for s in range(9):
            tiles[pl.ds(9 * j + s, 32, stride=32), :] = tail[32 * j : 32 * j + 32, 128 * s : 128 * s + 128]
    packed[:, WIDE:PACK] = tiles[...].astype(BF16)


def in_features(values, packed, tail, columns):
    return dot_nn(values[:, :MAIN], packed[:, columns]) + dot_nn(values[:, MAIN:], tail[:, columns])


def add_to_features(total_t, values_t, packed, tail):
    @pl.loop(0, 4)
    def _(b):
        rows = pl.ds(pl.multiple_of(b * 256, 256), 256)
        total_t[rows, :] += dot_nn(packed[rows, :WIDE], values_t[...])

    total_t[MAIN:, :] += dot_nn(tail[...], values_t[...])


def norm_forward(x, gain, bias):
    mean = jnp.sum(x, axis=1, keepdims=True) / D
    square = jnp.sum(x * x, axis=1, keepdims=True) / D
    inverse = lax.rsqrt(square - mean * mean + norm_epsilon)
    normed = (x - mean) * inverse
    return normed, inverse, (normed * gain + bias).astype(BF16)


def norm_reverse(grad, normed, inverse, gain):
    scaled = grad * gain
    first = jnp.sum(scaled, axis=1, keepdims=True) / D
    second = jnp.sum(scaled * normed, axis=1, keepdims=True) / D
    return inverse * (scaled - first - normed * second)


def permuted(pieces, perm):
    total = dot_nn(pieces[0].astype(F32).T.astype(BF16), perm[0])
    for c in range(1, 4):
        total += dot_nn(pieces[c].astype(F32).T.astype(BF16), perm[c])
    return total


def permuted_exact(pieces, perm):
    total = jnp.zeros((8, WIDE), F32)
    for c in range(4):
        left = pieces[c]
        for _ in range(3):
            part = left.astype(BF16)
            left = left - part.astype(F32)
            total += dot_nn(part, perm[c])
    return total


def real_features(values):
    lane = lax.broadcasted_iota(jnp.int32, values.shape, 1)
    return jnp.where(lane < D, values, 0.0)


def turned(values):
    return values.astype(F32).T.astype(BF16)


def own_half(core):
    return pl.ds(pl.multiple_of(core * QUARTER, QUARTER), QUARTER)


def load_weights(source, target, semaphores):
    copies = []
    for j in range(2):
        copy = pltpu.make_async_copy(source.at[j], target.at[j], semaphores.at[j])
        copy.start()
        copies.append(copy)
    return copies


def qkv_kernel(
    x4, v4, perm, w_ref, x_out, n1_out, v_out, msg, last, q16, w, qkv, qkv_out, tiles, wide, tail, load, send, recv, local
):
    me = Place()
    partner = me.partner()
    copies = load_weights(w_ref, w, load)
    greet([partner])
    x = permuted(x4, perm)
    vectors = permuted_exact(v4, perm)
    v_out[...] = vectors
    x_out[...] = x.astype(BF16)
    _, _, normed = norm_forward(x, vectors[0:1], vectors[1:2])
    n1_out[...] = normed
    tail[...] = jnp.zeros_like(tail)
    mine, theirs = own_half(me.core), own_half(1 - me.core)
    sent, own_copies, arrivals = [], [], []
    for j in range(2):
        copies[j].wait()
        packed = w.at[j]
        unpack_tail(packed, tiles, wide, tail)

        @pl.loop(0, 3)
        def _(b):
            columns = pl.ds(pl.multiple_of(b * 384, 128), 384)
            qkv[j, :, columns] = in_features(n1_out[...], packed, tail, columns).astype(BF16)

        own = pltpu.make_async_copy(qkv.at[j, mine, :], qkv_out.at[j, me.core], local.at[j])
        own.start()
        own_copies.append(own)
        copy = remote(qkv.at[j, theirs, :], qkv_out.at[j, me.core], send.at[j], recv.at[j], partner)
        copy.start()
        sent.append(copy)
        arrivals.append(
            remote(qkv.at[j, theirs, :], qkv_out.at[j, 1 - me.core], send.at[j], recv.at[j], partner)
        )
    for copy in arrivals:
        copy.wait_recv()
    for copy in own_copies:
        copy.wait()
    for n in range(3):
        for head in range(HEADS):
            block = columns_of(qkv_out, n * D + head * HEAD_DIM, QKV_COLS, 0)
            if head == 16:
                if n == 0:
                    q16[...] = block
                else:
                    last[:, 64 * (n - 1) : 64 * n] = block
            else:
                msg[head, 64 * n : 64 * n + 64, 0:64] = block[0:64]
                msg[head, 64 * n : 64 * n + 64, 64:128] = block[64:128]
    for copy in sent:
        copy.wait_send()


def columns_of(blocks, start, width, offset):
    pieces = []
    position = start
    while position < start + HEAD_DIM:
        c = position // width
        end = min(start + HEAD_DIM, (c + 1) * width)
        first = position - c * width + offset
        pieces.append(blocks[c // 2, c % 2, :, first : first + end - position])
        position = end
    return pieces[0] if len(pieces) == 1 else jnp.concatenate(pieces, axis=1)


def qkv_call(x4, v4, perm, weights):
    row = jax.ShapeDtypeStruct((PAIR, WIDE), BF16)
    return pl.pallas_call(
        qkv_kernel,
        out_shape=(
            row, row, jax.ShapeDtypeStruct((8, WIDE), F32), jax.ShapeDtypeStruct((16, 192, 128), BF16),
            jax.ShapeDtypeStruct((QUARTER, 128), BF16), jax.ShapeDtypeStruct((QUARTER, 64), BF16),
        ),
        in_specs=[VMEM_SPEC, VMEM_SPEC, VMEM_SPEC, ANY],
        out_specs=(VMEM_SPEC,) * 6,
        scratch_shapes=[
            pltpu.VMEM((2, MAIN, PACK), BF16), pltpu.VMEM((2, PAIR, WIDE), BF16),
            pltpu.VMEM((2, 2, QUARTER, WIDE), BF16),
            pltpu.VMEM((MAIN, 128), F32), pltpu.VMEM((128, WIDE), F32), pltpu.VMEM((128, WIDE), BF16),
            pltpu.SemaphoreType.DMA((2,)), pltpu.SemaphoreType.DMA((2,)), pltpu.SemaphoreType.DMA((2,)),
            pltpu.SemaphoreType.DMA((2,)),
        ],
        compiler_params=pltpu.CompilerParams(
            collective_id=4, has_side_effects=True, vmem_limit_bytes=VMEM_LIMIT
        ),
        name="norm_and_qkv",
    )(x4, v4, perm, weights)


def gelu_both(v):
    square = v * v
    tanh_value = jnp.tanh(gelu_coef * (v + 0.044715 * v * square))
    half = 0.5 * (1.0 + tanh_value)
    value = v * half
    slope = half + 0.5 * v * (1.0 - tanh_value * tanh_value) * gelu_coef * (1.0 + 0.134145 * square)
    return value, slope


def weight_gradient(rows_t, values, tiles, tail_sum, packed):
    @pl.loop(0, 4)
    def _(b):
        rows = pl.ds(pl.multiple_of(b * 256, 256), 256)
        packed[rows, :WIDE] = dot_nn(rows_t[rows, :], values[...]).astype(BF16)

    tail_sum[...] = dot_nn(rows_t[MAIN:, :], values[...])
    pack_tail(tail_sum, tiles, packed)


def swap_start(total_t, mine, theirs, ssem, rsem, partner):
    mine[...] = total_t[...].astype(BF16)
    copy = remote(mine, theirs, ssem, rsem, partner)
    copy.start()
    return copy


def swap_end(copy, mine, theirs):
    copy.wait_recv()
    return mine[...].astype(F32) + theirs[...].astype(F32)


def middle_kernel(
    x_ref, a0, w0_ref, w1_ref, w2_ref, g4, perm, vec,
    y4, dres_out, dresb_out, gr12_out, dmsg, dlast, vec_out,
    w0, w1, w2, gr1, gr2, resid, normed2, inverse2, n2, n2_t, cot, cot_t, total_t, dn2_t, hidden, dpre, turn1, turn2,
    dmix, tiles, out_tiles, tail1, tail2, tail_sum, mine1, theirs1, mine2, theirs2, mine_y, theirs_y, dmix_out,
    load, store, send, recv, local,
):
    me = Place()
    partner = me.partner()
    loads = [load_weights(source, target, load.at[n]) for n, (source, target) in enumerate(
        ((w0_ref, w0), (w1_ref, w1), (w2_ref, w2))
    )]
    greet([partner])
    for buffer in (tail1, tail2, out_tiles, total_t, dn2_t):
        buffer[...] = jnp.zeros_like(buffer)
    for j in range(2):
        turn1[...] = turned(a0[j])
        loads[0][j].wait()
        unpack_tail(w0.at[j], tiles, tail_sum, tail1)
        add_to_features(total_t, turn1, w0.at[j], tail1)
    first = swap_start(total_t, mine1, theirs1, send.at[0], recv.at[0], partner)
    cot_value = permuted(g4, perm)
    cot[...] = cot_value.astype(BF16)
    cot_t[...] = cot_value.T.astype(BF16)
    total_t[...] = jnp.zeros_like(total_t)
    attended = swap_end(first, mine1, theirs1)
    resid[...] = x_ref[...].astype(F32) + attended.T
    normed, inverse, n2_value = norm_forward(resid[...], vec[2:3], vec[3:4])
    normed2[...] = normed
    inverse2[...] = jnp.broadcast_to(inverse, inverse2.shape)
    n2[...] = n2_value
    n2_t[...] = turned(n2_value)
    stores = []
    for j in range(2):
        loads[1][j].wait()
        loads[2][j].wait()
        up, down = w1.at[j], w2.at[j]
        unpack_tail(up, tiles, tail_sum, tail1)
        unpack_tail(down, tiles, tail_sum, tail2)

        @pl.loop(0, 3)
        def _(b):
            columns = pl.ds(pl.multiple_of(b * 384, 128), 384)
            pre = in_features(n2[...], up, tail1, columns)
            d_hidden = in_features(cot[...], down, tail2, columns)
            value, slope = gelu_both(pre)
            hidden[:, columns] = value.astype(BF16)
            dpre[:, columns] = (d_hidden * slope).astype(BF16)

        turn1[...] = turned(hidden[...])
        turn2[...] = turned(dpre[...])
        add_to_features(total_t, turn1, down, tail2)
        add_to_features(dn2_t, turn2, up, tail1)
        if j == 1:
            second = swap_start(dn2_t, mine2, theirs2, send.at[1], recv.at[1], partner)
            half = own_half(1 - me.core)
            mine_y[...] = total_t[:, half].astype(BF16)
            third = remote(mine_y, theirs_y, send.at[2], recv.at[2], partner)
            third.start()
        weight_gradient(n2_t, dpre, out_tiles, tail_sum, gr1.at[j])
        weight_gradient(cot_t, hidden, out_tiles, tail_sum, gr2.at[j])
        for n, source in enumerate((gr1, gr2)):
            copy = pltpu.make_async_copy(source.at[j], gr12_out.at[j, :, pl.ds(PACK * n, PACK)], store.at[n, j])
            copy.start()
            stores.append(copy)
    grad = swap_end(second, mine2, theirs2).T
    normed = normed2[...]
    vec_out[...] = jnp.zeros_like(vec_out)
    vec_out[0:1, :] = jnp.sum(grad * normed, axis=0, keepdims=True)
    vec_out[1:2, :] = jnp.sum(grad, axis=0, keepdims=True)
    back = cot[...].astype(F32) + norm_reverse(grad, normed, inverse2[:, 0:1], vec[2:3])
    back = real_features(back)
    dres_out[...] = back
    dresb_out[...] = back.astype(BF16)
    sent, own_copies, arrivals = [first, second, third], [], []
    columns = slice(768, WIDE)
    for j in range(2):
        unpack_tail(w0.at[j], tiles, tail_sum, tail1)
        dmix[j] = in_features(dresb_out[...], w0.at[j], tail1, columns).astype(BF16)
        own = pltpu.make_async_copy(dmix.at[j, own_half(me.core), :], dmix_out.at[j, me.core], local.at[j])
        own.start()
        own_copies.append(own)
        theirs = dmix.at[j, own_half(1 - me.core), :]
        copy = remote(theirs, dmix_out.at[j, me.core], send.at[3 + j], recv.at[3 + j], partner)
        copy.start()
        sent.append(copy)
        arrivals.append(remote(theirs, dmix_out.at[j, 1 - me.core], send.at[3 + j], recv.at[3 + j], partner))
    half = own_half(me.core)
    third.wait_recv()
    y = (resid[half, :].T + (total_t[:, half] + theirs_y[...].astype(F32))).astype(BF16)
    for c in range(4):
        y4[c] = dot_nn(perm[c], y).astype(BF16)
    for copy in arrivals:
        copy.wait_recv()
    for copy in own_copies:
        copy.wait()
    for head in range(HEADS):
        block = columns_of(dmix_out, head * HEAD_DIM, 272, QKV_COLS - 768)
        if head == 16:
            dlast[...] = block
        else:
            dmsg[head, :, 0:64] = block[0:64]
            dmsg[head, :, 64:128] = block[64:128]
    for copy in stores:
        copy.wait()
    for copy in sent:
        copy.wait_send()


def middle_call(x, a0, w0, w1, w2, g4, perm, vec):
    weights = pltpu.VMEM((2, MAIN, PACK), BF16)
    row_f, row_b = pltpu.VMEM((PAIR, WIDE), F32), pltpu.VMEM((PAIR, WIDE), BF16)
    turn_f, turn_b = pltpu.VMEM((WIDE, PAIR), F32), pltpu.VMEM((WIDE, PAIR), BF16)
    tile, tail = pltpu.VMEM((MAIN, 128), F32), pltpu.VMEM((128, WIDE), BF16)
    half = pltpu.VMEM((WIDE, QUARTER), BF16)
    return pl.pallas_call(
        middle_kernel,
        out_shape=(
            jax.ShapeDtypeStruct((4, 272, QUARTER), BF16), jax.ShapeDtypeStruct((PAIR, WIDE), F32),
            jax.ShapeDtypeStruct((PAIR, WIDE), BF16), jax.ShapeDtypeStruct((2, MAIN, 2 * PACK), BF16),
            jax.ShapeDtypeStruct((16, 64, 128), BF16), jax.ShapeDtypeStruct((QUARTER, 64), BF16),
            jax.ShapeDtypeStruct((8, WIDE), F32),
        ),
        in_specs=[VMEM_SPEC, VMEM_SPEC, ANY, ANY, ANY, VMEM_SPEC, VMEM_SPEC, VMEM_SPEC],
        out_specs=(VMEM_SPEC, VMEM_SPEC, VMEM_SPEC, ANY, VMEM_SPEC, VMEM_SPEC, VMEM_SPEC),
        scratch_shapes=[
            weights, weights, weights, weights, weights, row_f, row_f, pltpu.VMEM((PAIR, 128), F32), row_b, turn_b,
            row_b, turn_b, turn_f, turn_f, row_b, row_b, turn_b, turn_b, pltpu.VMEM((2, PAIR, 384), BF16),
            tile, tile, tail, tail, pltpu.VMEM((128, WIDE), F32), turn_b, turn_b, turn_b, turn_b, half, half,
            pltpu.VMEM((2, 2, QUARTER, 384), BF16),
            pltpu.SemaphoreType.DMA((3, 2)), pltpu.SemaphoreType.DMA((2, 2)), pltpu.SemaphoreType.DMA((5,)),
            pltpu.SemaphoreType.DMA((5,)), pltpu.SemaphoreType.DMA((2,)),
        ],
        compiler_params=pltpu.CompilerParams(
            collective_id=5, has_side_effects=True, vmem_limit_bytes=VMEM_LIMIT
        ),
        name="feed_forward",
    )(x, a0, w0, w1, w2, g4, perm, vec)


def first_kernel(
    x_ref, n1, dresb, dres, back_ref, sums16, dq16, a0, w0_ref, perm, vec, vec2, early0, early1, early2,
    gin4, gr0_out, sums, early_out,
    dq_ref, w0, gr0, dq, n1_t, dres_t, turn, dn1_t, tiles, out_tiles, tail, tail_sum, mine, theirs,
    load, store, send, recv, local, *scratch,
):
    me = Place()
    partner = me.partner()
    loads = load_weights(w0_ref, w0, load)
    early = Reduction(me, None, EARLY_WIDTHS, scratch, early_out)
    early.load_first_stage((early0, early1, early2))
    greet(me.neighbours())
    early.second_stage(0)
    mine_rows = own_half(me.core)
    dq_ref[...] = jnp.zeros_like(dq_ref)
    last = jnp.zeros((QUARTER, 128), F32)
    for p in range(8):
        last += sums16[p].astype(F32)
    last = last.astype(BF16)
    for n in range(3):
        for head in range(HEADS):
            if head == 16:
                parts = ((0, QUARTER, dq16[...] if n == 0 else last[:, 64 * (n - 1) : 64 * n]),)
            else:
                block = back_ref[head, 64 * n : 64 * n + 64, :]
                parts = ((0, 64, block[:, 0:64]), (64, 64, block[:, 64:128]))
            start = n * D + head * HEAD_DIM
            position = start
            while position < start + HEAD_DIM:
                c = position // QKV_COLS
                end = min(start + HEAD_DIM, (c + 1) * QKV_COLS)
                lane = position - c * QKV_COLS
                for row, rows, value in parts:
                    dq_ref[c % 2, c // 2, row : row + rows, lane : lane + end - position] = value[
                        :, position - start : end - start
                    ]
                position = end
    copy = remote(dq_ref.at[1 - me.core], dq.at[:, mine_rows, :], send.at[0], recv.at[0], partner)
    copy.start()
    own = pltpu.make_async_copy(dq_ref.at[me.core], dq.at[:, mine_rows, :], local)
    own.start()
    early.second_stage(1)
    early.second_stage(2)
    for buffer in (tail, out_tiles, dn1_t):
        buffer[...] = jnp.zeros_like(buffer)
    n1_t[...] = turned(n1[...])
    dres_t[...] = turned(dresb[...])
    normed, inverse, _ = norm_forward(x_ref[...].astype(F32), vec[0:1], vec[1:2])
    own.wait()
    remote(
        dq_ref.at[me.core], dq.at[:, own_half(1 - me.core), :], send.at[0], recv.at[0], partner
    ).wait_recv()
    for j in range(2):
        loads[j].wait()
        unpack_tail(w0.at[j], tiles, tail_sum, tail)
        turn[...] = turned(dq[j])
        add_to_features(dn1_t, turn, w0.at[j], tail)
    early.second_stage(3)
    swap = swap_start(dn1_t, mine, theirs, send.at[1], recv.at[1], partner)
    stores = []
    for j in range(2):
        packed = gr0.at[j]

        @pl.loop(0, 4)
        def _(b):
            rows = pl.ds(pl.multiple_of(b * 256, 256), 256)
            packed[rows, :768] = dot_nn(n1_t[rows, :], dq[j, :, :768]).astype(BF16)
            packed[rows, 768:WIDE] = (
                dot_nn(n1_t[rows, :], dq[j, :, 768:]) + dot_nn(dres_t[rows, :], a0[j, :, 768:])
            ).astype(BF16)

        tail_sum[:, :768] = dot_nn(n1_t[MAIN:, :], dq[j, :, :768])
        tail_sum[:, 768:] = dot_nn(n1_t[MAIN:, :], dq[j, :, 768:]) + dot_nn(dres_t[MAIN:, :], a0[j, :, 768:])
        pack_tail(tail_sum, out_tiles, packed)
        out = pltpu.make_async_copy(packed, gr0_out.at[j], store.at[j])
        out.start()
        stores.append(out)
    for n in range(2):
        for piece in range(3):
            early.middle(piece, 2, n)
    grad = swap_end(swap, mine, theirs).T
    sums[...] = vec2[...]
    sums[4:5, :] = jnp.sum(grad * normed, axis=0, keepdims=True)
    sums[5:6, :] = jnp.sum(grad, axis=0, keepdims=True)
    back = dres[...] + norm_reverse(grad, normed, inverse, vec[0:1])
    dn1_t[...] = real_features(back).T
    back = dn1_t[:, mine_rows].astype(BF16)
    for c in range(4):
        gin4[c] = dot_nn(perm[c], back).astype(BF16)
    for piece in range(3):
        early.finish(piece, 2)
    early.wait_sent()
    for out in stores:
        out.wait()
    copy.wait_send()
    swap.wait_send()


def first_call(*args):
    weights = pltpu.VMEM((2, MAIN, PACK), BF16)
    turn_b = pltpu.VMEM((WIDE, PAIR), BF16)
    tile = pltpu.VMEM((MAIN, 128), F32)
    return pl.pallas_call(
        first_kernel,
        out_shape=(
            jax.ShapeDtypeStruct((4, 272, QUARTER), BF16), jax.ShapeDtypeStruct((2, MAIN, PACK), BF16),
            jax.ShapeDtypeStruct((8, WIDE), F32), jax.ShapeDtypeStruct((32, 2 * PACK), F32),
        ),
        in_specs=[VMEM_SPEC] * 8 + [ANY] + [VMEM_SPEC] * 3 + [ANY] * 3,
        out_specs=(VMEM_SPEC, ANY, VMEM_SPEC, VMEM_SPEC),
        scratch_shapes=[
            pltpu.VMEM((2, 2, QUARTER, WIDE), BF16),
            weights, weights, pltpu.VMEM((2, PAIR, WIDE), BF16), turn_b, turn_b, turn_b,
            pltpu.VMEM((WIDE, PAIR), F32), tile, tile, pltpu.VMEM((128, WIDE), BF16), pltpu.VMEM((128, WIDE), F32),
            turn_b, turn_b,
            pltpu.SemaphoreType.DMA((2,)), pltpu.SemaphoreType.DMA((2,)), pltpu.SemaphoreType.DMA((2,)),
            pltpu.SemaphoreType.DMA((2,)), pltpu.SemaphoreType.DMA,
        ] + Reduction.scratch(EARLY_WIDTHS, 1),
        compiler_params=pltpu.CompilerParams(
            collective_id=6, has_side_effects=True, vmem_limit_bytes=VMEM_LIMIT
        ),
        name="first_norm_back",
    )(*args)


def allowed_pairs(shape, key_start, query_start):
    key = key_start + lax.broadcasted_iota(jnp.int32, shape, 0)
    query = query_start + lax.broadcasted_iota(jnp.int32, shape, 1)
    return key <= query


def transposed(values):
    return values.astype(F32).T


def spread(block, target, row, rows=64):
    target[pl.ds(row, 64), :] = block[:, 0:64]
    target[pl.ds(row + 64, 64), :] = block[:, 64:128]


def attend_kernel(info, r_ref, kv16, q16, dense_out, o_out, o16_out, l_out, l16_out, query, key, value, value_t, value16_t):
    rank, wraps = info[0], info[1]

    @pl.loop(0, 16)
    def _(b):
        row = pl.multiple_of(b * 128, 128)
        spread(r_ref[b, 0:64, :] * jnp.asarray(0.125, BF16), query, row)
        spread(r_ref[b, 64:128, :], key, row)
        spread(r_ref[b, 128:192, :], value, row)

    @pl.loop(0, 4)
    def _(b):
        rows = pl.ds(pl.multiple_of(b * KEYS, KEYS), KEYS)
        value_t[:, rows] = transposed(value[rows, :]).astype(BF16)
        value16_t[:, rows] = transposed(kv16[rows, :])[64:128].astype(BF16)

    def step(q, k_ref, v_t, j, carry, query_start=None):
        peak, running, mixed = carry
        rows = pl.ds(pl.multiple_of(j * KEYS, KEYS), KEYS)
        scores = dot_nt(k_ref[rows, 0:64], q)
        if query_start is not None:
            scores = jnp.where(allowed_pairs(scores.shape, j * KEYS, query_start), scores, masked_score)
        new_peak = jnp.maximum(peak, jnp.max(scores, axis=0, keepdims=True))
        shrink = jnp.exp(peak - new_peak)
        weights = jnp.exp(scores - new_peak)
        running = running * shrink + jnp.sum(weights, axis=0, keepdims=True)
        mixed = mixed * shrink + dot_nn(v_t[:, rows], weights.astype(BF16))
        return new_peak, running, mixed

    def empty(width):
        return (
            jnp.full((1, width), masked_score, F32), jnp.zeros((1, width), F32), jnp.zeros((64, width), F32)
        )

    @pl.loop(0, 4)
    def _(i):
        rows = pl.ds(pl.multiple_of(i * KEYS, KEYS), KEYS)
        q = query[rows, :]
        start = jnp.where((wraps == 1) & (i >= 2), 2, 0)
        carry = lax.fori_loop(
            start, i, lambda j, carry: step(q, key, value_t, j, carry), empty(KEYS)
        )
        peak, running, mixed = step(q, key, value_t, i, carry, i * KEYS)
        result = (mixed / running).T.astype(BF16)
        o_out[rows, :] = result
        for n in range(4):
            dense_out[2 * i + n // 2, :, 64 * (n % 2) : 64 * (n % 2) + 64] = result[128 * n : 128 * n + 128]
        l_out[:, rows] = peak + jnp.log(running)

    q = q16[...] * jnp.asarray(0.125, BF16)
    start = jnp.where((wraps == 1) & (rank >= 8), 2, 0)
    peak, running, mixed = lax.fori_loop(
        start, rank // 4 + 1,
        lambda j, carry: step(q, kv16, value16_t, j, carry, rank * QUARTER), empty(QUARTER),
    )
    o16_out[...] = (mixed / running).T.astype(BF16)
    l16_out[...] = peak + jnp.log(running)


def attend_call(info, r, kv16, q16):
    tokens = jax.ShapeDtypeStruct((SEQ, 64), BF16)
    return pl.pallas_call(
        attend_kernel,
        out_shape=(
            jax.ShapeDtypeStruct((8, 128, 128), BF16), tokens, jax.ShapeDtypeStruct((QUARTER, 64), BF16),
            jax.ShapeDtypeStruct((1, SEQ), F32), jax.ShapeDtypeStruct((1, QUARTER), F32), tokens, tokens, tokens,
        ),
        in_specs=[SMEM_SPEC, VMEM_SPEC, VMEM_SPEC, VMEM_SPEC],
        out_specs=(VMEM_SPEC,) * 8,
        scratch_shapes=[pltpu.VMEM((64, SEQ), BF16), pltpu.VMEM((64, SEQ), BF16)],
        compiler_params=pltpu.CompilerParams(vmem_limit_bytes=VMEM_LIMIT),
        name="attend_forward",
    )(info, r, kv16, q16)


def attend_back_kernel(
    dmsg, gradients, query, key, value, kv16, q16, o_ref, o16, do16, l_ref, l16,
    back_out, sums_out, dq16_out, early0, early1, early2,
    do_dense, msg, part16, theirs, summed, do_ref, key_t, key16_t, delta, dq_t,
    send1, recv1, local1, send2, recv2, local2, swap_send, swap_recv, psend, precv, plocal, *scratch,
):
    me, group = Place(), Group()
    rank = group.rank
    wraps = (group.row < 2) | (group.row >= 30)
    reduction = Reduction(me, gradients, EARLY_WIDTHS, scratch, None)
    greet([group.device(lax.rem(rank + d, 16)) for d in range(1, 16)] + me.neighbours())
    first = group.all_to_all(dmsg, do_dense, send1, recv1, local1)
    reduction.load_all()
    reduction.begin_chunk(0)

    @pl.loop(0, 4)
    def _(b):
        rows = pl.ds(pl.multiple_of(b * KEYS, KEYS), KEYS)
        key_t[:, rows] = transposed(key[rows, :]).astype(BF16)
        key16_t[:, rows] = transposed(kv16[rows, :])[0:64].astype(BF16)
        dq_t[:, rows] = jnp.zeros((64, KEYS), F32)

    group.finish(*first)
    for u in (1, 2, 3):
        reduction.begin_chunk(u)

    @pl.loop(0, 16)
    def _(b):
        spread(do_dense[b], do_ref, pl.multiple_of(b * 128, 128))

    @pl.loop(0, 4)
    def _(b):
        rows = pl.ds(pl.multiple_of(b * KEYS, KEYS), KEYS)
        product = do_ref[rows, :].astype(F32) * o_ref[rows, :].astype(F32)
        delta[:, rows] = jnp.sum(product.T, axis=0, keepdims=True)

    def put(section, j, result):
        for n in range(4):
            for half in range(2):
                msg[4 * j + n, 64 * section : 64 * section + 64, 64 * half : 64 * half + 64] = result[
                    128 * n + 64 * half : 128 * n + 64 * half + 64
                ]

    def pair(keys, values, q, d_out, log_total, delta_row, mask):
        scores = dot_nt(keys, q)
        probs = jnp.exp(scores - log_total)
        if mask is not None:
            probs = jnp.where(mask(scores.shape), probs, 0.0)
        probs = probs.astype(BF16)
        d_prob = dot_nt(values, d_out)
        d_scores = (probs.astype(F32) * (d_prob - delta_row)).astype(BF16)
        return dot_nn(d_scores, q), dot_nn(probs, d_out), d_scores

    def key_block(j):
        rows = pl.ds(pl.multiple_of(j * KEYS, KEYS), KEYS)
        keys, values = key[rows, :], value[rows, :]

        def step(i, carry, mask=None):
            d_key, d_value = carry
            at = pl.ds(pl.multiple_of(i * KEYS, KEYS), KEYS)
            more_key, more_value, d_scores = pair(
                keys, values, query[at, :], do_ref[at, :], l_ref[:, at], delta[:, at], mask
            )
            dq_t[:, at] += dot_nn(key_t[:, rows], d_scores)
            return d_key + more_key, d_value + more_value

        zero = jnp.zeros((KEYS, 64), F32)
        carry = step(j, (zero, zero), lambda shape: allowed_pairs(shape, 0, 0))
        end = jnp.where(wraps & (j < 2), 2, 4)
        d_key, d_value = lax.fori_loop(j + 1, end, step, carry)
        put(1, j, d_key.astype(BF16))
        put(2, j, d_value.astype(BF16))

    q = q16[...] * jnp.asarray(0.125, BF16)
    d_out16 = do16[...]
    delta16 = jnp.sum((d_out16.astype(F32) * o16[...].astype(F32)).T, axis=0, keepdims=True)
    start = jnp.where(wraps & (rank >= 8), 2, 0)

    def last_step(j, dq):
        rows = pl.ds(pl.multiple_of(j * KEYS, KEYS), KEYS)
        d_key, d_value, d_scores = pair(
            kv16[rows, 0:64], kv16[rows, 64:128], q, d_out16, l16[...], delta16,
            lambda shape: allowed_pairs(shape, j * KEYS, rank * QUARTER),
        )
        for n in range(4):
            block = part16.at[2 * j + n // 2, n % 2]
            block[:, 0:64] = d_key[128 * n : 128 * n + 128].astype(BF16)
            block[:, 64:128] = d_value[128 * n : 128 * n + 128].astype(BF16)
        return dq + dot_nn(key16_t[:, rows], d_scores)

    part16[...] = jnp.zeros_like(part16)
    dq = lax.fori_loop(start, rank // 4 + 1, last_step, jnp.zeros((64, QUARTER), F32))
    dq16_out[...] = (dq * 0.125).T.astype(BF16)
    swap = remote(part16.at[:, 1 - group.core], theirs, swap_send, swap_recv, group.partner)
    swap.start()

    @pl.loop(0, 2)
    def _(j):
        key_block(j)

    reduction.middle_chunk(0)

    @pl.loop(2, 4)
    def _(j):
        key_block(j)

    @pl.loop(0, 4)
    def _(j):
        rows = pl.ds(pl.multiple_of(j * KEYS, KEYS), KEYS)
        put(0, j, (dq_t[:, rows] * 0.125).T.astype(BF16))

    second = group.all_to_all(msg, back_out, send2, recv2, local2)
    swap.wait_recv()

    @pl.loop(0, 8)
    def _(p):
        summed[p] = (part16[p, group.core].astype(F32) + theirs[p].astype(F32)).astype(BF16)

    own = pltpu.make_async_copy(summed.at[group.pair], sums_out.at[group.pair], plocal)
    own.start()
    sent = [swap]
    for e in range(1, 8):
        other = lax.rem(group.pair + e, 8)
        copy = remote(
            summed.at[other], sums_out.at[group.pair], psend.at[e], precv.at[e], group.device(other * 2 + group.core)
        )
        copy.start()
        sent.append(copy)
    for u in range(1, 4):
        reduction.middle_chunk(u)
        for piece in range(3):
            reduction.finish(piece, 0, u - 1)
    for piece in range(3):
        reduction.finish(piece, 0, 3)
    reduction.store_first_stage((early0, early1, early2))
    for e in range(1, 8):
        origin = lax.rem(group.pair + 8 - e, 8)
        block = sums_out.at[origin]
        remote(block, block, psend.at[e], precv.at[e], group.device(origin * 2 + group.core)).wait_recv()
    group.finish(*second)
    for copy in sent:
        copy.wait_send()
    own.wait()
    reduction.wait_sent()


def attend_back_call(*args):
    block = pltpu.VMEM((8, QUARTER, 128), BF16)
    eight = pltpu.SemaphoreType.DMA((8,))
    one = pltpu.SemaphoreType.DMA
    return pl.pallas_call(
        attend_back_kernel,
        out_shape=(
            jax.ShapeDtypeStruct((16, 192, 128), BF16), jax.ShapeDtypeStruct((8, QUARTER, 128), BF16),
            jax.ShapeDtypeStruct((QUARTER, 64), BF16),
            *(
                jax.ShapeDtypeStruct(buffer_shape(SCATTER_ORDERS[n][:1], 32, EARLY_WIDTHS[n]), BF16)
                for n in range(3)
            ),
        ),
        in_specs=[ANY, ANY] + [VMEM_SPEC] * 10,
        out_specs=(ANY, ANY, VMEM_SPEC, ANY, ANY, ANY),
        scratch_shapes=[
            pltpu.VMEM((16, 64, 128), BF16), pltpu.VMEM((16, 192, 128), BF16), pltpu.VMEM((8, 2, QUARTER, 128), BF16),
            block, block,
            pltpu.VMEM((SEQ, 64), BF16), pltpu.VMEM((64, SEQ), BF16), pltpu.VMEM((64, SEQ), BF16),
            pltpu.VMEM((1, SEQ), F32), pltpu.VMEM((64, SEQ), F32),
        ] + DIRECT + DIRECT + [one, one, eight, eight, one] + Reduction.scratch(EARLY_WIDTHS),
        compiler_params=pltpu.CompilerParams(
            collective_id=7, has_side_effects=True, vmem_limit_bytes=VMEM_LIMIT
        ),
        name="attend_backward",
    )(*args)


def permutation():
    feature = np.arange(D)
    block, inside = feature // 34, feature % 34
    place = np.where(inside < 32, 32 * block + inside, MAIN + 32 * (inside - 32) + block)
    chosen = np.zeros((D, WIDE), np.float32)
    chosen[feature, place] = 1.0
    return jnp.asarray(chosen.reshape(4, 272, WIDE).astype(ml_dtypes.bfloat16))


def per_device(
    layer_input,
    first_norm_gain,
    first_norm_bias,
    w_qkv,
    w_out,
    second_norm_gain,
    second_norm_bias,
    w_up,
    w_down,
    gradient_of_output,
):
    row, col = lax.axis_index("row"), lax.axis_index("col")
    rank, core = (row + 2) % 4 * 4 + col, col % 2
    wraps = ((row < 2) | (row >= 30)).astype(jnp.int32)
    info = jnp.stack([rank, wraps]).astype(jnp.int32)
    perm = permutation()
    vectors = jnp.concatenate(
        [
            jnp.stack([first_norm_gain, first_norm_bias, second_norm_gain, second_norm_bias]),
            jnp.zeros((4, 272), F32),
        ]
    )
    w0, w1, w2, x4, g4, v4 = gather_all(
        w_qkv, w_out.T, w_up, w_down.T, vectors, layer_input.T, gradient_of_output.T
    )
    w0, w1, w2 = (w.reshape(2, MAIN, PACK) for w in (w0, w1, w2))
    x, n1, vec, message, last, q16 = qkv_call(x4, v4, perm, w0)
    heads, kv16 = qkv_exchange(message, last)
    kv16 = kv16.reshape(SEQ, 128)
    dense, o, o16, log_total, log16, query, key, value = attend_call(info, heads, kv16, q16)
    mixed, both16 = mixed_exchange(dense, o16)
    attn = jnp.concatenate(
        [
            mixed.reshape(16, QUARTER, 2, HEAD_DIM).transpose(2, 1, 0, 3).reshape(PAIR, 1024),
            both16.reshape(PAIR, HEAD_DIM),
        ],
        axis=1,
    ).reshape(PAIR, 2, 2, 272)
    attn = lax.dynamic_index_in_dim(attn, core, 2, keepdims=False)
    a0 = jnp.pad(attn.transpose(1, 0, 2), ((0, 0), (0, 0), (QKV_COLS, WIDE - D)))
    y4, dres, dresb, gr12, dmsg, do16, vec2 = middle_call(x, a0, w0, w1, w2, g4, perm, vec)
    back, sums16, dq16, *early = attend_back_call(
        dmsg, gr12.reshape(2, 2, 4, 4, 32, 2 * PACK), query, key, value, kv16, q16, o, o16, do16, log_total, log16
    )
    gin4, gr0, sums4, early = first_call(
        x, n1, dresb, dres, back, sums16, dq16, a0, w0, perm, vec, vec2, *early
    )
    late, layer_output, gin, sums4 = scatter_all(gr0.reshape(2, 2, 4, 4, 32, PACK), y4, gin4, sums4)
    qkv_sum, out_sum, up_sum, down_sum, layer_output, gin, vg = results_call(
        info, late, early, layer_output, gin, sums4, perm
    )
    return (
        layer_output.T,
        gin.T,
        vg[4],
        vg[5],
        qkv_sum,
        out_sum.T,
        vg[0],
        vg[1],
        up_sum,
        down_sum.T,
    )


def solution(mesh):
    placed = (
        P("row", "col"),
        P("col"),
        P("col"),
        P("row", "col"),
        P("col", "row"),
        P("col"),
        P("col"),
        P("row", "col"),
        P("col", "row"),
        P("row", "col"),
    )
    return jax.shard_map(
        per_device,
        mesh=mesh,
        in_specs=placed,
        out_specs=(
            P("row", "col"),
            P("row", "col"),
            P("col"),
            P("col"),
            P("row", "col"),
            P("col", "row"),
            P("col"),
            P("col"),
            P("row", "col"),
            P("col", "row"),
        ),
        check_vma=False,
    )
```
